32 devices in a mesh: dp: 8 (over y, x, core), tensor: 4 (over z).
Axes of the slice: x: 2, y: 2, z: 4, core: 2. Of those that a mesh axis runs over, the one named last changes fastest.
Arguments:
- tokens: bfloat16 [16384, 2048], P(('dp', 'tensor')), may hold values from -6 to 6
- cotangent: bfloat16 [16384, 2048], P(('dp', 'tensor')), may hold values from -6 to 6
- live_mask: int32 [16384], P(('dp', 'tensor')), may hold values from 0 to 1, as said below
- inward: float32 [2048, 3, 2048], P('dp', None, 'tensor')
- inward_first: float32 [2048, 3, 2048], P('dp', None, 'tensor')
- inward_second: float32 [2048, 3, 2048], P('dp', None, 'tensor'), as said below
- outward: float32 [2048, 2048], P('tensor', 'dp')
- outward_first: float32 [2048, 2048], P('tensor', 'dp')
- outward_second: float32 [2048, 2048], P('tensor', 'dp'), as said below
- widening: float32 [2048, 4, 2048], P('dp', None, 'tensor')
- widening_first: float32 [2048, 4, 2048], P('dp', None, 'tensor')
- widening_second: float32 [2048, 4, 2048], P('dp', None, 'tensor'), as said below
- narrowing: float32 [4, 2048, 2048], P(None, 'tensor', 'dp')
- narrowing_first: float32 [4, 2048, 2048], P(None, 'tensor', 'dp')
- narrowing_second: float32 [4, 2048, 2048], P(None, 'tensor', 'dp'), as said below
- column_bias: float32 [6, 2048], P(None, 'tensor'), may hold values from -4 to 4
- column_first: float32 [6, 2048], P(None, 'tensor')
- column_second: float32 [6, 2048], P(None, 'tensor'), as said below
- vectors: float32 [6, 2048], replicated
- vectors_first: float32 [6, 2048], replicated
- vectors_second: float32 [6, 2048], replicated, as said below
Outputs:
- layer_output: bfloat16 [16384, 2048], P(('dp', 'tensor'))
- token_gradient: float32 [16384, 2048], P(('dp', 'tensor'))
- new_inward: float32 [2048, 3, 2048], P('dp', None, 'tensor')
- inward_mean: float32 [2048, 3, 2048], P('dp', None, 'tensor')
- inward_square: float32 [2048, 3, 2048], P('dp', None, 'tensor')
- inward_half: bfloat16 [2048, 3, 2048], P('dp', None, 'tensor')
- new_outward: float32 [2048, 2048], P('tensor', 'dp')
- outward_mean: float32 [2048, 2048], P('tensor', 'dp')
- outward_square: float32 [2048, 2048], P('tensor', 'dp')
- outward_half: bfloat16 [2048, 2048], P('tensor', 'dp')
- new_widening: float32 [2048, 4, 2048], P('dp', None, 'tensor')
- widening_mean: float32 [2048, 4, 2048], P('dp', None, 'tensor')
- widening_square: float32 [2048, 4, 2048], P('dp', None, 'tensor')
- widening_half: bfloat16 [2048, 4, 2048], P('dp', None, 'tensor')
- new_narrowing: float32 [4, 2048, 2048], P(None, 'tensor', 'dp')
- narrowing_mean: float32 [4, 2048, 2048], P(None, 'tensor', 'dp')
- narrowing_square: float32 [4, 2048, 2048], P(None, 'tensor', 'dp')
- narrowing_half: bfloat16 [4, 2048, 2048], P(None, 'tensor', 'dp')
- new_column: float32 [6, 2048], P(None, 'tensor')
- column_mean: float32 [6, 2048], P(None, 'tensor')
- query_square: float32 [2048], P('tensor')
- value_square: float32 [2048], P('tensor')
- hidden_square: float32 [4, 2048], P(None, 'tensor')
- new_vectors: float32 [6, 2048], replicated
- vectors_mean: float32 [6, 2048], replicated
- first_square: float32 [2, 2048], replicated
- vectors_square: float32 [4, 2048], replicated
- trust_norms: float32 [2, 13], replicated
The draws below stay inside these ranges and needn't reach their ends.
Inputs may be any that keep to these rules, and one draw needn't show every extreme that they name: live_mask is 1 at the first token of every sequence and at the first of every aligned block of 512 tokens. `inward_second`: positive. `outward_second`: positive. `widening_second`: positive. `narrowing_second`: positive. `column_second`: positive. `vectors_second`: positive.
All inputs are finite; a program needn't handle non-finite values.
Results may differ from the reference program's by a relative error of at most 0.018.
The reference program's roundings to bfloat16 on the way count: a program that leaves them out, or rounds other values in their place, can miss the bound.
Values may be sent and summed in bfloat16 or wider, within the bound.
A program may use at most 320 MiB of HBM per device.

```python
import math
import jax
import jax.numpy as jnp
from jax import lax

WIDTH = 2048
HEADS = 16
HEAD_DIM = 128
INNER = 8192
SEQ_LEN = 2048
QUERY_BLOCK = 512
STEP_COUNT = 10
SEQUENCES = 1
DEVICE_TOKENS = 512
TOKENS = 16384
GROUPS = 8


def ramp_factor(extent, dims, spread):
    factor = jnp.ones(extent, jnp.float32)
    for which_dim in dims:
        amount = extent[which_dim]
        places = jnp.arange(amount, dtype=jnp.float32) / max(amount - 1, 1)
        view = tuple((amount if number == which_dim else 1 for number in range(len(extent))))
        factor = factor * jnp.sqrt(1.0 + spread * places).reshape(view)
    return factor / (1.0 + 0.5 * spread) ** (0.5 * len(dims))


def normal_jitter(key, extent):
    return jax.random.normal(key, extent, jnp.float32)


def first_moment(key, extent, dims, slope_size):
    return jax.random.normal(key, extent, jnp.float32) * (0.11 * slope_size) * ramp_factor(extent, dims, 2.0)


def second_moment(key, extent, slope_size):
    levels = jax.random.uniform(key, extent, jnp.float32, math.log(0.5), math.log(8.0))
    return jnp.exp(levels) * (0.001 * slope_size * slope_size)


def row_sizes(numbers, base):
    return jnp.array(numbers, jnp.float32)[:, None] * base


def draw_inward(key, part):
    key = jax.random.fold_in(key, 11)
    extent = (WIDTH, 3, WIDTH)
    jitter = normal_jitter(key, extent)
    spread = 2.0
    return jitter * ramp_factor(extent, (0, 2), spread) * WIDTH ** (-0.5)


def draw_outward(key, part):
    key = jax.random.fold_in(key, 12)
    extent = (WIDTH, WIDTH)
    jitter = normal_jitter(key, extent)
    spread = 2.0
    return jitter * ramp_factor(extent, (0, 1), spread) * (SEQ_LEN / (4.0 * WIDTH)) ** 0.5


def draw_widening(key, part):
    key = jax.random.fold_in(key, 13)
    extent = (WIDTH, 4, WIDTH)
    jitter = normal_jitter(key, extent)
    spread = 2.0
    return jitter * ramp_factor(extent, (0, 2), spread) * WIDTH ** (-0.5)


def draw_narrowing(key, part):
    key = jax.random.fold_in(key, 14)
    extent = (4, WIDTH, WIDTH)
    jitter = normal_jitter(key, extent)
    spread = 2.0
    return jitter * ramp_factor(extent, (1, 2), spread) * INNER ** (-0.5)


def draw_vectors(key, part):
    key = jax.random.fold_in(key, 15)
    extent = (6, WIDTH)
    jitter = normal_jitter(key, extent)
    spread = 2.0
    places = jnp.arange(WIDTH, dtype=jnp.float32) / max(WIDTH - 1, 1)
    gains = jnp.sqrt(1.0 + spread * places)[None, :] * (1.0 + 0.15 * jitter)
    offsets = 0.3 * jitter
    chosen = jnp.array([1.0, 0.0, 0.0, 1.0, 0.0, 0.0], jnp.float32)[:, None]
    return chosen * gains + (1.0 - chosen) * offsets


def draw_inward_first(key, part):
    key = jax.random.fold_in(key, 21)
    return first_moment(key, (WIDTH, 3, WIDTH), (0, 2), 2.0 * TOKENS ** (-0.5))


def draw_inward_second(key, part):
    key = jax.random.fold_in(key, 31)
    return second_moment(key, (WIDTH, 3, WIDTH), 2.0 * TOKENS ** (-0.5))


def draw_outward_first(key, part):
    key = jax.random.fold_in(key, 22)
    return first_moment(key, (WIDTH, WIDTH), (0, 1), 12.0 * (TOKENS * SEQ_LEN) ** (-0.5))


def draw_outward_second(key, part):
    key = jax.random.fold_in(key, 32)
    return second_moment(key, (WIDTH, WIDTH), 12.0 * (TOKENS * SEQ_LEN) ** (-0.5))


def draw_widening_first(key, part):
    key = jax.random.fold_in(key, 23)
    return first_moment(key, (WIDTH, 4, WIDTH), (0, 2), 0.6 * TOKENS ** (-0.5))


def draw_widening_second(key, part):
    key = jax.random.fold_in(key, 33)
    return second_moment(key, (WIDTH, 4, WIDTH), 0.6 * TOKENS ** (-0.5))


def draw_narrowing_first(key, part):
    key = jax.random.fold_in(key, 24)
    return first_moment(key, (4, WIDTH, WIDTH), (1, 2), 0.8 * TOKENS ** (-0.5))


def draw_narrowing_second(key, part):
    key = jax.random.fold_in(key, 34)
    return second_moment(key, (4, WIDTH, WIDTH), 0.8 * TOKENS ** (-0.5))


def draw_column_first(key, part):
    key = jax.random.fold_in(key, 25)
    return first_moment(key, (6, WIDTH), (1,), row_sizes([2.0, 2.0, 0.5, 0.5, 0.5, 0.5], TOKENS ** (-0.5)))


def draw_column_second(key, part):
    key = jax.random.fold_in(key, 35)
    return second_moment(key, (6, WIDTH), row_sizes([2.0, 2.0, 0.5, 0.5, 0.5, 0.5], TOKENS ** (-0.5)))


def draw_vectors_first(key, part):
    key = jax.random.fold_in(key, 26)
    return first_moment(key, (6, WIDTH), (1,), row_sizes([3.0, 3.0, 1.5, 1.0, 1.0, 1.5], TOKENS ** (-0.5)))


def draw_vectors_second(key, part):
    key = jax.random.fold_in(key, 36)
    return second_moment(key, (6, WIDTH), row_sizes([3.0, 3.0, 1.5, 1.0, 1.0, 1.5], TOKENS ** (-0.5)))


def draw_live_mask(key, part):
    key = jax.random.fold_in(key, 51)
    places = jnp.arange(TOKENS, dtype=jnp.int32)
    group_rows = SEQUENCES * SEQ_LEN
    groups = places // group_rows
    inside = places % group_rows
    levels = (300 + 600 * groups // max(GROUPS - 1, 1)) * (350 + 650 * inside // max(group_rows - 1, 1)) // 1000
    rolled = jax.random.randint(key, (TOKENS,), 0, 1000, dtype=jnp.int32)
    forced = (places % DEVICE_TOKENS == 0) | (places % SEQ_LEN == 0)
    return jnp.where((rolled < levels) | forced, 1, 0).astype(jnp.int32)


def level_of(key, shape, split, smallest, top_value):
    gain, own = 1.0, jax.random.fold_in(key, 6)
    for axis_at, blocks in split:
        draws = jnp.exp(jax.random.uniform(jax.random.fold_in(own, axis_at), (blocks,), jnp.float32, smallest / len(split), top_value / len(split)))
        gain = gain * jnp.repeat(draws, shape[axis_at] // blocks).reshape([-1 if axis == axis_at else 1 for axis in range(len(shape))])
    return gain


def gaussian(key, shape, scale, most, split=(), held_as=jnp.bfloat16):
    drawn = jax.random.normal(key, shape, jnp.float32) * scale
    if len(split) > 0:
        drawn = level_of(key, shape, split, -0.22, 0.18) * drawn
    return jnp.clip(drawn, min=-most, max=most).astype(held_as)


def setup_inputs(seed: int = 0) -> dict:
    arg_keys = jax.random.split(jax.random.key(seed), 22)
    return {
        "tokens": gaussian(arg_keys[0], (TOKENS, WIDTH), 1.0, 6.0, ((0, 32),)),
        "cotangent": gaussian(arg_keys[1], (TOKENS, WIDTH), 1.0, 6.0, ((0, 32),)),
        "live_mask": draw_live_mask(jax.random.fold_in(arg_keys[21], 71), 0),
        "inward": draw_inward(jax.random.fold_in(arg_keys[21], 71), 0),
        "inward_first": draw_inward_first(jax.random.fold_in(arg_keys[21], 71), 0),
        "inward_second": draw_inward_second(jax.random.fold_in(arg_keys[21], 71), 0),
        "outward": draw_outward(jax.random.fold_in(arg_keys[21], 71), 0),
        "outward_first": draw_outward_first(jax.random.fold_in(arg_keys[21], 71), 0),
        "outward_second": draw_outward_second(jax.random.fold_in(arg_keys[21], 71), 0),
        "widening": draw_widening(jax.random.fold_in(arg_keys[21], 71), 0),
        "widening_first": draw_widening_first(jax.random.fold_in(arg_keys[21], 71), 0),
        "widening_second": draw_widening_second(jax.random.fold_in(arg_keys[21], 71), 0),
        "narrowing": draw_narrowing(jax.random.fold_in(arg_keys[21], 71), 0),
        "narrowing_first": draw_narrowing_first(jax.random.fold_in(arg_keys[21], 71), 0),
        "narrowing_second": draw_narrowing_second(jax.random.fold_in(arg_keys[21], 71), 0),
        "column_bias": gaussian(arg_keys[15], (6, WIDTH), 0.5, 4.0, ((1, 4),), jnp.float32),
        "column_first": draw_column_first(jax.random.fold_in(arg_keys[21], 71), 0),
        "column_second": draw_column_second(jax.random.fold_in(arg_keys[21], 71), 0),
        "vectors": draw_vectors(jax.random.fold_in(arg_keys[21], 71), 0),
        "vectors_first": draw_vectors_first(jax.random.fold_in(arg_keys[21], 71), 0),
        "vectors_second": draw_vectors_second(jax.random.fold_in(arg_keys[21], 71), 0),
    }


@jax.custom_vjp
def low(v):
    return lax.optimization_barrier(v.astype(jnp.bfloat16)).astype(jnp.float32)

@jax.custom_vjp
def low_back(v):
    return v

def low_keep(v):
    return (low(v), None)

def low_pass(kept, grad):
    return (grad,)

def back_keep(v):
    return (v, None)

def back_low(kept, grad):
    return (low(grad),)
low.defvjp(low_keep, low_pass)
low_back.defvjp(back_keep, back_low)
norm_epsilon = 1e-05
beta_one = 0.9
beta_two = 0.999
adam_epsilon = 1e-06
decay_rate = 0.01
learn_rate = 0.5
trust_epsilon = 1e-06
highest = lax.Precision.HIGHEST

def layer_norm(values, gain_row, shift_row):
    centre = values - lax.optimization_barrier(jnp.mean(values, axis=-1, keepdims=True))
    spread = lax.optimization_barrier(jnp.mean(centre * centre, axis=-1, keepdims=True))
    return centre * lax.rsqrt(spread + norm_epsilon) * gain_row + shift_row

def attend(query_rows, key_rows, values, living, offset):
    raw_scores = jnp.einsum('qhd,khd->hqk', query_rows, key_rows, precision=highest)
    scores = low_back(raw_scores * HEAD_DIM ** (-0.5))
    query_place = offset + jnp.arange(query_rows.shape[0], dtype=jnp.int32)
    key_place = jnp.arange(key_rows.shape[0], dtype=jnp.int32)
    allowed = (key_place[None, :] <= query_place[:, None]) & (living[None, :] > 0.5)
    scores = jnp.where(allowed[None], scores, -jnp.inf)
    peak_score = lax.optimization_barrier(jnp.max(scores, axis=-1, keepdims=True))
    weights = jnp.exp(scores - peak_score)
    chances = weights / lax.optimization_barrier(jnp.sum(weights, axis=-1, keepdims=True))
    return jnp.einsum('hqk,khd->qhd', low(chances), values, precision=highest)

def layer(tokens, inward, outward, widening, narrowing, column_bias, vectors, living):
    normed = low(layer_norm(tokens, vectors[0], vectors[1]))
    mixed = jnp.einsum('td,dkc->tkc', normed, inward, precision=highest)
    queries = low(low_back(mixed[:, 0] + column_bias[0]))
    key_rows = low(low_back(mixed[:, 1]))
    values = low(low_back(mixed[:, 2] + column_bias[1]))
    length = tokens.shape[0]
    head_shape = (length, HEADS, HEAD_DIM)
    query_heads = queries.reshape(head_shape)
    key_heads = key_rows.reshape(head_shape)
    value_heads = values.reshape(head_shape)
    amount = length // QUERY_BLOCK

    def one_block(scan_item):
        query_rows, offset = scan_item
        return attend(query_rows, key_heads, value_heads, living, offset)
    blocks = lax.map(jax.checkpoint(one_block), (query_heads.reshape(amount, QUERY_BLOCK, HEADS, HEAD_DIM), jnp.arange(amount, dtype=jnp.int32) * QUERY_BLOCK))
    context = low_back(low(blocks.reshape(length, HEADS * HEAD_DIM)))
    middle = tokens + low_back(jnp.dot(context, outward, precision=highest)) + vectors[2]
    normed_two = low(layer_norm(middle, vectors[3], vectors[4]))
    hidden = low_back(jnp.einsum('td,drc->trc', normed_two, widening, precision=highest) + column_bias[2:])
    active = low(jax.nn.gelu(hidden, approximate=True))
    return middle + jnp.einsum('trc,rcd->td', active, narrowing, precision=highest) + vectors[5]

def adapt_step(weight, moment_one, moment_two, slope, decay):
    mean_new = beta_one * moment_one + (1.0 - beta_one) * slope
    square_new = beta_two * moment_two + (1.0 - beta_two) * slope * slope
    direction = mean_new / (1.0 - beta_one ** STEP_COUNT) / (jnp.sqrt(square_new / (1.0 - beta_two ** STEP_COUNT)) + adam_epsilon) + decay * weight
    return (mean_new, square_new, direction)

def settle(weight, direction):
    weight_norm = jnp.sqrt(jnp.sum(weight * weight))
    update_norm = jnp.sqrt(jnp.sum(direction * direction))
    return (weight - learn_rate * weight_norm / (update_norm + trust_epsilon) * direction, weight_norm, update_norm)

def reference(tokens, cotangent, live_mask, inward, inward_first, inward_second, outward, outward_first, outward_second, widening, widening_first, widening_second, narrowing, narrowing_first, narrowing_second, column_bias, column_first, column_second, vectors, vectors_first, vectors_second):
    width = tokens.shape[1]
    amount = tokens.shape[0] // SEQ_LEN
    living = live_mask.astype(jnp.float32)
    inputs = tokens.astype(jnp.float32).reshape(amount, SEQ_LEN, width)
    cotangents = (cotangent.astype(jnp.float32) * living[:, None]).reshape(amount, SEQ_LEN, width)
    lives = living.reshape(amount, SEQ_LEN)
    params = (low(inward), low(outward), low(widening), low(narrowing), column_bias, vectors)

    def scan_step(totals, member):
        inputs_one, cotangent_one, living_one = member

        def apply_layer(tokens_one, inward_used, outward_used, widening_used, narrowing_used, column_used, vectors_used):
            return layer(tokens_one, inward_used, outward_used, widening_used, narrowing_used, column_used, vectors_used, living_one)
        result, pullback = jax.vjp(apply_layer, inputs_one, params[0], params[1], params[2], params[3], params[4], params[5])
        slopes = pullback(cotangent_one)
        totals = tuple((before + extra for before, extra in zip(totals, slopes[1:])))
        return (totals, (result.astype(jnp.bfloat16), slopes[0]))
    zeros = tuple((jnp.zeros(member.shape, jnp.float32) for member in params))
    totals, (outputs, back_inputs) = lax.scan(scan_step, zeros, (inputs, cotangents, lives))
    factor = 1.0 / jnp.sum(living)
    slopes = tuple((summed * factor for summed in totals))
    results = []
    weight_norms = []
    update_norms = []
    masters = (inward, outward, widening, narrowing)
    firsts = (inward_first, outward_first, widening_first, narrowing_first)
    seconds = (inward_second, outward_second, widening_second, narrowing_second)
    for ordinal in range(4):
        mean_new, square_new, direction = adapt_step(masters[ordinal], firsts[ordinal], seconds[ordinal], slopes[ordinal], decay_rate)
        fresh, weight_norm, update_norm = settle(masters[ordinal], direction)
        results = results + [fresh, mean_new, square_new, fresh.astype(jnp.bfloat16)]
        weight_norms.append(weight_norm)
        update_norms.append(update_norm)
    column_mean, column_square, column_direction = adapt_step(column_bias, column_first, column_second, slopes[4], 0.0)
    column_parts = []
    for row_start, row_stop in ((0, 1), (1, 2), (2, 6)):
        fresh, weight_norm, update_norm = settle(column_bias[row_start:row_stop], column_direction[row_start:row_stop])
        column_parts.append(fresh)
        weight_norms.append(weight_norm)
        update_norms.append(update_norm)
    vectors_mean, vectors_square, vectors_direction = adapt_step(vectors, vectors_first, vectors_second, slopes[5], 0.0)
    vector_parts = []
    for row_number in range(6):
        fresh, weight_norm, update_norm = settle(vectors[row_number], vectors_direction[row_number])
        vector_parts.append(fresh)
        weight_norms.append(weight_norm)
        update_norms.append(update_norm)
    trust_norms = jnp.stack([jnp.stack(weight_norms), jnp.stack(update_norms)])
    return (outputs.reshape(tokens.shape[0], width), back_inputs.reshape(tokens.shape[0], width) * factor, results[0], results[1], results[2], results[3], results[4], results[5], results[6], results[7], results[8], results[9], results[10], results[11], results[12], results[13], results[14], results[15], jnp.concatenate(column_parts, axis=0), column_mean, column_square[0], column_square[1], column_square[2:], jnp.stack(vector_parts), vectors_mean, vectors_square[0:2], vectors_square[2:], trust_norms)
```

```python
import functools

import jax
import jax.numpy as jnp
from jax import lax
from jax.experimental import pallas as pl
from jax.experimental.pallas import tpu as pltpu
from jax.sharding import PartitionSpec as P

HEAD_DIM = 128
QUERY_BLOCK = 512
STEP_COUNT = 10
LOG2E = 1.4426950408889634
MASKED = -1e30
VMEM_BYTES = 56 * 2**20
ROWS = (((1,), (1,)), ((), ()))
TOKENS = (((0,), (0,)), ((), ()))

norm_epsilon = 1e-05
beta_one = 0.9
beta_two = 0.999
adam_epsilon = 1e-06
decay_rate = 0.01
learn_rate = 0.5
trust_epsilon = 1e-06


def layer_norm(values, gain_row, shift_row):
    centre = values - jnp.mean(values, axis=-1, keepdims=True)
    spread = jnp.mean(centre * centre, axis=-1, keepdims=True)
    return centre * lax.rsqrt(spread + norm_epsilon) * gain_row + shift_row


def dot_as(left, right, dims, kind=jnp.float32):
    return lax.dot_general(left, right, dims, preferred_element_type=jnp.float32).astype(kind)


PLAIN = (((1,), (0,)), ((), ()))


def forward_kernel(q_ref, k_ref, v_ref, bias_ref, ctx_ref, wide_ref, total_ref, *, blocks, size):
    factor = HEAD_DIM**-0.5 * LOG2E
    which = pl.program_id(1)
    queries = q_ref[...]
    for last in range(blocks):

        @pl.when(which == last)
        def _():
            parts = []
            peak = None
            for at in range(last + 1):
                keys = slice(at * size, (at + 1) * size)
                scores = dot_as(queries, k_ref[keys, :], ROWS) + bias_ref[0:1, keys]
                if at == last:
                    row = lax.broadcasted_iota(jnp.int32, (size, size), 0)
                    col = lax.broadcasted_iota(jnp.int32, (size, size), 1)
                    scores = jnp.where(col <= row, scores, MASKED)
                top = jnp.max(scores, axis=1, keepdims=True)
                peak = top if peak is None else jnp.maximum(peak, top)
                parts.append(scores)
            low = peak * factor
            total = None
            context = None
            for at in range(last + 1):
                keys = slice(at * size, (at + 1) * size)
                weights = jnp.exp2(parts[at] * factor - low)
                more = jnp.sum(weights, axis=1, keepdims=True)
                total = more if total is None else total + more
                term = dot_as(weights.astype(jnp.bfloat16), v_ref[keys, :], PLAIN)
                context = term if context is None else context + term
            context = context * (1.0 / total)
            ctx_ref[...] = context.astype(jnp.bfloat16)
            wide_ref[...] = context
            logs = jnp.broadcast_to(low + jnp.log2(total), (size, 128))
            total_ref[...] = jnp.transpose(logs)[0:1, :].reshape(1, 1, size)


def attend_forward(queries, key_rows, values, bias_row):
    length, cols = queries.shape
    heads = cols // HEAD_DIM
    size = QUERY_BLOCK
    blocks = length // size
    part = pl.BlockSpec((size, HEAD_DIM), lambda h, i: (i, h))
    whole = pl.BlockSpec((length, HEAD_DIM), lambda h, i: (0, h))
    return pl.pallas_call(
        functools.partial(forward_kernel, blocks=blocks, size=size),
        grid=(heads, blocks),
        in_specs=[part, whole, whole, pl.BlockSpec((1, length), lambda h, i: (0, 0))],
        out_specs=[part, part, pl.BlockSpec((1, 1, size), lambda h, i: (h, 0, i))],
        out_shape=[
            jax.ShapeDtypeStruct((length, cols), jnp.bfloat16),
            jax.ShapeDtypeStruct((length, cols), jnp.float32),
            jax.ShapeDtypeStruct((heads, 1, length), jnp.float32),
        ],
        compiler_params=pltpu.CompilerParams(vmem_limit_bytes=VMEM_BYTES),
        cost_estimate=pl.CostEstimate(
            flops=4 * length * length * cols,
            bytes_accessed=12 * length * cols,
            transcendentals=heads * length * length // 2,
        ),
        name="attend_forward",
    )(queries, key_rows, values, bias_row)


def backward_kernel(
    q_ref, k_ref, v_ref, back_ref, wide_ref, total_ref, bias_ref, dq_ref, dk_ref, dv_ref, sum_ref,
    *, blocks, size
):
    scale = HEAD_DIM**-0.5
    factor = scale * LOG2E
    inner = []
    for at in range(blocks):
        rows = slice(at * size, (at + 1) * size)
        product = back_ref[rows, :].astype(jnp.float32) * wide_ref[rows, :]
        inner.append(jnp.sum(jnp.transpose(product), axis=0, keepdims=True))
    for key_at in range(blocks):
        keys = slice(key_at * size, (key_at + 1) * size)
        key_rows = k_ref[keys, :]
        values = v_ref[keys, :]
        bias = bias_ref[keys, 0:1]
        back_keys = None
        back_values = None
        for query_at in range(key_at, blocks):
            rows = slice(query_at * size, (query_at + 1) * size)
            queries = q_ref[rows, :]
            back = back_ref[rows, :]
            level = dot_as(key_rows, queries, ROWS) * factor - total_ref[0, 0:1, rows] + bias
            if query_at == key_at:
                row = lax.broadcasted_iota(jnp.int32, (size, size), 0)
                col = lax.broadcasted_iota(jnp.int32, (size, size), 1)
                level = jnp.where(row <= col, level, MASKED)
            chances = jnp.exp2(level)
            back_chances = dot_as(values, back, ROWS)
            back_scores = (chances * (back_chances - inner[query_at])).astype(jnp.bfloat16)
            more_values = dot_as(chances.astype(jnp.bfloat16), back, PLAIN)
            more_keys = dot_as(back_scores, queries, PLAIN)
            more_queries = dot_as(back_scores, key_rows, TOKENS)
            if key_at == 0:
                sum_ref[rows, :] = more_queries
            else:
                sum_ref[rows, :] += more_queries
            back_keys = more_keys if back_keys is None else back_keys + more_keys
            back_values = more_values if back_values is None else back_values + more_values
        dk_ref[keys, :] = (back_keys * scale).astype(jnp.bfloat16)
        dv_ref[keys, :] = back_values.astype(jnp.bfloat16)
    dq_ref[...] = (sum_ref[...] * scale).astype(jnp.bfloat16)


def attend_backward(queries, key_rows, values, back, wide, totals, bias_column):
    length, cols = queries.shape
    heads = cols // HEAD_DIM
    size = QUERY_BLOCK
    whole = pl.BlockSpec((length, HEAD_DIM), lambda h: (0, h))
    return pl.pallas_call(
        functools.partial(backward_kernel, blocks=length // size, size=size),
        grid=(heads,),
        in_specs=[whole] * 5
        + [
            pl.BlockSpec((1, 1, length), lambda h: (h, 0, 0)),
            pl.BlockSpec((length, 1), lambda h: (0, 0)),
        ],
        out_specs=[whole] * 3,
        out_shape=[jax.ShapeDtypeStruct((length, cols), jnp.bfloat16)] * 3,
        scratch_shapes=[pltpu.VMEM((length, HEAD_DIM), jnp.float32)],
        compiler_params=pltpu.CompilerParams(vmem_limit_bytes=VMEM_BYTES),
        cost_estimate=pl.CostEstimate(
            flops=10 * length * length * cols,
            bytes_accessed=18 * length * cols,
            transcendentals=heads * length * length // 2,
        ),
        name="attend_backward",
    )(queries, key_rows, values, back, wide, totals, bias_column)


def hidden_kernel(b_ref, weight_ref, bias_ref, back_ref, act_ref, dhid_ref, sum_ref):
    hidden = dot_as(b_ref[...], weight_ref[...], PLAIN) + bias_ref[...]
    root = 0.7978845608028654
    square = hidden * hidden
    bent = jnp.tanh(root * hidden * (1.0 + 0.044715 * square))
    half = 0.5 * (1.0 + bent)
    act_ref[...] = (hidden * half).astype(jnp.bfloat16)
    slope = half + 0.5 * hidden * (1.0 - bent * bent) * (root * (1.0 + 3.0 * 0.044715 * square))
    back = (back_ref[...] * slope).astype(jnp.bfloat16)
    dhid_ref[...] = back
    sum_ref[...] = jnp.sum(back.astype(jnp.float32), axis=0, keepdims=True)


def hidden_step(rows, weight, bias, back):
    amount, width = rows.shape
    units = weight.shape[1]
    tile = min(512, units)
    return pl.pallas_call(
        hidden_kernel,
        grid=(units // tile,),
        in_specs=[
            pl.BlockSpec((amount, width), lambda i: (0, 0)),
            pl.BlockSpec((width, tile), lambda i: (0, i)),
            pl.BlockSpec((1, tile), lambda i: (0, i)),
            pl.BlockSpec((amount, tile), lambda i: (0, i)),
        ],
        out_specs=[
            pl.BlockSpec((amount, tile), lambda i: (0, i)),
            pl.BlockSpec((amount, tile), lambda i: (0, i)),
            pl.BlockSpec((1, tile), lambda i: (0, i)),
        ],
        out_shape=[
            jax.ShapeDtypeStruct((amount, units), jnp.bfloat16),
            jax.ShapeDtypeStruct((amount, units), jnp.bfloat16),
            jax.ShapeDtypeStruct((1, units), jnp.float32),
        ],
        compiler_params=pltpu.CompilerParams(vmem_limit_bytes=VMEM_BYTES),
        cost_estimate=pl.CostEstimate(
            flops=2 * amount * width * units,
            bytes_accessed=2 * (amount * width + width * units) + 8 * amount * units,
            transcendentals=amount * units,
        ),
        name="hidden_step",
    )(rows, weight, bias, back)


def swap(values, axis, mask):
    count = lax.axis_size(axis)
    return lax.ppermute(values, axis, [(i, i ^ mask) for i in range(count)])


def gather_quads(rows):
    quads = lax.axis_size("dp") // 2
    if quads != 4:
        return [rows] + [swap(rows, "dp", 2 * m) for m in range(1, quads)]
    half = rows.shape[0] // 2
    first = swap(rows, "dp", 2)
    second = swap(rows, "dp", 4)
    return [
        rows,
        first,
        second,
        swap(first[:half], "dp", 4),
        swap(second[half:], "dp", 2),
    ]


def scatter_quads(parts):
    quads = lax.axis_size("dp") // 2
    wide = jnp.float32
    kind = jnp.bfloat16
    if quads != 4:
        total = parts[0].astype(wide)
        for m in range(1, quads):
            total = total + swap(parts[m].astype(kind), "dp", 2 * m).astype(wide)
        return total
    own, first, second, upper, lower = parts
    half = own.shape[0] // 2
    upper = swap(upper.astype(kind), "dp", 4).astype(wide)
    lower = swap(lower.astype(kind), "dp", 2).astype(wide)
    first_low = swap(first[half:].astype(kind), "dp", 2).astype(wide)
    second_up = swap(second[:half].astype(kind), "dp", 4).astype(wide)
    first_up = swap((first[:half].astype(wide) + upper).astype(kind), "dp", 2).astype(wide)
    second_low = swap((second[half:].astype(wide) + lower).astype(kind), "dp", 4).astype(wide)
    own = own.astype(wide)
    return jnp.concatenate(
        [
            own[:half] + first_up + second_up,
            own[half:] + first_low + second_low,
        ],
        axis=0,
    )


def quad_masks():
    quads = lax.axis_size("dp") // 2
    return [2 * m for m in range(quads)]


def gather_all(rows):
    count = lax.axis_size("dp")
    me = lax.axis_index("dp")
    parts = gather_quads(rows)
    if count == 8:
        parts = parts[:3] + [jnp.concatenate(parts[3:], axis=0)]
    near = jnp.stack(parts)
    far = swap(near, "dp", 1)
    held = jnp.stack([near, far], axis=1).reshape((count,) + rows.shape)
    return [lax.dynamic_index_in_dim(held, me ^ j, 0, keepdims=False) for j in range(count)]


def scatter_all(block_of):
    count = lax.axis_size("dp")
    me = lax.axis_index("dp")
    quads = count // 2
    far = jnp.stack([block_of(me ^ (2 * m + 1)) for m in range(quads)]).astype(jnp.bfloat16)
    far = swap(far, "dp", 1).astype(jnp.float32)
    parts = [block_of(me ^ (2 * m)) + far[m] for m in range(quads)]
    if quads == 4:
        half = parts[3].shape[0] // 2
        parts = parts[:3] + [parts[3][:half], parts[3][half:]]
    return scatter_quads(parts)


def trade(block_of):
    count = lax.axis_size("tensor")
    me = lax.axis_index("tensor")
    held = jnp.stack(
        [block_of(me)] + [swap(block_of(me ^ m), "tensor", m) for m in range(1, count)]
    )
    return [lax.dynamic_index_in_dim(held, me ^ j, 0, keepdims=False) for j in range(count)]


def sum_kernel(values_ref, out_ref, held, send_one, recv_one, send_two, recv_two, *, groups, slices):
    count = groups * slices
    me = lax.axis_index("dp") * slices + lax.axis_index("tensor")

    def target(step):
        other = lax.rem(me + step, count)
        return (other // slices, lax.rem(other, slices))

    barrier = pltpu.get_barrier_semaphore()

    def greet(step, carry):
        pl.semaphore_signal(
            barrier, inc=1, device_id=target(step), device_id_type=pl.DeviceIdType.MESH
        )
        return carry

    lax.fori_loop(1, count, greet, 0)
    pl.semaphore_wait(barrier, count - 1)

    def first(step):
        return pltpu.make_async_remote_copy(
            src_ref=values_ref.at[lax.rem(me + step, count)],
            dst_ref=held.at[step],
            send_sem=send_one.at[step],
            recv_sem=recv_one.at[step],
            device_id=target(step),
            device_id_type=pl.DeviceIdType.MESH,
        )

    def second(step):
        return pltpu.make_async_remote_copy(
            src_ref=held.at[0],
            dst_ref=out_ref.at[me],
            send_sem=send_two.at[step],
            recv_sem=recv_two.at[step],
            device_id=target(step),
            device_id_type=pl.DeviceIdType.MESH,
        )

    def start_first(step, carry):
        first(step).start()
        return carry

    def wait_first(step, total):
        first(step).wait()
        return total + held[step]

    def start_second(step, carry):
        second(step).start()
        return carry

    def wait_second(step, carry):
        second(step).wait()
        return carry

    lax.fori_loop(1, count, start_first, 0)
    total = lax.fori_loop(1, count, wait_first, values_ref[me])
    held[0] = total
    out_ref[me] = total
    lax.fori_loop(1, count, start_second, 0)
    lax.fori_loop(1, count, wait_second, 0)


def sum_everywhere(values):
    groups = lax.axis_size("dp")
    slices = lax.axis_size("tensor")
    count = groups * slices
    length = values.shape[0]
    room = count * 8 * 128
    packed = jnp.concatenate([values, jnp.zeros((room - length,), jnp.float32)])
    shape = (count, 8, 128)
    summed = pl.pallas_call(
        functools.partial(sum_kernel, groups=groups, slices=slices),
        in_specs=[pl.BlockSpec(memory_space=pltpu.VMEM)],
        out_specs=pl.BlockSpec(memory_space=pltpu.VMEM),
        out_shape=jax.ShapeDtypeStruct(shape, jnp.float32),
        scratch_shapes=[
            pltpu.VMEM(shape, jnp.float32),
            pltpu.SemaphoreType.DMA((count,)),
            pltpu.SemaphoreType.DMA((count,)),
            pltpu.SemaphoreType.DMA((count,)),
            pltpu.SemaphoreType.DMA((count,)),
        ],
        compiler_params=pltpu.CompilerParams(
            collective_id=0, has_side_effects=True, vmem_limit_bytes=8 * 2**20
        ),
        cost_estimate=pl.CostEstimate(
            flops=room, bytes_accessed=8 * room, transcendentals=0
        ),
        name="sum_everywhere",
    )(packed.reshape(shape))
    return summed.reshape(room)[:length]


def after(values, gate):
    return lax.optimization_barrier((values, gate))[0]


def adapt_step(weight, moment_one, moment_two, slope, decay):
    mean_new = beta_one * moment_one + (1.0 - beta_one) * slope
    square_new = beta_two * moment_two + (1.0 - beta_two) * slope * slope
    direction = (
        mean_new
        / (1.0 - beta_one**STEP_COUNT)
        / (jnp.sqrt(square_new / (1.0 - beta_two**STEP_COUNT)) + adam_epsilon)
        + decay * weight
    )
    return (mean_new, square_new, direction)


def trust_apply(weight, direction, weight_square, update_square):
    weight_norm = jnp.sqrt(weight_square)
    update_norm = jnp.sqrt(update_square)
    return (
        weight - learn_rate * weight_norm / (update_norm + trust_epsilon) * direction,
        weight_norm,
        update_norm,
    )


def on_device(
    tokens,
    cotangent,
    live_mask,
    inward,
    inward_first,
    inward_second,
    outward,
    outward_first,
    outward_second,
    widening,
    widening_first,
    widening_second,
    narrowing,
    narrowing_first,
    narrowing_second,
    column_bias,
    column_first,
    column_second,
    vectors,
    vectors_first,
    vectors_second,
):
    low = jnp.bfloat16
    wide = jnp.float32
    amount, width = tokens.shape
    cols = column_bias.shape[1]
    groups = lax.axis_size("dp")
    slices = lax.axis_size("tensor")
    me = lax.axis_index("dp")
    place = lax.axis_index("tensor")
    share = inward.shape[0]
    piece = 4 * cols // groups

    inputs = tokens.astype(wide)
    living_here = live_mask.astype(wide)
    normed = layer_norm(inputs, vectors[0], vectors[1]).astype(low)
    normed_full = lax.all_gather(normed, "tensor", axis=0, tiled=True)
    living_full = lax.all_gather(live_mask.astype(low), "tensor", axis=0, tiled=True)
    length = normed_full.shape[0]
    bias_keys = jnp.where(living_full > 0.5, 0.0, MASKED).astype(wide)

    inward_full = jnp.concatenate(
        gather_all(inward.astype(low).reshape(share, 3 * cols)), axis=0
    )

    back_out = (cotangent.astype(wide) * living_here[:, None]).astype(low)
    back_blocks = gather_quads(back_out)

    wide_own = widening.astype(low).reshape(share, groups, piece).transpose(1, 0, 2)
    wide_own = lax.all_to_all(wide_own, "dp", 0, 0, tiled=True).reshape(width, piece)
    wide_own = lax.all_gather(after(wide_own, normed_full), "tensor", axis=0)
    wide_own = wide_own.transpose(1, 0, 2).reshape(width, slices * piece)
    widening_full = jnp.concatenate([wide_own, swap(wide_own, "dp", 1)], axis=1)

    thin_own = narrowing.astype(low).reshape(groups, piece, narrowing.shape[2])
    thin_own = lax.all_to_all(thin_own, "dp", 0, 0, tiled=True)
    thin_own = thin_own.transpose(1, 0, 2).reshape(piece, width)
    thin_own = lax.all_gather(after(thin_own, wide_own), "tensor", axis=0, tiled=True)
    narrowing_full = jnp.concatenate([thin_own, swap(thin_own, "dp", 1)], axis=0)

    outward_low = outward.astype(low)
    outward_rows = jnp.concatenate(trade(lambda j: outward_low), axis=0)
    outward_full = jnp.concatenate(
        [part.T for part in gather_all(outward_rows.T)], axis=1
    )

    bias_all = lax.all_gather(column_bias[2:].reshape(4 * cols), "tensor", axis=0)
    hidden_bias = jnp.concatenate(
        [
            lax.dynamic_slice_in_dim(bias_all, (me ^ side) * piece, piece, 1).reshape(1, -1)
            for side in range(2)
        ],
        axis=1,
    )

    queries = (
        dot_as(normed_full, inward_full[:, :cols], PLAIN) + column_bias[0]
    ).astype(low)
    key_rows = dot_as(normed_full, inward_full[:, cols : 2 * cols], PLAIN, low)
    values = (
        dot_as(normed_full, inward_full[:, 2 * cols :], PLAIN) + column_bias[1]
    ).astype(low)
    context, context_wide, totals = attend_forward(
        queries, key_rows, values, bias_keys[None, :]
    )
    context_own = jnp.concatenate(
        trade(lambda j: lax.dynamic_slice_in_dim(context, j * amount, amount, 0)), axis=1
    )
    middle = inputs + dot_as(context_own, outward_full, PLAIN) + vectors[2]
    normed_two = layer_norm(middle, vectors[3], vectors[4]).astype(low)

    rows_two = gather_quads(normed_two)
    back_active = [dot_as(block, narrowing_full, ROWS) for block in back_blocks]
    active = []
    back_hidden = []
    hidden_sums = []
    for block, back in zip(rows_two, back_active):
        act, back, sums = hidden_step(block, widening_full, hidden_bias, back)
        active.append(act)
        back_hidden.append(back)
        hidden_sums.append(sums)
    partial = [dot_as(block, widening_full, ROWS, low) for block in back_hidden]
    back_normed_two = scatter_quads(partial)

    half_units = slices * piece
    active_all, back_hidden_all, rows_two_all, back_all = (
        jnp.concatenate(parts, axis=0)
        for parts in after((active, back_hidden, rows_two, back_blocks), partial)
    )

    def pair_sum(own, other):
        return (own + swap(other.astype(low), "dp", 1).astype(wide)).astype(low)

    slope_narrowing = pair_sum(
        dot_as(active_all[:, :half_units], back_all, TOKENS),
        dot_as(active_all[:, half_units:], back_all, TOKENS),
    )
    sum_narrowing = lax.psum_scatter(slope_narrowing, "tensor", scatter_dimension=0, tiled=True)
    slope_widening = pair_sum(
        dot_as(rows_two_all, back_hidden_all[:, :half_units], TOKENS),
        dot_as(rows_two_all, back_hidden_all[:, half_units:], TOKENS),
    )

    _, norm_two_pull = jax.vjp(layer_norm, middle, vectors[3], vectors[4])
    back_middle_norm, slope_gain_two, slope_shift_two = norm_two_pull(back_normed_two)
    back_middle = back_out.astype(wide) + back_middle_norm
    back_low = back_middle.astype(low)

    back_context = dot_as(back_low, outward_full, ROWS, low)
    back_context_full = jnp.concatenate(
        trade(lambda j: lax.dynamic_slice_in_dim(back_context, j * cols, cols, 1)), axis=0
    )
    active, context_own, back_low = after((active, context_own, back_low), back_context)
    widened = scatter_quads([dot_as(block, narrowing_full, PLAIN, low) for block in active])
    layer_output = (middle + widened + vectors[5]).astype(low)

    slope_outward = dot_as(context_own, back_low, TOKENS)
    out_share = outward.shape[1]
    slope_outward = (
        scatter_all(
            lambda j: lax.dynamic_slice_in_dim(slope_outward, j * out_share, out_share, 1).T
        )
        .T.astype(low)
    )
    out_rows = outward.shape[0]
    sum_outward = functools.reduce(
        jnp.add,
        [
            part.astype(wide)
            for part in trade(
                lambda j: lax.dynamic_slice_in_dim(slope_outward, j * out_rows, out_rows, 0)
            )
        ],
    )

    slope_widening = after(slope_widening, (back_context_full, sum_narrowing))
    slope_widening = slope_widening.reshape(width, slices, piece).transpose(1, 0, 2)
    sum_widening = lax.psum_scatter(slope_widening, "tensor", scatter_dimension=0, tiled=True)

    back_queries, back_keys, back_values = attend_backward(
        queries, key_rows, values, back_context_full, context_wide, totals, bias_keys[:, None]
    )
    back_mixed = jnp.concatenate([back_queries, back_keys, back_values], axis=1)
    back_normed_part = dot_as(back_mixed, inward_full, ROWS, low)
    back_normed = lax.psum_scatter(
        after(back_normed_part, sum_widening), "tensor", scatter_dimension=0, tiled=True
    ).astype(wide)
    back_mixed = after(back_mixed, back_normed_part)
    slope_inward = dot_as(normed_full, back_mixed, TOKENS)
    sum_inward = scatter_all(
        lambda j: lax.dynamic_slice_in_dim(slope_inward, j * share, share, 0)
    ).reshape(inward.shape)

    sum_narrowing = lax.all_to_all(
        sum_narrowing.reshape(piece, groups, -1).transpose(1, 0, 2), "dp", 0, 0, tiled=True
    ).reshape(narrowing.shape)
    sum_widening = (
        lax.all_to_all(sum_widening.reshape(groups, share, piece), "dp", 0, 0, tiled=True)
        .transpose(1, 0, 2)
        .reshape(widening.shape)
    )

    hidden_total = hidden_sums[0]
    for sums in hidden_sums[1:]:
        hidden_total = hidden_total + sums
    hidden_total = hidden_total.reshape(2, 1, slices, piece)
    hidden_slots = jnp.zeros((groups, slices, piece), wide)
    hidden_slots = lax.dynamic_update_slice(hidden_slots, hidden_total[0], (me, 0, 0))
    hidden_slots = lax.dynamic_update_slice(hidden_slots, hidden_total[1], (me ^ 1, 0, 0))
    mixed_sums = jnp.stack(
        [
            jnp.sum(back_queries, axis=0, dtype=wide),
            jnp.sum(back_values, axis=0, dtype=wide),
        ]
    )
    mixed_slots = lax.dynamic_update_slice(
        jnp.zeros((slices, 2, cols), wide), mixed_sums[None], (place, 0, 0)
    )
    late_rows = jnp.stack(
        [
            jnp.sum(back_middle, axis=0),
            slope_gain_two,
            slope_shift_two,
            jnp.sum(back_out, axis=0, dtype=wide),
        ]
    )
    packed = sum_everywhere(
        jnp.concatenate(
            [
                hidden_slots.reshape(-1),
                mixed_slots.reshape(-1),
                late_rows.reshape(-1),
                jnp.sum(living_here)[None],
            ]
        )
    )
    first_cut = groups * slices * piece
    second_cut = first_cut + slices * 2 * cols
    factor = 1.0 / packed[-1]
    hidden_slots = packed[:first_cut].reshape(groups, slices, piece)
    hidden_rows = lax.dynamic_slice_in_dim(hidden_slots, place, 1, 1).reshape(4, cols)
    mixed_rows = lax.dynamic_index_in_dim(
        packed[first_cut:second_cut].reshape(slices, 2, cols), place, 0, keepdims=False
    )
    late_rows = packed[second_cut:-1].reshape(4, width)
    column_total = jnp.concatenate([mixed_rows, hidden_rows], axis=0)

    _, norm_one_pull = jax.vjp(layer_norm, inputs, vectors[0], vectors[1])
    back_inputs_norm, slope_gain_one, slope_shift_one = norm_one_pull(back_normed)
    back_inputs = back_middle + back_inputs_norm

    masters = (inward, outward, widening, narrowing)
    firsts = (inward_first, outward_first, widening_first, narrowing_first)
    seconds = (inward_second, outward_second, widening_second, narrowing_second)
    summed_all = (sum_inward, sum_outward, sum_widening, sum_narrowing)
    matrix_steps = [
        adapt_step(
            masters[ordinal],
            firsts[ordinal],
            seconds[ordinal],
            summed_all[ordinal].astype(wide) * factor,
            decay_rate,
        )
        for ordinal in range(4)
    ]
    column_mean, column_square, column_direction = adapt_step(
        column_bias, column_first, column_second, column_total * factor, 0.0
    )
    column_groups = ((0, 1), (1, 2), (2, 6))

    def square_sum(array):
        return jnp.sum(array * array)

    squares = [square_sum(master) for master in masters]
    squares += [square_sum(column_bias[start:stop]) / groups for start, stop in column_groups]
    squares += [square_sum(step[2]) for step in matrix_steps]
    squares += [square_sum(column_direction[start:stop]) / groups for start, stop in column_groups]
    norm_totals = sum_everywhere(jnp.stack(squares)).reshape(2, 7)

    early_rows = sum_everywhere(
        after(jnp.concatenate([slope_gain_one, slope_shift_one]), norm_totals)
    ).reshape(2, width)
    vector_total = jnp.concatenate([early_rows, late_rows], axis=0)

    results = []
    weight_norms = []
    update_norms = []
    for ordinal in range(4):
        fresh, weight_norm, update_norm = trust_apply(
            masters[ordinal],
            matrix_steps[ordinal][2],
            norm_totals[0, ordinal],
            norm_totals[1, ordinal],
        )
        results += [
            fresh,
            matrix_steps[ordinal][0],
            matrix_steps[ordinal][1],
            fresh.astype(low),
        ]
        weight_norms.append(weight_norm)
        update_norms.append(update_norm)
    column_parts = []
    for ordinal in range(3):
        start, stop = column_groups[ordinal]
        fresh, weight_norm, update_norm = trust_apply(
            column_bias[start:stop],
            column_direction[start:stop],
            norm_totals[0, 4 + ordinal],
            norm_totals[1, 4 + ordinal],
        )
        column_parts.append(fresh)
        weight_norms.append(weight_norm)
        update_norms.append(update_norm)
    vectors_mean, vectors_square, vectors_direction = adapt_step(
        vectors, vectors_first, vectors_second, vector_total * factor, 0.0
    )
    new_vectors, vector_weight_norms, vector_update_norms = trust_apply(
        vectors,
        vectors_direction,
        jnp.sum(vectors * vectors, axis=1, keepdims=True),
        jnp.sum(vectors_direction * vectors_direction, axis=1, keepdims=True),
    )
    trust_norms = jnp.stack(
        [
            jnp.concatenate([jnp.stack(weight_norms), vector_weight_norms[:, 0]]),
            jnp.concatenate([jnp.stack(update_norms), vector_update_norms[:, 0]]),
        ]
    )
    return (
        layer_output,
        back_inputs * factor,
        *results,
        jnp.concatenate(column_parts, axis=0),
        column_mean,
        column_square[0],
        column_square[1],
        column_square[2:],
        new_vectors,
        vectors_mean,
        vectors_square[0:2],
        vectors_square[2:],
        trust_norms,
    )


def solution(mesh):
    in_specs = (
        P(("dp", "tensor"), None),
        P(("dp", "tensor"), None),
        P(("dp", "tensor")),
        P("dp", None, "tensor"),
        P("dp", None, "tensor"),
        P("dp", None, "tensor"),
        P("tensor", "dp"),
        P("tensor", "dp"),
        P("tensor", "dp"),
        P("dp", None, "tensor"),
        P("dp", None, "tensor"),
        P("dp", None, "tensor"),
        P(None, "tensor", "dp"),
        P(None, "tensor", "dp"),
        P(None, "tensor", "dp"),
        P(None, "tensor"),
        P(None, "tensor"),
        P(None, "tensor"),
        P(),
        P(),
        P(),
    )
    out_specs = (
        P(("dp", "tensor"), None),
        P(("dp", "tensor"), None),
        P("dp", None, "tensor"),
        P("dp", None, "tensor"),
        P("dp", None, "tensor"),
        P("dp", None, "tensor"),
        P("tensor", "dp"),
        P("tensor", "dp"),
        P("tensor", "dp"),
        P("tensor", "dp"),
        P("dp", None, "tensor"),
        P("dp", None, "tensor"),
        P("dp", None, "tensor"),
        P("dp", None, "tensor"),
        P(None, "tensor", "dp"),
        P(None, "tensor", "dp"),
        P(None, "tensor", "dp"),
        P(None, "tensor", "dp"),
        P(None, "tensor"),
        P(None, "tensor"),
        P("tensor"),
        P("tensor"),
        P(None, "tensor"),
        P(),
        P(),
        P(),
        P(),
        P(),
    )
    return jax.shard_map(
        on_device, mesh=mesh, in_specs=in_specs, out_specs=out_specs, check_vma=False
    )
```

```python
import functools

import jax
import jax.numpy as jnp
from jax import lax
from jax.experimental import pallas as pl
from jax.experimental.layout import Layout, with_layout_constraint
from jax.experimental.pallas import tpu as pltpu
from jax.sharding import PartitionSpec as P

HEAD_DIM = 128
QUERY_BLOCK = 512
STEP_COUNT = 10
LOG2E = 1.4426950408889634
MASKED = -1e30
VMEM_BYTES = 56 * 2**20
ROWS = (((1,), (1,)), ((), ()))
TOKENS = (((0,), (0,)), ((), ()))

norm_epsilon = 1e-05
beta_one = 0.9
beta_two = 0.999
adam_epsilon = 1e-06
decay_rate = 0.01
learn_rate = 0.5
trust_epsilon = 1e-06


def layer_norm(values, gain_row, shift_row):
    centre = values - jnp.mean(values, axis=-1, keepdims=True)
    spread = jnp.mean(centre * centre, axis=-1, keepdims=True)
    return centre * lax.rsqrt(spread + norm_epsilon) * gain_row + shift_row


def dot_as(left, right, dims, kind=jnp.float32):
    return lax.dot_general(left, right, dims, preferred_element_type=jnp.float32).astype(kind)


PLAIN = (((1,), (0,)), ((), ()))


def forward_kernel(
    q_ref, k_ref, v_ref, bias_ref, back_ref, wide_ref, total_ref, own_ref, back_out,
    held, send_sem, recv_sem, keep_sem, e_send, e_recv,
    *, heads, blocks, size, slices, groups
):
    factor = HEAD_DIM**-0.5 * LOG2E
    head = pl.program_id(0)
    which = pl.program_id(1)
    me = lax.axis_index("dp")
    place = lax.axis_index("tensor")
    rows = own_ref.shape[0]
    queries = q_ref[...]
    masks = direct_masks(groups // 2)
    hops = two_hops(groups // 2)

    def across(mask):
        return (flip(me, mask), place)

    def e_hops():
        result = []
        half_rows = rows // 2
        for number, (mask, half, goal) in enumerate(hops):
            start = (masks.index(mask) + 1) * rows + half * half_rows
            source = back_ref.at[pl.ds(start, half_rows)]
            target = back_out.at[pl.ds(3 * rows + half * half_rows, half_rows)]
            result.append(
                remote(source, target, e_send.at[number], e_recv.at[number], across(goal))
            )
        return result

    @pl.when(jnp.logical_and(head == 0, which == 0))
    def _():
        greet_all(
            [(me, lax.rem(place + step, slices)) for step in range(1, slices)]
            + [across(goal) for _, _, goal in hops]
        )
        for copy in e_hops():
            copy.start()

    for last in range(blocks):

        @pl.when(which == last)
        def _():
            parts = []
            peak = None
            for at in range(last + 1):
                keys = slice(at * size, (at + 1) * size)
                scores = dot_as(queries, k_ref[keys, :], ROWS) + bias_ref[0:1, keys]
                if at == last:
                    row = lax.broadcasted_iota(jnp.int32, (size, size), 0)
                    col = lax.broadcasted_iota(jnp.int32, (size, size), 1)
                    scores = jnp.where(col <= row, scores, MASKED)
                top = jnp.max(scores, axis=1, keepdims=True)
                peak = top if peak is None else jnp.maximum(peak, top)
                parts.append(scores)
            low = peak * factor
            total = None
            context = None
            for at in range(last + 1):
                keys = slice(at * size, (at + 1) * size)
                weights = jnp.exp2(parts[at] * factor - low)
                more = jnp.sum(weights, axis=1, keepdims=True)
                total = more if total is None else total + more
                term = dot_as(weights.astype(jnp.bfloat16), v_ref[keys, :], PLAIN)
                context = term if context is None else context + term
            context = context * (1.0 / total)
            held[head, last * size : (last + 1) * size, :] = context.astype(jnp.bfloat16)
            wide_ref[...] = context
            logs = jnp.broadcast_to(low + jnp.log2(total), (size, 128))
            total_ref[...] = jnp.transpose(logs)[0:1, :].reshape(1, 1, size)

    def to_owner(owner, number):
        step = lax.rem(owner - place + slices, slices)
        return remote(
            held.at[number, pl.ds(pl.multiple_of(owner * rows, rows), rows)],
            own_ref.at[:, columns(place, number)],
            send_sem.at[step, number],
            recv_sem.at[step, number],
            (me, owner),
        )

    def columns(other, number):
        start = (other * heads + number) * HEAD_DIM
        return pl.ds(pl.multiple_of(start, HEAD_DIM), HEAD_DIM)

    def stay(number):
        return pltpu.make_async_copy(
            held.at[number, pl.ds(pl.multiple_of(place * rows, rows), rows)],
            own_ref.at[:, columns(place, number)],
            keep_sem.at[number],
        )

    for part in range(size // rows):
        owner = which * (size // rows) + part
        pl.when(owner == place)(lambda: stay(head).start())
        pl.when(owner != place)(lambda: to_owner(owner, head).start())

    @pl.when(jnp.logical_and(head == heads - 1, which == blocks - 1))
    def _():
        for copy in e_hops():
            copy.wait()
        for number in range(heads):
            stay(number).wait()
            for step in range(1, slices):
                to_owner(lax.rem(place + step, slices), number).wait_send()
                source = lax.rem(place + slices - step, slices)
                remote(
                    held.at[number, pl.ds(0, rows)],
                    own_ref.at[:, columns(source, number)],
                    send_sem.at[step, number],
                    recv_sem.at[step, number],
                    (me, source),
                ).wait_recv()


def attend_forward(mixed, bias_row, back, rows):
    slices = lax.axis_size("tensor")
    groups = lax.axis_size("dp")
    hops = max(1, len(two_hops(groups // 2)))
    length = mixed.shape[0]
    cols = mixed.shape[1] // 3
    heads = cols // HEAD_DIM
    size = QUERY_BLOCK
    blocks = length // size
    part = pl.BlockSpec((size, HEAD_DIM), lambda h, i: (i, h))
    keys = pl.BlockSpec((length, HEAD_DIM), lambda h, i: (0, heads + h))
    values = pl.BlockSpec((length, HEAD_DIM), lambda h, i: (0, 2 * heads + h))
    dma = pltpu.SemaphoreType.DMA
    return pl.pallas_call(
        functools.partial(
            forward_kernel, heads=heads, blocks=blocks, size=size, slices=slices, groups=groups
        ),
        grid=(heads, blocks),
        in_specs=[
            part,
            keys,
            values,
            pl.BlockSpec((1, length), lambda h, i: (0, 0)),
            pl.BlockSpec(memory_space=pl.ANY),
        ],
        out_specs=[
            part,
            pl.BlockSpec((1, 1, size), lambda h, i: (h, 0, i)),
            pl.BlockSpec(memory_space=pl.ANY),
            pl.BlockSpec(memory_space=pl.ANY),
        ],
        input_output_aliases={4: 3},
        out_shape=[
            jax.ShapeDtypeStruct((length, cols), jnp.float32),
            jax.ShapeDtypeStruct((heads, 1, length), jnp.float32),
            jax.ShapeDtypeStruct((rows, slices * cols), jnp.bfloat16),
            jax.ShapeDtypeStruct(back.shape, back.dtype),
        ],
        scratch_shapes=[
            pltpu.VMEM((heads, length, HEAD_DIM), jnp.bfloat16),
            dma((slices, heads)),
            dma((slices, heads)),
            dma((heads,)),
            dma((hops,)),
            dma((hops,)),
        ],
        compiler_params=pltpu.CompilerParams(
            collective_id=3, has_side_effects=True, vmem_limit_bytes=VMEM_BYTES
        ),
        cost_estimate=pl.CostEstimate(
            flops=4 * length * length * cols,
            bytes_accessed=100 * 2**20,
            transcendentals=heads * length * length // 2,
        ),
        name="attend_forward",
    )(mixed, mixed, mixed, bias_row, back)


def backward_kernel(
    low_ref, out_ref, mixed_ref, wide_ref, total_ref, bias_ref, grad_ref,
    sent, back_buf, sum_ref, send_sem, recv_sem,
    *, blocks, size, slices
):
    scale = HEAD_DIM**-0.5
    factor = scale * LOG2E
    me = lax.axis_index("dp")
    place = lax.axis_index("tensor")
    rows = low_ref.shape[0]
    cols = back_buf.shape[1]
    heads = cols // HEAD_DIM
    greet_all([(me, lax.rem(place + step, slices)) for step in range(1, slices)])

    def span(start, size):
        return pl.ds(pl.multiple_of(start, size), size)

    def product(owner):
        return dot_as(low_ref[...], out_ref[span(owner * cols, cols), :], ROWS, jnp.bfloat16)

    def to_owner(step, head):
        return remote(
            sent.at[step, :, span(head * HEAD_DIM, HEAD_DIM)],
            back_buf.at[span(place * rows, rows), span(head * HEAD_DIM, HEAD_DIM)],
            send_sem.at[step, head],
            recv_sem.at[step, head],
            (me, lax.rem(place + step, slices)),
        )

    for step in range(1, slices):
        sent[step] = product(lax.rem(place + step, slices))
    for head in range(heads):
        for step in range(1, slices):
            to_owner(step, head).start()
    back_buf[span(place * rows, rows), :] = product(place)

    def one_head(head, carry):
        for step in range(1, slices):
            source = lax.rem(place + slices - step, slices)
            remote(
                sent.at[step, :, span(head * HEAD_DIM, HEAD_DIM)],
                back_buf.at[span(source * rows, rows), span(head * HEAD_DIM, HEAD_DIM)],
                send_sem.at[step, head],
                recv_sem.at[step, head],
                (me, source),
            ).wait_recv()
        here = span(head * HEAD_DIM, HEAD_DIM)
        key_here = span(cols + head * HEAD_DIM, HEAD_DIM)
        value_here = span(2 * cols + head * HEAD_DIM, HEAD_DIM)
        inner = []
        for at in range(blocks):
            part = slice(at * size, (at + 1) * size)
            pairs = back_buf[part, here].astype(jnp.float32) * wide_ref[part, here]
            inner.append(jnp.sum(jnp.transpose(pairs), axis=0, keepdims=True))
        for key_at in range(blocks):
            keys = slice(key_at * size, (key_at + 1) * size)
            key_rows = mixed_ref[keys, key_here]
            values = mixed_ref[keys, value_here]
            bias = bias_ref[keys, 0:1]
            back_keys = None
            back_values = None
            for query_at in range(key_at, blocks):
                part = slice(query_at * size, (query_at + 1) * size)
                queries = mixed_ref[part, here]
                back = back_buf[part, here]
                level = dot_as(key_rows, queries, ROWS) * factor - total_ref[head, 0:1, part] + bias
                if query_at == key_at:
                    row = lax.broadcasted_iota(jnp.int32, (size, size), 0)
                    col = lax.broadcasted_iota(jnp.int32, (size, size), 1)
                    level = jnp.where(row <= col, level, MASKED)
                chances = jnp.exp2(level)
                back_chances = dot_as(values, back, ROWS)
                back_scores = (chances * (back_chances - inner[query_at])).astype(jnp.bfloat16)
                more_values = dot_as(chances.astype(jnp.bfloat16), back, PLAIN)
                more_keys = dot_as(back_scores, queries, PLAIN)
                more_queries = dot_as(back_scores, key_rows, TOKENS)
                if key_at == 0:
                    sum_ref[part, :] = more_queries
                else:
                    sum_ref[part, :] += more_queries
                back_keys = more_keys if back_keys is None else back_keys + more_keys
                back_values = more_values if back_values is None else back_values + more_values
            grad_ref[keys, key_here] = (back_keys * scale).astype(jnp.bfloat16)
            grad_ref[keys, value_here] = back_values.astype(jnp.bfloat16)
        grad_ref[:, here] = (sum_ref[...] * scale).astype(jnp.bfloat16)
        return carry

    lax.fori_loop(0, heads, one_head, 0)
    for head in range(heads):
        for step in range(1, slices):
            to_owner(step, head).wait_send()


def attend_backward(back_low, outward, mixed, wide, totals, bias_column):
    slices = lax.axis_size("tensor")
    rows = back_low.shape[0]
    length, cols = wide.shape
    heads = cols // HEAD_DIM
    size = QUERY_BLOCK
    vmem = pl.BlockSpec(memory_space=pltpu.VMEM)
    dma = pltpu.SemaphoreType.DMA
    return pl.pallas_call(
        functools.partial(backward_kernel, blocks=length // size, size=size, slices=slices),
        in_specs=[vmem] * 6,
        out_specs=vmem,
        out_shape=jax.ShapeDtypeStruct((length, 3 * cols), jnp.bfloat16),
        scratch_shapes=[
            pltpu.VMEM((slices, rows, cols), jnp.bfloat16),
            pltpu.VMEM((length, cols), jnp.bfloat16),
            pltpu.VMEM((length, HEAD_DIM), jnp.float32),
            dma((slices, heads)),
            dma((slices, heads)),
        ],
        compiler_params=pltpu.CompilerParams(
            collective_id=4, has_side_effects=True, vmem_limit_bytes=VMEM_BYTES
        ),
        cost_estimate=pl.CostEstimate(
            flops=10 * length * length * cols,
            bytes_accessed=150 * 2**20,
            transcendentals=heads * length * length // 2,
        ),
        name="attend_backward",
    )(back_low, outward, mixed, wide, totals, bias_column)


def back_kernel(e_ref, weight_ref, hid_ref, *refs):
    act_ref, dhid_ref, sum_ref = refs[-3:]
    back = dot_as(e_ref[...], weight_ref[...], ROWS)
    hidden = hid_ref[...]
    root = 0.7978845608028654
    square = hidden * hidden
    bent = jnp.tanh(root * hidden * (1.0 + 0.044715 * square))
    half = 0.5 * (1.0 + bent)
    act_ref[...] = (hidden * half).astype(jnp.bfloat16)
    slope = half + 0.5 * hidden * (1.0 - bent * bent) * (root * (1.0 + 3.0 * 0.044715 * square))
    back = (back * slope).astype(jnp.bfloat16)
    dhid_ref[...] = back
    sum_ref[0] = jnp.sum(back.astype(jnp.float32), axis=0, keepdims=True)


def back_step(back, weight, hidden, first, amount, rows, held=()):
    length, width = back.shape
    units = weight.shape[0]
    tile = min(512, units)
    here = pl.BlockSpec((rows, tile), lambda m, i: (first + m, i))
    whole = jax.ShapeDtypeStruct((length, units), jnp.bfloat16)
    return pl.pallas_call(
        back_kernel,
        grid=(amount, units // tile),
        in_specs=[
            pl.BlockSpec((rows, width), lambda m, i: (first + m, 0)),
            pl.BlockSpec((tile, width), lambda m, i: (i, 0)),
            here,
        ]
        + [pl.BlockSpec(memory_space=pl.ANY)] * len(held),
        out_specs=[here, here, pl.BlockSpec((1, 1, tile), lambda m, i: (m, 0, i))],
        out_shape=[whole, whole, jax.ShapeDtypeStruct((amount, 1, units), jnp.float32)],
        input_output_aliases={3: 0, 4: 1} if held else {},
        compiler_params=pltpu.CompilerParams(vmem_limit_bytes=VMEM_BYTES),
        cost_estimate=pl.CostEstimate(
            flops=2 * amount * rows * width * units,
            bytes_accessed=2 * (amount * rows * width + width * units) + 8 * amount * rows * units,
            transcendentals=amount * rows * units,
        ),
        name="back_step",
    )(back, weight, hidden, *held)


def flip(index, mask):
    result = index
    bit = 1
    while bit <= mask:
        if mask & bit:
            result = result + bit - 2 * bit * lax.rem(lax.div(index, bit), 2)
        bit *= 2
    return result


def greet_all(peers):
    barrier = pltpu.get_barrier_semaphore()
    for peer in peers:
        pl.semaphore_signal(barrier, inc=1, device_id=peer, device_id_type=pl.DeviceIdType.MESH)
    pl.semaphore_wait(barrier, len(peers))


def remote(source, target, send, receive, device):
    return pltpu.make_async_remote_copy(
        src_ref=source,
        dst_ref=target,
        send_sem=send,
        recv_sem=receive,
        device_id=device,
        device_id_type=pl.DeviceIdType.MESH,
    )


def direct_masks(quads):
    return [2, 4] if quads == 4 else [2 * m for m in range(1, quads)]


def two_hops(quads):
    return [(2, 0, 4), (4, 1, 2)] if quads == 4 else []


def open_kernel(
    a_ref, w_ref, e_ref, bias_ref, small_ref, count_ref, wide_ref, thin_ref, out_ref,
    full_ref, weight_ref, mixed_ref, back_ref, all_ref, counts_ref, wide_all, thin_all, out_all,
    a_buf, w_buf, wide_buf, thin_buf, out_buf,
    line_send, line_recv, small_send, small_recv, w_send, w_recv, pair_send, pair_recv,
    e_send, e_recv, local_sem, keep_sem, count_send, count_recv,
    wide_send, wide_recv, thin_send, thin_recv, out_send, out_recv, plane_send, plane_recv,
    *, groups, slices, piece
):
    quads = groups // 2
    count = groups * slices
    me = lax.axis_index("dp")
    place = lax.axis_index("tensor")
    rows = a_ref.shape[0]
    share = w_buf.shape[0] // groups
    cols = w_buf.shape[1] // 3
    out_cols = out_all.shape[1] // groups
    masks = direct_masks(quads)
    hops = two_hops(quads)
    low = jnp.bfloat16
    raw = piece % 128 == 0

    def across(mask):
        return (flip(me, mask), place)

    def along(other):
        return (me, other)

    def beside(step):
        return (me, lax.rem(place + step, slices))

    def anyone(step):
        other = lax.rem(me * slices + place + step, count)
        return (lax.div(other, slices), lax.rem(other, slices))

    barrier = pltpu.get_barrier_semaphore()

    def greet(step, carry):
        pl.semaphore_signal(
            barrier, inc=1, device_id=anyone(step), device_id_type=pl.DeviceIdType.MESH
        )
        return carry

    lax.fori_loop(1, count, greet, 0)

    def w_rows(mask, half=None):
        start = flip(me, mask) * share
        if half is None:
            return w_buf.at[pl.ds(pl.multiple_of(start, share), share)]
        size = share // 2
        return w_buf.at[pl.ds(pl.multiple_of(start + half * size, size), size)]

    here = pl.ds(pl.multiple_of(me * share, share), share)
    for part in range(3):
        w_buf[here, part * cols : (part + 1) * cols] = w_ref[part].astype(low)
    a_buf[pl.ds(pl.multiple_of(place * rows, rows), rows), :] = a_ref[...]
    pl.semaphore_wait(barrier, count - 1)

    def a_rows(block):
        return a_buf.at[pl.ds(pl.multiple_of(block * rows, rows), rows)]

    def keep(block):
        return pltpu.make_async_copy(
            a_rows(block),
            full_ref.at[pl.ds(pl.multiple_of(block * rows, rows), rows)],
            keep_sem.at[block],
        )

    def to_right(step):
        block = place - step
        return remote(
            a_rows(block), a_rows(block), line_send.at[0, step], line_recv.at[0, step],
            along(place + 1),
        )

    def to_left(step):
        block = place + step
        return remote(
            a_rows(block), a_rows(block), line_send.at[1, step], line_recv.at[1, step],
            along(place - 1),
        )

    def from_left(step):
        block = place - 1 - step
        return remote(
            a_rows(block), a_rows(block), line_send.at[0, step], line_recv.at[0, step],
            along(place - 1),
        )

    def from_right(step):
        block = place + 1 + step
        return remote(
            a_rows(block), a_rows(block), line_send.at[1, step], line_recv.at[1, step],
            along(place + 1),
        )

    def sends_right(step):
        return jnp.logical_and(place - step >= 0, place + 1 < slices)

    def sends_left(step):
        return jnp.logical_and(place + step < slices, place >= 1)

    pl.when(sends_right(0))(lambda: to_right(0).start())
    pl.when(sends_left(0))(lambda: to_left(0).start())

    w_copies = []
    for at, mask in enumerate(masks):
        copy = remote(w_rows(0), w_rows(0), w_send.at[at], w_recv.at[at], across(mask))
        copy.start()
        w_copies.append(copy)

    keep(place).start()
    all_ref[place] = small_ref[...]
    small_copies = []
    for step in range(1, slices):
        copy = remote(
            small_ref, all_ref.at[place], small_send.at[step], small_recv.at[step], beside(step)
        )
        copy.start()
        small_copies.append(copy)

    def tell(step):
        return remote(
            count_ref, counts_ref.at[step], count_send.at[step], count_recv.at[step], anyone(step)
        )

    counts_ref[0] = count_ref[...]
    lax.fori_loop(1, count, lambda step, carry: (tell(step).start(), carry)[1], 0)

    out_here = pl.ds(pl.multiple_of(place * cols, cols), cols)
    out_buf[out_here, :] = out_ref[...].astype(low)
    out_copies = []
    for step in range(1, slices):
        target = out_buf.at[out_here]
        copy = remote(target, target, out_send.at[step], out_recv.at[step], beside(step))
        copy.start()
        out_copies.append(copy)

    for part in range(groups):
        if raw:
            row = part * piece // cols
            start = part * piece % cols
            wide_buf[part] = wide_ref[:, row, start : start + piece].astype(low)
            thin_buf[part] = thin_ref[row, start : start + piece, :].astype(low)
        else:
            wide_buf[part] = wide_ref[part]
            thin_buf[part] = thin_ref[part]
    thin_cols = thin_buf.shape[2]
    wide_here = wide_all.at[here]
    thin_here = thin_all.at[:, pl.ds(pl.multiple_of(me * thin_cols, thin_cols), thin_cols)]

    def to_group(step):
        other = lax.rem(me + step, groups)
        device = (other, place)
        return (
            remote(wide_buf.at[other], wide_here, wide_send.at[step], wide_recv.at[step], device),
            remote(thin_buf.at[other], thin_here, thin_send.at[step], thin_recv.at[step], device),
        )

    own_wide = pltpu.make_async_copy(wide_buf.at[me], wide_here, local_sem.at[2])
    own_wide.start()
    own_thin = pltpu.make_async_copy(thin_buf.at[me], thin_here, local_sem.at[3])
    own_thin.start()
    for step in range(1, groups):
        for copy in to_group(step):
            copy.start()

    pair_copies = []

    def to_pair(source):
        at = len(pair_copies)
        copy = remote(source, source, pair_send.at[at], pair_recv.at[at], across(1))
        copy.start()
        pair_copies.append(copy)

    to_pair(w_rows(0))
    for at, copy in enumerate(w_copies):
        remote(
            w_rows(masks[at]), w_rows(masks[at]), w_send.at[at], w_recv.at[at], across(masks[at])
        ).wait_recv()
    hop_copies = []
    for number, (mask, half, goal) in enumerate(hops):
        at = len(masks) + number
        source = w_rows(mask, half)
        copy = remote(source, source, w_send.at[at], w_recv.at[at], across(goal))
        copy.start()
        hop_copies.append(copy)
    for mask in masks:
        to_pair(w_rows(mask))

    own = pltpu.make_async_copy(e_ref, back_ref.at[pl.ds(0, rows)], local_sem.at[0])
    own.start()
    e_copies = []
    for at, mask in enumerate(masks):
        target = back_ref.at[pl.ds((at + 1) * rows, rows)]
        copy = remote(e_ref, target, e_send.at[at], e_recv.at[at], across(mask))
        copy.start()
        e_copies.append(copy)

    for number, (mask, half, goal) in enumerate(hops):
        at = len(masks) + number
        landed = w_rows(2 + 4, half)
        remote(landed, landed, w_send.at[at], w_recv.at[at], across(goal)).wait_recv()
        to_pair(landed)
    sources = [0] + masks
    for at, mask in enumerate(sources):
        landed = w_rows(mask + 1)
        remote(landed, landed, pair_send.at[at], pair_recv.at[at], across(1)).wait_recv()
    for number, (mask, half, goal) in enumerate(hops):
        at = len(sources) + number
        landed = w_rows(2 + 4 + 1, half)
        remote(landed, landed, pair_send.at[at], pair_recv.at[at], across(1)).wait_recv()
    weights_out = pltpu.make_async_copy(w_buf, weight_ref, local_sem.at[1])
    weights_out.start()

    def multiply(block):
        where = pl.ds(pl.multiple_of(block * rows, rows), rows)
        left = a_buf[where, :]
        for part in range(3):
            columns = slice(part * cols, (part + 1) * cols)
            product = dot_as(left, w_buf[:, columns], PLAIN) + bias_ref[0:1, columns]
            mixed_ref[where, columns] = product.astype(low)

    multiply(place)

    def out_at(mask, half=None):
        start = pl.multiple_of(flip(me, mask) * out_cols, out_cols)
        size = out_all.shape[0] // 2
        if half is None:
            return out_all.at[:, pl.ds(start, out_cols)]
        return out_all.at[half * size : (half + 1) * size, pl.ds(start, out_cols)]

    own_out = pltpu.make_async_copy(out_buf, out_at(0), local_sem.at[4])

    def plane(at, source, target, device):
        return remote(source, target, plane_send.at[at], plane_recv.at[at], device)

    def plane_first():
        return [
            plane(at, out_buf, out_at(0), across(mask)) for at, mask in enumerate([1] + masks)
        ]

    def plane_landed():
        return [
            plane(at, out_buf, out_at(mask), across(mask)) for at, mask in enumerate([1] + masks)
        ]

    def plane_hops():
        return [
            plane(1 + len(masks) + number, out_at(mask, half), out_at(mask, half), across(goal))
            for number, (mask, half, goal) in enumerate(hops)
        ]

    def plane_pairs():
        return [
            plane(1 + len(masks) + len(hops) + at, out_at(mask), out_at(mask), across(1))
            for at, mask in enumerate(masks)
        ]

    def plane_last():
        return [
            plane(
                1 + 2 * len(masks) + len(hops) + number, out_at(6, half), out_at(6, half), across(1)
            )
            for number, (mask, half, goal) in enumerate(hops)
        ]

    def pass_on(step, carry):
        got_left = place - 1 - step >= 0
        got_right = place + 1 + step < slices

        @pl.when(got_left)
        def _():
            from_left(step).wait_recv()

            @pl.when(jnp.logical_and(step + 1 < slices - 1, sends_right(step + 1)))
            def _():
                to_right(step + 1).start()

            keep(place - 1 - step).start()

        @pl.when(got_right)
        def _():
            from_right(step).wait_recv()

            @pl.when(jnp.logical_and(step + 1 < slices - 1, sends_left(step + 1)))
            def _():
                to_left(step + 1).start()

            keep(place + 1 + step).start()

        @pl.when(step == 0)
        def _():
            for copy in out_copies:
                copy.wait_recv()
            own_out.start()
            for copy in plane_first():
                copy.start()

        @pl.when(got_left)
        def _():
            multiply(place - 1 - step)

        @pl.when(got_right)
        def _():
            multiply(place + 1 + step)

        @pl.when(step == 1)
        def _():
            for copy in plane_landed():
                copy.wait_recv()
            for copy in plane_hops() + plane_pairs():
                copy.start()

        return carry

    lax.fori_loop(0, slices - 1, pass_on, 0)

    for number, (mask, half, goal) in enumerate(hops):
        at = 1 + len(masks) + number
        plane(at, out_at(6, half), out_at(6, half), across(goal)).wait_recv()
    for copy in plane_last():
        copy.start()
    for at, mask in enumerate(masks):
        landed = out_at(mask + 1)
        plane(1 + len(masks) + len(hops) + at, landed, landed, across(1)).wait_recv()
    for number, (mask, half, goal) in enumerate(hops):
        landed = out_at(7, half)
        plane(1 + 2 * len(masks) + len(hops) + number, landed, landed, across(1)).wait_recv()
    for copy in plane_first() + plane_hops() + plane_pairs() + plane_last():
        copy.wait_send()
    for at, mask in enumerate(masks):
        landed = back_ref.at[pl.ds((at + 1) * rows, rows)]
        remote(e_ref, landed, e_send.at[at], e_recv.at[at], across(mask)).wait_recv()
    for copy in e_copies + w_copies + hop_copies + pair_copies + out_copies:
        copy.wait_send()
    for copy in small_copies:
        copy.wait()
    for step in range(1, groups):
        other = lax.rem(me + groups - step, groups)
        wide_from = wide_all.at[pl.ds(pl.multiple_of(other * share, share), share)]
        thin_from = thin_all.at[
            :, pl.ds(pl.multiple_of(other * thin_cols, thin_cols), thin_cols)
        ]
        device = (other, place)
        remote(
            wide_buf.at[other], wide_from, wide_send.at[step], wide_recv.at[step], device
        ).wait_recv()
        remote(
            thin_buf.at[other], thin_from, thin_send.at[step], thin_recv.at[step], device
        ).wait_recv()
        for copy in to_group(step):
            copy.wait_send()
    lax.fori_loop(1, count, lambda step, carry: (tell(step).wait(), carry)[1], 0)
    for copy in (own, weights_out, own_wide, own_thin, own_out):
        copy.wait()

    def finish(step, carry):
        pl.when(sends_right(step))(lambda: to_right(step).wait_send())
        pl.when(sends_left(step))(lambda: to_left(step).wait_send())
        return carry

    lax.fori_loop(0, slices - 1, finish, 0)
    for block in range(slices):
        keep(block).wait()


def open_step(normed, inward, back, bias, small, living, widening, narrowing, outward):
    groups = lax.axis_size("dp")
    slices = lax.axis_size("tensor")
    count = groups * slices
    quads = groups // 2
    rows, width = normed.shape
    share, _, cols = inward.shape
    piece = 4 * cols // groups
    out_cols = outward.shape[1]
    hops = len(two_hops(quads))
    direct = len(direct_masks(quads))
    dma = pltpu.SemaphoreType.DMA
    vmem = pl.BlockSpec(memory_space=pltpu.VMEM)
    hbm = pl.BlockSpec(memory_space=pl.ANY)
    low = jnp.bfloat16
    wide = jnp.float32
    if piece % 128:
        widening = widening.astype(low).reshape(share, groups, piece).transpose(1, 0, 2)
        narrowing = narrowing.astype(low).reshape(groups, piece, out_cols)
    shape = jax.ShapeDtypeStruct
    planes = 1 + 2 * direct + 2 * hops
    return pl.pallas_call(
        functools.partial(open_kernel, groups=groups, slices=slices, piece=piece),
        in_specs=[vmem, vmem, hbm, vmem, vmem, vmem, vmem, vmem, vmem],
        out_specs=[hbm, hbm, vmem, hbm, vmem, vmem, hbm, hbm, hbm],
        out_shape=[
            shape((slices * rows, width), low),
            shape((width, 3 * cols), low),
            shape((slices * rows, 3 * cols), low),
            shape((quads * rows, width), low),
            shape((slices,) + small.shape, wide),
            shape((count, 8, 128), wide),
            shape((width, piece), low),
            shape((piece, width), low),
            shape((width, width), low),
        ],
        scratch_shapes=[
            pltpu.VMEM((slices * rows, width), low),
            pltpu.VMEM((width, 3 * cols), low),
            pltpu.VMEM((groups, share, piece), low),
            pltpu.VMEM((groups, piece, out_cols), low),
            pltpu.VMEM((slices * cols, out_cols), low),
            dma((2, slices)),
            dma((2, slices)),
            dma((slices,)),
            dma((slices,)),
            dma((direct + hops,)),
            dma((direct + hops,)),
            dma((1 + direct + hops,)),
            dma((1 + direct + hops,)),
            dma((direct,)),
            dma((direct,)),
            dma((5,)),
            dma((slices,)),
            dma((count,)),
            dma((count,)),
            dma((groups,)),
            dma((groups,)),
            dma((groups,)),
            dma((groups,)),
            dma((slices,)),
            dma((slices,)),
            dma((planes,)),
            dma((planes,)),
        ],
        compiler_params=pltpu.CompilerParams(
            collective_id=1, has_side_effects=True, vmem_limit_bytes=VMEM_BYTES
        ),
        cost_estimate=pl.CostEstimate(
            flops=2 * slices * rows * width * 3 * cols,
            bytes_accessed=400 * 2**20,
            transcendentals=0,
        ),
        name="open_step",
    )(
        normed, inward.transpose(1, 0, 2), back, bias, small, living, widening, narrowing, outward
    )


def hidden_gather_kernel(
    b_ref, weight_ref, bias_ref, all_ref, hid_ref, full_ref,
    b_buf, w_buf, stage, b_send, b_recv, keep_sem, stage_sem, w_sem, pair_sem, out_sem,
    *, groups
):
    quads = groups // 2
    me = lax.axis_index("dp")
    place = lax.axis_index("tensor")
    rows = b_ref.shape[0]
    tiles, _, tile = weight_ref.shape
    masks = direct_masks(quads)
    hops = two_hops(quads)
    half_rows = rows // 2

    def across(mask):
        return (flip(me, mask), place)

    load = pltpu.make_async_copy(weight_ref, w_buf.at[pl.ds(0, tiles)], w_sem)
    load.start()
    greet_all([across(mask) for mask in [1] + masks])

    def block(at):
        return b_buf.at[pl.ds(at * rows, rows)]

    def piece(at, half):
        return b_buf.at[pl.ds(at * rows + half * half_rows, half_rows)]

    copies = []
    for at, mask in enumerate(masks):
        copy = remote(b_ref, block(at + 1), b_send.at[at], b_recv.at[at], across(mask))
        copy.start()
        copies.append(copy)
    pair = remote(
        weight_ref, w_buf.at[pl.ds(tiles, tiles)], pair_sem.at[0], pair_sem.at[1], across(1)
    )
    pair.start()
    b_buf[0:rows, :] = b_ref[...]
    keeps = []
    stores = []

    def keep(at):
        copy = pltpu.make_async_copy(
            block(at), all_ref.at[pl.ds(at * rows, rows)], keep_sem.at[at]
        )
        copy.start()
        keeps.append(copy)

    def multiply(at, first, amount):
        def part(number, carry):
            columns = pl.ds(pl.multiple_of(number * tile, tile), tile)
            stage[at % 2, :, columns] = (
                dot_as(b_buf[at * rows : (at + 1) * rows, :], w_buf[number], PLAIN)
                + bias_ref[0:1, columns]
            )
            return carry

        lax.fori_loop(first, first + amount, part, 0)

    def store(at):
        copy = pltpu.make_async_copy(
            stage.at[at % 2], hid_ref.at[pl.ds(at * rows, rows)], stage_sem.at[at]
        )
        copy.start()
        stores.append(copy)

    keep(0)
    load.wait()
    multiply(0, 0, tiles)
    pair.wait_recv()
    multiply(0, tiles, tiles)
    store(0)
    outs = []
    for number in range(2 * tiles):
        copy = pltpu.make_async_copy(
            w_buf.at[number],
            full_ref.at[:, pl.ds(number * tile, tile)],
            out_sem.at[number],
        )
        copy.start()
        outs.append(copy)
    for at in range(len(masks)):
        copies[at].wait_recv()
    for number, (mask, half, goal) in enumerate(hops):
        at = len(masks) + number
        copy = remote(
            piece(masks.index(mask) + 1, half), piece(3, half), b_send.at[at], b_recv.at[at],
            across(goal),
        )
        copy.start()
        copies.append(copy)
    for at in range(1, quads):
        if at == 1 + len(masks):
            for copy in copies[len(masks) :]:
                copy.wait_recv()
        keep(at)
        if at >= 2:
            stores[at - 2].wait()
        multiply(at, 0, 2 * tiles)
        store(at)
    for copy in copies + [pair]:
        copy.wait_send()
    for copy in keeps + stores[-2:] + outs:
        copy.wait()


def hidden_gather(rows_own, weight, bias):
    groups = lax.axis_size("dp")
    quads = groups // 2
    rows, width = rows_own.shape
    tiles, _, tile = weight.shape
    units = 2 * tiles * tile
    pieces = len(two_hops(quads)) + len(direct_masks(quads))
    dma = pltpu.SemaphoreType.DMA
    vmem = pl.BlockSpec(memory_space=pltpu.VMEM)
    hbm = pl.BlockSpec(memory_space=pl.ANY)
    return pl.pallas_call(
        functools.partial(hidden_gather_kernel, groups=groups),
        in_specs=[vmem, hbm, vmem],
        out_specs=[hbm, hbm, hbm],
        out_shape=[
            jax.ShapeDtypeStruct((quads * rows, width), jnp.bfloat16),
            jax.ShapeDtypeStruct((quads * rows, units), jnp.float32),
            jax.ShapeDtypeStruct((width, units), jnp.bfloat16),
        ],
        scratch_shapes=[
            pltpu.VMEM((quads * rows, width), jnp.bfloat16),
            pltpu.VMEM((2 * tiles, width, tile), jnp.bfloat16),
            pltpu.VMEM((2, rows, units), jnp.float32),
            dma((pieces,)),
            dma((pieces,)),
            dma((quads,)),
            dma((quads,)),
            dma,
            dma((2,)),
            dma((2 * tiles,)),
        ],
        compiler_params=pltpu.CompilerParams(
            collective_id=2, has_side_effects=True, vmem_limit_bytes=VMEM_BYTES
        ),
        cost_estimate=pl.CostEstimate(
            flops=2 * quads * rows * width * units,
            bytes_accessed=200 * 2**20,
            transcendentals=0,
        ),
        name="hidden_gather",
    )(rows_own, weight, bias)


def swap(values, axis, mask):
    count = lax.axis_size(axis)
    return lax.ppermute(values, axis, [(i, i ^ mask) for i in range(count)])


def gather_quads(rows):
    quads = lax.axis_size("dp") // 2
    if quads != 4:
        return [rows] + [swap(rows, "dp", 2 * m) for m in range(1, quads)]
    half = rows.shape[0] // 2
    first = swap(rows, "dp", 2)
    second = swap(rows, "dp", 4)
    return [
        rows,
        first,
        second,
        swap(first[:half], "dp", 4),
        swap(second[half:], "dp", 2),
    ]


def scatter_quads(parts):
    quads = lax.axis_size("dp") // 2
    wide = jnp.float32
    kind = jnp.bfloat16
    if quads != 4:
        total = parts[0].astype(wide)
        for m in range(1, quads):
            total = total + swap(parts[m].astype(kind), "dp", 2 * m).astype(wide)
        return total
    own, first, second, upper, lower = parts
    half = own.shape[0] // 2
    upper = swap(upper.astype(kind), "dp", 4).astype(wide)
    lower = swap(lower.astype(kind), "dp", 2).astype(wide)
    first_low = swap(first[half:].astype(kind), "dp", 2).astype(wide)
    second_up = swap(second[:half].astype(kind), "dp", 4).astype(wide)
    first_up = swap((first[:half].astype(wide) + upper).astype(kind), "dp", 2).astype(wide)
    second_low = swap((second[half:].astype(wide) + lower).astype(kind), "dp", 4).astype(wide)
    own = own.astype(wide)
    return jnp.concatenate(
        [
            own[:half] + first_up + second_up,
            own[half:] + first_low + second_low,
        ],
        axis=0,
    )


def quad_masks():
    quads = lax.axis_size("dp") // 2
    return [2 * m for m in range(quads)]


def gather_all(rows):
    count = lax.axis_size("dp")
    me = lax.axis_index("dp")
    parts = gather_quads(rows)
    if count == 8:
        parts = parts[:3] + [jnp.concatenate(parts[3:], axis=0)]
    near = jnp.stack(parts)
    far = swap(near, "dp", 1)
    held = jnp.stack([near, far], axis=1).reshape((count,) + rows.shape)
    return [lax.dynamic_index_in_dim(held, me ^ j, 0, keepdims=False) for j in range(count)]


def scatter_all(block_of):
    count = lax.axis_size("dp")
    me = lax.axis_index("dp")
    quads = count // 2
    far = jnp.stack([block_of(me ^ (2 * m + 1)) for m in range(quads)]).astype(jnp.bfloat16)
    far = swap(far, "dp", 1).astype(jnp.float32)
    parts = [block_of(me ^ (2 * m)) + far[m] for m in range(quads)]
    if quads == 4:
        half = parts[3].shape[0] // 2
        parts = parts[:3] + [parts[3][:half], parts[3][half:]]
    return scatter_quads(parts)


def trade(block_of):
    count = lax.axis_size("tensor")
    me = lax.axis_index("tensor")
    held = jnp.stack(
        [block_of(me)] + [swap(block_of(me ^ m), "tensor", m) for m in range(1, count)]
    )
    return [lax.dynamic_index_in_dim(held, me ^ j, 0, keepdims=False) for j in range(count)]


def sum_kernel(values_ref, out_ref, held, send_one, recv_one, send_two, recv_two, *, groups, slices):
    count = groups * slices
    me = lax.axis_index("dp") * slices + lax.axis_index("tensor")

    def target(step):
        other = lax.rem(me + step, count)
        return (other // slices, lax.rem(other, slices))

    barrier = pltpu.get_barrier_semaphore()

    def greet(step, carry):
        pl.semaphore_signal(
            barrier, inc=1, device_id=target(step), device_id_type=pl.DeviceIdType.MESH
        )
        return carry

    lax.fori_loop(1, count, greet, 0)
    pl.semaphore_wait(barrier, count - 1)

    def first(step):
        return pltpu.make_async_remote_copy(
            src_ref=values_ref.at[lax.rem(me + step, count)],
            dst_ref=held.at[step],
            send_sem=send_one.at[step],
            recv_sem=recv_one.at[step],
            device_id=target(step),
            device_id_type=pl.DeviceIdType.MESH,
        )

    def second(step):
        return pltpu.make_async_remote_copy(
            src_ref=held.at[0],
            dst_ref=out_ref.at[me],
            send_sem=send_two.at[step],
            recv_sem=recv_two.at[step],
            device_id=target(step),
            device_id_type=pl.DeviceIdType.MESH,
        )

    def start_first(step, carry):
        first(step).start()
        return carry

    def wait_first(step, total):
        first(step).wait()
        return total + held[step]

    def start_second(step, carry):
        second(step).start()
        return carry

    def wait_second(step, carry):
        second(step).wait()
        return carry

    lax.fori_loop(1, count, start_first, 0)
    total = lax.fori_loop(1, count, wait_first, values_ref[me])
    held[0] = total
    out_ref[me] = total
    lax.fori_loop(1, count, start_second, 0)
    lax.fori_loop(1, count, wait_second, 0)


def sum_everywhere(values):
    groups = lax.axis_size("dp")
    slices = lax.axis_size("tensor")
    count = groups * slices
    length = values.shape[0]
    room = count * 8 * 128
    packed = jnp.concatenate([values, jnp.zeros((room - length,), jnp.float32)])
    shape = (count, 8, 128)
    summed = pl.pallas_call(
        functools.partial(sum_kernel, groups=groups, slices=slices),
        in_specs=[pl.BlockSpec(memory_space=pltpu.VMEM)],
        out_specs=pl.BlockSpec(memory_space=pltpu.VMEM),
        out_shape=jax.ShapeDtypeStruct(shape, jnp.float32),
        scratch_shapes=[
            pltpu.VMEM(shape, jnp.float32),
            pltpu.SemaphoreType.DMA((count,)),
            pltpu.SemaphoreType.DMA((count,)),
            pltpu.SemaphoreType.DMA((count,)),
            pltpu.SemaphoreType.DMA((count,)),
        ],
        compiler_params=pltpu.CompilerParams(
            collective_id=0, has_side_effects=True, vmem_limit_bytes=8 * 2**20
        ),
        cost_estimate=pl.CostEstimate(
            flops=room, bytes_accessed=8 * room, transcendentals=0
        ),
        name="sum_everywhere",
    )(packed.reshape(shape))
    return summed.reshape(room)[:length]


def after(values, gate):
    return lax.optimization_barrier((values, gate))[0]


def adapt_step(weight, moment_one, moment_two, slope, decay):
    mean_new = beta_one * moment_one + (1.0 - beta_one) * slope
    square_new = beta_two * moment_two + (1.0 - beta_two) * slope * slope
    direction = (
        mean_new
        / (1.0 - beta_one**STEP_COUNT)
        / (jnp.sqrt(square_new / (1.0 - beta_two**STEP_COUNT)) + adam_epsilon)
        + decay * weight
    )
    return (mean_new, square_new, direction)


def trust_apply(weight, direction, weight_square, update_square):
    weight_norm = jnp.sqrt(weight_square)
    update_norm = jnp.sqrt(update_square)
    return (
        weight - learn_rate * weight_norm / (update_norm + trust_epsilon) * direction,
        weight_norm,
        update_norm,
    )


def on_device(
    tokens,
    cotangent,
    live_mask,
    inward,
    inward_first,
    inward_second,
    outward,
    outward_first,
    outward_second,
    widening,
    widening_first,
    widening_second,
    narrowing,
    narrowing_first,
    narrowing_second,
    column_bias,
    column_first,
    column_second,
    vectors,
    vectors_first,
    vectors_second,
):
    low = jnp.bfloat16
    wide = jnp.float32
    amount, width = tokens.shape
    cols = column_bias.shape[1]
    groups = lax.axis_size("dp")
    slices = lax.axis_size("tensor")
    me = lax.axis_index("dp")
    place = lax.axis_index("tensor")
    share = inward.shape[0]
    piece = 4 * cols // groups

    inputs = tokens.astype(wide)
    living_here = live_mask.astype(wide)
    normed = layer_norm(inputs, vectors[0], vectors[1]).astype(low)
    back_out = (cotangent.astype(wide) * living_here[:, None]).astype(low)
    mixed_bias = jnp.concatenate(
        [column_bias[0], jnp.zeros((cols,), wide), column_bias[1]]
    ).reshape(1, 3 * cols)
    small_length = amount + 4 * cols
    small_rows = -(-small_length // 1024) * 8
    small = jnp.concatenate(
        [
            living_here,
            column_bias[2:].reshape(4 * cols),
            jnp.zeros((small_rows * 128 - small_length,), wide),
        ]
    ).reshape(small_rows, 128)
    (
        normed_full,
        inward_full,
        mixed,
        back_all,
        small_all,
        counts,
        wide_own,
        thin_own,
        outward_full,
    ) = open_step(
        normed,
        inward,
        back_out,
        mixed_bias,
        small,
        jnp.full((8, 128), jnp.sum(living_here)),
        widening,
        narrowing,
        outward,
    )
    factor = 1.0 / jnp.sum(counts[:, 0, 0])
    small_all = small_all.reshape(slices, small_rows * 128)
    length = normed_full.shape[0]
    bias_keys = jnp.where(small_all[:, :amount].reshape(length) > 0.5, 0.0, MASKED)
    bias_all = small_all[:, amount:small_length]

    wide_own = lax.all_gather(wide_own, "tensor", axis=0)
    if piece % 128:
        wide_own = wide_own.transpose(1, 0, 2).reshape(1, width, slices * piece)

    hidden_bias = jnp.concatenate(
        [
            lax.dynamic_slice_in_dim(bias_all, (me ^ side) * piece, piece, 1).reshape(1, -1)
            for side in range(2)
        ],
        axis=1,
    )

    context_wide, totals, context_own, back_all = attend_forward(
        mixed, bias_keys[None, :], back_all, amount
    )
    thin_own = lax.all_gather(
        after(thin_own, (wide_own, context_own)), "tensor", axis=0, tiled=True
    )
    middle = inputs + dot_as(context_own, outward_full, PLAIN) + vectors[2]
    normed_two = layer_norm(middle, vectors[3], vectors[4]).astype(low)

    quads = groups // 2
    rows_two_all, hidden, widening_full = hidden_gather(normed_two, wide_own, hidden_bias)
    thin_own = after(thin_own, hidden)
    narrowing_full = jnp.concatenate([thin_own, swap(thin_own, "dp", 1)], axis=0)
    last = quads - 1
    last = quads - 1
    active_all, back_hidden_all, far_sums = back_step(
        back_all, narrowing_full, hidden, last, 1, amount
    )

    def partial_of(at):
        rows = back_hidden_all[at * amount : (at + 1) * amount]
        return dot_as(rows, widening_full, ROWS, low if at else wide)

    partial = {last: partial_of(last)}
    active_all, back_hidden_all, near_sums = back_step(
        after(back_all, partial[last]), narrowing_full, hidden, 0, last, amount,
        (active_all, back_hidden_all),
    )
    for at in list(range(1, last)) + [0]:
        partial[at] = partial_of(at)
    partial_own = partial[0]
    parts = [partial[at] for at in range(quads)]
    if quads == 4:
        parts = parts[:3] + [parts[3][: amount // 2], parts[3][amount // 2 :]]
    back_normed_two = scatter_quads(parts)

    half_units = slices * piece
    hidden_sums = [far_sums[0]] + [near_sums[at] for at in range(last)]

    def pair_sum(own, other):
        return (own + swap(other.astype(low), "dp", 1).astype(wide)).astype(low)

    active_all, back_all = after((active_all, back_all), list(partial.values()))
    slope_narrowing = pair_sum(
        dot_as(active_all[:, :half_units], back_all, TOKENS),
        dot_as(active_all[:, half_units:], back_all, TOKENS),
    )
    sum_narrowing = lax.psum_scatter(slope_narrowing, "tensor", scatter_dimension=0, tiled=True)
    rows_two_all, back_hidden_all = after((rows_two_all, back_hidden_all), slope_narrowing)
    slope_widening = pair_sum(
        dot_as(rows_two_all, back_hidden_all[:, :half_units], TOKENS),
        dot_as(rows_two_all, back_hidden_all[:, half_units:], TOKENS),
    )

    _, norm_two_pull = jax.vjp(layer_norm, middle, vectors[3], vectors[4])
    back_middle_norm, slope_gain_two, slope_shift_two = norm_two_pull(back_normed_two)
    back_middle = back_out.astype(wide) + back_middle_norm
    back_low = back_middle.astype(low)

    back_mixed = attend_backward(
        after(back_low, slope_widening), outward_full, mixed, context_wide, totals, bias_keys[:, None]
    )
    active_all, context_own, back_low = after((active_all, context_own, back_low), back_mixed)
    widened = dot_as(active_all, narrowing_full, PLAIN, low)
    widened = [widened[at * amount : (at + 1) * amount] for at in range(quads)]
    if quads == 4:
        widened = widened[:3] + [widened[3][: amount // 2], widened[3][amount // 2 :]]
    widened = scatter_quads(widened)
    layer_output = (middle + widened + vectors[5]).astype(low)

    slope_outward = dot_as(context_own, back_low, TOKENS)
    out_share = outward.shape[1]
    slope_outward = (
        scatter_all(
            lambda j: lax.dynamic_slice_in_dim(slope_outward, j * out_share, out_share, 1).T
        )
        .T.astype(low)
    )
    out_rows = outward.shape[0]
    sum_outward = functools.reduce(
        jnp.add,
        [
            part.astype(wide)
            for part in trade(
                lambda j: lax.dynamic_slice_in_dim(slope_outward, j * out_rows, out_rows, 0)
            )
        ],
    )

    slope_widening = after(slope_widening, sum_narrowing)
    slope_widening = slope_widening.reshape(width, slices, piece).transpose(1, 0, 2)
    sum_widening = lax.psum_scatter(slope_widening, "tensor", scatter_dimension=0, tiled=True)

    back_normed_part = dot_as(back_mixed, inward_full, ROWS, low)
    back_normed = lax.psum_scatter(
        after(back_normed_part, sum_widening), "tensor", scatter_dimension=0, tiled=True
    )
    back_mixed = after(back_mixed, back_normed_part)
    slope_inward = dot_as(normed_full, back_mixed, TOKENS)
    sum_inward = scatter_all(
        lambda j: lax.dynamic_slice_in_dim(slope_inward, j * share, share, 0)
    ).reshape(inward.shape)

    sum_narrowing = lax.all_to_all(
        sum_narrowing.reshape(piece, groups, -1).transpose(1, 0, 2), "dp", 0, 0, tiled=True
    ).reshape(narrowing.shape)
    sum_widening = (
        lax.all_to_all(sum_widening.reshape(groups, share, piece), "dp", 0, 0, tiled=True)
        .transpose(1, 0, 2)
        .reshape(widening.shape)
    )

    hidden_total = hidden_sums[0]
    for sums in hidden_sums[1:]:
        hidden_total = hidden_total + sums
    hidden_total = hidden_total.reshape(2, 1, slices, piece)
    hidden_slots = jnp.zeros((groups, slices, piece), wide)
    hidden_slots = lax.dynamic_update_slice(hidden_slots, hidden_total[0], (me, 0, 0))
    hidden_slots = lax.dynamic_update_slice(hidden_slots, hidden_total[1], (me ^ 1, 0, 0))
    mixed_sums = jnp.stack(
        [
            jnp.sum(back_mixed[:, :cols], axis=0, dtype=wide),
            jnp.sum(back_mixed[:, 2 * cols :], axis=0, dtype=wide),
        ]
    )
    mixed_slots = lax.dynamic_update_slice(
        jnp.zeros((slices, 2, cols), wide), mixed_sums[None], (place, 0, 0)
    )
    late_rows = jnp.stack(
        [
            jnp.sum(back_middle, axis=0),
            slope_gain_two,
            slope_shift_two,
            jnp.sum(back_out, axis=0, dtype=wide),
        ]
    )
    packed = sum_everywhere(
        jnp.concatenate(
            [
                hidden_slots.reshape(-1),
                mixed_slots.reshape(-1),
                late_rows.reshape(-1),
            ]
        )
    )
    first_cut = groups * slices * piece
    second_cut = first_cut + slices * 2 * cols
    hidden_slots = packed[:first_cut].reshape(groups, slices, piece)
    hidden_rows = lax.dynamic_slice_in_dim(hidden_slots, place, 1, 1).reshape(4, cols)
    mixed_rows = lax.dynamic_index_in_dim(
        packed[first_cut:second_cut].reshape(slices, 2, cols), place, 0, keepdims=False
    )
    late_rows = packed[second_cut:].reshape(4, width)
    column_total = jnp.concatenate([mixed_rows, hidden_rows], axis=0)

    masters = (inward, outward, widening, narrowing)
    firsts = (inward_first, outward_first, widening_first, narrowing_first)
    seconds = (inward_second, outward_second, widening_second, narrowing_second)
    orders = ((1, 0, 2), (0, 1), (0, 1, 2), (0, 1, 2))
    summed_all = [
        with_layout_constraint(summed.astype(wide), Layout(order))
        for summed, order in zip(
            (sum_inward, sum_outward, sum_widening, sum_narrowing), orders
        )
    ]
    matrix_steps = [
        adapt_step(
            masters[ordinal],
            firsts[ordinal],
            seconds[ordinal],
            summed_all[ordinal] * factor,
            decay_rate,
        )
        for ordinal in range(4)
    ]
    column_mean, column_square, column_direction = adapt_step(
        column_bias, column_first, column_second, column_total * factor, 0.0
    )
    column_groups = ((0, 1), (1, 2), (2, 6))

    def square_sum(array):
        return jnp.sum(array * array)

    squares = [square_sum(master) for master in masters]
    squares += [square_sum(column_bias[start:stop]) / groups for start, stop in column_groups]
    squares += [square_sum(step[2]) for step in matrix_steps]
    squares += [square_sum(column_direction[start:stop]) / groups for start, stop in column_groups]
    norm_totals = sum_everywhere(jnp.stack(squares)).reshape(2, 7)

    results = []
    weight_norms = []
    update_norms = []
    for ordinal in range(4):
        fresh, weight_norm, update_norm = trust_apply(
            masters[ordinal],
            matrix_steps[ordinal][2],
            norm_totals[0, ordinal],
            norm_totals[1, ordinal],
        )
        results += [
            fresh,
            matrix_steps[ordinal][0],
            matrix_steps[ordinal][1],
            fresh.astype(low),
        ]
        weight_norms.append(weight_norm)
        update_norms.append(update_norm)
    column_parts = []
    for ordinal in range(3):
        start, stop = column_groups[ordinal]
        fresh, weight_norm, update_norm = trust_apply(
            column_bias[start:stop],
            column_direction[start:stop],
            norm_totals[0, 4 + ordinal],
            norm_totals[1, 4 + ordinal],
        )
        column_parts.append(fresh)
        weight_norms.append(weight_norm)
        update_norms.append(update_norm)
    _, norm_one_pull = jax.vjp(layer_norm, inputs, vectors[0], vectors[1])
    back_inputs_norm, slope_gain_one, slope_shift_one = norm_one_pull(
        after(back_normed, results).astype(wide)
    )
    back_inputs = back_middle + back_inputs_norm

    early_rows = sum_everywhere(
        after(jnp.concatenate([slope_gain_one, slope_shift_one]), norm_totals)
    ).reshape(2, width)
    vector_total = jnp.concatenate([early_rows, late_rows], axis=0)

    vectors_mean, vectors_square, vectors_direction = adapt_step(
        vectors, vectors_first, vectors_second, vector_total * factor, 0.0
    )
    new_vectors, vector_weight_norms, vector_update_norms = trust_apply(
        vectors,
        vectors_direction,
        jnp.sum(vectors * vectors, axis=1, keepdims=True),
        jnp.sum(vectors_direction * vectors_direction, axis=1, keepdims=True),
    )
    trust_norms = jnp.stack(
        [
            jnp.concatenate([jnp.stack(weight_norms), vector_weight_norms[:, 0]]),
            jnp.concatenate([jnp.stack(update_norms), vector_update_norms[:, 0]]),
        ]
    )
    return (
        layer_output,
        back_inputs * factor,
        *results,
        jnp.concatenate(column_parts, axis=0),
        column_mean,
        column_square[0],
        column_square[1],
        column_square[2:],
        new_vectors,
        vectors_mean,
        vectors_square[0:2],
        vectors_square[2:],
        trust_norms,
    )


def solution(mesh):
    in_specs = (
        P(("dp", "tensor"), None),
        P(("dp", "tensor"), None),
        P(("dp", "tensor")),
        P("dp", None, "tensor"),
        P("dp", None, "tensor"),
        P("dp", None, "tensor"),
        P("tensor", "dp"),
        P("tensor", "dp"),
        P("tensor", "dp"),
        P("dp", None, "tensor"),
        P("dp", None, "tensor"),
        P("dp", None, "tensor"),
        P(None, "tensor", "dp"),
        P(None, "tensor", "dp"),
        P(None, "tensor", "dp"),
        P(None, "tensor"),
        P(None, "tensor"),
        P(None, "tensor"),
        P(),
        P(),
        P(),
    )
    out_specs = (
        P(("dp", "tensor"), None),
        P(("dp", "tensor"), None),
        P("dp", None, "tensor"),
        P("dp", None, "tensor"),
        P("dp", None, "tensor"),
        P("dp", None, "tensor"),
        P("tensor", "dp"),
        P("tensor", "dp"),
        P("tensor", "dp"),
        P("tensor", "dp"),
        P("dp", None, "tensor"),
        P("dp", None, "tensor"),
        P("dp", None, "tensor"),
        P("dp", None, "tensor"),
        P(None, "tensor", "dp"),
        P(None, "tensor", "dp"),
        P(None, "tensor", "dp"),
        P(None, "tensor", "dp"),
        P(None, "tensor"),
        P(None, "tensor"),
        P("tensor"),
        P("tensor"),
        P(None, "tensor"),
        P(),
        P(),
        P(),
        P(),
        P(),
    )
    return jax.shard_map(
        on_device, mesh=mesh, in_specs=in_specs, out_specs=out_specs, check_vma=False
    )
```

```python
import functools

import jax
import jax.numpy as jnp
from jax import lax
from jax.experimental import pallas as pl
from jax.experimental.layout import Layout, with_layout_constraint
from jax.experimental.pallas import tpu as pltpu
from jax.sharding import PartitionSpec as P

HEAD_DIM = 128
QUERY_BLOCK = 512
STEP_COUNT = 10
LOG2E = 1.4426950408889634
MASKED = -1e30
VMEM_BYTES = 56 * 2**20
ROWS = (((1,), (1,)), ((), ()))
TOKENS = (((0,), (0,)), ((), ()))

norm_epsilon = 1e-05
beta_one = 0.9
beta_two = 0.999
adam_epsilon = 1e-06
decay_rate = 0.01
learn_rate = 0.5
trust_epsilon = 1e-06


def layer_norm(values, gain_row, shift_row):
    centre = values - jnp.mean(values, axis=-1, keepdims=True)
    spread = jnp.mean(centre * centre, axis=-1, keepdims=True)
    return centre * lax.rsqrt(spread + norm_epsilon) * gain_row + shift_row


def dot_as(left, right, dims, kind=jnp.float32):
    return lax.dot_general(left, right, dims, preferred_element_type=jnp.float32).astype(kind)


PLAIN = (((1,), (0,)), ((), ()))


def flip(index, mask):
    result = index
    bit = 1
    while bit <= mask:
        if mask & bit:
            result = result + bit - 2 * bit * lax.rem(lax.div(index, bit), 2)
        bit *= 2
    return result


def greet_all(peers):
    barrier = pltpu.get_barrier_semaphore()
    for peer in peers:
        pl.semaphore_signal(barrier, inc=1, device_id=peer, device_id_type=pl.DeviceIdType.MESH)
    pl.semaphore_wait(barrier, len(peers))


def remote(source, target, send, receive, device):
    return pltpu.make_async_remote_copy(
        src_ref=source,
        dst_ref=target,
        send_sem=send,
        recv_sem=receive,
        device_id=device,
        device_id_type=pl.DeviceIdType.MESH,
    )


def everyone(groups, slices):
    count = groups * slices
    me = lax.axis_index("dp") * slices + lax.axis_index("tensor")

    def anyone(step):
        other = lax.rem(me + step, count)
        return (lax.div(other, slices), lax.rem(other, slices))

    def greet():
        barrier = pltpu.get_barrier_semaphore()

        def signal(step, carry):
            pl.semaphore_signal(
                barrier, inc=1, device_id=anyone(step), device_id_type=pl.DeviceIdType.MESH
            )
            return carry

        lax.fori_loop(1, count, signal, 0)
        pl.semaphore_wait(barrier, count - 1)

    return anyone, greet


def spread_sum(
    values_ref, out_ref, held, send_one, recv_one, send_two, recv_two, anyone, groups, slices
):
    count = groups * slices
    me = lax.axis_index("dp") * slices + lax.axis_index("tensor")

    def first(step):
        source = values_ref.at[lax.rem(me + step, count)]
        return remote(
            source, held.at[step], send_one.at[step], recv_one.at[step], anyone(step)
        )

    def second(step):
        return remote(
            held.at[0], out_ref.at[me], send_two.at[step], recv_two.at[step], anyone(step)
        )

    def each(action):
        lax.fori_loop(1, count, lambda step, carry: (action(step), carry)[1], 0)

    def wait_first(step, total):
        first(step).wait()
        return total + held[step]

    def start():
        each(lambda step: first(step).start())

    def middle():
        total = lax.fori_loop(1, count, wait_first, values_ref[me])
        held[0] = total
        out_ref[me] = total
        each(lambda step: second(step).start())

    def end():
        each(lambda step: second(step).wait())

    return start, middle, end


def sum_scratch(count):
    dma = pltpu.SemaphoreType.DMA
    return [pltpu.VMEM((count, 8, 128), jnp.float32)] + [dma((count,))] * 4


def direct_masks(quads):
    return [2, 4] if quads == 4 else [2 * m for m in range(1, quads)]


def two_hops(quads):
    return [(2, 0, 4), (4, 1, 2)] if quads == 4 else []


def square_reduce(quads, rows, across, send, receive, parts, sums, hop_buf, in_buf):
    masks = direct_masks(quads)
    half_rows = rows // 2

    def landing(at, half):
        return in_buf.at[at, pl.ds(half * half_rows, half_rows)]

    def hop(half):
        goal = 4 if half == 0 else 2
        return remote(
            parts(3, half), hop_buf.at[half], send.at[half], receive.at[half], across(goal)
        )

    def plain(at, half, source):
        number = 2 + 2 * at + half
        return remote(
            source, landing(at, half), send.at[number], receive.at[number], across(masks[at])
        )

    def whole(at):
        return remote(
            parts(at + 1, None), in_buf.at[at], send.at[at], receive.at[at], across(masks[at])
        )

    def early(block):
        if quads != 4:
            whole(block - 1).start()
        elif block == 3:
            hop(0).start()
            hop(1).start()
        else:
            half = 1 if block == 1 else 0
            plain(block - 1, half, parts(block, half)).start()

    def middle():
        if quads != 4:
            return
        for block, half in ((1, 0), (2, 1)):
            hop(half).wait_recv()
            target = sums(block, half)
            target[...] = (
                target[...].astype(jnp.float32) + hop_buf[half].astype(jnp.float32)
            ).astype(jnp.bfloat16)
            plain(block - 1, half, target).start()

    def end():
        if quads != 4:
            for at in range(quads - 1):
                whole(at).wait()
            return
        for half in range(2):
            hop(half).wait_send()
            for block in (1, 2):
                plain(block - 1, half, parts(block, half)).wait()

    return early, middle, end


def pair_reduce(quads, me, across, block_of, near, far, send, receive, load_sem):
    copies = []
    for m in range(quads):
        copies.append(
            remote(
                block_of(flip(me, 2 * m + 1)), far.at[m], send.at[m], receive.at[m], across(1)
            )
        )
    loads = [
        pltpu.make_async_copy(block_of(flip(me, 2 * m)), near.at[m], load_sem.at[m])
        for m in range(quads)
    ]

    def start():
        for copy in copies + loads:
            copy.start()

    def finish(m):
        loads[m].wait()
        copies[m].wait()
        near[m] = (near[m].astype(jnp.float32) + far[m].astype(jnp.float32)).astype(near.dtype)

    return start, finish


def reduce_scratch(quads, rows, width):
    dma = pltpu.SemaphoreType.DMA
    return [
        pltpu.VMEM((2, rows // 2, width), jnp.bfloat16),
        pltpu.VMEM((len(direct_masks(quads)), rows, width), jnp.bfloat16),
        dma((max(6, quads - 1),)),
        dma((max(6, quads - 1),)),
    ]


def forward_kernel(
    q_ref, k_ref, v_ref, bias_ref, back_ref, wide_ref, total_ref, own_ref, back_out,
    held, send_sem, recv_sem, keep_sem, e_send, e_recv,
    *, heads, blocks, size, slices, groups
):
    factor = HEAD_DIM**-0.5 * LOG2E
    head = pl.program_id(0)
    which = pl.program_id(1)
    me = lax.axis_index("dp")
    place = lax.axis_index("tensor")
    rows = own_ref.shape[0]
    queries = q_ref[...]
    masks = direct_masks(groups // 2)
    hops = two_hops(groups // 2)

    def across(mask):
        return (flip(me, mask), place)

    def e_hops():
        result = []
        half_rows = rows // 2
        for number, (mask, half, goal) in enumerate(hops):
            start = (masks.index(mask) + 1) * rows + half * half_rows
            source = back_ref.at[pl.ds(start, half_rows)]
            target = back_out.at[pl.ds(3 * rows + half * half_rows, half_rows)]
            result.append(
                remote(source, target, e_send.at[number], e_recv.at[number], across(goal))
            )
        return result

    @pl.when(jnp.logical_and(head == 0, which == 0))
    def _():
        greet_all(
            [(me, lax.rem(place + step, slices)) for step in range(1, slices)]
            + [across(goal) for _, _, goal in hops]
        )
        for copy in e_hops():
            copy.start()

    for last in range(blocks):

        @pl.when(which == last)
        def _():
            parts = []
            peak = None
            for at in range(last + 1):
                keys = slice(at * size, (at + 1) * size)
                scores = dot_as(queries, k_ref[keys, :], ROWS) + bias_ref[0:1, keys]
                if at == last:
                    row = lax.broadcasted_iota(jnp.int32, (size, size), 0)
                    col = lax.broadcasted_iota(jnp.int32, (size, size), 1)
                    scores = jnp.where(col <= row, scores, MASKED)
                top = jnp.max(scores, axis=1, keepdims=True)
                peak = top if peak is None else jnp.maximum(peak, top)
                parts.append(scores)
            low = peak * factor
            total = None
            context = None
            for at in range(last + 1):
                keys = slice(at * size, (at + 1) * size)
                weights = jnp.exp2(parts[at] * factor - low)
                more = jnp.sum(weights, axis=1, keepdims=True)
                total = more if total is None else total + more
                term = dot_as(weights.astype(jnp.bfloat16), v_ref[keys, :], PLAIN)
                context = term if context is None else context + term
            context = context * (1.0 / total)
            held[head, last * size : (last + 1) * size, :] = context.astype(jnp.bfloat16)
            wide_ref[...] = context
            logs = jnp.broadcast_to(low + jnp.log2(total), (size, 128))
            total_ref[...] = jnp.transpose(logs)[0:1, :].reshape(1, 1, size)

    def to_owner(owner, number):
        step = lax.rem(owner - place + slices, slices)
        return remote(
            held.at[number, pl.ds(pl.multiple_of(owner * rows, rows), rows)],
            own_ref.at[:, columns(place, number)],
            send_sem.at[step, number],
            recv_sem.at[step, number],
            (me, owner),
        )

    def columns(other, number):
        start = (other * heads + number) * HEAD_DIM
        return pl.ds(pl.multiple_of(start, HEAD_DIM), HEAD_DIM)

    def stay(number):
        return pltpu.make_async_copy(
            held.at[number, pl.ds(pl.multiple_of(place * rows, rows), rows)],
            own_ref.at[:, columns(place, number)],
            keep_sem.at[number],
        )

    for part in range(size // rows):
        owner = which * (size // rows) + part
        pl.when(owner == place)(lambda: stay(head).start())
        pl.when(owner != place)(lambda: to_owner(owner, head).start())

    @pl.when(jnp.logical_and(head == heads - 1, which == blocks - 1))
    def _():
        for copy in e_hops():
            copy.wait()
        for number in range(heads):
            stay(number).wait()
            for step in range(1, slices):
                to_owner(lax.rem(place + step, slices), number).wait_send()
                source = lax.rem(place + slices - step, slices)
                remote(
                    held.at[number, pl.ds(0, rows)],
                    own_ref.at[:, columns(source, number)],
                    send_sem.at[step, number],
                    recv_sem.at[step, number],
                    (me, source),
                ).wait_recv()


def attend_forward(mixed, bias_row, back, rows):
    slices = lax.axis_size("tensor")
    groups = lax.axis_size("dp")
    hops = max(1, len(two_hops(groups // 2)))
    length = mixed.shape[0]
    cols = mixed.shape[1] // 3
    heads = cols // HEAD_DIM
    size = QUERY_BLOCK
    blocks = length // size
    part = pl.BlockSpec((size, HEAD_DIM), lambda h, i: (i, h))
    keys = pl.BlockSpec((length, HEAD_DIM), lambda h, i: (0, heads + h))
    values = pl.BlockSpec((length, HEAD_DIM), lambda h, i: (0, 2 * heads + h))
    dma = pltpu.SemaphoreType.DMA
    return pl.pallas_call(
        functools.partial(
            forward_kernel, heads=heads, blocks=blocks, size=size, slices=slices, groups=groups
        ),
        grid=(heads, blocks),
        in_specs=[
            part,
            keys,
            values,
            pl.BlockSpec((1, length), lambda h, i: (0, 0)),
            pl.BlockSpec(memory_space=pltpu.HBM),
        ],
        out_specs=[
            part,
            pl.BlockSpec((1, 1, size), lambda h, i: (h, 0, i)),
            pl.BlockSpec(memory_space=pltpu.HBM),
            pl.BlockSpec(memory_space=pltpu.HBM),
        ],
        input_output_aliases={4: 3},
        out_shape=[
            jax.ShapeDtypeStruct((length, cols), jnp.float32),
            jax.ShapeDtypeStruct((heads, 1, length), jnp.float32),
            jax.ShapeDtypeStruct((rows, slices * cols), jnp.bfloat16),
            jax.ShapeDtypeStruct(back.shape, back.dtype),
        ],
        scratch_shapes=[
            pltpu.VMEM((heads, length, HEAD_DIM), jnp.bfloat16),
            dma((slices, heads)),
            dma((slices, heads)),
            dma((heads,)),
            dma((hops,)),
            dma((hops,)),
        ],
        compiler_params=pltpu.CompilerParams(
            collective_id=3, has_side_effects=True, vmem_limit_bytes=VMEM_BYTES
        ),
        cost_estimate=pl.CostEstimate(
            flops=4 * length * length * cols,
            bytes_accessed=100 * 2**20,
            transcendentals=heads * length * length // 2,
        ),
        name="attend_forward",
    )(mixed, mixed, mixed, bias_row, back)


def backward_kernel(
    low_ref, out_ref, mixed_ref, wide_ref, total_ref, bias_ref, part_ref, thin_ref,
    grad_ref, layer_ref, thin_sum,
    sent, back_buf, sum_ref, half_buf, own_buf, hop_buf, in_buf, send, receive,
    send_sem, recv_sem, load_sem, thin_send, thin_recv, thin_load,
    *, blocks, size, slices, groups
):
    scale = HEAD_DIM**-0.5
    factor = scale * LOG2E
    me = lax.axis_index("dp")
    place = lax.axis_index("tensor")
    rows = low_ref.shape[0]
    cols = back_buf.shape[1]
    heads = cols // HEAD_DIM
    quads = groups // 2
    half_rows = rows // 2

    def across(mask):
        return (flip(me, mask), place)

    def parts(block, side):
        if side is None:
            return part_ref.at[pl.ds(block * rows, rows)]
        return part_ref.at[pl.ds(block * rows + side * half_rows, half_rows)]

    def sums(block, side):
        return half_buf.at[side]

    loads = [pltpu.make_async_copy(parts(0, None), own_buf, load_sem.at[0])]
    if quads == 4:
        for block, side in ((1, 0), (2, 1)):
            loads.append(
                pltpu.make_async_copy(parts(block, side), half_buf.at[side], load_sem.at[1 + side])
            )
    for copy in loads:
        copy.start()
    greet_all(
        [(me, lax.rem(place + step, slices)) for step in range(1, slices)]
        + [(lax.rem(me + step, groups), place) for step in range(1, groups)]
    )
    early, middle, end = square_reduce(
        quads, rows, across, send, receive, parts, sums, hop_buf, in_buf
    )

    thin_rows, thin_cols = thin_ref.shape[0], thin_sum.shape[1]

    def thin_columns(other):
        return thin_ref.at[:, pl.ds(pl.multiple_of(other * thin_cols, thin_cols), thin_cols)]

    def thin_place(other):
        return thin_sum.at[pl.ds(pl.multiple_of(other * thin_rows, thin_rows), thin_rows)]

    def thin_to(step):
        other = lax.rem(me + step, groups)
        return remote(
            thin_columns(other), thin_place(me), thin_send.at[step], thin_recv.at[step],
            (other, place),
        )

    def thin_from(step):
        other = lax.rem(me + groups - step, groups)
        return remote(
            thin_columns(other), thin_place(other), thin_send.at[step], thin_recv.at[step],
            (other, place),
        )

    thin_own = pltpu.make_async_copy(thin_columns(me), thin_place(me), thin_load)
    for block in [quads - 1] + list(range(1, quads - 1)):
        early(block)
    thin_own.start()
    for step in range(1, groups):
        thin_to(step).start()

    def span(start, size):
        return pl.ds(pl.multiple_of(start, size), size)

    def product(owner):
        return dot_as(low_ref[...], out_ref[span(owner * cols, cols), :], ROWS, jnp.bfloat16)

    def to_owner(step, head):
        return remote(
            sent.at[step - 1, :, span(head * HEAD_DIM, HEAD_DIM)],
            back_buf.at[span(place * rows, rows), span(head * HEAD_DIM, HEAD_DIM)],
            send_sem.at[step, head],
            recv_sem.at[step, head],
            (me, lax.rem(place + step, slices)),
        )

    for step in range(1, slices):
        sent[step - 1] = product(lax.rem(place + step, slices))
    for head in range(heads):
        for step in range(1, slices):
            to_owner(step, head).start()
    back_buf[span(place * rows, rows), :] = product(place)

    def one_head(head, carry):
        for step in range(1, slices):
            source = lax.rem(place + slices - step, slices)
            remote(
                sent.at[step - 1, :, span(head * HEAD_DIM, HEAD_DIM)],
                back_buf.at[span(source * rows, rows), span(head * HEAD_DIM, HEAD_DIM)],
                send_sem.at[step, head],
                recv_sem.at[step, head],
                (me, source),
            ).wait_recv()
        here = span(head * HEAD_DIM, HEAD_DIM)
        key_here = span(cols + head * HEAD_DIM, HEAD_DIM)
        value_here = span(2 * cols + head * HEAD_DIM, HEAD_DIM)
        inner = []
        for at in range(blocks):
            part = slice(at * size, (at + 1) * size)
            pairs = back_buf[part, here].astype(jnp.float32) * wide_ref[part, here]
            inner.append(jnp.sum(jnp.transpose(pairs), axis=0, keepdims=True))
        for key_at in range(blocks):
            keys = slice(key_at * size, (key_at + 1) * size)
            key_rows = mixed_ref[keys, key_here]
            values = mixed_ref[keys, value_here]
            bias = bias_ref[keys, 0:1]
            back_keys = None
            back_values = None
            for query_at in range(key_at, blocks):
                part = slice(query_at * size, (query_at + 1) * size)
                queries = mixed_ref[part, here]
                back = back_buf[part, here]
                level = dot_as(key_rows, queries, ROWS) * factor - total_ref[head, 0:1, part] + bias
                if query_at == key_at:
                    row = lax.broadcasted_iota(jnp.int32, (size, size), 0)
                    col = lax.broadcasted_iota(jnp.int32, (size, size), 1)
                    level = jnp.where(row <= col, level, MASKED)
                chances = jnp.exp2(level)
                back_chances = dot_as(values, back, ROWS)
                back_scores = (chances * (back_chances - inner[query_at])).astype(jnp.bfloat16)
                more_values = dot_as(chances.astype(jnp.bfloat16), back, PLAIN)
                more_keys = dot_as(back_scores, queries, PLAIN)
                more_queries = dot_as(back_scores, key_rows, TOKENS)
                if key_at == 0:
                    sum_ref[part, :] = more_queries
                else:
                    sum_ref[part, :] += more_queries
                back_keys = more_keys if back_keys is None else back_keys + more_keys
                back_values = more_values if back_values is None else back_values + more_values
            grad_ref[keys, key_here] = (back_keys * scale).astype(jnp.bfloat16)
            grad_ref[keys, value_here] = back_values.astype(jnp.bfloat16)
        grad_ref[:, here] = (sum_ref[...] * scale).astype(jnp.bfloat16)

        @pl.when(head == heads // 2 - 1)
        def _():
            for copy in loads:
                copy.wait()
            middle()

        return carry

    lax.fori_loop(0, heads, one_head, 0)
    end()
    total = own_buf[...].astype(jnp.float32)
    for at in range(len(direct_masks(quads))):
        total = total + in_buf[at].astype(jnp.float32)
    layer_ref[...] = total
    thin_own.wait()
    for step in range(1, groups):
        thin_from(step).wait_recv()
        thin_to(step).wait_send()
    for head in range(heads):
        for step in range(1, slices):
            to_owner(step, head).wait_send()


def attend_backward(back_low, outward, mixed, wide, totals, bias_column, widened, thin):
    slices = lax.axis_size("tensor")
    groups = lax.axis_size("dp")
    quads = groups // 2
    rows, width = back_low.shape
    length, cols = wide.shape
    heads = cols // HEAD_DIM
    size = QUERY_BLOCK
    vmem = pl.BlockSpec(memory_space=pltpu.VMEM)
    hbm = pl.BlockSpec(memory_space=pltpu.HBM)
    dma = pltpu.SemaphoreType.DMA
    low = jnp.bfloat16
    return pl.pallas_call(
        functools.partial(
            backward_kernel, blocks=length // size, size=size, slices=slices, groups=groups
        ),
        in_specs=[vmem] * 6 + [hbm] * 2,
        out_specs=[vmem, vmem, hbm],
        out_shape=[
            jax.ShapeDtypeStruct((length, 3 * cols), low),
            jax.ShapeDtypeStruct((rows, width), jnp.float32),
            jax.ShapeDtypeStruct((groups * thin.shape[0], width // groups), low),
        ],
        scratch_shapes=[
            pltpu.VMEM((slices - 1, rows, cols), low),
            pltpu.VMEM((length, cols), low),
            pltpu.VMEM((length, HEAD_DIM), jnp.float32),
            pltpu.VMEM((2, rows // 2, width), low),
            pltpu.VMEM((rows, width), low),
        ]
        + reduce_scratch(quads, rows, width)
        + [dma((slices, heads)), dma((slices, heads)), dma((3,))]
        + [dma((groups,)), dma((groups,)), dma],
        compiler_params=pltpu.CompilerParams(
            collective_id=4, has_side_effects=True, vmem_limit_bytes=VMEM_BYTES
        ),
        cost_estimate=pl.CostEstimate(
            flops=10 * length * length * cols,
            bytes_accessed=150 * 2**20,
            transcendentals=heads * length * length // 2,
        ),
        name="attend_backward",
    )(back_low, outward, mixed, wide, totals, bias_column, widened, thin)


def back_kernel(
    e_ref, slope_ref, thin_ref, wide_ref, grad_ref,
    own_ref, dhid_ref, sum_ref, full_ref, share_ref,
    thin_buf, wide_buf, e_buf, slope_buf, dhid_buf, part_buf, hop_buf, in_buf, send, receive,
    load_sem, pair_sem, full_sem, e_sem, slope_sem, dhid_sem, grad_send, grad_recv, grad_sem,
    *, groups, slices
):
    quads = groups // 2
    me = lax.axis_index("dp")
    place = lax.axis_index("tensor")
    rows, width = own_ref.shape
    units = wide_buf.shape[1]
    half = units // 2
    tile = min(512, half)
    slab = min(512, width)

    def across(mask):
        return (flip(me, mask), place)

    def load_block(number, at):
        target = pl.ds(at * rows, rows)
        return (
            pltpu.make_async_copy(e_ref.at[target], e_buf.at[number % 2], e_sem.at[number]),
            pltpu.make_async_copy(
                slope_ref.at[target], slope_buf.at[number % 2], slope_sem.at[number]
            ),
        )

    order = [quads - 1] + list(range(1, quads - 1)) + [0]
    thin_load = pltpu.make_async_copy(thin_ref, thin_buf.at[pl.ds(0, half)], load_sem.at[0])
    thin_load.start()
    for copy in load_block(0, order[0]):
        copy.start()
    wide_load = pltpu.make_async_copy(wide_ref, wide_buf, load_sem.at[1])
    wide_load.start()
    greet_all(
        [across(mask) for mask in [1] + direct_masks(quads)]
        + [(me, lax.rem(place + step, slices)) for step in range(1, slices)]
    )
    span = share_ref.shape[1]

    def grad_rows(owner):
        return grad_ref.at[pl.ds(pl.multiple_of(owner * span, span), span)]

    def grad_to(step):
        owner = lax.rem(place + step, slices)
        return remote(
            grad_rows(owner), share_ref.at[step], grad_send.at[step], grad_recv.at[step],
            (me, owner),
        )

    for step in range(1, slices):
        grad_to(step).start()
    grad_own = pltpu.make_async_copy(grad_rows(place), share_ref.at[0], grad_sem)
    grad_own.start()
    pair = remote(
        thin_ref, thin_buf.at[pl.ds(half, half)], pair_sem.at[0], pair_sem.at[1], across(1)
    )
    pair.start()

    half_rows = rows // 2

    def parts(block, side):
        if side is None:
            return part_buf.at[block - 1]
        return part_buf.at[block - 1, pl.ds(side * half_rows, half_rows)]

    early, middle, end = square_reduce(
        quads, rows, across, send, receive, parts, parts, hop_buf, in_buf
    )
    sum_ref[...] = jnp.zeros_like(sum_ref)
    stores = []
    full = pltpu.make_async_copy(thin_buf, full_ref, full_sem)
    for number, at in enumerate(order):
        slot = number % 2
        if number + 1 < quads:
            for copy in load_block(number + 1, order[number + 1]):
                copy.start()
        if number == 0:
            thin_load.wait()
        for copy in load_block(number, at):
            copy.wait()
        if number >= 2:
            stores[number - 2].wait()

        def back_tile(index, carry):
            columns = pl.ds(pl.multiple_of(index * tile, tile), tile)
            back = dot_as(e_buf[slot], thin_buf[columns, :], ROWS)
            back = (back * slope_buf[slot, :, columns]).astype(jnp.bfloat16)
            dhid_buf[slot, :, columns] = back
            sum_ref[:, columns] += jnp.sum(back.astype(jnp.float32), axis=0, keepdims=True)
            return carry

        if number == 0:
            lax.fori_loop(0, half // tile, back_tile, 0)
            pair.wait_recv()
            full.start()
            lax.fori_loop(half // tile, units // tile, back_tile, 0)
            wide_load.wait()
        else:
            lax.fori_loop(0, units // tile, back_tile, 0)
        store = pltpu.make_async_copy(
            dhid_buf.at[slot], dhid_ref.at[pl.ds(at * rows, rows)], dhid_sem.at[number]
        )
        store.start()
        stores.append(store)

        def slab_of(index, carry):
            here = pl.ds(pl.multiple_of(index * slab, slab), slab)
            product = dot_as(dhid_buf[slot], wide_buf[here, :], ROWS)
            if at:
                part_buf[at - 1, :, here] = product.astype(jnp.bfloat16)
            else:
                own_ref[:, here] = product
            return carry

        lax.fori_loop(0, width // slab, slab_of, 0)
        if at:
            early(at)
        if number == quads - 2:
            middle()
    end()
    for at in range(len(direct_masks(quads))):
        own_ref[...] += in_buf[at].astype(jnp.float32)
    pair.wait_send()
    full.wait()
    for store in stores[-2:]:
        store.wait()
    for step in range(1, slices):
        grad_to(step).wait()
    grad_own.wait()


def back_step(back, slope, thin, wide, grad):
    groups = lax.axis_size("dp")
    slices = lax.axis_size("tensor")
    quads = groups // 2
    length, width = back.shape
    rows = length // quads
    units = slope.shape[1]
    dma = pltpu.SemaphoreType.DMA
    vmem = pl.BlockSpec(memory_space=pltpu.VMEM)
    hbm = pl.BlockSpec(memory_space=pltpu.HBM)
    low = jnp.bfloat16
    return pl.pallas_call(
        functools.partial(back_kernel, groups=groups, slices=slices),
        in_specs=[hbm] * 5,
        out_specs=[vmem, hbm, vmem, hbm, hbm],
        out_shape=[
            jax.ShapeDtypeStruct((rows, width), jnp.float32),
            jax.ShapeDtypeStruct((length, units), low),
            jax.ShapeDtypeStruct((1, units), jnp.float32),
            jax.ShapeDtypeStruct((units, width), low),
            jax.ShapeDtypeStruct((slices, grad.shape[0] // slices, width), low),
        ],
        scratch_shapes=[
            pltpu.VMEM((units, width), low),
            pltpu.VMEM((width, units), low),
            pltpu.VMEM((2, rows, width), low),
            pltpu.VMEM((2, rows, units), jnp.float32),
            pltpu.VMEM((2, rows, units), low),
            pltpu.VMEM((quads - 1, rows, width), low),
        ]
        + reduce_scratch(quads, rows, width)
        + [dma((2,)), dma((2,)), dma, dma((quads,)), dma((quads,)), dma((quads,))]
        + [dma((slices,)), dma((slices,)), dma],
        compiler_params=pltpu.CompilerParams(
            collective_id=5, has_side_effects=True, vmem_limit_bytes=60 * 2**20
        ),
        cost_estimate=pl.CostEstimate(
            flops=4 * length * width * units,
            bytes_accessed=150 * 2**20,
            transcendentals=0,
        ),
        name="back_step",
    )(back, slope, thin, wide, grad)


def open_kernel(
    a_ref, w_ref, e_ref, bias_ref, small_ref, count_ref, wide_ref, thin_ref, out_ref,
    full_ref, weight_ref, mixed_ref, back_ref, all_ref, counts_ref, wide_all, thin_all, out_all,
    a_buf, w_buf, wide_buf, thin_buf, out_buf,
    line_send, line_recv, small_send, small_recv, w_send, w_recv, pair_send, pair_recv,
    e_send, e_recv, local_sem, keep_sem, count_send, count_recv,
    wide_send, wide_recv, thin_send, thin_recv, out_send, out_recv, plane_send, plane_recv,
    run_send, run_recv,
    *, groups, slices, piece
):
    quads = groups // 2
    count = groups * slices
    me = lax.axis_index("dp")
    place = lax.axis_index("tensor")
    rows = a_ref.shape[0]
    share = w_buf.shape[0] // groups
    cols = w_buf.shape[1] // 3
    out_cols = out_all.shape[1] // groups
    masks = direct_masks(quads)
    hops = two_hops(quads)
    low = jnp.bfloat16
    raw = piece % 128 == 0

    def across(mask):
        return (flip(me, mask), place)

    def along(other):
        return (me, other)

    def beside(step):
        return (me, lax.rem(place + step, slices))

    def anyone(step):
        other = lax.rem(me * slices + place + step, count)
        return (lax.div(other, slices), lax.rem(other, slices))

    barrier = pltpu.get_barrier_semaphore()

    def greet(step, carry):
        pl.semaphore_signal(
            barrier, inc=1, device_id=anyone(step), device_id_type=pl.DeviceIdType.MESH
        )
        return carry

    lax.fori_loop(1, count, greet, 0)

    def w_rows(mask, half=None):
        start = flip(me, mask) * share
        if half is None:
            return w_buf.at[pl.ds(pl.multiple_of(start, share), share)]
        size = share // 2
        return w_buf.at[pl.ds(pl.multiple_of(start + half * size, size), size)]

    here = pl.ds(pl.multiple_of(me * share, share), share)
    for part in range(3):
        w_buf[here, part * cols : (part + 1) * cols] = w_ref[part].astype(low)
    a_buf[pl.ds(pl.multiple_of(place * rows, rows), rows), :] = a_ref[...]
    pl.semaphore_wait(barrier, count - 1)

    def a_rows(block):
        return a_buf.at[pl.ds(pl.multiple_of(block * rows, rows), rows)]

    def keep(block):
        return pltpu.make_async_copy(
            a_rows(block),
            full_ref.at[pl.ds(pl.multiple_of(block * rows, rows), rows)],
            keep_sem.at[block],
        )

    def to_right(step):
        block = place - step
        return remote(
            a_rows(block), a_rows(block), line_send.at[0, step], line_recv.at[0, step],
            along(place + 1),
        )

    def to_left(step):
        block = place + step
        return remote(
            a_rows(block), a_rows(block), line_send.at[1, step], line_recv.at[1, step],
            along(place - 1),
        )

    def from_left(step):
        block = place - 1 - step
        return remote(
            a_rows(block), a_rows(block), line_send.at[0, step], line_recv.at[0, step],
            along(place - 1),
        )

    def from_right(step):
        block = place + 1 + step
        return remote(
            a_rows(block), a_rows(block), line_send.at[1, step], line_recv.at[1, step],
            along(place + 1),
        )

    def sends_right(step):
        return jnp.logical_and(place - step >= 0, place + 1 < slices)

    def sends_left(step):
        return jnp.logical_and(place + step < slices, place >= 1)

    pl.when(sends_right(0))(lambda: to_right(0).start())
    pl.when(sends_left(0))(lambda: to_left(0).start())

    w_copies = []
    for at, mask in enumerate(masks):
        copy = remote(w_rows(0), w_rows(0), w_send.at[at], w_recv.at[at], across(mask))
        copy.start()
        w_copies.append(copy)

    keep(place).start()
    all_ref[place] = small_ref[...]
    small_copies = []
    for step in range(1, slices):
        copy = remote(
            small_ref, all_ref.at[place], small_send.at[step], small_recv.at[step], beside(step)
        )
        copy.start()
        small_copies.append(copy)

    def tell(step):
        return remote(
            count_ref, counts_ref.at[step], count_send.at[step], count_recv.at[step], anyone(step)
        )

    counts_ref[0] = count_ref[...]
    lax.fori_loop(1, count, lambda step, carry: (tell(step).start(), carry)[1], 0)

    out_here = pl.ds(pl.multiple_of(place * cols, cols), cols)
    out_buf[out_here, :] = out_ref[...].astype(low)
    out_copies = []
    for step in range(1, slices):
        target = out_buf.at[out_here]
        copy = remote(target, target, out_send.at[step], out_recv.at[step], beside(step))
        copy.start()
        out_copies.append(copy)

    for part in range(groups):
        if raw:
            row = part * piece // cols
            start = part * piece % cols
            wide_buf[part] = wide_ref[:, row, start : start + piece].astype(low)
            thin_buf[part] = thin_ref[row, start : start + piece, :].astype(low)
        else:
            wide_buf[part] = wide_ref[part]
            thin_buf[part] = thin_ref[part]
    thin_cols = thin_buf.shape[2]
    wide_here = wide_all.at[place, here]
    thin_here = thin_all.at[:, pl.ds(pl.multiple_of(me * thin_cols, thin_cols), thin_cols)]

    def to_group(step):
        other = lax.rem(me + step, groups)
        device = (other, place)
        return (
            remote(wide_buf.at[other], wide_here, wide_send.at[step], wide_recv.at[step], device),
            remote(thin_buf.at[other], thin_here, thin_send.at[step], thin_recv.at[step], device),
        )

    own_wide = pltpu.make_async_copy(wide_buf.at[me], wide_here, local_sem.at[2])
    own_wide.start()
    own_thin = pltpu.make_async_copy(thin_buf.at[me], thin_here, local_sem.at[3])
    own_thin.start()
    for step in range(1, groups):
        for copy in to_group(step):
            copy.start()

    pair_copies = []

    def to_pair(source):
        at = len(pair_copies)
        copy = remote(source, source, pair_send.at[at], pair_recv.at[at], across(1))
        copy.start()
        pair_copies.append(copy)

    to_pair(w_rows(0))
    for at, copy in enumerate(w_copies):
        remote(
            w_rows(masks[at]), w_rows(masks[at]), w_send.at[at], w_recv.at[at], across(masks[at])
        ).wait_recv()
    hop_copies = []
    for number, (mask, half, goal) in enumerate(hops):
        at = len(masks) + number
        source = w_rows(mask, half)
        copy = remote(source, source, w_send.at[at], w_recv.at[at], across(goal))
        copy.start()
        hop_copies.append(copy)
    for mask in masks:
        to_pair(w_rows(mask))

    own = pltpu.make_async_copy(e_ref, back_ref.at[pl.ds(0, rows)], local_sem.at[0])
    own.start()
    e_copies = []
    for at, mask in enumerate(masks):
        target = back_ref.at[pl.ds((at + 1) * rows, rows)]
        copy = remote(e_ref, target, e_send.at[at], e_recv.at[at], across(mask))
        copy.start()
        e_copies.append(copy)

    for number, (mask, half, goal) in enumerate(hops):
        at = len(masks) + number
        landed = w_rows(2 + 4, half)
        remote(landed, landed, w_send.at[at], w_recv.at[at], across(goal)).wait_recv()
        to_pair(landed)
    sources = [0] + masks
    for at, mask in enumerate(sources):
        landed = w_rows(mask + 1)
        remote(landed, landed, pair_send.at[at], pair_recv.at[at], across(1)).wait_recv()
    for number, (mask, half, goal) in enumerate(hops):
        at = len(sources) + number
        landed = w_rows(2 + 4 + 1, half)
        remote(landed, landed, pair_send.at[at], pair_recv.at[at], across(1)).wait_recv()
    weights_out = pltpu.make_async_copy(w_buf, weight_ref, local_sem.at[1])
    weights_out.start()

    def multiply(block):
        where = pl.ds(pl.multiple_of(block * rows, rows), rows)
        left = a_buf[where, :]
        for part in range(3):
            columns = slice(part * cols, (part + 1) * cols)
            product = dot_as(left, w_buf[:, columns], PLAIN) + bias_ref[0:1, columns]
            mixed_ref[where, columns] = product.astype(low)

    multiply(place)

    def out_at(mask, half=None):
        start = pl.multiple_of(flip(me, mask) * out_cols, out_cols)
        size = out_all.shape[0] // 2
        if half is None:
            return out_all.at[:, pl.ds(start, out_cols)]
        return out_all.at[half * size : (half + 1) * size, pl.ds(start, out_cols)]

    own_out = pltpu.make_async_copy(out_buf, out_at(0), local_sem.at[4])

    def plane(at, source, target, device):
        return remote(source, target, plane_send.at[at], plane_recv.at[at], device)

    def plane_first():
        return [
            plane(at, out_buf, out_at(0), across(mask)) for at, mask in enumerate([1] + masks)
        ]

    def plane_landed():
        return [
            plane(at, out_buf, out_at(mask), across(mask)) for at, mask in enumerate([1] + masks)
        ]

    def plane_hops():
        return [
            plane(1 + len(masks) + number, out_at(mask, half), out_at(mask, half), across(goal))
            for number, (mask, half, goal) in enumerate(hops)
        ]

    def plane_pairs():
        return [
            plane(1 + len(masks) + len(hops) + at, out_at(mask), out_at(mask), across(1))
            for at, mask in enumerate(masks)
        ]

    def plane_last():
        return [
            plane(
                1 + 2 * len(masks) + len(hops) + number, out_at(6, half), out_at(6, half), across(1)
            )
            for number, (mask, half, goal) in enumerate(hops)
        ]

    def wide_move(step, side, outgoing):
        back = step if outgoing else step + 1
        block = place - back if side == 0 else place + back
        towards = (side == 0) == outgoing
        return remote(
            wide_all.at[block], wide_all.at[block], run_send.at[side, step], run_recv.at[side, step],
            along(place + 1 if towards else place - 1),
        )

    def wide_arrived():
        own_wide.wait()
        for step in range(1, groups):
            other = lax.rem(me + groups - step, groups)
            wide_from = wide_all.at[
                place, pl.ds(pl.multiple_of(other * share, share), share)
            ]
            remote(
                wide_buf.at[other], wide_from, wide_send.at[step], wide_recv.at[step],
                (other, place),
            ).wait_recv()
        pl.when(sends_right(0))(lambda: wide_move(0, 0, True).start())
        pl.when(sends_left(0))(lambda: wide_move(0, 1, True).start())

    def pass_on(step, carry):
        got_left = place - 1 - step >= 0
        got_right = place + 1 + step < slices

        @pl.when(got_left)
        def _():
            from_left(step).wait_recv()

            @pl.when(jnp.logical_and(step + 1 < slices - 1, sends_right(step + 1)))
            def _():
                to_right(step + 1).start()

            keep(place - 1 - step).start()

        @pl.when(got_right)
        def _():
            from_right(step).wait_recv()

            @pl.when(jnp.logical_and(step + 1 < slices - 1, sends_left(step + 1)))
            def _():
                to_left(step + 1).start()

            keep(place + 1 + step).start()

        @pl.when(step == 0)
        def _():
            for copy in out_copies:
                copy.wait_recv()
            own_out.start()
            for copy in plane_first():
                copy.start()

        @pl.when(got_left)
        def _():
            multiply(place - 1 - step)

        @pl.when(got_right)
        def _():
            multiply(place + 1 + step)

        @pl.when(step == 1)
        def _():
            for copy in plane_landed():
                copy.wait_recv()
            for copy in plane_hops() + plane_pairs():
                copy.start()
            wide_arrived()

        return carry

    lax.fori_loop(0, slices - 1, pass_on, 0)

    def wide_on(step, carry):
        @pl.when(place - 1 - step >= 0)
        def _():
            wide_move(step, 0, False).wait_recv()

            @pl.when(jnp.logical_and(step + 1 < slices - 1, sends_right(step + 1)))
            def _():
                wide_move(step + 1, 0, True).start()

        @pl.when(place + 1 + step < slices)
        def _():
            wide_move(step, 1, False).wait_recv()

            @pl.when(jnp.logical_and(step + 1 < slices - 1, sends_left(step + 1)))
            def _():
                wide_move(step + 1, 1, True).start()

        return carry

    lax.fori_loop(0, slices - 1, wide_on, 0)

    for number, (mask, half, goal) in enumerate(hops):
        at = 1 + len(masks) + number
        plane(at, out_at(6, half), out_at(6, half), across(goal)).wait_recv()
    for copy in plane_last():
        copy.start()
    for at, mask in enumerate(masks):
        landed = out_at(mask + 1)
        plane(1 + len(masks) + len(hops) + at, landed, landed, across(1)).wait_recv()
    for number, (mask, half, goal) in enumerate(hops):
        landed = out_at(7, half)
        plane(1 + 2 * len(masks) + len(hops) + number, landed, landed, across(1)).wait_recv()
    for copy in plane_first() + plane_hops() + plane_pairs() + plane_last():
        copy.wait_send()
    for at, mask in enumerate(masks):
        landed = back_ref.at[pl.ds((at + 1) * rows, rows)]
        remote(e_ref, landed, e_send.at[at], e_recv.at[at], across(mask)).wait_recv()
    for copy in e_copies + w_copies + hop_copies + pair_copies + out_copies:
        copy.wait_send()
    for copy in small_copies:
        copy.wait()
    for step in range(1, groups):
        other = lax.rem(me + groups - step, groups)
        thin_from = thin_all.at[
            :, pl.ds(pl.multiple_of(other * thin_cols, thin_cols), thin_cols)
        ]
        device = (other, place)
        remote(
            thin_buf.at[other], thin_from, thin_send.at[step], thin_recv.at[step], device
        ).wait_recv()
        for copy in to_group(step):
            copy.wait_send()
    lax.fori_loop(1, count, lambda step, carry: (tell(step).wait(), carry)[1], 0)
    for copy in (own, weights_out, own_thin, own_out):
        copy.wait()

    def finish(step, carry):
        pl.when(sends_right(step))(lambda: to_right(step).wait_send())
        pl.when(sends_left(step))(lambda: to_left(step).wait_send())
        pl.when(sends_right(step))(lambda: wide_move(step, 0, True).wait_send())
        pl.when(sends_left(step))(lambda: wide_move(step, 1, True).wait_send())
        return carry

    lax.fori_loop(0, slices - 1, finish, 0)
    for block in range(slices):
        keep(block).wait()


def open_step(normed, inward, back, bias, small, living, widening, narrowing, outward):
    groups = lax.axis_size("dp")
    slices = lax.axis_size("tensor")
    count = groups * slices
    quads = groups // 2
    rows, width = normed.shape
    share, _, cols = inward.shape
    piece = 4 * cols // groups
    out_cols = outward.shape[1]
    hops = len(two_hops(quads))
    direct = len(direct_masks(quads))
    dma = pltpu.SemaphoreType.DMA
    vmem = pl.BlockSpec(memory_space=pltpu.VMEM)
    hbm = pl.BlockSpec(memory_space=pltpu.HBM)
    low = jnp.bfloat16
    wide = jnp.float32
    if piece % 128:
        widening = widening.astype(low).reshape(share, groups, piece).transpose(1, 0, 2)
        narrowing = narrowing.astype(low).reshape(groups, piece, out_cols)
    shape = jax.ShapeDtypeStruct
    planes = 1 + 2 * direct + 2 * hops
    return pl.pallas_call(
        functools.partial(open_kernel, groups=groups, slices=slices, piece=piece),
        in_specs=[vmem, vmem, hbm, vmem, vmem, vmem, vmem, vmem, vmem],
        out_specs=[hbm, hbm, vmem, hbm, vmem, vmem, hbm, hbm, hbm],
        out_shape=[
            shape((slices * rows, width), low),
            shape((width, 3 * cols), low),
            shape((slices * rows, 3 * cols), low),
            shape((quads * rows, width), low),
            shape((slices,) + small.shape, wide),
            shape((count, 8, 128), wide),
            shape((slices, width, piece), low),
            shape((piece, width), low),
            shape((width, width), low),
        ],
        scratch_shapes=[
            pltpu.VMEM((slices * rows, width), low),
            pltpu.VMEM((width, 3 * cols), low),
            pltpu.VMEM((groups, share, piece), low),
            pltpu.VMEM((groups, piece, out_cols), low),
            pltpu.VMEM((slices * cols, out_cols), low),
            dma((2, slices)),
            dma((2, slices)),
            dma((slices,)),
            dma((slices,)),
            dma((direct + hops,)),
            dma((direct + hops,)),
            dma((1 + direct + hops,)),
            dma((1 + direct + hops,)),
            dma((direct,)),
            dma((direct,)),
            dma((5,)),
            dma((slices,)),
            dma((count,)),
            dma((count,)),
            dma((groups,)),
            dma((groups,)),
            dma((groups,)),
            dma((groups,)),
            dma((slices,)),
            dma((slices,)),
            dma((planes,)),
            dma((planes,)),
            dma((2, slices)),
            dma((2, slices)),
        ],
        compiler_params=pltpu.CompilerParams(
            collective_id=1, has_side_effects=True, vmem_limit_bytes=VMEM_BYTES
        ),
        cost_estimate=pl.CostEstimate(
            flops=2 * slices * rows * width * 3 * cols,
            bytes_accessed=400 * 2**20,
            transcendentals=0,
        ),
        name="open_step",
    )(
        normed, inward.transpose(1, 0, 2), back, bias, small, living, widening, narrowing, outward
    )


def hidden_gather_kernel(
    b_ref, weight_ref, bias_ref, all_ref, act_ref, slope_ref, full_ref,
    b_buf, w_buf, act_buf, slope_buf,
    b_send, b_recv, keep_sem, act_sem, slope_sem, w_sem, pair_sem, out_sem,
    *, groups
):
    quads = groups // 2
    me = lax.axis_index("dp")
    place = lax.axis_index("tensor")
    rows = b_ref.shape[0]
    tiles, _, tile = weight_ref.shape
    masks = direct_masks(quads)
    hops = two_hops(quads)
    half_rows = rows // 2

    def across(mask):
        return (flip(me, mask), place)

    load = pltpu.make_async_copy(weight_ref, w_buf.at[pl.ds(0, tiles)], w_sem)
    load.start()
    greet_all([across(mask) for mask in [1] + masks])

    def block(at):
        return b_buf.at[pl.ds(at * rows, rows)]

    def piece(at, half):
        return b_buf.at[pl.ds(at * rows + half * half_rows, half_rows)]

    copies = []
    for at, mask in enumerate(masks):
        copy = remote(b_ref, block(at + 1), b_send.at[at], b_recv.at[at], across(mask))
        copy.start()
        copies.append(copy)
    pair = remote(
        weight_ref, w_buf.at[pl.ds(tiles, tiles)], pair_sem.at[0], pair_sem.at[1], across(1)
    )
    pair.start()
    b_buf[0:rows, :] = b_ref[...]
    keeps = []
    stores = []

    def keep(at):
        copy = pltpu.make_async_copy(
            block(at), all_ref.at[pl.ds(at * rows, rows)], keep_sem.at[at]
        )
        copy.start()
        keeps.append(copy)

    def multiply(at, first, amount):
        def part(number, carry):
            columns = pl.ds(pl.multiple_of(number * tile, tile), tile)
            hidden = (
                dot_as(b_buf[at * rows : (at + 1) * rows, :], w_buf[number], PLAIN)
                + bias_ref[0:1, columns]
            )
            root = 0.7978845608028654
            square = hidden * hidden
            bent = jnp.tanh(root * hidden * (1.0 + 0.044715 * square))
            half = 0.5 * (1.0 + bent)
            act_buf[at % 2, :, columns] = (hidden * half).astype(jnp.bfloat16)
            slope_buf[at % 2, :, columns] = half + 0.5 * hidden * (1.0 - bent * bent) * (
                root * (1.0 + 3.0 * 0.044715 * square)
            )
            return carry

        lax.fori_loop(first, first + amount, part, 0)

    def store(at):
        target = pl.ds(at * rows, rows)
        pair_of = [
            pltpu.make_async_copy(act_buf.at[at % 2], act_ref.at[target], act_sem.at[at]),
            pltpu.make_async_copy(slope_buf.at[at % 2], slope_ref.at[target], slope_sem.at[at]),
        ]
        for copy in pair_of:
            copy.start()
        stores.append(pair_of)

    keep(0)
    load.wait()
    multiply(0, 0, tiles)
    pair.wait_recv()
    multiply(0, tiles, tiles)
    store(0)
    outs = []
    for number in range(2 * tiles):
        copy = pltpu.make_async_copy(
            w_buf.at[number],
            full_ref.at[:, pl.ds(number * tile, tile)],
            out_sem.at[number],
        )
        copy.start()
        outs.append(copy)
    for at in range(len(masks)):
        copies[at].wait_recv()
    for number, (mask, half, goal) in enumerate(hops):
        at = len(masks) + number
        copy = remote(
            piece(masks.index(mask) + 1, half), piece(3, half), b_send.at[at], b_recv.at[at],
            across(goal),
        )
        copy.start()
        copies.append(copy)
    for at in range(1, quads):
        if at == 1 + len(masks):
            for copy in copies[len(masks) :]:
                copy.wait_recv()
        keep(at)
        if at >= 2:
            for copy in stores[at - 2]:
                copy.wait()
        multiply(at, 0, 2 * tiles)
        store(at)
    for copy in copies + [pair]:
        copy.wait_send()
    for copy in keeps + outs + sum(stores[-2:], []):
        copy.wait()


def hidden_gather(rows_own, weight, bias):
    groups = lax.axis_size("dp")
    quads = groups // 2
    rows, width = rows_own.shape
    tiles, _, tile = weight.shape
    units = 2 * tiles * tile
    pieces = len(two_hops(quads)) + len(direct_masks(quads))
    dma = pltpu.SemaphoreType.DMA
    vmem = pl.BlockSpec(memory_space=pltpu.VMEM)
    hbm = pl.BlockSpec(memory_space=pltpu.HBM)
    return pl.pallas_call(
        functools.partial(hidden_gather_kernel, groups=groups),
        in_specs=[vmem, hbm, vmem],
        out_specs=[hbm, hbm, hbm, hbm],
        out_shape=[
            jax.ShapeDtypeStruct((quads * rows, width), jnp.bfloat16),
            jax.ShapeDtypeStruct((quads * rows, units), jnp.bfloat16),
            jax.ShapeDtypeStruct((quads * rows, units), jnp.float32),
            jax.ShapeDtypeStruct((width, units), jnp.bfloat16),
        ],
        scratch_shapes=[
            pltpu.VMEM((quads * rows, width), jnp.bfloat16),
            pltpu.VMEM((2 * tiles, width, tile), jnp.bfloat16),
            pltpu.VMEM((2, rows, units), jnp.bfloat16),
            pltpu.VMEM((2, rows, units), jnp.float32),
            dma((pieces,)),
            dma((pieces,)),
            dma((quads,)),
            dma((quads,)),
            dma((quads,)),
            dma,
            dma((2,)),
            dma((2 * tiles,)),
        ],
        compiler_params=pltpu.CompilerParams(
            collective_id=2, has_side_effects=True, vmem_limit_bytes=VMEM_BYTES
        ),
        cost_estimate=pl.CostEstimate(
            flops=2 * quads * rows * width * units,
            bytes_accessed=200 * 2**20,
            transcendentals=0,
        ),
        name="hidden_gather",
    )(rows_own, weight, bias)


def inward_kernel(
    grad_ref, outer_ref, wide_ref, values_ref, own_ref, outer_sum, wide_sum, all_ref,
    near, far, pair_send, pair_recv, pair_load, hop_buf, in_buf, send, receive,
    outer_near, outer_far, outer_pair_send, outer_pair_recv, outer_load,
    outer_hop, outer_in, outer_send, outer_recv,
    line_buf, line_send, line_recv, wide_send, wide_recv, wide_load, *sum_refs,
    groups, slices
):
    quads = groups // 2
    me = lax.axis_index("dp")
    place = lax.axis_index("tensor")
    share = near.shape[1]
    half_rows = share // 2
    piece = wide_ref.shape[0]

    def across(mask):
        return (flip(me, mask), place)

    anyone, greet = everyone(groups, slices)
    greet()
    sum_start, sum_middle, sum_end = spread_sum(
        values_ref, all_ref, *sum_refs, anyone, groups, slices
    )

    def block_of(other):
        return grad_ref.at[pl.ds(pl.multiple_of(other * share, share), share)]

    def parts(block, side):
        if side is None:
            return near.at[block]
        return near.at[block, pl.ds(side * half_rows, half_rows)]

    start, finish = pair_reduce(
        quads, me, across, block_of, near, far, pair_send, pair_recv, pair_load
    )
    early, middle, end = square_reduce(
        quads, share, across, send, receive, parts, parts, hop_buf, in_buf
    )

    out_cols = outer_sum.shape[1]
    long = outer_near.shape[1]
    half_long = long // 2

    def outer_block(other):
        return outer_ref.at[:, pl.ds(pl.multiple_of(other * out_cols, out_cols), out_cols)]

    def outer_parts(block, side):
        if side is None:
            return outer_near.at[block]
        return outer_near.at[block, pl.ds(side * half_long, half_long)]

    outer_start, outer_finish = pair_reduce(
        quads, me, across, outer_block, outer_near, outer_far,
        outer_pair_send, outer_pair_recv, outer_load,
    )
    outer_early, outer_middle, outer_end = square_reduce(
        quads, long, across, outer_send, outer_recv, outer_parts, outer_parts, outer_hop, outer_in
    )
    line_rows = outer_sum.shape[0]

    def line_block(owner):
        return outer_near.at[0, pl.ds(pl.multiple_of(owner * line_rows, line_rows), line_rows)]

    def line_to(step):
        owner = lax.rem(place + step, slices)
        return remote(
            line_block(owner), line_buf.at[step - 1], line_send.at[step], line_recv.at[step],
            (me, owner),
        )

    def columns_of(other):
        return wide_ref.at[:, pl.ds(pl.multiple_of(other * share, share), share)]

    def rows_of(other):
        return wide_sum.at[pl.ds(pl.multiple_of(other * piece, piece), piece)]

    def wide_to(step):
        other = lax.rem(me + step, groups)
        return remote(
            columns_of(other), rows_of(me), wide_send.at[step], wide_recv.at[step], (other, place)
        )

    def wide_from(step):
        other = lax.rem(me + groups - step, groups)
        return remote(
            columns_of(other), rows_of(other), wide_send.at[step], wide_recv.at[step],
            (other, place),
        )

    order = [quads - 1] + list(range(1, quads - 1))
    outer_start()
    start()
    sum_start()
    for m in order:
        outer_finish(m)
        outer_early(m)
    for m in order:
        finish(m)
        early(m)
    wide_own = pltpu.make_async_copy(columns_of(me), rows_of(me), wide_load)
    wide_own.start()
    outer_finish(0)
    outer_middle()
    for step in range(1, groups):
        wide_to(step).start()
    finish(0)
    sum_middle()
    middle()
    outer_end()
    outer = outer_near[0].astype(jnp.float32)
    for at in range(len(direct_masks(quads))):
        outer = outer + outer_in[at].astype(jnp.float32)
    outer_near[0] = outer.astype(outer_near.dtype)
    for step in range(1, slices):
        line_to(step).start()
    end()
    total = near[0].astype(jnp.float32)
    for at in range(len(direct_masks(quads))):
        total = total + in_buf[at].astype(jnp.float32)
    cols = own_ref.shape[2]
    for part in range(3):
        own_ref[part] = total[:, part * cols : (part + 1) * cols]
    final = line_block(place)[...].astype(jnp.float32)
    for step in range(1, slices):
        line_to(step).wait()
        final = final + line_buf[step - 1].astype(jnp.float32)
    outer_sum[...] = final
    wide_own.wait()
    for step in range(1, groups):
        wide_from(step).wait_recv()
        wide_to(step).wait_send()
    sum_end()


def inward_reduce(grad, outer, wide, values):
    groups = lax.axis_size("dp")
    slices = lax.axis_size("tensor")
    quads = groups // 2
    width = grad.shape[0]
    share = width // groups
    columns = grad.shape[1]
    piece = wide.shape[0]
    out_cols = outer.shape[1] // groups
    out_rows = outer.shape[0] // slices
    packed = sum_room(values)
    dma = pltpu.SemaphoreType.DMA
    vmem = pl.BlockSpec(memory_space=pltpu.VMEM)
    hbm = pl.BlockSpec(memory_space=pltpu.HBM)
    low = jnp.bfloat16

    def pair_scratch(rows, cols):
        return [
            pltpu.VMEM((quads, rows, cols), low),
            pltpu.VMEM((quads, rows, cols), low),
            dma((quads,)),
            dma((quads,)),
            dma((quads,)),
        ] + reduce_scratch(quads, rows, cols)

    return pl.pallas_call(
        functools.partial(inward_kernel, groups=groups, slices=slices),
        in_specs=[hbm, hbm, hbm, vmem],
        out_specs=[vmem, vmem, hbm, vmem],
        out_shape=[
            jax.ShapeDtypeStruct((3, share, columns // 3), jnp.float32),
            jax.ShapeDtypeStruct((out_rows, out_cols), jnp.float32),
            jax.ShapeDtypeStruct((groups * piece, share), low),
            jax.ShapeDtypeStruct(packed.shape, jnp.float32),
        ],
        scratch_shapes=pair_scratch(share, columns)
        + pair_scratch(width, out_cols)
        + [
            pltpu.VMEM((slices - 1, out_rows, out_cols), low),
            dma((slices,)),
            dma((slices,)),
            dma((groups,)),
            dma((groups,)),
            dma,
        ]
        + sum_scratch(groups * slices),
        compiler_params=pltpu.CompilerParams(
            collective_id=6, has_side_effects=True, vmem_limit_bytes=VMEM_BYTES
        ),
        cost_estimate=pl.CostEstimate(
            flops=8 * grad.size, bytes_accessed=250 * 2**20, transcendentals=0
        ),
        name="inward_reduce",
    )(grad, outer, wide, packed)


def swap(values, axis, mask):
    count = lax.axis_size(axis)
    return lax.ppermute(values, axis, [(i, i ^ mask) for i in range(count)])


def sum_kernel(values_ref, out_ref, *scratch, groups, slices):
    anyone, greet = everyone(groups, slices)
    greet()
    start, middle, end = spread_sum(values_ref, out_ref, *scratch, anyone, groups, slices)
    start()
    middle()
    end()


def sum_room(values):
    count = lax.axis_size("dp") * lax.axis_size("tensor")
    room = count * 8 * 128
    packed = jnp.concatenate([values, jnp.zeros((room - values.shape[0],), jnp.float32)])
    return packed.reshape(count, 8, 128)


def sum_everywhere(values):
    groups = lax.axis_size("dp")
    slices = lax.axis_size("tensor")
    packed = sum_room(values)
    summed = pl.pallas_call(
        functools.partial(sum_kernel, groups=groups, slices=slices),
        in_specs=[pl.BlockSpec(memory_space=pltpu.VMEM)],
        out_specs=pl.BlockSpec(memory_space=pltpu.VMEM),
        out_shape=jax.ShapeDtypeStruct(packed.shape, jnp.float32),
        scratch_shapes=sum_scratch(groups * slices),
        compiler_params=pltpu.CompilerParams(
            collective_id=0, has_side_effects=True, vmem_limit_bytes=8 * 2**20
        ),
        cost_estimate=pl.CostEstimate(
            flops=packed.size, bytes_accessed=8 * packed.size, transcendentals=0
        ),
        name="sum_everywhere",
    )(packed)
    return summed.reshape(-1)[: values.shape[0]]


def after(values, gate):
    return lax.optimization_barrier((values, gate))[0]


def adapt_step(weight, moment_one, moment_two, slope, decay):
    mean_new = beta_one * moment_one + (1.0 - beta_one) * slope
    square_new = beta_two * moment_two + (1.0 - beta_two) * slope * slope
    direction = (
        mean_new
        / (1.0 - beta_one**STEP_COUNT)
        / (jnp.sqrt(square_new / (1.0 - beta_two**STEP_COUNT)) + adam_epsilon)
        + decay * weight
    )
    return (mean_new, square_new, direction)


def trust_apply(weight, direction, weight_square, update_square):
    weight_norm = jnp.sqrt(weight_square)
    update_norm = jnp.sqrt(update_square)
    return (
        weight - learn_rate * weight_norm / (update_norm + trust_epsilon) * direction,
        weight_norm,
        update_norm,
    )


def on_device(
    tokens,
    cotangent,
    live_mask,
    inward,
    inward_first,
    inward_second,
    outward,
    outward_first,
    outward_second,
    widening,
    widening_first,
    widening_second,
    narrowing,
    narrowing_first,
    narrowing_second,
    column_bias,
    column_first,
    column_second,
    vectors,
    vectors_first,
    vectors_second,
):
    low = jnp.bfloat16
    wide = jnp.float32
    amount, width = tokens.shape
    cols = column_bias.shape[1]
    groups = lax.axis_size("dp")
    slices = lax.axis_size("tensor")
    me = lax.axis_index("dp")
    place = lax.axis_index("tensor")
    share = inward.shape[0]
    piece = 4 * cols // groups

    inputs = tokens.astype(wide)
    living_here = live_mask.astype(wide)
    normed = layer_norm(inputs, vectors[0], vectors[1]).astype(low)
    back_out = (cotangent.astype(wide) * living_here[:, None]).astype(low)
    mixed_bias = jnp.concatenate(
        [column_bias[0], jnp.zeros((cols,), wide), column_bias[1]]
    ).reshape(1, 3 * cols)
    small_length = amount + 4 * cols
    small_rows = -(-small_length // 1024) * 8
    small = jnp.concatenate(
        [
            living_here,
            column_bias[2:].reshape(4 * cols),
            jnp.zeros((small_rows * 128 - small_length,), wide),
        ]
    ).reshape(small_rows, 128)
    (
        normed_full,
        inward_full,
        mixed,
        back_all,
        small_all,
        counts,
        wide_own,
        thin_own,
        outward_full,
    ) = open_step(
        normed,
        inward,
        back_out,
        mixed_bias,
        small,
        jnp.full((8, 128), jnp.sum(living_here)),
        widening,
        narrowing,
        outward,
    )
    factor = 1.0 / jnp.sum(counts[:, 0, 0])
    small_all = small_all.reshape(slices, small_rows * 128)
    length = normed_full.shape[0]
    bias_keys = jnp.where(small_all[:, :amount].reshape(length) > 0.5, 0.0, MASKED)
    bias_all = small_all[:, amount:small_length]

    if piece % 128:
        wide_own = wide_own.transpose(1, 0, 2).reshape(1, width, slices * piece)

    hidden_bias = jnp.concatenate(
        [
            lax.dynamic_slice_in_dim(bias_all, (me ^ side) * piece, piece, 1).reshape(1, -1)
            for side in range(2)
        ],
        axis=1,
    )

    context_wide, totals, context_own, back_all = attend_forward(
        mixed, bias_keys[None, :], back_all, amount
    )
    thin_own = lax.all_gather(
        after(thin_own, context_own), "tensor", axis=0, tiled=True
    )
    middle = inputs + dot_as(context_own, outward_full, PLAIN) + vectors[2]
    normed_two = layer_norm(middle, vectors[3], vectors[4]).astype(low)

    rows_two_all, active_all, slope, widening_full = hidden_gather(
        normed_two, wide_own, hidden_bias
    )
    half_units = slices * piece

    def pair_sum(left, right):
        other = left(slice(half_units, None), right, low)
        own = left(slice(0, half_units), after(right, other), wide)
        return (own + swap(other, "dp", 1).astype(wide)).astype(low)

    slope_narrowing = pair_sum(
        lambda part, right, kind: dot_as(active_all[:, part], right, TOKENS, kind),
        after(back_all, thin_own),
    )
    back_normed_two, back_hidden_all, hidden_sums, narrowing_full, thin_parts = back_step(
        back_all, slope, thin_own, widening_full, slope_narrowing
    )
    thin_slope = jnp.sum(thin_parts.astype(wide), axis=0).astype(low)
    slope_widening = pair_sum(
        lambda part, right, kind: dot_as(back_hidden_all[:, part], right, TOKENS, kind),
        rows_two_all,
    )
    wide_slope = lax.psum_scatter(slope_widening, "tensor", scatter_dimension=0, tiled=True)

    _, norm_two_pull = jax.vjp(layer_norm, middle, vectors[3], vectors[4])
    back_middle_norm, slope_gain_two, slope_shift_two = norm_two_pull(back_normed_two)
    back_middle = back_out.astype(wide) + back_middle_norm
    back_low = back_middle.astype(low)

    widened_all = dot_as(after(active_all, slope_widening), narrowing_full, PLAIN, low)
    back_mixed, widened, sum_narrowing = attend_backward(
        after(back_low, slope_widening),
        outward_full,
        mixed,
        context_wide,
        totals,
        bias_keys[:, None],
        widened_all,
        thin_slope,
    )
    layer_output = (middle + widened + vectors[5]).astype(low)

    back_normed_part = dot_as(back_mixed, inward_full, ROWS, low)
    back_normed = lax.psum_scatter(
        after(back_normed_part, wide_slope), "tensor", scatter_dimension=0, tiled=True
    )
    back_mixed = after(back_mixed, back_normed_part)
    slope_inward = dot_as(normed_full, back_mixed, TOKENS, low)
    slope_outward = dot_as(after(context_own, slope_inward), back_low, TOKENS, low)
    hidden_total = hidden_sums.reshape(2, 1, slices, piece)
    hidden_slots = jnp.zeros((groups, slices, piece), wide)
    hidden_slots = lax.dynamic_update_slice(hidden_slots, hidden_total[0], (me, 0, 0))
    hidden_slots = lax.dynamic_update_slice(hidden_slots, hidden_total[1], (me ^ 1, 0, 0))
    mixed_sums = jnp.stack(
        [
            jnp.sum(back_mixed[:, :cols], axis=0, dtype=wide),
            jnp.sum(back_mixed[:, 2 * cols :], axis=0, dtype=wide),
        ]
    )
    mixed_slots = lax.dynamic_update_slice(
        jnp.zeros((slices, 2, cols), wide), mixed_sums[None], (place, 0, 0)
    )
    late_rows = jnp.stack(
        [
            jnp.sum(back_middle, axis=0),
            slope_gain_two,
            slope_shift_two,
            jnp.sum(back_out, axis=0, dtype=wide),
        ]
    )
    packed = jnp.concatenate(
        [hidden_slots.reshape(-1), mixed_slots.reshape(-1), late_rows.reshape(-1)]
    )
    amount_packed = packed.shape[0]
    sum_inward, sum_outward, sum_widening, packed = inward_reduce(
        slope_inward, slope_outward, wide_slope, packed
    )
    packed = packed.reshape(-1)[:amount_packed]
    sum_inward = sum_inward.transpose(1, 0, 2)
    sum_widening = sum_widening.T.reshape(widening.shape)
    sum_narrowing = sum_narrowing.reshape(narrowing.shape)

    first_cut = groups * slices * piece
    second_cut = first_cut + slices * 2 * cols
    hidden_slots = packed[:first_cut].reshape(groups, slices, piece)
    hidden_rows = lax.dynamic_slice_in_dim(hidden_slots, place, 1, 1).reshape(4, cols)
    mixed_rows = lax.dynamic_index_in_dim(
        packed[first_cut:second_cut].reshape(slices, 2, cols), place, 0, keepdims=False
    )
    late_rows = packed[second_cut:].reshape(4, width)
    column_total = jnp.concatenate([mixed_rows, hidden_rows], axis=0)

    masters = (inward, outward, widening, narrowing)
    firsts = (inward_first, outward_first, widening_first, narrowing_first)
    seconds = (inward_second, outward_second, widening_second, narrowing_second)
    orders = ((1, 0, 2), (0, 1), (0, 1, 2), (0, 1, 2))
    summed_all = [
        with_layout_constraint(summed.astype(wide), Layout(order))
        for summed, order in zip(
            (sum_inward, sum_outward, sum_widening, sum_narrowing), orders
        )
    ]
    matrix_steps = [
        adapt_step(
            masters[ordinal],
            firsts[ordinal],
            seconds[ordinal],
            summed_all[ordinal] * factor,
            decay_rate,
        )
        for ordinal in range(4)
    ]
    column_mean, column_square, column_direction = adapt_step(
        column_bias, column_first, column_second, column_total * factor, 0.0
    )
    column_groups = ((0, 1), (1, 2), (2, 6))

    def square_sum(array):
        lanes = jnp.sum(array * array, axis=tuple(range(array.ndim - 1)))
        return jnp.concatenate([lanes, jnp.zeros((cols - lanes.shape[0],), wide)])

    squares = [square_sum(master) for master in masters]
    squares += [square_sum(column_bias[start:stop]) / groups for start, stop in column_groups]
    squares += [square_sum(step[2]) for step in matrix_steps]
    squares += [square_sum(column_direction[start:stop]) / groups for start, stop in column_groups]
    squares = jnp.concatenate(squares)

    _, norm_one_pull = jax.vjp(layer_norm, inputs, vectors[0], vectors[1])
    back_inputs_norm, slope_gain_one, slope_shift_one = norm_one_pull(
        after(back_normed, squares).astype(wide)
    )
    back_inputs = back_middle + back_inputs_norm
    last_sums = sum_everywhere(jnp.concatenate([squares, slope_gain_one, slope_shift_one]))
    norm_totals = jnp.sum(last_sums[: 14 * cols].reshape(2, 7, cols), axis=-1)
    early_rows = last_sums[14 * cols :].reshape(2, width)
    vector_total = jnp.concatenate([early_rows, late_rows], axis=0)

    results = []
    weight_norms = []
    update_norms = []
    for ordinal in range(4):
        fresh, weight_norm, update_norm = trust_apply(
            masters[ordinal],
            matrix_steps[ordinal][2],
            norm_totals[0, ordinal],
            norm_totals[1, ordinal],
        )
        results += [
            fresh,
            matrix_steps[ordinal][0],
            matrix_steps[ordinal][1],
            fresh.astype(low),
        ]
        weight_norms.append(weight_norm)
        update_norms.append(update_norm)
    column_parts = []
    for ordinal in range(3):
        start, stop = column_groups[ordinal]
        fresh, weight_norm, update_norm = trust_apply(
            column_bias[start:stop],
            column_direction[start:stop],
            norm_totals[0, 4 + ordinal],
            norm_totals[1, 4 + ordinal],
        )
        column_parts.append(fresh)
        weight_norms.append(weight_norm)
        update_norms.append(update_norm)
    vectors_mean, vectors_square, vectors_direction = adapt_step(
        vectors, vectors_first, vectors_second, vector_total * factor, 0.0
    )
    new_vectors, vector_weight_norms, vector_update_norms = trust_apply(
        vectors,
        vectors_direction,
        jnp.sum(vectors * vectors, axis=1, keepdims=True),
        jnp.sum(vectors_direction * vectors_direction, axis=1, keepdims=True),
    )
    trust_norms = jnp.stack(
        [
            jnp.concatenate([jnp.stack(weight_norms), vector_weight_norms[:, 0]]),
            jnp.concatenate([jnp.stack(update_norms), vector_update_norms[:, 0]]),
        ]
    )
    return (
        layer_output,
        back_inputs * factor,
        *results,
        jnp.concatenate(column_parts, axis=0),
        column_mean,
        column_square[0],
        column_square[1],
        column_square[2:],
        new_vectors,
        vectors_mean,
        vectors_square[0:2],
        vectors_square[2:],
        trust_norms,
    )


def solution(mesh):
    in_specs = (
        P(("dp", "tensor"), None),
        P(("dp", "tensor"), None),
        P(("dp", "tensor")),
        P("dp", None, "tensor"),
        P("dp", None, "tensor"),
        P("dp", None, "tensor"),
        P("tensor", "dp"),
        P("tensor", "dp"),
        P("tensor", "dp"),
        P("dp", None, "tensor"),
        P("dp", None, "tensor"),
        P("dp", None, "tensor"),
        P(None, "tensor", "dp"),
        P(None, "tensor", "dp"),
        P(None, "tensor", "dp"),
        P(None, "tensor"),
        P(None, "tensor"),
        P(None, "tensor"),
        P(),
        P(),
        P(),
    )
    out_specs = (
        P(("dp", "tensor"), None),
        P(("dp", "tensor"), None),
        P("dp", None, "tensor"),
        P("dp", None, "tensor"),
        P("dp", None, "tensor"),
        P("dp", None, "tensor"),
        P("tensor", "dp"),
        P("tensor", "dp"),
        P("tensor", "dp"),
        P("tensor", "dp"),
        P("dp", None, "tensor"),
        P("dp", None, "tensor"),
        P("dp", None, "tensor"),
        P("dp", None, "tensor"),
        P(None, "tensor", "dp"),
        P(None, "tensor", "dp"),
        P(None, "tensor", "dp"),
        P(None, "tensor", "dp"),
        P(None, "tensor"),
        P(None, "tensor"),
        P("tensor"),
        P("tensor"),
        P(None, "tensor"),
        P(),
        P(),
        P(),
        P(),
        P(),
    )
    return jax.shard_map(
        on_device, mesh=mesh, in_specs=in_specs, out_specs=out_specs, check_vma=False
    )
```

```python
import functools

import jax
import jax.numpy as jnp
from jax import lax
from jax.experimental import pallas as pl
from jax.experimental.layout import Layout, with_layout_constraint
from jax.experimental.pallas import tpu as pltpu
from jax.sharding import PartitionSpec as P

HEAD_DIM = 128
QUERY_BLOCK = 512
STEP_COUNT = 10
LOG2E = 1.4426950408889634
MASKED = -1e30
VMEM_BYTES = 56 * 2**20
ROWS = (((1,), (1,)), ((), ()))
TOKENS = (((0,), (0,)), ((), ()))

norm_epsilon = 1e-05
beta_one = 0.9
beta_two = 0.999
adam_epsilon = 1e-06
decay_rate = 0.01
learn_rate = 0.5
trust_epsilon = 1e-06


def layer_norm(values, gain_row, shift_row):
    centre = values - jnp.mean(values, axis=-1, keepdims=True)
    spread = jnp.mean(centre * centre, axis=-1, keepdims=True)
    return centre * lax.rsqrt(spread + norm_epsilon) * gain_row + shift_row


def dot_as(left, right, dims, kind=jnp.float32):
    return lax.dot_general(left, right, dims, preferred_element_type=jnp.float32).astype(kind)


PLAIN = (((1,), (0,)), ((), ()))


def flip(index, mask):
    result = index
    bit = 1
    while bit <= mask:
        if mask & bit:
            result = result + bit - 2 * bit * lax.rem(lax.div(index, bit), 2)
        bit *= 2
    return result


def greet_all(peers):
    barrier = pltpu.get_barrier_semaphore()
    for peer in peers:
        pl.semaphore_signal(barrier, inc=1, device_id=peer, device_id_type=pl.DeviceIdType.MESH)
    pl.semaphore_wait(barrier, len(peers))


def remote(source, target, send, receive, device):
    return pltpu.make_async_remote_copy(
        src_ref=source,
        dst_ref=target,
        send_sem=send,
        recv_sem=receive,
        device_id=device,
        device_id_type=pl.DeviceIdType.MESH,
    )


def everyone(groups, slices):
    count = groups * slices
    me = lax.axis_index("dp") * slices + lax.axis_index("tensor")

    def anyone(step):
        other = lax.rem(me + step, count)
        return (lax.div(other, slices), lax.rem(other, slices))

    def greet():
        barrier = pltpu.get_barrier_semaphore()

        def signal(step, carry):
            pl.semaphore_signal(
                barrier, inc=1, device_id=anyone(step), device_id_type=pl.DeviceIdType.MESH
            )
            return carry

        lax.fori_loop(1, count, signal, 0)
        pl.semaphore_wait(barrier, count - 1)

    return anyone, greet


def spread_sum(
    values_ref, out_ref, held, send_one, recv_one, send_two, recv_two, anyone, groups, slices
):
    count = groups * slices
    me = lax.axis_index("dp") * slices + lax.axis_index("tensor")

    def first(step):
        source = values_ref.at[lax.rem(me + step, count)]
        return remote(
            source, held.at[step], send_one.at[step], recv_one.at[step], anyone(step)
        )

    def second(step):
        return remote(
            held.at[0], out_ref.at[me], send_two.at[step], recv_two.at[step], anyone(step)
        )

    def each(action):
        lax.fori_loop(1, count, lambda step, carry: (action(step), carry)[1], 0)

    def wait_first(step, total):
        first(step).wait()
        return total + held[step]

    def start():
        each(lambda step: first(step).start())

    def middle():
        total = lax.fori_loop(1, count, wait_first, values_ref[me])
        held[0] = total
        out_ref[me] = total
        each(lambda step: second(step).start())

    def end():
        each(lambda step: second(step).wait())

    return start, middle, end


def sum_scratch(count):
    dma = pltpu.SemaphoreType.DMA
    return [pltpu.VMEM((count, 8, 128), jnp.float32)] + [dma((count,))] * 4


def direct_masks(quads):
    return [2, 4] if quads == 4 else [2 * m for m in range(1, quads)]


def two_hops(quads):
    return [(2, 0, 4), (4, 1, 2)] if quads == 4 else []


def square_reduce(quads, rows, across, send, receive, parts, sums, hop_buf, in_buf):
    masks = direct_masks(quads)
    half_rows = rows // 2

    def landing(at, half):
        return in_buf.at[at, pl.ds(half * half_rows, half_rows)]

    def hop(half):
        goal = 4 if half == 0 else 2
        return remote(
            parts(3, half), hop_buf.at[half], send.at[half], receive.at[half], across(goal)
        )

    def plain(at, half, source):
        number = 2 + 2 * at + half
        return remote(
            source, landing(at, half), send.at[number], receive.at[number], across(masks[at])
        )

    def whole(at):
        return remote(
            parts(at + 1, None), in_buf.at[at], send.at[at], receive.at[at], across(masks[at])
        )

    def early(block):
        if quads != 4:
            whole(block - 1).start()
        elif block == 3:
            hop(0).start()
            hop(1).start()
        else:
            half = 1 if block == 1 else 0
            plain(block - 1, half, parts(block, half)).start()

    def middle():
        if quads != 4:
            return
        for block, half in ((1, 0), (2, 1)):
            hop(half).wait_recv()
            target = sums(block, half)
            target[...] = (
                target[...].astype(jnp.float32) + hop_buf[half].astype(jnp.float32)
            ).astype(jnp.bfloat16)
            plain(block - 1, half, target).start()

    def end():
        if quads != 4:
            for at in range(quads - 1):
                whole(at).wait()
            return
        for half in range(2):
            hop(half).wait_send()
            for block in (1, 2):
                plain(block - 1, half, parts(block, half)).wait()

    return early, middle, end


def pair_reduce(quads, me, across, block_of, near, far, send, receive, load_sem):
    copies = []
    for m in range(quads):
        copies.append(
            remote(
                block_of(flip(me, 2 * m + 1)), far.at[m], send.at[m], receive.at[m], across(1)
            )
        )
    loads = [
        pltpu.make_async_copy(block_of(flip(me, 2 * m)), near.at[m], load_sem.at[m])
        for m in range(quads)
    ]

    def start():
        for copy in copies + loads:
            copy.start()

    def finish(m):
        loads[m].wait()
        copies[m].wait()
        near[m] = (near[m].astype(jnp.float32) + far[m].astype(jnp.float32)).astype(near.dtype)

    return start, finish


def reduce_scratch(quads, rows, width):
    dma = pltpu.SemaphoreType.DMA
    return [
        pltpu.VMEM((2, rows // 2, width), jnp.bfloat16),
        pltpu.VMEM((len(direct_masks(quads)), rows, width), jnp.bfloat16),
        dma((max(6, quads - 1),)),
        dma((max(6, quads - 1),)),
    ]


def forward_kernel(
    q_ref, k_ref, v_ref, bias_ref, back_ref, wide_ref, total_ref, own_ref, back_out,
    held, send_sem, recv_sem, keep_sem, e_send, e_recv,
    *, heads, blocks, size, slices, groups
):
    factor = HEAD_DIM**-0.5 * LOG2E
    head = pl.program_id(0)
    which = pl.program_id(1)
    me = lax.axis_index("dp")
    place = lax.axis_index("tensor")
    rows = own_ref.shape[0]
    queries = q_ref[...]
    masks = direct_masks(groups // 2)
    hops = two_hops(groups // 2)

    def across(mask):
        return (flip(me, mask), place)

    def e_hops():
        result = []
        half_rows = rows // 2
        for number, (mask, half, goal) in enumerate(hops):
            start = (masks.index(mask) + 1) * rows + half * half_rows
            source = back_ref.at[pl.ds(start, half_rows)]
            target = back_out.at[pl.ds(3 * rows + half * half_rows, half_rows)]
            result.append(
                remote(source, target, e_send.at[number], e_recv.at[number], across(goal))
            )
        return result

    @pl.when(jnp.logical_and(head == 0, which == 0))
    def _():
        greet_all(
            [(me, lax.rem(place + step, slices)) for step in range(1, slices)]
            + [across(goal) for _, _, goal in hops]
        )
        for copy in e_hops():
            copy.start()

    for last in range(blocks):

        @pl.when(which == last)
        def _():
            parts = []
            peak = None
            for at in range(last + 1):
                keys = slice(at * size, (at + 1) * size)
                scores = dot_as(queries, k_ref[keys, :], ROWS) + bias_ref[0:1, keys]
                if at == last:
                    row = lax.broadcasted_iota(jnp.int32, (size, size), 0)
                    col = lax.broadcasted_iota(jnp.int32, (size, size), 1)
                    scores = jnp.where(col <= row, scores, MASKED)
                top = jnp.max(scores, axis=1, keepdims=True)
                peak = top if peak is None else jnp.maximum(peak, top)
                parts.append(scores)
            low = peak * factor
            total = None
            context = None
            for at in range(last + 1):
                keys = slice(at * size, (at + 1) * size)
                weights = jnp.exp2(parts[at] * factor - low)
                more = jnp.sum(weights, axis=1, keepdims=True)
                total = more if total is None else total + more
                term = dot_as(weights.astype(jnp.bfloat16), v_ref[keys, :], PLAIN)
                context = term if context is None else context + term
            context = context * (1.0 / total)
            held[head, last * size : (last + 1) * size, :] = context.astype(jnp.bfloat16)
            wide_ref[...] = context
            logs = jnp.broadcast_to(low + jnp.log2(total), (size, 128))
            total_ref[...] = jnp.transpose(logs)[0:1, :].reshape(1, 1, size)

    def to_owner(owner, number):
        step = lax.rem(owner - place + slices, slices)
        return remote(
            held.at[number, pl.ds(pl.multiple_of(owner * rows, rows), rows)],
            own_ref.at[:, columns(place, number)],
            send_sem.at[step, number],
            recv_sem.at[step, number],
            (me, owner),
        )

    def columns(other, number):
        start = (other * heads + number) * HEAD_DIM
        return pl.ds(pl.multiple_of(start, HEAD_DIM), HEAD_DIM)

    def stay(number):
        return pltpu.make_async_copy(
            held.at[number, pl.ds(pl.multiple_of(place * rows, rows), rows)],
            own_ref.at[:, columns(place, number)],
            keep_sem.at[number],
        )

    for part in range(size // rows):
        owner = which * (size // rows) + part
        pl.when(owner == place)(lambda: stay(head).start())
        pl.when(owner != place)(lambda: to_owner(owner, head).start())

    @pl.when(jnp.logical_and(head == heads - 1, which == blocks - 1))
    def _():
        for copy in e_hops():
            copy.wait()
        for number in range(heads):
            stay(number).wait()
            for step in range(1, slices):
                to_owner(lax.rem(place + step, slices), number).wait_send()
                source = lax.rem(place + slices - step, slices)
                remote(
                    held.at[number, pl.ds(0, rows)],
                    own_ref.at[:, columns(source, number)],
                    send_sem.at[step, number],
                    recv_sem.at[step, number],
                    (me, source),
                ).wait_recv()


def attend_forward(mixed, bias_row, back, rows):
    slices = lax.axis_size("tensor")
    groups = lax.axis_size("dp")
    hops = max(1, len(two_hops(groups // 2)))
    length = mixed.shape[0]
    cols = mixed.shape[1] // 3
    heads = cols // HEAD_DIM
    size = QUERY_BLOCK
    blocks = length // size
    part = pl.BlockSpec((size, HEAD_DIM), lambda h, i: (i, h))
    keys = pl.BlockSpec((length, HEAD_DIM), lambda h, i: (0, heads + h))
    values = pl.BlockSpec((length, HEAD_DIM), lambda h, i: (0, 2 * heads + h))
    dma = pltpu.SemaphoreType.DMA
    return pl.pallas_call(
        functools.partial(
            forward_kernel, heads=heads, blocks=blocks, size=size, slices=slices, groups=groups
        ),
        grid=(heads, blocks),
        in_specs=[
            part,
            keys,
            values,
            pl.BlockSpec((1, length), lambda h, i: (0, 0)),
            pl.BlockSpec(memory_space=pltpu.HBM),
        ],
        out_specs=[
            part,
            pl.BlockSpec((1, 1, size), lambda h, i: (h, 0, i)),
            pl.BlockSpec(memory_space=pltpu.HBM),
            pl.BlockSpec(memory_space=pltpu.HBM),
        ],
        input_output_aliases={4: 3},
        out_shape=[
            jax.ShapeDtypeStruct((length, cols), jnp.float32),
            jax.ShapeDtypeStruct((heads, 1, length), jnp.float32),
            jax.ShapeDtypeStruct((rows, slices * cols), jnp.bfloat16),
            jax.ShapeDtypeStruct(back.shape, back.dtype),
        ],
        scratch_shapes=[
            pltpu.VMEM((heads, length, HEAD_DIM), jnp.bfloat16),
            dma((slices, heads)),
            dma((slices, heads)),
            dma((heads,)),
            dma((hops,)),
            dma((hops,)),
        ],
        compiler_params=pltpu.CompilerParams(
            collective_id=3, has_side_effects=True, vmem_limit_bytes=VMEM_BYTES
        ),
        cost_estimate=pl.CostEstimate(
            flops=4 * length * length * cols,
            bytes_accessed=100 * 2**20,
            transcendentals=heads * length * length // 2,
        ),
        name="attend_forward",
    )(mixed, mixed, mixed, bias_row, back)


def backward_kernel(
    low_ref, out_ref, mixed_ref, wide_ref, total_ref, bias_ref, part_ref, thin_ref,
    grad_ref, layer_ref, thin_sum,
    sent, back_buf, sum_ref, half_buf, own_buf, hop_buf, in_buf, send, receive,
    send_sem, recv_sem, load_sem, thin_send, thin_recv, thin_load,
    *, blocks, size, slices, groups
):
    scale = HEAD_DIM**-0.5
    factor = scale * LOG2E
    me = lax.axis_index("dp")
    place = lax.axis_index("tensor")
    rows = low_ref.shape[0]
    cols = back_buf.shape[1]
    heads = cols // HEAD_DIM
    quads = groups // 2
    half_rows = rows // 2

    def across(mask):
        return (flip(me, mask), place)

    def parts(block, side):
        if side is None:
            return part_ref.at[pl.ds(block * rows, rows)]
        return part_ref.at[pl.ds(block * rows + side * half_rows, half_rows)]

    def sums(block, side):
        return half_buf.at[side]

    loads = [pltpu.make_async_copy(parts(0, None), own_buf, load_sem.at[0])]
    if quads == 4:
        for block, side in ((1, 0), (2, 1)):
            loads.append(
                pltpu.make_async_copy(parts(block, side), half_buf.at[side], load_sem.at[1 + side])
            )
    for copy in loads:
        copy.start()
    greet_all(
        [(me, lax.rem(place + step, slices)) for step in range(1, slices)]
        + [(lax.rem(me + step, groups), place) for step in range(1, groups)]
    )
    early, middle, end = square_reduce(
        quads, rows, across, send, receive, parts, sums, hop_buf, in_buf
    )

    thin_rows, thin_cols = thin_ref.shape[0], thin_sum.shape[1]

    def thin_columns(other):
        return thin_ref.at[:, pl.ds(pl.multiple_of(other * thin_cols, thin_cols), thin_cols)]

    def thin_place(other):
        return thin_sum.at[pl.ds(pl.multiple_of(other * thin_rows, thin_rows), thin_rows)]

    def thin_to(step):
        other = lax.rem(me + step, groups)
        return remote(
            thin_columns(other), thin_place(me), thin_send.at[step], thin_recv.at[step],
            (other, place),
        )

    def thin_from(step):
        other = lax.rem(me + groups - step, groups)
        return remote(
            thin_columns(other), thin_place(other), thin_send.at[step], thin_recv.at[step],
            (other, place),
        )

    thin_own = pltpu.make_async_copy(thin_columns(me), thin_place(me), thin_load)
    early(quads - 1)

    def span(start, size):
        return pl.ds(pl.multiple_of(start, size), size)

    def product(owner):
        return dot_as(low_ref[...], out_ref[span(owner * cols, cols), :], ROWS, jnp.bfloat16)

    def to_owner(step, head):
        return remote(
            sent.at[step - 1, :, span(head * HEAD_DIM, HEAD_DIM)],
            back_buf.at[span(place * rows, rows), span(head * HEAD_DIM, HEAD_DIM)],
            send_sem.at[step, head],
            recv_sem.at[step, head],
            (me, lax.rem(place + step, slices)),
        )

    for step in range(1, slices):
        sent[step - 1] = product(lax.rem(place + step, slices))
    for head in range(heads):
        for step in range(1, slices):
            to_owner(step, head).start()
    back_buf[span(place * rows, rows), :] = product(place)

    def one_head(head, carry):
        for step in range(1, slices):
            source = lax.rem(place + slices - step, slices)
            remote(
                sent.at[step - 1, :, span(head * HEAD_DIM, HEAD_DIM)],
                back_buf.at[span(source * rows, rows), span(head * HEAD_DIM, HEAD_DIM)],
                send_sem.at[step, head],
                recv_sem.at[step, head],
                (me, source),
            ).wait_recv()
        here = span(head * HEAD_DIM, HEAD_DIM)
        key_here = span(cols + head * HEAD_DIM, HEAD_DIM)
        value_here = span(2 * cols + head * HEAD_DIM, HEAD_DIM)
        inner = []
        for at in range(blocks):
            part = slice(at * size, (at + 1) * size)
            pairs = back_buf[part, here].astype(jnp.float32) * wide_ref[part, here]
            inner.append(jnp.sum(jnp.transpose(pairs), axis=0, keepdims=True))
        for key_at in range(blocks):
            keys = slice(key_at * size, (key_at + 1) * size)
            key_rows = mixed_ref[keys, key_here]
            values = mixed_ref[keys, value_here]
            bias = bias_ref[keys, 0:1]
            back_keys = None
            back_values = None
            for query_at in range(key_at, blocks):
                part = slice(query_at * size, (query_at + 1) * size)
                queries = mixed_ref[part, here]
                back = back_buf[part, here]
                level = dot_as(key_rows, queries, ROWS) * factor - total_ref[head, 0:1, part] + bias
                if query_at == key_at:
                    row = lax.broadcasted_iota(jnp.int32, (size, size), 0)
                    col = lax.broadcasted_iota(jnp.int32, (size, size), 1)
                    level = jnp.where(row <= col, level, MASKED)
                chances = jnp.exp2(level)
                back_chances = dot_as(values, back, ROWS)
                back_scores = (chances * (back_chances - inner[query_at])).astype(jnp.bfloat16)
                more_values = dot_as(chances.astype(jnp.bfloat16), back, PLAIN)
                more_keys = dot_as(back_scores, queries, PLAIN)
                more_queries = dot_as(back_scores, key_rows, TOKENS)
                if key_at == 0:
                    sum_ref[part, :] = more_queries
                else:
                    sum_ref[part, :] += more_queries
                back_keys = more_keys if back_keys is None else back_keys + more_keys
                back_values = more_values if back_values is None else back_values + more_values
            grad_ref[keys, key_here] = (back_keys * scale).astype(jnp.bfloat16)
            grad_ref[keys, value_here] = back_values.astype(jnp.bfloat16)
        grad_ref[:, here] = (sum_ref[...] * scale).astype(jnp.bfloat16)

        @pl.when(head == 0)
        def _():
            for block in range(1, quads - 1):
                early(block)

        @pl.when(head == heads // 2 - 1)
        def _():
            for copy in loads:
                copy.wait()
            middle()

        @pl.when(head == min(2, heads - 1))
        def _():
            thin_own.start()
            for step in range(1, groups):
                thin_to(step).start()

        return carry

    lax.fori_loop(0, heads, one_head, 0)
    end()
    total = own_buf[...].astype(jnp.float32)
    for at in range(len(direct_masks(quads))):
        total = total + in_buf[at].astype(jnp.float32)
    layer_ref[...] = total
    thin_own.wait()
    for step in range(1, groups):
        thin_from(step).wait_recv()
        thin_to(step).wait_send()
    for head in range(heads):
        for step in range(1, slices):
            to_owner(step, head).wait_send()


def attend_backward(back_low, outward, mixed, wide, totals, bias_column, widened, thin):
    slices = lax.axis_size("tensor")
    groups = lax.axis_size("dp")
    quads = groups // 2
    rows, width = back_low.shape
    length, cols = wide.shape
    heads = cols // HEAD_DIM
    size = QUERY_BLOCK
    vmem = pl.BlockSpec(memory_space=pltpu.VMEM)
    hbm = pl.BlockSpec(memory_space=pltpu.HBM)
    dma = pltpu.SemaphoreType.DMA
    low = jnp.bfloat16
    return pl.pallas_call(
        functools.partial(
            backward_kernel, blocks=length // size, size=size, slices=slices, groups=groups
        ),
        in_specs=[vmem] * 6 + [hbm] * 2,
        out_specs=[vmem, vmem, hbm],
        out_shape=[
            jax.ShapeDtypeStruct((length, 3 * cols), low),
            jax.ShapeDtypeStruct((rows, width), jnp.float32),
            jax.ShapeDtypeStruct((groups * thin.shape[0], width // groups), low),
        ],
        scratch_shapes=[
            pltpu.VMEM((slices - 1, rows, cols), low),
            pltpu.VMEM((length, cols), low),
            pltpu.VMEM((length, HEAD_DIM), jnp.float32),
            pltpu.VMEM((2, rows // 2, width), low),
            pltpu.VMEM((rows, width), low),
        ]
        + reduce_scratch(quads, rows, width)
        + [dma((slices, heads)), dma((slices, heads)), dma((3,))]
        + [dma((groups,)), dma((groups,)), dma],
        compiler_params=pltpu.CompilerParams(
            collective_id=4, has_side_effects=True, vmem_limit_bytes=VMEM_BYTES
        ),
        cost_estimate=pl.CostEstimate(
            flops=10 * length * length * cols,
            bytes_accessed=150 * 2**20,
            transcendentals=heads * length * length // 2,
        ),
        name="attend_backward",
    )(back_low, outward, mixed, wide, totals, bias_column, widened, thin)


def back_kernel(
    e_ref, slope_ref, thin_ref, wide_ref, grad_ref, act_ref,
    own_ref, dhid_ref, sum_ref, layer_ref, share_ref,
    thin_buf, wide_buf, e_buf, slope_buf, dhid_buf, part_buf, hop_buf, in_buf, send, receive,
    load_sem, pair_sem, e_sem, slope_sem, dhid_sem, act_sem, layer_sem, grad_send, grad_recv, grad_sem,
    *, groups, slices
):
    quads = groups // 2
    me = lax.axis_index("dp")
    place = lax.axis_index("tensor")
    rows, width = own_ref.shape
    units = wide_buf.shape[1]
    half = units // 2
    tile = min(512, half)
    slab = min(512, width)

    def across(mask):
        return (flip(me, mask), place)

    def load_block(number, at):
        target = pl.ds(at * rows, rows)
        return (
            pltpu.make_async_copy(
                e_ref.at[target], e_buf.at[number % 2, :, pl.ds(0, width)], e_sem.at[number]
            ),
            pltpu.make_async_copy(
                slope_ref.at[target], slope_buf.at[number % 2], slope_sem.at[number]
            ),
        )

    order = [quads - 1] + list(range(1, quads - 1)) + [0]
    thin_load = pltpu.make_async_copy(thin_ref, thin_buf.at[pl.ds(0, half)], load_sem.at[0])
    thin_load.start()
    for copy in load_block(0, order[0]):
        copy.start()
    wide_load = pltpu.make_async_copy(wide_ref, wide_buf, load_sem.at[1])
    wide_load.start()
    greet_all(
        [across(mask) for mask in [1] + direct_masks(quads)]
        + [(me, lax.rem(place + step, slices)) for step in range(1, slices)]
    )
    span = share_ref.shape[1]

    def grad_rows(owner):
        return grad_ref.at[pl.ds(pl.multiple_of(owner * span, span), span)]

    def grad_to(step):
        owner = lax.rem(place + step, slices)
        return remote(
            grad_rows(owner), share_ref.at[step], grad_send.at[step], grad_recv.at[step],
            (me, owner),
        )

    for step in range(1, slices):
        grad_to(step).start()
    grad_own = pltpu.make_async_copy(grad_rows(place), share_ref.at[0], grad_sem)
    grad_own.start()
    pair = remote(
        thin_ref, thin_buf.at[pl.ds(half, half)], pair_sem.at[0], pair_sem.at[1], across(1)
    )
    pair.start()

    half_rows = rows // 2

    def parts(block, side):
        if side is None:
            return part_buf.at[block - 1]
        return part_buf.at[block - 1, pl.ds(side * half_rows, half_rows)]

    early, middle, end = square_reduce(
        quads, rows, across, send, receive, parts, parts, hop_buf, in_buf
    )
    sum_ref[...] = jnp.zeros_like(sum_ref)
    stores = []
    for number, at in enumerate(order):
        slot = number % 2
        if number + 1 < quads:
            for copy in load_block(number + 1, order[number + 1]):
                copy.start()
        if number == 0:
            thin_load.wait()
        for copy in load_block(number, at):
            copy.wait()
        if number >= 2:
            stores[number - 2].wait()

        def back_tile(index, carry):
            columns = pl.ds(pl.multiple_of(index * tile, tile), tile)
            back = dot_as(e_buf[slot, :, :width], thin_buf[columns, :], ROWS)
            back = (back * slope_buf[slot, :, columns]).astype(jnp.bfloat16)
            dhid_buf[slot, :, columns] = back
            sum_ref[:, columns] += jnp.sum(back.astype(jnp.float32), axis=0, keepdims=True)
            return carry

        if number == 0:
            lax.fori_loop(0, half // tile, back_tile, 0)
            pair.wait_recv()
            lax.fori_loop(half // tile, units // tile, back_tile, 0)
            wide_load.wait()
        else:
            lax.fori_loop(0, units // tile, back_tile, 0)
        store = pltpu.make_async_copy(
            dhid_buf.at[slot, :, pl.ds(0, units)],
            dhid_ref.at[pl.ds(at * rows, rows)],
            dhid_sem.at[number],
        )
        store.start()
        stores.append(store)

        def slab_of(index, carry):
            here = pl.ds(pl.multiple_of(index * slab, slab), slab)
            product = dot_as(dhid_buf[slot, :, :units], wide_buf[here, :], ROWS)
            if at:
                part_buf[at - 1, :, here] = product.astype(jnp.bfloat16)
            else:
                own_ref[:, here] = product
            return carry

        lax.fori_loop(0, width // slab, slab_of, 0)
        if at:
            early(at)
        if number == quads - 2:
            middle()
    for store in stores[-2:]:
        store.wait()

    def load_act(number):
        return pltpu.make_async_copy(
            act_ref.at[pl.ds(number * rows, rows)],
            e_buf.at[number % 2, :, pl.ds(0, units)],
            act_sem.at[number],
        )

    outs = []
    load_act(0).start()
    for number in range(quads):
        slot = number % 2
        if number + 1 < quads:
            load_act(number + 1).start()
        load_act(number).wait()
        if number >= 2:
            outs[number - 2].wait()

        def out_of(index, carry):
            here = pl.ds(pl.multiple_of(index * slab, slab), slab)
            dhid_buf[slot, :, here] = dot_as(
                e_buf[slot, :, :units], thin_buf[:, here], PLAIN, jnp.bfloat16
            )
            return carry

        lax.fori_loop(0, width // slab, out_of, 0)
        out = pltpu.make_async_copy(
            dhid_buf.at[slot, :, pl.ds(0, width)],
            layer_ref.at[pl.ds(number * rows, rows)],
            layer_sem.at[number],
        )
        out.start()
        outs.append(out)
    end()
    for at in range(len(direct_masks(quads))):
        own_ref[...] += in_buf[at].astype(jnp.float32)
    pair.wait_send()
    for out in outs[-2:]:
        out.wait()
    for step in range(1, slices):
        grad_to(step).wait()
    grad_own.wait()


def back_step(back, slope, thin, wide, grad, active):
    groups = lax.axis_size("dp")
    slices = lax.axis_size("tensor")
    quads = groups // 2
    length, width = back.shape
    rows = length // quads
    units = slope.shape[1]
    dma = pltpu.SemaphoreType.DMA
    vmem = pl.BlockSpec(memory_space=pltpu.VMEM)
    hbm = pl.BlockSpec(memory_space=pltpu.HBM)
    low = jnp.bfloat16
    return pl.pallas_call(
        functools.partial(back_kernel, groups=groups, slices=slices),
        in_specs=[hbm] * 6,
        out_specs=[vmem, hbm, vmem, hbm, hbm],
        out_shape=[
            jax.ShapeDtypeStruct((rows, width), jnp.float32),
            jax.ShapeDtypeStruct((length, units), low),
            jax.ShapeDtypeStruct((1, units), jnp.float32),
            jax.ShapeDtypeStruct((length, width), low),
            jax.ShapeDtypeStruct((slices, grad.shape[0] // slices, width), low),
        ],
        scratch_shapes=[
            pltpu.VMEM((units, width), low),
            pltpu.VMEM((width, units), low),
            pltpu.VMEM((2, rows, max(units, width)), low),
            pltpu.VMEM((2, rows, units), jnp.float32),
            pltpu.VMEM((2, rows, max(units, width)), low),
            pltpu.VMEM((quads - 1, rows, width), low),
        ]
        + reduce_scratch(quads, rows, width)
        + [dma((2,)), dma((2,))] + [dma((quads,))] * 5
        + [dma((slices,)), dma((slices,)), dma],
        compiler_params=pltpu.CompilerParams(
            collective_id=5, has_side_effects=True, vmem_limit_bytes=60 * 2**20
        ),
        cost_estimate=pl.CostEstimate(
            flops=4 * length * width * units,
            bytes_accessed=150 * 2**20,
            transcendentals=0,
        ),
        name="back_step",
    )(back, slope, thin, wide, grad, active)


def open_kernel(
    a_ref, w_ref, e_ref, bias_ref, small_ref, count_ref, wide_ref, thin_ref, out_ref,
    full_ref, weight_ref, mixed_ref, back_ref, all_ref, counts_ref, wide_all, thin_all, out_all,
    a_buf, w_buf, wide_buf, thin_buf, out_buf,
    line_send, line_recv, small_send, small_recv, w_send, w_recv, pair_send, pair_recv,
    e_send, e_recv, local_sem, keep_sem, count_send, count_recv,
    wide_send, wide_recv, thin_send, thin_recv, out_send, out_recv, plane_send, plane_recv,
    run_send, run_recv,
    *, groups, slices, piece
):
    quads = groups // 2
    count = groups * slices
    me = lax.axis_index("dp")
    place = lax.axis_index("tensor")
    rows = a_ref.shape[0]
    share = w_buf.shape[0] // groups
    cols = w_buf.shape[1] // 3
    out_cols = out_all.shape[1] // groups
    masks = direct_masks(quads)
    hops = two_hops(quads)
    low = jnp.bfloat16
    raw = piece % 128 == 0

    def across(mask):
        return (flip(me, mask), place)

    def along(other):
        return (me, other)

    def beside(step):
        return (me, lax.rem(place + step, slices))

    def anyone(step):
        other = lax.rem(me * slices + place + step, count)
        return (lax.div(other, slices), lax.rem(other, slices))

    barrier = pltpu.get_barrier_semaphore()

    def greet(step, carry):
        pl.semaphore_signal(
            barrier, inc=1, device_id=anyone(step), device_id_type=pl.DeviceIdType.MESH
        )
        return carry

    lax.fori_loop(1, count, greet, 0)

    def w_rows(mask, half=None):
        start = flip(me, mask) * share
        if half is None:
            return w_buf.at[pl.ds(pl.multiple_of(start, share), share)]
        size = share // 2
        return w_buf.at[pl.ds(pl.multiple_of(start + half * size, size), size)]

    here = pl.ds(pl.multiple_of(me * share, share), share)
    for part in range(3):
        w_buf[here, part * cols : (part + 1) * cols] = w_ref[part].astype(low)
    a_buf[pl.ds(pl.multiple_of(place * rows, rows), rows), :] = a_ref[...]
    pl.semaphore_wait(barrier, count - 1)

    def a_rows(block):
        return a_buf.at[pl.ds(pl.multiple_of(block * rows, rows), rows)]

    def keep(block):
        return pltpu.make_async_copy(
            a_rows(block),
            full_ref.at[pl.ds(pl.multiple_of(block * rows, rows), rows)],
            keep_sem.at[block],
        )

    def a_half(block, half):
        size = rows // 2
        return a_buf.at[pl.ds(pl.multiple_of(block * rows + half * size, size), size)]

    def a_move(step, side, half, outgoing):
        back = step if outgoing else step + 1
        block = place - back if side == 0 else place + back
        towards = (side == 0) == outgoing
        return remote(
            a_half(block, half), a_half(block, half),
            line_send.at[side, half, step], line_recv.at[side, half, step],
            along(place + 1 if towards else place - 1),
        )

    def sends_right(step):
        return jnp.logical_and(place - step >= 0, place + 1 < slices)

    def sends_left(step):
        return jnp.logical_and(place + step < slices, place >= 1)

    for half in range(2):
        pl.when(sends_right(0))(lambda: a_move(0, 0, half, True).start())
        pl.when(sends_left(0))(lambda: a_move(0, 1, half, True).start())

    w_copies = []
    for at, mask in enumerate(masks):
        copy = remote(w_rows(0), w_rows(0), w_send.at[at], w_recv.at[at], across(mask))
        copy.start()
        w_copies.append(copy)

    keep(place).start()
    all_ref[place] = small_ref[...]
    small_copies = []
    for step in range(1, slices):
        copy = remote(
            small_ref, all_ref.at[place], small_send.at[step], small_recv.at[step], beside(step)
        )
        copy.start()
        small_copies.append(copy)

    def tell(step):
        return remote(
            count_ref, counts_ref.at[step], count_send.at[step], count_recv.at[step], anyone(step)
        )

    counts_ref[0] = count_ref[...]
    lax.fori_loop(1, count, lambda step, carry: (tell(step).start(), carry)[1], 0)

    out_here = pl.ds(pl.multiple_of(place * cols, cols), cols)
    out_buf[out_here, :] = out_ref[...].astype(low)
    out_copies = []
    for step in range(1, slices):
        target = out_buf.at[out_here]
        copy = remote(target, target, out_send.at[step], out_recv.at[step], beside(step))
        copy.start()
        out_copies.append(copy)

    for part in range(groups):
        if raw:
            row = part * piece // cols
            start = part * piece % cols
            wide_buf[part] = wide_ref[:, row, start : start + piece].astype(low)
            thin_buf[part] = thin_ref[row, start : start + piece, :].astype(low)
        else:
            wide_buf[part] = wide_ref[part]
            thin_buf[part] = thin_ref[part]
    thin_cols = thin_buf.shape[2]
    wide_here = wide_all.at[place, here]
    thin_here = thin_all.at[:, pl.ds(pl.multiple_of(me * thin_cols, thin_cols), thin_cols)]

    def wide_to(step):
        other = lax.rem(me + step, groups)
        return remote(
            wide_buf.at[other], wide_here, wide_send.at[step], wide_recv.at[step], (other, place)
        )

    def thin_to(step):
        other = lax.rem(me + step, groups)
        return remote(
            thin_buf.at[other], thin_here, thin_send.at[step], thin_recv.at[step], (other, place)
        )

    own_wide = pltpu.make_async_copy(wide_buf.at[me], wide_here, local_sem.at[2])
    own_wide.start()
    own_thin = pltpu.make_async_copy(thin_buf.at[me], thin_here, local_sem.at[3])
    own_thin.start()
    for step in range(1, groups):
        wide_to(step).start()

    pair_copies = []

    def to_pair(source):
        at = len(pair_copies)
        copy = remote(source, source, pair_send.at[at], pair_recv.at[at], across(1))
        copy.start()
        pair_copies.append(copy)

    to_pair(w_rows(0))
    for at, copy in enumerate(w_copies):
        remote(
            w_rows(masks[at]), w_rows(masks[at]), w_send.at[at], w_recv.at[at], across(masks[at])
        ).wait_recv()
    hop_copies = []
    for number, (mask, half, goal) in enumerate(hops):
        at = len(masks) + number
        source = w_rows(mask, half)
        copy = remote(source, source, w_send.at[at], w_recv.at[at], across(goal))
        copy.start()
        hop_copies.append(copy)
    for mask in masks:
        to_pair(w_rows(mask))

    own = pltpu.make_async_copy(e_ref, back_ref.at[pl.ds(0, rows)], local_sem.at[0])
    own.start()

    def e_moves():
        return [
            remote(
                e_ref, back_ref.at[pl.ds((at + 1) * rows, rows)], e_send.at[at], e_recv.at[at],
                across(mask),
            )
            for at, mask in enumerate(masks)
        ]

    for number, (mask, half, goal) in enumerate(hops):
        at = len(masks) + number
        landed = w_rows(2 + 4, half)
        remote(landed, landed, w_send.at[at], w_recv.at[at], across(goal)).wait_recv()
        to_pair(landed)
    sources = [0] + masks
    for at, mask in enumerate(sources):
        landed = w_rows(mask + 1)
        remote(landed, landed, pair_send.at[at], pair_recv.at[at], across(1)).wait_recv()
    for number, (mask, half, goal) in enumerate(hops):
        at = len(sources) + number
        landed = w_rows(2 + 4 + 1, half)
        remote(landed, landed, pair_send.at[at], pair_recv.at[at], across(1)).wait_recv()
    weights_out = pltpu.make_async_copy(w_buf, weight_ref, local_sem.at[1])
    weights_out.start()

    def multiply(block):
        where = pl.ds(pl.multiple_of(block * rows, rows), rows)
        left = a_buf[where, :]
        for part in range(3):
            columns = slice(part * cols, (part + 1) * cols)
            product = dot_as(left, w_buf[:, columns], PLAIN) + bias_ref[0:1, columns]
            mixed_ref[where, columns] = product.astype(low)

    multiply(place)

    def out_at(mask, half=None):
        start = pl.multiple_of(flip(me, mask) * out_cols, out_cols)
        size = out_all.shape[0] // 2
        if half is None:
            return out_all.at[:, pl.ds(start, out_cols)]
        return out_all.at[half * size : (half + 1) * size, pl.ds(start, out_cols)]

    own_out = pltpu.make_async_copy(out_buf, out_at(0), local_sem.at[4])

    def plane(at, source, target, device):
        return remote(source, target, plane_send.at[at], plane_recv.at[at], device)

    def plane_first():
        return [
            plane(at, out_buf, out_at(0), across(mask)) for at, mask in enumerate([1] + masks)
        ]

    def plane_landed():
        return [
            plane(at, out_buf, out_at(mask), across(mask)) for at, mask in enumerate([1] + masks)
        ]

    def plane_hops():
        return [
            plane(1 + len(masks) + number, out_at(mask, half), out_at(mask, half), across(goal))
            for number, (mask, half, goal) in enumerate(hops)
        ]

    def plane_pairs():
        return [
            plane(1 + len(masks) + len(hops) + at, out_at(mask), out_at(mask), across(1))
            for at, mask in enumerate(masks)
        ]

    def plane_last():
        return [
            plane(
                1 + 2 * len(masks) + len(hops) + number, out_at(6, half), out_at(6, half), across(1)
            )
            for number, (mask, half, goal) in enumerate(hops)
        ]

    def wide_move(step, side, half, outgoing):
        back = step if outgoing else step + 1
        block = place - back if side == 0 else place + back
        towards = (side == 0) == outgoing
        size = wide_all.shape[1] // 2
        part = wide_all.at[block, pl.ds(half * size, size)]
        return remote(
            part, part, run_send.at[side, half, step], run_recv.at[side, half, step],
            along(place + 1 if towards else place - 1),
        )

    def wide_arrived():
        own_wide.wait()
        for step in range(1, groups):
            other = lax.rem(me + groups - step, groups)
            wide_from = wide_all.at[
                place, pl.ds(pl.multiple_of(other * share, share), share)
            ]
            remote(
                wide_buf.at[other], wide_from, wide_send.at[step], wide_recv.at[step],
                (other, place),
            ).wait_recv()
        for half in range(2):
            pl.when(sends_right(0))(lambda: wide_move(0, 0, half, True).start())
            pl.when(sends_left(0))(lambda: wide_move(0, 1, half, True).start())

    def pass_on(step, carry):
        got_left = place - 1 - step >= 0
        got_right = place + 1 + step < slices

        for half in range(2):
            for side, got, sends in ((0, got_left, sends_right), (1, got_right, sends_left)):

                @pl.when(got)
                def _():
                    a_move(step, side, half, False).wait_recv()

                    @pl.when(jnp.logical_and(step + 1 < slices - 1, sends(step + 1)))
                    def _():
                        a_move(step + 1, side, half, True).start()

        pl.when(got_left)(lambda: keep(place - 1 - step).start())
        pl.when(got_right)(lambda: keep(place + 1 + step).start())

        @pl.when(step == 0)
        def _():
            for copy in out_copies:
                copy.wait_recv()
            own_out.start()
            for copy in plane_first():
                copy.start()
            for step_to in range(1, groups):
                thin_to(step_to).start()
            for copy in e_moves():
                copy.start()

        @pl.when(got_left)
        def _():
            multiply(place - 1 - step)

        @pl.when(got_right)
        def _():
            multiply(place + 1 + step)

        @pl.when(step == 1)
        def _():
            wide_arrived()
            for copy in plane_landed():
                copy.wait_recv()
            for copy in plane_hops() + plane_pairs():
                copy.start()

        return carry

    lax.fori_loop(0, slices - 1, pass_on, 0)

    def wide_on(step, carry):
        gots = (place - 1 - step >= 0, place + 1 + step < slices)
        for half in range(2):
            for side, sends in ((0, sends_right), (1, sends_left)):

                @pl.when(gots[side])
                def _():
                    wide_move(step, side, half, False).wait_recv()

                    @pl.when(jnp.logical_and(step + 1 < slices - 1, sends(step + 1)))
                    def _():
                        wide_move(step + 1, side, half, True).start()

        return carry

    lax.fori_loop(0, slices - 1, wide_on, 0)

    for number, (mask, half, goal) in enumerate(hops):
        at = 1 + len(masks) + number
        plane(at, out_at(6, half), out_at(6, half), across(goal)).wait_recv()
    for copy in plane_last():
        copy.start()
    for at, mask in enumerate(masks):
        landed = out_at(mask + 1)
        plane(1 + len(masks) + len(hops) + at, landed, landed, across(1)).wait_recv()
    for number, (mask, half, goal) in enumerate(hops):
        landed = out_at(7, half)
        plane(1 + 2 * len(masks) + len(hops) + number, landed, landed, across(1)).wait_recv()
    for copy in plane_first() + plane_hops() + plane_pairs() + plane_last():
        copy.wait_send()
    for at, mask in enumerate(masks):
        landed = back_ref.at[pl.ds((at + 1) * rows, rows)]
        remote(e_ref, landed, e_send.at[at], e_recv.at[at], across(mask)).wait_recv()
    for copy in e_moves() + w_copies + hop_copies + pair_copies + out_copies:
        copy.wait_send()
    for copy in small_copies:
        copy.wait()
    for step in range(1, groups):
        other = lax.rem(me + groups - step, groups)
        thin_from = thin_all.at[
            :, pl.ds(pl.multiple_of(other * thin_cols, thin_cols), thin_cols)
        ]
        device = (other, place)
        remote(
            thin_buf.at[other], thin_from, thin_send.at[step], thin_recv.at[step], device
        ).wait_recv()
        wide_to(step).wait_send()
        thin_to(step).wait_send()
    lax.fori_loop(1, count, lambda step, carry: (tell(step).wait(), carry)[1], 0)
    for copy in (own, weights_out, own_thin, own_out):
        copy.wait()

    def finish(step, carry):
        for half in range(2):
            pl.when(sends_right(step))(lambda: a_move(step, 0, half, True).wait_send())
            pl.when(sends_left(step))(lambda: a_move(step, 1, half, True).wait_send())
            pl.when(sends_right(step))(lambda: wide_move(step, 0, half, True).wait_send())
            pl.when(sends_left(step))(lambda: wide_move(step, 1, half, True).wait_send())
        return carry

    lax.fori_loop(0, slices - 1, finish, 0)
    for block in range(slices):
        keep(block).wait()


def open_step(normed, inward, back, bias, small, living, widening, narrowing, outward):
    groups = lax.axis_size("dp")
    slices = lax.axis_size("tensor")
    count = groups * slices
    quads = groups // 2
    rows, width = normed.shape
    share, _, cols = inward.shape
    piece = 4 * cols // groups
    out_cols = outward.shape[1]
    hops = len(two_hops(quads))
    direct = len(direct_masks(quads))
    dma = pltpu.SemaphoreType.DMA
    vmem = pl.BlockSpec(memory_space=pltpu.VMEM)
    hbm = pl.BlockSpec(memory_space=pltpu.HBM)
    low = jnp.bfloat16
    wide = jnp.float32
    if piece % 128:
        widening = widening.astype(low).reshape(share, groups, piece).transpose(1, 0, 2)
        narrowing = narrowing.astype(low).reshape(groups, piece, out_cols)
    shape = jax.ShapeDtypeStruct
    planes = 1 + 2 * direct + 2 * hops
    return pl.pallas_call(
        functools.partial(open_kernel, groups=groups, slices=slices, piece=piece),
        in_specs=[vmem, vmem, hbm, vmem, vmem, vmem, vmem, vmem, vmem],
        out_specs=[hbm, hbm, vmem, hbm, vmem, vmem, hbm, hbm, hbm],
        out_shape=[
            shape((slices * rows, width), low),
            shape((width, 3 * cols), low),
            shape((slices * rows, 3 * cols), low),
            shape((quads * rows, width), low),
            shape((slices,) + small.shape, wide),
            shape((count, 8, 128), wide),
            shape((slices, width, piece), low),
            shape((piece, width), low),
            shape((width, width), low),
        ],
        scratch_shapes=[
            pltpu.VMEM((slices * rows, width), low),
            pltpu.VMEM((width, 3 * cols), low),
            pltpu.VMEM((groups, share, piece), low),
            pltpu.VMEM((groups, piece, out_cols), low),
            pltpu.VMEM((slices * cols, out_cols), low),
            dma((2, 2, slices)),
            dma((2, 2, slices)),
            dma((slices,)),
            dma((slices,)),
            dma((direct + hops,)),
            dma((direct + hops,)),
            dma((1 + direct + hops,)),
            dma((1 + direct + hops,)),
            dma((direct,)),
            dma((direct,)),
            dma((5,)),
            dma((slices,)),
            dma((count,)),
            dma((count,)),
            dma((groups,)),
            dma((groups,)),
            dma((groups,)),
            dma((groups,)),
            dma((slices,)),
            dma((slices,)),
            dma((planes,)),
            dma((planes,)),
            dma((2, 2, slices)),
            dma((2, 2, slices)),
        ],
        compiler_params=pltpu.CompilerParams(
            collective_id=1, has_side_effects=True, vmem_limit_bytes=VMEM_BYTES
        ),
        cost_estimate=pl.CostEstimate(
            flops=2 * slices * rows * width * 3 * cols,
            bytes_accessed=400 * 2**20,
            transcendentals=0,
        ),
        name="open_step",
    )(
        normed, inward.transpose(1, 0, 2), back, bias, small, living, widening, narrowing, outward
    )


def hidden_gather_kernel(
    b_ref, weight_ref, bias_ref, all_ref, act_ref, slope_ref, full_ref,
    b_buf, w_buf, act_buf, slope_buf,
    b_send, b_recv, keep_sem, act_sem, slope_sem, w_sem, pair_sem, out_sem,
    *, groups
):
    quads = groups // 2
    me = lax.axis_index("dp")
    place = lax.axis_index("tensor")
    rows = b_ref.shape[0]
    tiles, _, tile = weight_ref.shape
    masks = direct_masks(quads)
    hops = two_hops(quads)
    half_rows = rows // 2

    def across(mask):
        return (flip(me, mask), place)

    load = pltpu.make_async_copy(weight_ref, w_buf.at[pl.ds(0, tiles)], w_sem)
    load.start()
    greet_all([across(mask) for mask in [1] + masks])

    def block(at):
        return b_buf.at[pl.ds(at * rows, rows)]

    def piece(at, half):
        return b_buf.at[pl.ds(at * rows + half * half_rows, half_rows)]

    copies = []
    for at, mask in enumerate(masks):
        copy = remote(b_ref, block(at + 1), b_send.at[at], b_recv.at[at], across(mask))
        copy.start()
        copies.append(copy)
    pair = remote(
        weight_ref, w_buf.at[pl.ds(tiles, tiles)], pair_sem.at[0], pair_sem.at[1], across(1)
    )
    pair.start()
    b_buf[0:rows, :] = b_ref[...]
    keeps = []
    stores = []

    def keep(at):
        copy = pltpu.make_async_copy(
            block(at), all_ref.at[pl.ds(at * rows, rows)], keep_sem.at[at]
        )
        copy.start()
        keeps.append(copy)

    def multiply(at, first, amount):
        def part(number, carry):
            columns = pl.ds(pl.multiple_of(number * tile, tile), tile)
            hidden = (
                dot_as(b_buf[at * rows : (at + 1) * rows, :], w_buf[number], PLAIN)
                + bias_ref[0:1, columns]
            )
            root = 0.7978845608028654
            square = hidden * hidden
            bent = jnp.tanh(root * hidden * (1.0 + 0.044715 * square))
            half = 0.5 * (1.0 + bent)
            act_buf[at % 2, :, columns] = (hidden * half).astype(jnp.bfloat16)
            slope_buf[at % 2, :, columns] = half + 0.5 * hidden * (1.0 - bent * bent) * (
                root * (1.0 + 3.0 * 0.044715 * square)
            )
            return carry

        lax.fori_loop(first, first + amount, part, 0)

    def store(at):
        target = pl.ds(at * rows, rows)
        pair_of = [
            pltpu.make_async_copy(act_buf.at[at % 2], act_ref.at[target], act_sem.at[at]),
            pltpu.make_async_copy(slope_buf.at[at % 2], slope_ref.at[target], slope_sem.at[at]),
        ]
        for copy in pair_of:
            copy.start()
        stores.append(pair_of)

    keep(0)
    load.wait()
    multiply(0, 0, tiles)
    pair.wait_recv()
    multiply(0, tiles, tiles)
    store(0)
    outs = []
    for number in range(2 * tiles):
        copy = pltpu.make_async_copy(
            w_buf.at[number],
            full_ref.at[:, pl.ds(number * tile, tile)],
            out_sem.at[number],
        )
        copy.start()
        outs.append(copy)
    for at in range(len(masks)):
        copies[at].wait_recv()
    for number, (mask, half, goal) in enumerate(hops):
        at = len(masks) + number
        copy = remote(
            piece(masks.index(mask) + 1, half), piece(3, half), b_send.at[at], b_recv.at[at],
            across(goal),
        )
        copy.start()
        copies.append(copy)
    for at in range(1, quads):
        if at == 1 + len(masks):
            for copy in copies[len(masks) :]:
                copy.wait_recv()
        keep(at)
        if at >= 2:
            for copy in stores[at - 2]:
                copy.wait()
        multiply(at, 0, 2 * tiles)
        store(at)
    for copy in copies + [pair]:
        copy.wait_send()
    for copy in keeps + outs + sum(stores[-2:], []):
        copy.wait()


def hidden_gather(rows_own, weight, bias):
    groups = lax.axis_size("dp")
    quads = groups // 2
    rows, width = rows_own.shape
    tiles, _, tile = weight.shape
    units = 2 * tiles * tile
    pieces = len(two_hops(quads)) + len(direct_masks(quads))
    dma = pltpu.SemaphoreType.DMA
    vmem = pl.BlockSpec(memory_space=pltpu.VMEM)
    hbm = pl.BlockSpec(memory_space=pltpu.HBM)
    return pl.pallas_call(
        functools.partial(hidden_gather_kernel, groups=groups),
        in_specs=[vmem, hbm, vmem],
        out_specs=[hbm, hbm, hbm, hbm],
        out_shape=[
            jax.ShapeDtypeStruct((quads * rows, width), jnp.bfloat16),
            jax.ShapeDtypeStruct((quads * rows, units), jnp.bfloat16),
            jax.ShapeDtypeStruct((quads * rows, units), jnp.float32),
            jax.ShapeDtypeStruct((width, units), jnp.bfloat16),
        ],
        scratch_shapes=[
            pltpu.VMEM((quads * rows, width), jnp.bfloat16),
            pltpu.VMEM((2 * tiles, width, tile), jnp.bfloat16),
            pltpu.VMEM((2, rows, units), jnp.bfloat16),
            pltpu.VMEM((2, rows, units), jnp.float32),
            dma((pieces,)),
            dma((pieces,)),
            dma((quads,)),
            dma((quads,)),
            dma((quads,)),
            dma,
            dma((2,)),
            dma((2 * tiles,)),
        ],
        compiler_params=pltpu.CompilerParams(
            collective_id=2, has_side_effects=True, vmem_limit_bytes=VMEM_BYTES
        ),
        cost_estimate=pl.CostEstimate(
            flops=2 * quads * rows * width * units,
            bytes_accessed=200 * 2**20,
            transcendentals=0,
        ),
        name="hidden_gather",
    )(rows_own, weight, bias)


def inward_kernel(
    grad_ref, outer_ref, wide_ref, values_ref, own_ref, outer_sum, wide_sum, all_ref,
    near, far, pair_send, pair_recv, pair_load, hop_buf, in_buf, send, receive,
    outer_near, outer_far, outer_pair_send, outer_pair_recv, outer_load,
    outer_hop, outer_in, outer_send, outer_recv,
    line_buf, line_send, line_recv, wide_send, wide_recv, wide_load, *sum_refs,
    groups, slices
):
    quads = groups // 2
    me = lax.axis_index("dp")
    place = lax.axis_index("tensor")
    share = near.shape[1]
    half_rows = share // 2
    piece = wide_ref.shape[0]

    def across(mask):
        return (flip(me, mask), place)

    anyone, greet = everyone(groups, slices)
    greet()
    sum_start, sum_middle, sum_end = spread_sum(
        values_ref, all_ref, *sum_refs, anyone, groups, slices
    )

    def block_of(other):
        return grad_ref.at[pl.ds(pl.multiple_of(other * share, share), share)]

    def parts(block, side):
        if side is None:
            return near.at[block]
        return near.at[block, pl.ds(side * half_rows, half_rows)]

    start, finish = pair_reduce(
        quads, me, across, block_of, near, far, pair_send, pair_recv, pair_load
    )
    early, middle, end = square_reduce(
        quads, share, across, send, receive, parts, parts, hop_buf, in_buf
    )

    out_cols = outer_sum.shape[1]
    long = outer_near.shape[1]
    half_long = long // 2

    def outer_block(other):
        return outer_ref.at[:, pl.ds(pl.multiple_of(other * out_cols, out_cols), out_cols)]

    def outer_parts(block, side):
        if side is None:
            return outer_near.at[block]
        return outer_near.at[block, pl.ds(side * half_long, half_long)]

    outer_start, outer_finish = pair_reduce(
        quads, me, across, outer_block, outer_near, outer_far,
        outer_pair_send, outer_pair_recv, outer_load,
    )
    outer_early, outer_middle, outer_end = square_reduce(
        quads, long, across, outer_send, outer_recv, outer_parts, outer_parts, outer_hop, outer_in
    )
    line_rows = outer_sum.shape[0]

    def line_block(owner):
        return outer_near.at[0, pl.ds(pl.multiple_of(owner * line_rows, line_rows), line_rows)]

    def line_to(step):
        owner = lax.rem(place + step, slices)
        return remote(
            line_block(owner), line_buf.at[step - 1], line_send.at[step], line_recv.at[step],
            (me, owner),
        )

    def columns_of(other):
        return wide_ref.at[:, pl.ds(pl.multiple_of(other * share, share), share)]

    def rows_of(other):
        return wide_sum.at[pl.ds(pl.multiple_of(other * piece, piece), piece)]

    def wide_to(step):
        other = lax.rem(me + step, groups)
        return remote(
            columns_of(other), rows_of(me), wide_send.at[step], wide_recv.at[step], (other, place)
        )

    def wide_from(step):
        other = lax.rem(me + groups - step, groups)
        return remote(
            columns_of(other), rows_of(other), wide_send.at[step], wide_recv.at[step],
            (other, place),
        )

    order = [quads - 1] + list(range(1, quads - 1))
    outer_start()
    start()
    sum_start()
    for m in order:
        outer_finish(m)
        outer_early(m)
    for m in order:
        finish(m)
        early(m)
    wide_own = pltpu.make_async_copy(columns_of(me), rows_of(me), wide_load)
    wide_own.start()
    outer_finish(0)
    outer_middle()
    for step in range(1, groups):
        wide_to(step).start()
    finish(0)
    sum_middle()
    middle()
    outer_end()
    outer = outer_near[0].astype(jnp.float32)
    for at in range(len(direct_masks(quads))):
        outer = outer + outer_in[at].astype(jnp.float32)
    outer_near[0] = outer.astype(outer_near.dtype)
    for step in range(1, slices):
        line_to(step).start()
    end()
    total = near[0].astype(jnp.float32)
    for at in range(len(direct_masks(quads))):
        total = total + in_buf[at].astype(jnp.float32)
    cols = own_ref.shape[2]
    for part in range(3):
        own_ref[part] = total[:, part * cols : (part + 1) * cols]
    final = line_block(place)[...].astype(jnp.float32)
    for step in range(1, slices):
        line_to(step).wait()
        final = final + line_buf[step - 1].astype(jnp.float32)
    outer_sum[...] = final
    wide_own.wait()
    for step in range(1, groups):
        wide_from(step).wait_recv()
        wide_to(step).wait_send()
    sum_end()


def inward_reduce(grad, outer, wide, values):
    groups = lax.axis_size("dp")
    slices = lax.axis_size("tensor")
    quads = groups // 2
    width = grad.shape[0]
    share = width // groups
    columns = grad.shape[1]
    piece = wide.shape[0]
    out_cols = outer.shape[1] // groups
    out_rows = outer.shape[0] // slices
    packed = sum_room(values)
    dma = pltpu.SemaphoreType.DMA
    vmem = pl.BlockSpec(memory_space=pltpu.VMEM)
    hbm = pl.BlockSpec(memory_space=pltpu.HBM)
    low = jnp.bfloat16

    def pair_scratch(rows, cols):
        return [
            pltpu.VMEM((quads, rows, cols), low),
            pltpu.VMEM((quads, rows, cols), low),
            dma((quads,)),
            dma((quads,)),
            dma((quads,)),
        ] + reduce_scratch(quads, rows, cols)

    return pl.pallas_call(
        functools.partial(inward_kernel, groups=groups, slices=slices),
        in_specs=[hbm, hbm, hbm, vmem],
        out_specs=[vmem, vmem, hbm, vmem],
        out_shape=[
            jax.ShapeDtypeStruct((3, share, columns // 3), jnp.float32),
            jax.ShapeDtypeStruct((out_rows, out_cols), jnp.float32),
            jax.ShapeDtypeStruct((groups * piece, share), low),
            jax.ShapeDtypeStruct(packed.shape, jnp.float32),
        ],
        scratch_shapes=pair_scratch(share, columns)
        + pair_scratch(width, out_cols)
        + [
            pltpu.VMEM((slices - 1, out_rows, out_cols), low),
            dma((slices,)),
            dma((slices,)),
            dma((groups,)),
            dma((groups,)),
            dma,
        ]
        + sum_scratch(groups * slices),
        compiler_params=pltpu.CompilerParams(
            collective_id=6, has_side_effects=True, vmem_limit_bytes=VMEM_BYTES
        ),
        cost_estimate=pl.CostEstimate(
            flops=8 * grad.size, bytes_accessed=250 * 2**20, transcendentals=0
        ),
        name="inward_reduce",
    )(grad, outer, wide, packed)


def swap(values, axis, mask):
    count = lax.axis_size(axis)
    return lax.ppermute(values, axis, [(i, i ^ mask) for i in range(count)])


def sum_room(values):
    count = lax.axis_size("dp") * lax.axis_size("tensor")
    room = count * 8 * 128
    packed = jnp.concatenate([values, jnp.zeros((room - values.shape[0],), jnp.float32)])
    return packed.reshape(count, 8, 128)


def last_kernel(
    values_ref, factor_ref, late_ref, vectors_ref, first_ref, second_ref, bias_ref, slope_ref,
    *refs, groups, slices
):
    masters, directions = refs[:4], refs[4:8]
    fresh, halves = refs[8:12], refs[12:16]
    column_out, vectors_out, mean_out, square_out, square_late, norms_out, all_ref = refs[16:23]
    held, send_one, recv_one, send_two, recv_two = refs[23:28]
    buffers, load_sem = refs[28:36], refs[36]
    loads = [
        pltpu.make_async_copy(source, target, load_sem.at[at])
        for at, (source, target) in enumerate(zip(masters + directions, buffers))
    ]
    for load in loads:
        load.start()
    anyone, greet = everyone(groups, slices)
    greet()
    start, middle, end = spread_sum(
        values_ref, all_ref, held, send_one, recv_one, send_two, recv_two, anyone, groups, slices
    )
    start()
    middle()
    end()

    cols = bias_ref.shape[1]
    step = cols // 128
    lanes = first_ref.shape[1] // 128
    need = -(-(14 * step + 2 * lanes) // 8)
    rows = all_ref[0:need].reshape(need * 8, 128)

    def total(at):
        return jnp.sqrt(jnp.sum(rows[at * step : (at + 1) * step], keepdims=True))

    weight_norms = [total(at) for at in range(7)]
    update_norms = [total(7 + at) for at in range(7)]

    def rate(weight_norm, update_norm):
        return learn_rate * weight_norm / (update_norm + trust_epsilon)

    for at in range(4):
        loads[at].wait()
        loads[4 + at].wait()
        factor = rate(weight_norms[at], update_norms[at])
        master, direction = buffers[at], buffers[4 + at]
        length = master.shape[0]
        chunk = min(length, 32) if len(master.shape) == 3 and length > 4 else length
        if len(master.shape) == 2:
            chunk = min(length, 128)
        scale = factor.reshape((1,) * len(master.shape))
        for begin in range(0, length, chunk):
            part = slice(begin, begin + chunk)
            updated = master[part] - scale * direction[part]
            fresh[at][part] = updated
            halves[at][part] = updated.astype(jnp.bfloat16)
    for at, (begin, stop) in enumerate(((0, 1), (1, 2), (2, 6))):
        column_out[begin:stop, :] = bias_ref[begin:stop, :] - (
            rate(weight_norms[4 + at], update_norms[4 + at]) * slope_ref[begin:stop, :]
        )
    early = [
        jnp.concatenate(
            [rows[14 * step + row * lanes + at][None, :] for at in range(lanes)], axis=1
        )
        for row in range(2)
    ]
    slopes = jnp.concatenate(early + [late_ref[...]], axis=0) * factor_ref[0:1, 0:1]
    weights = vectors_ref[...]
    mean_new, square_new, direction = adapt_step(
        weights, first_ref[...], second_ref[...], slopes, 0.0
    )
    mean_out[...] = mean_new
    square_out[...] = square_new[0:2]
    square_late[...] = square_new[2:6]
    own = jnp.sqrt(jnp.sum(weights * weights, axis=1, keepdims=True))
    step_norms = jnp.sqrt(jnp.sum(direction * direction, axis=1, keepdims=True))
    vectors_out[...] = weights - rate(own, step_norms) * direction
    for row in range(6):
        weight_norms.append(own[row : row + 1])
        update_norms.append(step_norms[row : row + 1])
    lane = lax.broadcasted_iota(jnp.int32, (8, 128), 1)
    line = lax.broadcasted_iota(jnp.int32, (8, 128), 0)
    norms = jnp.zeros((8, 128), jnp.float32)
    for at in range(13):
        norms = jnp.where((lane == at) & (line == 0), weight_norms[at], norms)
        norms = jnp.where((lane == at) & (line == 1), update_norms[at], norms)
    norms_out[...] = norms[0:2, 0:13]


def last_step(values, factor, late, vectors, first, second, bias, slope, masters, directions):
    groups = lax.axis_size("dp")
    slices = lax.axis_size("tensor")
    packed = sum_room(values)
    width = vectors.shape[1]
    wide = jnp.float32
    vmem = pl.BlockSpec(memory_space=pltpu.VMEM)
    hbm = pl.BlockSpec(memory_space=pltpu.HBM)

    masters = list(masters)
    directions = list(directions)
    masters[0] = masters[0].transpose(1, 0, 2)
    directions[0] = directions[0].transpose(1, 0, 2)
    shapes = [master.shape for master in masters]
    like = jax.ShapeDtypeStruct
    results = pl.pallas_call(
        functools.partial(last_kernel, groups=groups, slices=slices),
        in_specs=[vmem] * 8 + [hbm] * 8,
        out_specs=[vmem] * 15,
        out_shape=[like(shape, wide) for shape in shapes]
        + [like(shape, jnp.bfloat16) for shape in shapes]
        + [like(bias.shape, wide)]
        + [like((rows, width), wide) for rows in (6, 6, 2, 4)]
        + [like((2, 13), wide), like(packed.shape, wide)],
        scratch_shapes=sum_scratch(groups * slices)
        + [pltpu.VMEM(shape, wide) for shape in shapes]
        + [pltpu.VMEM(shape, wide) for shape in shapes]
        + [pltpu.SemaphoreType.DMA((8,))],
        compiler_params=pltpu.CompilerParams(
            collective_id=0, has_side_effects=True, vmem_limit_bytes=VMEM_BYTES
        ),
        cost_estimate=pl.CostEstimate(
            flops=packed.size, bytes_accessed=80 * 2**20, transcendentals=0
        ),
        name="last_step",
    )(
        packed,
        jnp.full((8, 128), factor),
        late,
        vectors,
        first,
        second,
        bias,
        slope,
        *masters,
        *directions,
    )
    fresh = list(results[:4])
    halves = list(results[4:8])
    fresh[0] = fresh[0].transpose(1, 0, 2)
    halves[0] = halves[0].transpose(1, 0, 2)
    return (fresh, halves) + tuple(results[8:14])


def after(values, gate):
    return lax.optimization_barrier((values, gate))[0]


def adapt_step(weight, moment_one, moment_two, slope, decay):
    mean_new = beta_one * moment_one + (1.0 - beta_one) * slope
    square_new = beta_two * moment_two + (1.0 - beta_two) * slope * slope
    direction = (
        mean_new
        / (1.0 - beta_one**STEP_COUNT)
        / (jnp.sqrt(square_new / (1.0 - beta_two**STEP_COUNT)) + adam_epsilon)
        + decay * weight
    )
    return (mean_new, square_new, direction)


def on_device(
    tokens,
    cotangent,
    live_mask,
    inward,
    inward_first,
    inward_second,
    outward,
    outward_first,
    outward_second,
    widening,
    widening_first,
    widening_second,
    narrowing,
    narrowing_first,
    narrowing_second,
    column_bias,
    column_first,
    column_second,
    vectors,
    vectors_first,
    vectors_second,
):
    low = jnp.bfloat16
    wide = jnp.float32
    amount, width = tokens.shape
    cols = column_bias.shape[1]
    groups = lax.axis_size("dp")
    slices = lax.axis_size("tensor")
    me = lax.axis_index("dp")
    place = lax.axis_index("tensor")
    share = inward.shape[0]
    piece = 4 * cols // groups

    inputs = tokens.astype(wide)
    living_here = live_mask.astype(wide)
    normed = layer_norm(inputs, vectors[0], vectors[1]).astype(low)
    back_out = (cotangent.astype(wide) * living_here[:, None]).astype(low)
    mixed_bias = jnp.concatenate(
        [column_bias[0], jnp.zeros((cols,), wide), column_bias[1]]
    ).reshape(1, 3 * cols)
    small_length = amount + 4 * cols
    small_rows = -(-small_length // 1024) * 8
    small = jnp.concatenate(
        [
            living_here,
            column_bias[2:].reshape(4 * cols),
            jnp.zeros((small_rows * 128 - small_length,), wide),
        ]
    ).reshape(small_rows, 128)
    (
        normed_full,
        inward_full,
        mixed,
        back_all,
        small_all,
        counts,
        wide_own,
        thin_own,
        outward_full,
    ) = open_step(
        normed,
        inward,
        back_out,
        mixed_bias,
        small,
        jnp.full((8, 128), jnp.sum(living_here)),
        widening,
        narrowing,
        outward,
    )
    factor = 1.0 / jnp.sum(counts[:, 0, 0])
    small_all = small_all.reshape(slices, small_rows * 128)
    length = normed_full.shape[0]
    bias_keys = jnp.where(small_all[:, :amount].reshape(length) > 0.5, 0.0, MASKED)
    bias_all = small_all[:, amount:small_length]

    if piece % 128:
        wide_own = wide_own.transpose(1, 0, 2).reshape(1, width, slices * piece)

    hidden_bias = jnp.concatenate(
        [
            lax.dynamic_slice_in_dim(bias_all, (me ^ side) * piece, piece, 1).reshape(1, -1)
            for side in range(2)
        ],
        axis=1,
    )

    context_wide, totals, context_own, back_all = attend_forward(
        mixed, bias_keys[None, :], back_all, amount
    )
    thin_own = lax.all_gather(
        after(thin_own, context_own), "tensor", axis=0, tiled=True
    )
    middle = inputs + dot_as(context_own, outward_full, PLAIN) + vectors[2]
    normed_two = layer_norm(middle, vectors[3], vectors[4]).astype(low)

    rows_two_all, active_all, slope, widening_full = hidden_gather(
        normed_two, wide_own, hidden_bias
    )
    half_units = slices * piece

    def pair_sum(left, right):
        other = left(slice(half_units, None), right, low)
        own = left(slice(0, half_units), after(right, other), wide)
        return (own + swap(other, "dp", 1).astype(wide)).astype(low)

    slope_narrowing = pair_sum(
        lambda part, right, kind: dot_as(active_all[:, part], right, TOKENS, kind),
        after(back_all, thin_own),
    )
    back_normed_two, back_hidden_all, hidden_sums, widened_all, thin_parts = back_step(
        back_all, slope, thin_own, widening_full, slope_narrowing, active_all
    )
    thin_slope = jnp.sum(thin_parts.astype(wide), axis=0).astype(low)
    slope_widening = pair_sum(
        lambda part, right, kind: dot_as(back_hidden_all[:, part], right, TOKENS, kind),
        rows_two_all,
    )
    wide_slope = lax.psum_scatter(slope_widening, "tensor", scatter_dimension=0, tiled=True)

    _, norm_two_pull = jax.vjp(layer_norm, middle, vectors[3], vectors[4])
    back_middle_norm, slope_gain_two, slope_shift_two = norm_two_pull(back_normed_two)
    back_middle = back_out.astype(wide) + back_middle_norm
    back_low = back_middle.astype(low)

    back_mixed, widened, sum_narrowing = attend_backward(
        after(back_low, slope_widening),
        outward_full,
        mixed,
        context_wide,
        totals,
        bias_keys[:, None],
        widened_all,
        thin_slope,
    )
    layer_output = (middle + widened + vectors[5]).astype(low)

    back_normed_part = dot_as(back_mixed, inward_full, ROWS, low)
    back_normed = lax.psum_scatter(
        after(back_normed_part, wide_slope), "tensor", scatter_dimension=0, tiled=True
    )
    back_mixed = after(back_mixed, back_normed_part)
    slope_inward = dot_as(normed_full, back_mixed, TOKENS, low)
    slope_outward = dot_as(after(context_own, slope_inward), back_low, TOKENS, low)
    hidden_total = hidden_sums.reshape(2, 1, slices, piece)
    hidden_slots = jnp.zeros((groups, slices, piece), wide)
    hidden_slots = lax.dynamic_update_slice(hidden_slots, hidden_total[0], (me, 0, 0))
    hidden_slots = lax.dynamic_update_slice(hidden_slots, hidden_total[1], (me ^ 1, 0, 0))
    mixed_sums = jnp.stack(
        [
            jnp.sum(back_mixed[:, :cols], axis=0, dtype=wide),
            jnp.sum(back_mixed[:, 2 * cols :], axis=0, dtype=wide),
        ]
    )
    mixed_slots = lax.dynamic_update_slice(
        jnp.zeros((slices, 2, cols), wide), mixed_sums[None], (place, 0, 0)
    )
    late_rows = jnp.stack(
        [
            jnp.sum(back_middle, axis=0),
            slope_gain_two,
            slope_shift_two,
            jnp.sum(back_out, axis=0, dtype=wide),
        ]
    )
    packed = jnp.concatenate(
        [hidden_slots.reshape(-1), mixed_slots.reshape(-1), late_rows.reshape(-1)]
    )
    amount_packed = packed.shape[0]
    sum_inward, sum_outward, sum_widening, packed = inward_reduce(
        slope_inward, slope_outward, wide_slope, packed
    )
    packed = packed.reshape(-1)[:amount_packed]
    sum_inward = sum_inward.transpose(1, 0, 2)
    sum_widening = sum_widening.T.reshape(widening.shape)
    sum_narrowing = sum_narrowing.reshape(narrowing.shape)

    first_cut = groups * slices * piece
    second_cut = first_cut + slices * 2 * cols
    hidden_slots = packed[:first_cut].reshape(groups, slices, piece)
    hidden_rows = lax.dynamic_slice_in_dim(hidden_slots, place, 1, 1).reshape(4, cols)
    mixed_rows = lax.dynamic_index_in_dim(
        packed[first_cut:second_cut].reshape(slices, 2, cols), place, 0, keepdims=False
    )
    late_rows = packed[second_cut:].reshape(4, width)
    column_total = jnp.concatenate([mixed_rows, hidden_rows], axis=0)

    masters = (inward, outward, widening, narrowing)
    firsts = (inward_first, outward_first, widening_first, narrowing_first)
    seconds = (inward_second, outward_second, widening_second, narrowing_second)
    orders = ((1, 0, 2), (0, 1), (0, 1, 2), (0, 1, 2))
    summed_all = [
        with_layout_constraint(summed.astype(wide), Layout(order))
        for summed, order in zip(
            (sum_inward, sum_outward, sum_widening, sum_narrowing), orders
        )
    ]
    matrix_steps = [
        adapt_step(
            masters[ordinal],
            firsts[ordinal],
            seconds[ordinal],
            summed_all[ordinal] * factor,
            decay_rate,
        )
        for ordinal in range(4)
    ]
    column_mean, column_square, column_direction = adapt_step(
        column_bias, column_first, column_second, column_total * factor, 0.0
    )
    column_groups = ((0, 1), (1, 2), (2, 6))

    def square_sum(array):
        lanes = jnp.sum(array * array, axis=tuple(range(array.ndim - 1)))
        return jnp.concatenate([lanes, jnp.zeros((cols - lanes.shape[0],), wide)])

    squares = [square_sum(master) for master in masters]
    squares += [square_sum(column_bias[start:stop]) / groups for start, stop in column_groups]
    squares += [square_sum(step[2]) for step in matrix_steps]
    squares += [square_sum(column_direction[start:stop]) / groups for start, stop in column_groups]
    squares = jnp.concatenate(squares)

    _, norm_one_pull = jax.vjp(layer_norm, inputs, vectors[0], vectors[1])
    back_inputs_norm, slope_gain_one, slope_shift_one = norm_one_pull(
        after(back_normed, squares).astype(wide)
    )
    back_inputs = back_middle + back_inputs_norm
    (
        fresh,
        halves,
        new_column,
        new_vectors,
        vectors_mean,
        first_square,
        vectors_square,
        trust_norms,
    ) = last_step(
        jnp.concatenate([squares, slope_gain_one, slope_shift_one]),
        factor,
        late_rows,
        vectors,
        vectors_first,
        vectors_second,
        column_bias,
        column_direction,
        masters,
        [step[2] for step in matrix_steps],
    )
    results = []
    for ordinal in range(4):
        results += [
            fresh[ordinal],
            matrix_steps[ordinal][0],
            matrix_steps[ordinal][1],
            halves[ordinal],
        ]
    return (
        layer_output,
        back_inputs * factor,
        *results,
        new_column,
        column_mean,
        column_square[0],
        column_square[1],
        column_square[2:],
        new_vectors,
        vectors_mean,
        first_square,
        vectors_square,
        trust_norms,
    )


def solution(mesh):
    in_specs = (
        P(("dp", "tensor"), None),
        P(("dp", "tensor"), None),
        P(("dp", "tensor")),
        P("dp", None, "tensor"),
        P("dp", None, "tensor"),
        P("dp", None, "tensor"),
        P("tensor", "dp"),
        P("tensor", "dp"),
        P("tensor", "dp"),
        P("dp", None, "tensor"),
        P("dp", None, "tensor"),
        P("dp", None, "tensor"),
        P(None, "tensor", "dp"),
        P(None, "tensor", "dp"),
        P(None, "tensor", "dp"),
        P(None, "tensor"),
        P(None, "tensor"),
        P(None, "tensor"),
        P(),
        P(),
        P(),
    )
    out_specs = (
        P(("dp", "tensor"), None),
        P(("dp", "tensor"), None),
        P("dp", None, "tensor"),
        P("dp", None, "tensor"),
        P("dp", None, "tensor"),
        P("dp", None, "tensor"),
        P("tensor", "dp"),
        P("tensor", "dp"),
        P("tensor", "dp"),
        P("tensor", "dp"),
        P("dp", None, "tensor"),
        P("dp", None, "tensor"),
        P("dp", None, "tensor"),
        P("dp", None, "tensor"),
        P(None, "tensor", "dp"),
        P(None, "tensor", "dp"),
        P(None, "tensor", "dp"),
        P(None, "tensor", "dp"),
        P(None, "tensor"),
        P(None, "tensor"),
        P("tensor"),
        P("tensor"),
        P(None, "tensor"),
        P(),
        P(),
        P(),
        P(),
        P(),
    )
    return jax.shard_map(
        on_device, mesh=mesh, in_specs=in_specs, out_specs=out_specs, check_vma=False
    )
```

```python
import functools

import jax
import jax.numpy as jnp
from jax import lax
from jax.experimental import pallas as pl
from jax.experimental.layout import Layout, with_layout_constraint
from jax.experimental.pallas import tpu as pltpu
from jax.sharding import PartitionSpec as P

HEAD_DIM = 128
QUERY_BLOCK = 512
STEP_COUNT = 10
LOG2E = 1.4426950408889634
MASKED = -1e30
VMEM_BYTES = 56 * 2**20
ROWS = (((1,), (1,)), ((), ()))
TOKENS = (((0,), (0,)), ((), ()))

norm_epsilon = 1e-05
beta_one = 0.9
beta_two = 0.999
adam_epsilon = 1e-06
decay_rate = 0.01
learn_rate = 0.5
trust_epsilon = 1e-06


def layer_norm(values, gain_row, shift_row):
    centre = values - jnp.mean(values, axis=-1, keepdims=True)
    spread = jnp.mean(centre * centre, axis=-1, keepdims=True)
    return centre * lax.rsqrt(spread + norm_epsilon) * gain_row + shift_row


def dot_as(left, right, dims, kind=jnp.float32):
    return lax.dot_general(left, right, dims, preferred_element_type=jnp.float32).astype(kind)


PLAIN = (((1,), (0,)), ((), ()))


def flip(index, mask):
    result = index
    bit = 1
    while bit <= mask:
        if mask & bit:
            result = result + bit - 2 * bit * lax.rem(lax.div(index, bit), 2)
        bit *= 2
    return result


def greet_all(peers):
    barrier = pltpu.get_barrier_semaphore()
    for peer in peers:
        pl.semaphore_signal(barrier, inc=1, device_id=peer, device_id_type=pl.DeviceIdType.MESH)
    pl.semaphore_wait(barrier, len(peers))


def remote(source, target, send, receive, device):
    return pltpu.make_async_remote_copy(
        src_ref=source,
        dst_ref=target,
        send_sem=send,
        recv_sem=receive,
        device_id=device,
        device_id_type=pl.DeviceIdType.MESH,
    )


def everyone(groups, slices):
    count = groups * slices
    me = lax.axis_index("dp") * slices + lax.axis_index("tensor")

    def anyone(step):
        other = lax.rem(me + step, count)
        return (lax.div(other, slices), lax.rem(other, slices))

    def greet():
        barrier = pltpu.get_barrier_semaphore()

        def signal(step, carry):
            pl.semaphore_signal(
                barrier, inc=1, device_id=anyone(step), device_id_type=pl.DeviceIdType.MESH
            )
            return carry

        lax.fori_loop(1, count, signal, 0)
        pl.semaphore_wait(barrier, count - 1)

    return anyone, greet


def spread_sum(
    values_ref, out_ref, held, send_one, recv_one, send_two, recv_two, anyone, groups, slices
):
    count = groups * slices
    me = lax.axis_index("dp") * slices + lax.axis_index("tensor")

    def first(step):
        source = values_ref.at[lax.rem(me + step, count)]
        return remote(
            source, held.at[step], send_one.at[step], recv_one.at[step], anyone(step)
        )

    def second(step):
        return remote(
            held.at[0], out_ref.at[me], send_two.at[step], recv_two.at[step], anyone(step)
        )

    def each(action):
        lax.fori_loop(1, count, lambda step, carry: (action(step), carry)[1], 0)

    def wait_first(step, total):
        first(step).wait()
        return total + held[step]

    def start():
        each(lambda step: first(step).start())

    def middle():
        total = lax.fori_loop(1, count, wait_first, values_ref[me])
        held[0] = total
        out_ref[me] = total
        each(lambda step: second(step).start())

    def end():
        each(lambda step: second(step).wait())

    return start, middle, end


def sum_scratch(count):
    dma = pltpu.SemaphoreType.DMA
    return [pltpu.VMEM((count, 8, 128), jnp.float32)] + [dma((count,))] * 4


def direct_masks(quads):
    return [2, 4] if quads == 4 else [2 * m for m in range(1, quads)]


def two_hops(quads):
    return [(2, 0, 4), (4, 1, 2)] if quads == 4 else []


def square_reduce(quads, rows, across, send, receive, parts, sums, hop_buf, in_buf):
    masks = direct_masks(quads)
    half_rows = rows // 2

    def landing(at, half):
        return in_buf.at[at, pl.ds(half * half_rows, half_rows)]

    def hop(half):
        goal = 4 if half == 0 else 2
        return remote(
            parts(3, half), hop_buf.at[half], send.at[half], receive.at[half], across(goal)
        )

    def plain(at, half, source):
        number = 2 + 2 * at + half
        return remote(
            source, landing(at, half), send.at[number], receive.at[number], across(masks[at])
        )

    def whole(at):
        return remote(
            parts(at + 1, None), in_buf.at[at], send.at[at], receive.at[at], across(masks[at])
        )

    def early(block):
        if quads != 4:
            whole(block - 1).start()
        elif block == 3:
            hop(0).start()
            hop(1).start()
        else:
            half = 1 if block == 1 else 0
            plain(block - 1, half, parts(block, half)).start()

    def middle():
        if quads != 4:
            return
        for block, half in ((1, 0), (2, 1)):
            hop(half).wait_recv()
            target = sums(block, half)
            target[...] = (
                target[...].astype(jnp.float32) + hop_buf[half].astype(jnp.float32)
            ).astype(jnp.bfloat16)
            plain(block - 1, half, target).start()

    def end():
        if quads != 4:
            for at in range(quads - 1):
                whole(at).wait()
            return
        for half in range(2):
            hop(half).wait_send()
            for block in (1, 2):
                plain(block - 1, half, parts(block, half)).wait()

    return early, middle, end


def pair_reduce(quads, me, across, block_of, near, far, send, receive, load_sem):
    copies = []
    for m in range(quads):
        copies.append(
            remote(
                block_of(flip(me, 2 * m + 1)), far.at[m], send.at[m], receive.at[m], across(1)
            )
        )
    loads = [
        pltpu.make_async_copy(block_of(flip(me, 2 * m)), near.at[m], load_sem.at[m])
        for m in range(quads)
    ]

    def start():
        for copy in copies + loads:
            copy.start()

    def finish(m):
        loads[m].wait()
        copies[m].wait()
        near[m] = (near[m].astype(jnp.float32) + far[m].astype(jnp.float32)).astype(near.dtype)

    return start, finish


def reduce_scratch(quads, rows, width):
    dma = pltpu.SemaphoreType.DMA
    return [
        pltpu.VMEM((2, rows // 2, width), jnp.bfloat16),
        pltpu.VMEM((len(direct_masks(quads)), rows, width), jnp.bfloat16),
        dma((max(6, quads - 1),)),
        dma((max(6, quads - 1),)),
    ]


def forward_kernel(
    q_ref, k_ref, v_ref, bias_ref, back_ref, wide_ref, total_ref, own_ref, back_out,
    held, send_sem, recv_sem, keep_sem, e_send, e_recv,
    *, heads, blocks, size, slices, groups
):
    factor = HEAD_DIM**-0.5 * LOG2E
    head = pl.program_id(0)
    which = pl.program_id(1)
    me = lax.axis_index("dp")
    place = lax.axis_index("tensor")
    rows = own_ref.shape[0]
    queries = q_ref[...]
    masks = direct_masks(groups // 2)
    hops = two_hops(groups // 2)

    def across(mask):
        return (flip(me, mask), place)

    def e_hops():
        result = []
        half_rows = rows // 2
        for number, (mask, half, goal) in enumerate(hops):
            start = (masks.index(mask) + 1) * rows + half * half_rows
            source = back_ref.at[pl.ds(start, half_rows)]
            target = back_out.at[pl.ds(3 * rows + half * half_rows, half_rows)]
            result.append(
                remote(source, target, e_send.at[number], e_recv.at[number], across(goal))
            )
        return result

    @pl.when(jnp.logical_and(head == 0, which == 0))
    def _():
        greet_all(
            [(me, lax.rem(place + step, slices)) for step in range(1, slices)]
            + [across(goal) for _, _, goal in hops]
        )
        for copy in e_hops():
            copy.start()

    for last in range(blocks):

        @pl.when(which == last)
        def _():
            parts = []
            peak = None
            for at in range(last + 1):
                keys = slice(at * size, (at + 1) * size)
                scores = dot_as(queries, k_ref[keys, :], ROWS) + bias_ref[0:1, keys]
                if at == last:
                    row = lax.broadcasted_iota(jnp.int32, (size, size), 0)
                    col = lax.broadcasted_iota(jnp.int32, (size, size), 1)
                    scores = jnp.where(col <= row, scores, MASKED)
                top = jnp.max(scores, axis=1, keepdims=True)
                peak = top if peak is None else jnp.maximum(peak, top)
                parts.append(scores)
            low = peak * factor
            total = None
            context = None
            for at in range(last + 1):
                keys = slice(at * size, (at + 1) * size)
                weights = jnp.exp2(parts[at] * factor - low)
                more = jnp.sum(weights, axis=1, keepdims=True)
                total = more if total is None else total + more
                term = dot_as(weights.astype(jnp.bfloat16), v_ref[keys, :], PLAIN)
                context = term if context is None else context + term
            context = context * (1.0 / total)
            held[head, last * size : (last + 1) * size, :] = context.astype(jnp.bfloat16)
            wide_ref[...] = context
            logs = jnp.broadcast_to(low + jnp.log2(total), (size, 128))
            total_ref[...] = jnp.transpose(logs)[0:1, :].reshape(1, 1, size)

    def to_owner(owner, number):
        step = lax.rem(owner - place + slices, slices)
        return remote(
            held.at[number, pl.ds(pl.multiple_of(owner * rows, rows), rows)],
            own_ref.at[:, columns(place, number)],
            send_sem.at[step, number],
            recv_sem.at[step, number],
            (me, owner),
        )

    def columns(other, number):
        start = (other * heads + number) * HEAD_DIM
        return pl.ds(pl.multiple_of(start, HEAD_DIM), HEAD_DIM)

    def stay(number):
        return pltpu.make_async_copy(
            held.at[number, pl.ds(pl.multiple_of(place * rows, rows), rows)],
            own_ref.at[:, columns(place, number)],
            keep_sem.at[number],
        )

    for part in range(size // rows):
        owner = which * (size // rows) + part
        pl.when(owner == place)(lambda: stay(head).start())
        pl.when(owner != place)(lambda: to_owner(owner, head).start())

    @pl.when(jnp.logical_and(head == heads - 1, which == blocks - 1))
    def _():
        for copy in e_hops():
            copy.wait()
        for number in range(heads):
            stay(number).wait()
            for step in range(1, slices):
                to_owner(lax.rem(place + step, slices), number).wait_send()
                source = lax.rem(place + slices - step, slices)
                remote(
                    held.at[number, pl.ds(0, rows)],
                    own_ref.at[:, columns(source, number)],
                    send_sem.at[step, number],
                    recv_sem.at[step, number],
                    (me, source),
                ).wait_recv()


def attend_forward(mixed, bias_row, back, rows):
    slices = lax.axis_size("tensor")
    groups = lax.axis_size("dp")
    hops = max(1, len(two_hops(groups // 2)))
    length = mixed.shape[0]
    cols = mixed.shape[1] // 3
    heads = cols // HEAD_DIM
    size = QUERY_BLOCK
    blocks = length // size
    part = pl.BlockSpec((size, HEAD_DIM), lambda h, i: (i, h))
    keys = pl.BlockSpec((length, HEAD_DIM), lambda h, i: (0, heads + h))
    values = pl.BlockSpec((length, HEAD_DIM), lambda h, i: (0, 2 * heads + h))
    dma = pltpu.SemaphoreType.DMA
    return pl.pallas_call(
        functools.partial(
            forward_kernel, heads=heads, blocks=blocks, size=size, slices=slices, groups=groups
        ),
        grid=(heads, blocks),
        in_specs=[
            part,
            keys,
            values,
            pl.BlockSpec((1, length), lambda h, i: (0, 0)),
            pl.BlockSpec(memory_space=pltpu.HBM),
        ],
        out_specs=[
            part,
            pl.BlockSpec((1, 1, size), lambda h, i: (h, 0, i)),
            pl.BlockSpec(memory_space=pltpu.HBM),
            pl.BlockSpec(memory_space=pltpu.HBM),
        ],
        input_output_aliases={4: 3},
        out_shape=[
            jax.ShapeDtypeStruct((length, cols), jnp.float32),
            jax.ShapeDtypeStruct((heads, 1, length), jnp.float32),
            jax.ShapeDtypeStruct((rows, slices * cols), jnp.bfloat16),
            jax.ShapeDtypeStruct(back.shape, back.dtype),
        ],
        scratch_shapes=[
            pltpu.VMEM((heads, length, HEAD_DIM), jnp.bfloat16),
            dma((slices, heads)),
            dma((slices, heads)),
            dma((heads,)),
            dma((hops,)),
            dma((hops,)),
        ],
        compiler_params=pltpu.CompilerParams(
            collective_id=3, has_side_effects=True, vmem_limit_bytes=VMEM_BYTES
        ),
        cost_estimate=pl.CostEstimate(
            flops=4 * length * length * cols,
            bytes_accessed=100 * 2**20,
            transcendentals=heads * length * length // 2,
        ),
        name="attend_forward",
    )(mixed, mixed, mixed, bias_row, back)


def backward_kernel(
    low_ref, out_ref, mixed_ref, wide_ref, total_ref, bias_ref, part_ref, thin_ref,
    grad_ref, layer_ref, thin_sum,
    sent, back_buf, sum_ref, half_buf, own_buf, hop_buf, in_buf, send, receive,
    send_sem, recv_sem, load_sem, thin_send, thin_recv, thin_load,
    *, blocks, size, slices, groups
):
    scale = HEAD_DIM**-0.5
    factor = scale * LOG2E
    me = lax.axis_index("dp")
    place = lax.axis_index("tensor")
    rows = low_ref.shape[0]
    cols = back_buf.shape[1]
    heads = cols // HEAD_DIM
    quads = groups // 2
    half_rows = rows // 2

    def across(mask):
        return (flip(me, mask), place)

    def parts(block, side):
        if side is None:
            return part_ref.at[pl.ds(block * rows, rows)]
        return part_ref.at[pl.ds(block * rows + side * half_rows, half_rows)]

    def sums(block, side):
        return half_buf.at[side]

    loads = [pltpu.make_async_copy(parts(0, None), own_buf, load_sem.at[0])]
    if quads == 4:
        for block, side in ((1, 0), (2, 1)):
            loads.append(
                pltpu.make_async_copy(parts(block, side), half_buf.at[side], load_sem.at[1 + side])
            )
    for copy in loads:
        copy.start()
    greet_all(
        [(me, lax.rem(place + step, slices)) for step in range(1, slices)]
        + [(lax.rem(me + step, groups), place) for step in range(1, groups)]
    )
    early, middle, end = square_reduce(
        quads, rows, across, send, receive, parts, sums, hop_buf, in_buf
    )

    thin_rows, thin_cols = thin_ref.shape[0], thin_sum.shape[1]

    def thin_columns(other):
        return thin_ref.at[:, pl.ds(pl.multiple_of(other * thin_cols, thin_cols), thin_cols)]

    def thin_place(other):
        return thin_sum.at[pl.ds(pl.multiple_of(other * thin_rows, thin_rows), thin_rows)]

    def thin_to(step):
        other = lax.rem(me + step, groups)
        return remote(
            thin_columns(other), thin_place(me), thin_send.at[step], thin_recv.at[step],
            (other, place),
        )

    def thin_from(step):
        other = lax.rem(me + groups - step, groups)
        return remote(
            thin_columns(other), thin_place(other), thin_send.at[step], thin_recv.at[step],
            (other, place),
        )

    thin_own = pltpu.make_async_copy(thin_columns(me), thin_place(me), thin_load)
    early(quads - 1)

    def span(start, size):
        return pl.ds(pl.multiple_of(start, size), size)

    def product(owner):
        return dot_as(low_ref[...], out_ref[span(owner * cols, cols), :], ROWS, jnp.bfloat16)

    def to_owner(step, head):
        return remote(
            sent.at[step - 1, :, span(head * HEAD_DIM, HEAD_DIM)],
            back_buf.at[span(place * rows, rows), span(head * HEAD_DIM, HEAD_DIM)],
            send_sem.at[step, head],
            recv_sem.at[step, head],
            (me, lax.rem(place + step, slices)),
        )

    for step in range(1, slices):
        sent[step - 1] = product(lax.rem(place + step, slices))
    for head in range(heads):
        for step in range(1, slices):
            to_owner(step, head).start()
    back_buf[span(place * rows, rows), :] = product(place)

    def one_head(head, carry):
        for step in range(1, slices):
            source = lax.rem(place + slices - step, slices)
            remote(
                sent.at[step - 1, :, span(head * HEAD_DIM, HEAD_DIM)],
                back_buf.at[span(source * rows, rows), span(head * HEAD_DIM, HEAD_DIM)],
                send_sem.at[step, head],
                recv_sem.at[step, head],
                (me, source),
            ).wait_recv()
        here = span(head * HEAD_DIM, HEAD_DIM)
        key_here = span(cols + head * HEAD_DIM, HEAD_DIM)
        value_here = span(2 * cols + head * HEAD_DIM, HEAD_DIM)
        inner = []
        for at in range(blocks):
            part = slice(at * size, (at + 1) * size)
            pairs = back_buf[part, here].astype(jnp.float32) * wide_ref[part, here]
            inner.append(jnp.sum(jnp.transpose(pairs), axis=0, keepdims=True))
        for key_at in range(blocks):
            keys = slice(key_at * size, (key_at + 1) * size)
            key_rows = mixed_ref[keys, key_here]
            values = mixed_ref[keys, value_here]
            bias = bias_ref[keys, 0:1]
            back_keys = None
            back_values = None
            for query_at in range(key_at, blocks):
                part = slice(query_at * size, (query_at + 1) * size)
                queries = mixed_ref[part, here]
                back = back_buf[part, here]
                level = dot_as(key_rows, queries, ROWS) * factor - total_ref[head, 0:1, part] + bias
                if query_at == key_at:
                    row = lax.broadcasted_iota(jnp.int32, (size, size), 0)
                    col = lax.broadcasted_iota(jnp.int32, (size, size), 1)
                    level = jnp.where(row <= col, level, MASKED)
                chances = jnp.exp2(level)
                back_chances = dot_as(values, back, ROWS)
                back_scores = (chances * (back_chances - inner[query_at])).astype(jnp.bfloat16)
                more_values = dot_as(chances.astype(jnp.bfloat16), back, PLAIN)
                more_keys = dot_as(back_scores, queries, PLAIN)
                more_queries = dot_as(back_scores, key_rows, TOKENS)
                if key_at == 0:
                    sum_ref[part, :] = more_queries
                else:
                    sum_ref[part, :] += more_queries
                back_keys = more_keys if back_keys is None else back_keys + more_keys
                back_values = more_values if back_values is None else back_values + more_values
            grad_ref[keys, key_here] = (back_keys * scale).astype(jnp.bfloat16)
            grad_ref[keys, value_here] = back_values.astype(jnp.bfloat16)
        grad_ref[:, here] = (sum_ref[...] * scale).astype(jnp.bfloat16)

        @pl.when(head == 0)
        def _():
            for block in range(1, quads - 1):
                early(block)

        @pl.when(head == heads // 2 - 1)
        def _():
            for copy in loads:
                copy.wait()
            middle()

        @pl.when(head == min(2, heads - 1))
        def _():
            thin_own.start()
            for step in range(1, groups):
                thin_to(step).start()

        return carry

    lax.fori_loop(0, heads, one_head, 0)
    end()
    total = own_buf[...].astype(jnp.float32)
    for at in range(len(direct_masks(quads))):
        total = total + in_buf[at].astype(jnp.float32)
    layer_ref[...] = total
    thin_own.wait()
    for step in range(1, groups):
        thin_from(step).wait_recv()
        thin_to(step).wait_send()
    for head in range(heads):
        for step in range(1, slices):
            to_owner(step, head).wait_send()


def attend_backward(back_low, outward, mixed, wide, totals, bias_column, widened, thin):
    slices = lax.axis_size("tensor")
    groups = lax.axis_size("dp")
    quads = groups // 2
    rows, width = back_low.shape
    length, cols = wide.shape
    heads = cols // HEAD_DIM
    size = QUERY_BLOCK
    vmem = pl.BlockSpec(memory_space=pltpu.VMEM)
    hbm = pl.BlockSpec(memory_space=pltpu.HBM)
    dma = pltpu.SemaphoreType.DMA
    low = jnp.bfloat16
    return pl.pallas_call(
        functools.partial(
            backward_kernel, blocks=length // size, size=size, slices=slices, groups=groups
        ),
        in_specs=[vmem] * 6 + [hbm] * 2,
        out_specs=[vmem, vmem, hbm],
        out_shape=[
            jax.ShapeDtypeStruct((length, 3 * cols), low),
            jax.ShapeDtypeStruct((rows, width), jnp.float32),
            jax.ShapeDtypeStruct((groups * thin.shape[0], width // groups), low),
        ],
        scratch_shapes=[
            pltpu.VMEM((slices - 1, rows, cols), low),
            pltpu.VMEM((length, cols), low),
            pltpu.VMEM((length, HEAD_DIM), jnp.float32),
            pltpu.VMEM((2, rows // 2, width), low),
            pltpu.VMEM((rows, width), low),
        ]
        + reduce_scratch(quads, rows, width)
        + [dma((slices, heads)), dma((slices, heads)), dma((3,))]
        + [dma((groups,)), dma((groups,)), dma],
        compiler_params=pltpu.CompilerParams(
            collective_id=4, has_side_effects=True, vmem_limit_bytes=VMEM_BYTES
        ),
        cost_estimate=pl.CostEstimate(
            flops=10 * length * length * cols,
            bytes_accessed=150 * 2**20,
            transcendentals=heads * length * length // 2,
        ),
        name="attend_backward",
    )(back_low, outward, mixed, wide, totals, bias_column, widened, thin)


def back_kernel(
    e_ref, slope_ref, thin_ref, wide_ref, grad_ref, act_ref,
    own_ref, dhid_ref, sum_ref, layer_ref, share_ref,
    thin_buf, wide_buf, e_buf, slope_buf, dhid_buf, part_buf, hop_buf, in_buf, send, receive,
    load_sem, pair_sem, e_sem, slope_sem, dhid_sem, act_sem, layer_sem, grad_send, grad_recv, grad_sem,
    *, groups, slices
):
    quads = groups // 2
    me = lax.axis_index("dp")
    place = lax.axis_index("tensor")
    rows, width = own_ref.shape
    units = wide_buf.shape[1]
    half = units // 2
    tile = min(512, half)
    slab = min(512, width)

    def across(mask):
        return (flip(me, mask), place)

    def load_block(number, at):
        target = pl.ds(at * rows, rows)
        return (
            pltpu.make_async_copy(
                e_ref.at[target], e_buf.at[number % 2, :, pl.ds(0, width)], e_sem.at[number]
            ),
            pltpu.make_async_copy(
                slope_ref.at[target], slope_buf.at[number % 2], slope_sem.at[number]
            ),
        )

    order = [quads - 1] + list(range(1, quads - 1)) + [0]
    thin_load = pltpu.make_async_copy(thin_ref, thin_buf.at[pl.ds(0, half)], load_sem.at[0])
    thin_load.start()
    for copy in load_block(0, order[0]):
        copy.start()
    wide_load = pltpu.make_async_copy(wide_ref, wide_buf, load_sem.at[1])
    wide_load.start()
    greet_all(
        [across(mask) for mask in [1] + direct_masks(quads)]
        + [(me, lax.rem(place + step, slices)) for step in range(1, slices)]
    )
    span = share_ref.shape[1]

    def grad_rows(owner):
        return grad_ref.at[pl.ds(pl.multiple_of(owner * span, span), span)]

    def grad_to(step):
        owner = lax.rem(place + step, slices)
        return remote(
            grad_rows(owner), share_ref.at[step], grad_send.at[step], grad_recv.at[step],
            (me, owner),
        )

    for step in range(1, slices):
        grad_to(step).start()
    grad_own = pltpu.make_async_copy(grad_rows(place), share_ref.at[0], grad_sem)
    grad_own.start()
    pair = remote(
        thin_ref, thin_buf.at[pl.ds(half, half)], pair_sem.at[0], pair_sem.at[1], across(1)
    )
    pair.start()

    half_rows = rows // 2

    def parts(block, side):
        if side is None:
            return part_buf.at[block - 1]
        return part_buf.at[block - 1, pl.ds(side * half_rows, half_rows)]

    early, middle, end = square_reduce(
        quads, rows, across, send, receive, parts, parts, hop_buf, in_buf
    )
    sum_ref[...] = jnp.zeros_like(sum_ref)
    stores = []
    for number, at in enumerate(order):
        slot = number % 2
        if number + 1 < quads:
            for copy in load_block(number + 1, order[number + 1]):
                copy.start()
        if number == 0:
            thin_load.wait()
        for copy in load_block(number, at):
            copy.wait()
        if number >= 2:
            stores[number - 2].wait()

        def back_tile(index, carry):
            columns = pl.ds(pl.multiple_of(index * tile, tile), tile)
            back = dot_as(e_buf[slot, :, :width], thin_buf[columns, :], ROWS)
            back = (back * slope_buf[slot, :, columns]).astype(jnp.bfloat16)
            dhid_buf[slot, :, columns] = back
            sum_ref[:, columns] += jnp.sum(back.astype(jnp.float32), axis=0, keepdims=True)
            return carry

        if number == 0:
            lax.fori_loop(0, half // tile, back_tile, 0)
            pair.wait_recv()
            lax.fori_loop(half // tile, units // tile, back_tile, 0)
            wide_load.wait()
        else:
            lax.fori_loop(0, units // tile, back_tile, 0)
        store = pltpu.make_async_copy(
            dhid_buf.at[slot, :, pl.ds(0, units)],
            dhid_ref.at[pl.ds(at * rows, rows)],
            dhid_sem.at[number],
        )
        store.start()
        stores.append(store)

        def slab_of(index, carry):
            here = pl.ds(pl.multiple_of(index * slab, slab), slab)
            product = dot_as(dhid_buf[slot, :, :units], wide_buf[here, :], ROWS)
            if at:
                part_buf[at - 1, :, here] = product.astype(jnp.bfloat16)
            else:
                own_ref[:, here] = product
            return carry

        lax.fori_loop(0, width // slab, slab_of, 0)
        if at:
            early(at)
        if number == quads - 2:
            middle()
    for store in stores[-2:]:
        store.wait()

    def load_act(number):
        return pltpu.make_async_copy(
            act_ref.at[pl.ds(number * rows, rows)],
            e_buf.at[number % 2, :, pl.ds(0, units)],
            act_sem.at[number],
        )

    outs = []
    load_act(0).start()
    for number in range(quads):
        slot = number % 2
        if number + 1 < quads:
            load_act(number + 1).start()
        load_act(number).wait()
        if number >= 2:
            outs[number - 2].wait()

        def out_of(index, carry):
            here = pl.ds(pl.multiple_of(index * slab, slab), slab)
            dhid_buf[slot, :, here] = dot_as(
                e_buf[slot, :, :units], thin_buf[:, here], PLAIN, jnp.bfloat16
            )
            return carry

        lax.fori_loop(0, width // slab, out_of, 0)
        out = pltpu.make_async_copy(
            dhid_buf.at[slot, :, pl.ds(0, width)],
            layer_ref.at[pl.ds(number * rows, rows)],
            layer_sem.at[number],
        )
        out.start()
        outs.append(out)
    end()
    for at in range(len(direct_masks(quads))):
        own_ref[...] += in_buf[at].astype(jnp.float32)
    pair.wait_send()
    for out in outs[-2:]:
        out.wait()
    for step in range(1, slices):
        grad_to(step).wait()
    grad_own.wait()


def back_step(back, slope, thin, wide, grad, active):
    groups = lax.axis_size("dp")
    slices = lax.axis_size("tensor")
    quads = groups // 2
    length, width = back.shape
    rows = length // quads
    units = slope.shape[1]
    dma = pltpu.SemaphoreType.DMA
    vmem = pl.BlockSpec(memory_space=pltpu.VMEM)
    hbm = pl.BlockSpec(memory_space=pltpu.HBM)
    low = jnp.bfloat16
    return pl.pallas_call(
        functools.partial(back_kernel, groups=groups, slices=slices),
        in_specs=[hbm] * 6,
        out_specs=[vmem, hbm, vmem, hbm, hbm],
        out_shape=[
            jax.ShapeDtypeStruct((rows, width), jnp.float32),
            jax.ShapeDtypeStruct((length, units), low),
            jax.ShapeDtypeStruct((1, units), jnp.float32),
            jax.ShapeDtypeStruct((length, width), low),
            jax.ShapeDtypeStruct((slices, grad.shape[0] // slices, width), low),
        ],
        scratch_shapes=[
            pltpu.VMEM((units, width), low),
            pltpu.VMEM((width, units), low),
            pltpu.VMEM((2, rows, max(units, width)), low),
            pltpu.VMEM((2, rows, units), jnp.float32),
            pltpu.VMEM((2, rows, max(units, width)), low),
            pltpu.VMEM((quads - 1, rows, width), low),
        ]
        + reduce_scratch(quads, rows, width)
        + [dma((2,)), dma((2,))] + [dma((quads,))] * 5
        + [dma((slices,)), dma((slices,)), dma],
        compiler_params=pltpu.CompilerParams(
            collective_id=5, has_side_effects=True, vmem_limit_bytes=60 * 2**20
        ),
        cost_estimate=pl.CostEstimate(
            flops=4 * length * width * units,
            bytes_accessed=150 * 2**20,
            transcendentals=0,
        ),
        name="back_step",
    )(back, slope, thin, wide, grad, active)


def open_kernel(
    x_ref, w_ref, c_ref, live_ref, norm_ref, bias_ref, small_ref, count_ref, wide_ref, thin_ref, out_ref,
    full_ref, weight_ref, mixed_ref, back_ref, all_ref, counts_ref, wide_all, thin_all, out_all,
    a_buf, w_buf, e_ref, wide_buf, thin_buf, out_buf,
    line_send, line_recv, small_send, small_recv, w_send, w_recv, pair_send, pair_recv,
    e_send, e_recv, local_sem, keep_sem, count_send, count_recv,
    wide_send, wide_recv, thin_send, thin_recv, out_send, out_recv, plane_send, plane_recv,
    run_send, run_recv,
    *, groups, slices, piece
):
    quads = groups // 2
    count = groups * slices
    me = lax.axis_index("dp")
    place = lax.axis_index("tensor")
    rows = x_ref.shape[0]
    share = w_buf.shape[0] // groups
    cols = w_buf.shape[1] // 3
    out_cols = out_all.shape[1] // groups
    masks = direct_masks(quads)
    hops = two_hops(quads)
    low = jnp.bfloat16
    raw = piece % 128 == 0

    def across(mask):
        return (flip(me, mask), place)

    def along(other):
        return (me, other)

    def beside(step):
        return (me, lax.rem(place + step, slices))

    def anyone(step):
        other = lax.rem(me * slices + place + step, count)
        return (lax.div(other, slices), lax.rem(other, slices))

    barrier = pltpu.get_barrier_semaphore()

    def greet(step, carry):
        pl.semaphore_signal(
            barrier, inc=1, device_id=anyone(step), device_id_type=pl.DeviceIdType.MESH
        )
        return carry

    lax.fori_loop(1, count, greet, 0)

    def w_rows(mask, half=None):
        start = flip(me, mask) * share
        if half is None:
            return w_buf.at[pl.ds(pl.multiple_of(start, share), share)]
        size = share // 2
        return w_buf.at[pl.ds(pl.multiple_of(start + half * size, size), size)]

    here = pl.ds(pl.multiple_of(me * share, share), share)
    for part in range(3):
        w_buf[here, part * cols : (part + 1) * cols] = w_ref[part].astype(low)
    chunk = 64

    def norm_chunk(at, carry):
        part = pl.ds(pl.multiple_of(at * chunk, chunk), chunk)
        normed = layer_norm(x_ref[part, :].astype(jnp.float32), norm_ref[0:1, :], norm_ref[1:2, :])
        target = pl.ds(pl.multiple_of(place * rows + at * chunk, chunk), chunk)
        a_buf[target, :] = normed.astype(low)
        return carry

    lax.fori_loop(0, rows // chunk, norm_chunk, 0)
    pl.semaphore_wait(barrier, count - 1)

    def a_rows(block):
        return a_buf.at[pl.ds(pl.multiple_of(block * rows, rows), rows)]

    def keep(block):
        return pltpu.make_async_copy(
            a_rows(block),
            full_ref.at[pl.ds(pl.multiple_of(block * rows, rows), rows)],
            keep_sem.at[block],
        )

    def a_half(block, half):
        size = rows // 2
        return a_buf.at[pl.ds(pl.multiple_of(block * rows + half * size, size), size)]

    def a_move(step, side, half, outgoing):
        back = step if outgoing else step + 1
        block = place - back if side == 0 else place + back
        towards = (side == 0) == outgoing
        return remote(
            a_half(block, half), a_half(block, half),
            line_send.at[side, half, step], line_recv.at[side, half, step],
            along(place + 1 if towards else place - 1),
        )

    def sends_right(step):
        return jnp.logical_and(place - step >= 0, place + 1 < slices)

    def sends_left(step):
        return jnp.logical_and(place + step < slices, place >= 1)

    for half in range(2):
        pl.when(sends_right(0))(lambda: a_move(0, 0, half, True).start())
        pl.when(sends_left(0))(lambda: a_move(0, 1, half, True).start())

    w_copies = []
    for at, mask in enumerate(masks):
        copy = remote(w_rows(0), w_rows(0), w_send.at[at], w_recv.at[at], across(mask))
        copy.start()
        w_copies.append(copy)

    e_ref[...] = (c_ref[...].astype(jnp.float32) * live_ref[...]).astype(low)
    keep(place).start()
    all_ref[place] = small_ref[...]
    small_copies = []
    for step in range(1, slices):
        copy = remote(
            small_ref, all_ref.at[place], small_send.at[step], small_recv.at[step], beside(step)
        )
        copy.start()
        small_copies.append(copy)

    def tell(step):
        return remote(
            count_ref, counts_ref.at[step], count_send.at[step], count_recv.at[step], anyone(step)
        )

    counts_ref[0] = count_ref[...]
    lax.fori_loop(1, count, lambda step, carry: (tell(step).start(), carry)[1], 0)

    out_here = pl.ds(pl.multiple_of(place * cols, cols), cols)
    out_buf[out_here, :] = out_ref[...].astype(low)
    out_copies = []
    for step in range(1, slices):
        target = out_buf.at[out_here]
        copy = remote(target, target, out_send.at[step], out_recv.at[step], beside(step))
        copy.start()
        out_copies.append(copy)

    for part in range(groups):
        if raw:
            row = part * piece // cols
            start = part * piece % cols
            wide_buf[part] = wide_ref[:, row, start : start + piece].astype(low)
            thin_buf[part] = thin_ref[row, start : start + piece, :].astype(low)
        else:
            wide_buf[part] = wide_ref[part]
            thin_buf[part] = thin_ref[part]
    thin_cols = thin_buf.shape[2]
    wide_here = wide_all.at[place, here]
    thin_here = thin_all.at[:, pl.ds(pl.multiple_of(me * thin_cols, thin_cols), thin_cols)]

    def wide_to(step):
        other = lax.rem(me + step, groups)
        return remote(
            wide_buf.at[other], wide_here, wide_send.at[step], wide_recv.at[step], (other, place)
        )

    def thin_to(step):
        other = lax.rem(me + step, groups)
        return remote(
            thin_buf.at[other], thin_here, thin_send.at[step], thin_recv.at[step], (other, place)
        )

    own_wide = pltpu.make_async_copy(wide_buf.at[me], wide_here, local_sem.at[2])
    own_wide.start()
    own_thin = pltpu.make_async_copy(thin_buf.at[me], thin_here, local_sem.at[3])
    own_thin.start()
    for step in range(1, groups):
        wide_to(step).start()

    pair_copies = []

    def to_pair(source):
        at = len(pair_copies)
        copy = remote(source, source, pair_send.at[at], pair_recv.at[at], across(1))
        copy.start()
        pair_copies.append(copy)

    to_pair(w_rows(0))
    for at, copy in enumerate(w_copies):
        remote(
            w_rows(masks[at]), w_rows(masks[at]), w_send.at[at], w_recv.at[at], across(masks[at])
        ).wait_recv()
    hop_copies = []
    for number, (mask, half, goal) in enumerate(hops):
        at = len(masks) + number
        source = w_rows(mask, half)
        copy = remote(source, source, w_send.at[at], w_recv.at[at], across(goal))
        copy.start()
        hop_copies.append(copy)
    for mask in masks:
        to_pair(w_rows(mask))

    own = pltpu.make_async_copy(e_ref, back_ref.at[pl.ds(0, rows)], local_sem.at[0])
    own.start()

    def e_moves():
        return [
            remote(
                e_ref, back_ref.at[pl.ds((at + 1) * rows, rows)], e_send.at[at], e_recv.at[at],
                across(mask),
            )
            for at, mask in enumerate(masks)
        ]

    for number, (mask, half, goal) in enumerate(hops):
        at = len(masks) + number
        landed = w_rows(2 + 4, half)
        remote(landed, landed, w_send.at[at], w_recv.at[at], across(goal)).wait_recv()
        to_pair(landed)
    sources = [0] + masks
    for at, mask in enumerate(sources):
        landed = w_rows(mask + 1)
        remote(landed, landed, pair_send.at[at], pair_recv.at[at], across(1)).wait_recv()
    for number, (mask, half, goal) in enumerate(hops):
        at = len(sources) + number
        landed = w_rows(2 + 4 + 1, half)
        remote(landed, landed, pair_send.at[at], pair_recv.at[at], across(1)).wait_recv()
    weights_out = pltpu.make_async_copy(w_buf, weight_ref, local_sem.at[1])
    weights_out.start()

    def multiply(block):
        where = pl.ds(pl.multiple_of(block * rows, rows), rows)
        left = a_buf[where, :]
        for part in range(3):
            columns = slice(part * cols, (part + 1) * cols)
            product = dot_as(left, w_buf[:, columns], PLAIN) + bias_ref[0:1, columns]
            mixed_ref[where, columns] = product.astype(low)

    multiply(place)

    def out_at(mask, half=None):
        start = pl.multiple_of(flip(me, mask) * out_cols, out_cols)
        size = out_all.shape[0] // 2
        if half is None:
            return out_all.at[:, pl.ds(start, out_cols)]
        return out_all.at[half * size : (half + 1) * size, pl.ds(start, out_cols)]

    own_out = pltpu.make_async_copy(out_buf, out_at(0), local_sem.at[4])

    def plane(at, source, target, device):
        return remote(source, target, plane_send.at[at], plane_recv.at[at], device)

    def plane_first():
        return [
            plane(at, out_buf, out_at(0), across(mask)) for at, mask in enumerate([1] + masks)
        ]

    def plane_landed():
        return [
            plane(at, out_buf, out_at(mask), across(mask)) for at, mask in enumerate([1] + masks)
        ]

    def plane_hops():
        return [
            plane(1 + len(masks) + number, out_at(mask, half), out_at(mask, half), across(goal))
            for number, (mask, half, goal) in enumerate(hops)
        ]

    def plane_pairs():
        return [
            plane(1 + len(masks) + len(hops) + at, out_at(mask), out_at(mask), across(1))
            for at, mask in enumerate(masks)
        ]

    def plane_last():
        return [
            plane(
                1 + 2 * len(masks) + len(hops) + number, out_at(6, half), out_at(6, half), across(1)
            )
            for number, (mask, half, goal) in enumerate(hops)
        ]

    def wide_move(step, side, half, outgoing):
        back = step if outgoing else step + 1
        block = place - back if side == 0 else place + back
        towards = (side == 0) == outgoing
        size = wide_all.shape[1] // 2
        part = wide_all.at[block, pl.ds(half * size, size)]
        return remote(
            part, part, run_send.at[side, half, step], run_recv.at[side, half, step],
            along(place + 1 if towards else place - 1),
        )

    def wide_arrived():
        own_wide.wait()
        for step in range(1, groups):
            other = lax.rem(me + groups - step, groups)
            wide_from = wide_all.at[
                place, pl.ds(pl.multiple_of(other * share, share), share)
            ]
            remote(
                wide_buf.at[other], wide_from, wide_send.at[step], wide_recv.at[step],
                (other, place),
            ).wait_recv()
        for half in range(2):
            pl.when(sends_right(0))(lambda: wide_move(0, 0, half, True).start())
            pl.when(sends_left(0))(lambda: wide_move(0, 1, half, True).start())

    def pass_on(step, carry):
        got_left = place - 1 - step >= 0
        got_right = place + 1 + step < slices

        for half in range(2):
            for side, got, sends in ((0, got_left, sends_right), (1, got_right, sends_left)):

                @pl.when(got)
                def _():
                    a_move(step, side, half, False).wait_recv()

                    @pl.when(jnp.logical_and(step + 1 < slices - 1, sends(step + 1)))
                    def _():
                        a_move(step + 1, side, half, True).start()

        pl.when(got_left)(lambda: keep(place - 1 - step).start())
        pl.when(got_right)(lambda: keep(place + 1 + step).start())

        @pl.when(step == 0)
        def _():
            for copy in out_copies:
                copy.wait_recv()
            own_out.start()
            for copy in plane_first():
                copy.start()
            for step_to in range(1, groups):
                thin_to(step_to).start()
            for copy in e_moves():
                copy.start()

        @pl.when(got_left)
        def _():
            multiply(place - 1 - step)

        @pl.when(got_right)
        def _():
            multiply(place + 1 + step)

        @pl.when(step == 1)
        def _():
            wide_arrived()
            for copy in plane_landed():
                copy.wait_recv()
            for copy in plane_hops() + plane_pairs():
                copy.start()

        return carry

    lax.fori_loop(0, slices - 1, pass_on, 0)

    def wide_on(step, carry):
        gots = (place - 1 - step >= 0, place + 1 + step < slices)
        for half in range(2):
            for side, sends in ((0, sends_right), (1, sends_left)):

                @pl.when(gots[side])
                def _():
                    wide_move(step, side, half, False).wait_recv()

                    @pl.when(jnp.logical_and(step + 1 < slices - 1, sends(step + 1)))
                    def _():
                        wide_move(step + 1, side, half, True).start()

        return carry

    lax.fori_loop(0, slices - 1, wide_on, 0)

    for number, (mask, half, goal) in enumerate(hops):
        at = 1 + len(masks) + number
        plane(at, out_at(6, half), out_at(6, half), across(goal)).wait_recv()
    for copy in plane_last():
        copy.start()
    for at, mask in enumerate(masks):
        landed = out_at(mask + 1)
        plane(1 + len(masks) + len(hops) + at, landed, landed, across(1)).wait_recv()
    for number, (mask, half, goal) in enumerate(hops):
        landed = out_at(7, half)
        plane(1 + 2 * len(masks) + len(hops) + number, landed, landed, across(1)).wait_recv()
    for copy in plane_first() + plane_hops() + plane_pairs() + plane_last():
        copy.wait_send()
    for at, mask in enumerate(masks):
        landed = back_ref.at[pl.ds((at + 1) * rows, rows)]
        remote(e_ref, landed, e_send.at[at], e_recv.at[at], across(mask)).wait_recv()
    for copy in e_moves() + w_copies + hop_copies + pair_copies + out_copies:
        copy.wait_send()
    for copy in small_copies:
        copy.wait()
    for step in range(1, groups):
        other = lax.rem(me + groups - step, groups)
        thin_from = thin_all.at[
            :, pl.ds(pl.multiple_of(other * thin_cols, thin_cols), thin_cols)
        ]
        device = (other, place)
        remote(
            thin_buf.at[other], thin_from, thin_send.at[step], thin_recv.at[step], device
        ).wait_recv()
        wide_to(step).wait_send()
        thin_to(step).wait_send()
    lax.fori_loop(1, count, lambda step, carry: (tell(step).wait(), carry)[1], 0)
    for copy in (own, weights_out, own_thin, own_out):
        copy.wait()

    def finish(step, carry):
        for half in range(2):
            pl.when(sends_right(step))(lambda: a_move(step, 0, half, True).wait_send())
            pl.when(sends_left(step))(lambda: a_move(step, 1, half, True).wait_send())
            pl.when(sends_right(step))(lambda: wide_move(step, 0, half, True).wait_send())
            pl.when(sends_left(step))(lambda: wide_move(step, 1, half, True).wait_send())
        return carry

    lax.fori_loop(0, slices - 1, finish, 0)
    for block in range(slices):
        keep(block).wait()


def open_step(
    tokens, inward, cotangent, live, norms, bias, small, living, widening, narrowing, outward
):
    groups = lax.axis_size("dp")
    slices = lax.axis_size("tensor")
    count = groups * slices
    quads = groups // 2
    rows, width = tokens.shape
    share, _, cols = inward.shape
    piece = 4 * cols // groups
    out_cols = outward.shape[1]
    hops = len(two_hops(quads))
    direct = len(direct_masks(quads))
    dma = pltpu.SemaphoreType.DMA
    vmem = pl.BlockSpec(memory_space=pltpu.VMEM)
    hbm = pl.BlockSpec(memory_space=pltpu.HBM)
    low = jnp.bfloat16
    wide = jnp.float32
    if piece % 128:
        widening = widening.astype(low).reshape(share, groups, piece).transpose(1, 0, 2)
        narrowing = narrowing.astype(low).reshape(groups, piece, out_cols)
    shape = jax.ShapeDtypeStruct
    planes = 1 + 2 * direct + 2 * hops
    return pl.pallas_call(
        functools.partial(open_kernel, groups=groups, slices=slices, piece=piece),
        in_specs=[vmem] * 11,
        out_specs=[hbm, hbm, vmem, hbm, vmem, vmem, hbm, hbm, hbm],
        out_shape=[
            shape((slices * rows, width), low),
            shape((width, 3 * cols), low),
            shape((slices * rows, 3 * cols), low),
            shape((quads * rows, width), low),
            shape((slices,) + small.shape, wide),
            shape((count, 8, 128), wide),
            shape((slices, width, piece), low),
            shape((piece, width), low),
            shape((width, width), low),
        ],
        scratch_shapes=[
            pltpu.VMEM((slices * rows, width), low),
            pltpu.VMEM((width, 3 * cols), low),
            pltpu.VMEM((rows, width), low),
            pltpu.VMEM((groups, share, piece), low),
            pltpu.VMEM((groups, piece, out_cols), low),
            pltpu.VMEM((slices * cols, out_cols), low),
            dma((2, 2, slices)),
            dma((2, 2, slices)),
            dma((slices,)),
            dma((slices,)),
            dma((direct + hops,)),
            dma((direct + hops,)),
            dma((1 + direct + hops,)),
            dma((1 + direct + hops,)),
            dma((direct,)),
            dma((direct,)),
            dma((5,)),
            dma((slices,)),
            dma((count,)),
            dma((count,)),
            dma((groups,)),
            dma((groups,)),
            dma((groups,)),
            dma((groups,)),
            dma((slices,)),
            dma((slices,)),
            dma((planes,)),
            dma((planes,)),
            dma((2, 2, slices)),
            dma((2, 2, slices)),
        ],
        compiler_params=pltpu.CompilerParams(
            collective_id=1, has_side_effects=True, vmem_limit_bytes=VMEM_BYTES
        ),
        cost_estimate=pl.CostEstimate(
            flops=2 * slices * rows * width * 3 * cols,
            bytes_accessed=400 * 2**20,
            transcendentals=0,
        ),
        name="open_step",
    )(
        tokens,
        inward.transpose(1, 0, 2),
        cotangent,
        live,
        norms,
        bias,
        small,
        living,
        widening,
        narrowing,
        outward,
    )


def hidden_gather_kernel(
    b_ref, weight_ref, bias_ref, all_ref, act_ref, slope_ref, full_ref,
    b_buf, w_buf, act_buf, slope_buf,
    b_send, b_recv, keep_sem, act_sem, slope_sem, w_sem, pair_sem, out_sem,
    *, groups
):
    quads = groups // 2
    me = lax.axis_index("dp")
    place = lax.axis_index("tensor")
    rows = b_ref.shape[0]
    tiles, _, tile = weight_ref.shape
    masks = direct_masks(quads)
    hops = two_hops(quads)
    half_rows = rows // 2

    def across(mask):
        return (flip(me, mask), place)

    load = pltpu.make_async_copy(weight_ref, w_buf.at[pl.ds(0, tiles)], w_sem)
    load.start()
    greet_all([across(mask) for mask in [1] + masks])

    def block(at):
        return b_buf.at[pl.ds(at * rows, rows)]

    def piece(at, half):
        return b_buf.at[pl.ds(at * rows + half * half_rows, half_rows)]

    copies = []
    for at, mask in enumerate(masks):
        copy = remote(b_ref, block(at + 1), b_send.at[at], b_recv.at[at], across(mask))
        copy.start()
        copies.append(copy)
    pair = remote(
        weight_ref, w_buf.at[pl.ds(tiles, tiles)], pair_sem.at[0], pair_sem.at[1], across(1)
    )
    pair.start()
    b_buf[0:rows, :] = b_ref[...]
    keeps = []
    stores = []

    def keep(at):
        copy = pltpu.make_async_copy(
            block(at), all_ref.at[pl.ds(at * rows, rows)], keep_sem.at[at]
        )
        copy.start()
        keeps.append(copy)

    def multiply(at, first, amount):
        def part(number, carry):
            columns = pl.ds(pl.multiple_of(number * tile, tile), tile)
            hidden = (
                dot_as(b_buf[at * rows : (at + 1) * rows, :], w_buf[number], PLAIN)
                + bias_ref[0:1, columns]
            )
            root = 0.7978845608028654
            square = hidden * hidden
            bent = jnp.tanh(root * hidden * (1.0 + 0.044715 * square))
            half = 0.5 * (1.0 + bent)
            act_buf[at % 2, :, columns] = (hidden * half).astype(jnp.bfloat16)
            slope_buf[at % 2, :, columns] = half + 0.5 * hidden * (1.0 - bent * bent) * (
                root * (1.0 + 3.0 * 0.044715 * square)
            )
            return carry

        lax.fori_loop(first, first + amount, part, 0)

    def store(at):
        target = pl.ds(at * rows, rows)
        pair_of = [
            pltpu.make_async_copy(act_buf.at[at % 2], act_ref.at[target], act_sem.at[at]),
            pltpu.make_async_copy(slope_buf.at[at % 2], slope_ref.at[target], slope_sem.at[at]),
        ]
        for copy in pair_of:
            copy.start()
        stores.append(pair_of)

    keep(0)
    load.wait()
    multiply(0, 0, tiles)
    pair.wait_recv()
    multiply(0, tiles, tiles)
    store(0)
    outs = []
    for number in range(2 * tiles):
        copy = pltpu.make_async_copy(
            w_buf.at[number],
            full_ref.at[:, pl.ds(number * tile, tile)],
            out_sem.at[number],
        )
        copy.start()
        outs.append(copy)
    for at in range(len(masks)):
        copies[at].wait_recv()
    for number, (mask, half, goal) in enumerate(hops):
        at = len(masks) + number
        copy = remote(
            piece(masks.index(mask) + 1, half), piece(3, half), b_send.at[at], b_recv.at[at],
            across(goal),
        )
        copy.start()
        copies.append(copy)
    for at in range(1, quads):
        if at == 1 + len(masks):
            for copy in copies[len(masks) :]:
                copy.wait_recv()
        keep(at)
        if at >= 2:
            for copy in stores[at - 2]:
                copy.wait()
        multiply(at, 0, 2 * tiles)
        store(at)
    for copy in copies + [pair]:
        copy.wait_send()
    for copy in keeps + outs + sum(stores[-2:], []):
        copy.wait()


def hidden_gather(rows_own, weight, bias):
    groups = lax.axis_size("dp")
    quads = groups // 2
    rows, width = rows_own.shape
    tiles, _, tile = weight.shape
    units = 2 * tiles * tile
    pieces = len(two_hops(quads)) + len(direct_masks(quads))
    dma = pltpu.SemaphoreType.DMA
    vmem = pl.BlockSpec(memory_space=pltpu.VMEM)
    hbm = pl.BlockSpec(memory_space=pltpu.HBM)
    return pl.pallas_call(
        functools.partial(hidden_gather_kernel, groups=groups),
        in_specs=[vmem, hbm, vmem],
        out_specs=[hbm, hbm, hbm, hbm],
        out_shape=[
            jax.ShapeDtypeStruct((quads * rows, width), jnp.bfloat16),
            jax.ShapeDtypeStruct((quads * rows, units), jnp.bfloat16),
            jax.ShapeDtypeStruct((quads * rows, units), jnp.float32),
            jax.ShapeDtypeStruct((width, units), jnp.bfloat16),
        ],
        scratch_shapes=[
            pltpu.VMEM((quads * rows, width), jnp.bfloat16),
            pltpu.VMEM((2 * tiles, width, tile), jnp.bfloat16),
            pltpu.VMEM((2, rows, units), jnp.bfloat16),
            pltpu.VMEM((2, rows, units), jnp.float32),
            dma((pieces,)),
            dma((pieces,)),
            dma((quads,)),
            dma((quads,)),
            dma((quads,)),
            dma,
            dma((2,)),
            dma((2 * tiles,)),
        ],
        compiler_params=pltpu.CompilerParams(
            collective_id=2, has_side_effects=True, vmem_limit_bytes=VMEM_BYTES
        ),
        cost_estimate=pl.CostEstimate(
            flops=2 * quads * rows * width * units,
            bytes_accessed=200 * 2**20,
            transcendentals=0,
        ),
        name="hidden_gather",
    )(rows_own, weight, bias)


def inward_kernel(
    grad_ref, outer_ref, wide_ref, values_ref, own_ref, outer_sum, wide_sum, all_ref,
    near, far, pair_send, pair_recv, pair_load, hop_buf, in_buf, send, receive,
    outer_near, outer_far, outer_pair_send, outer_pair_recv, outer_load,
    outer_hop, outer_in, outer_send, outer_recv,
    line_buf, line_send, line_recv, wide_send, wide_recv, wide_load, *sum_refs,
    groups, slices
):
    quads = groups // 2
    me = lax.axis_index("dp")
    place = lax.axis_index("tensor")
    share = near.shape[1]
    half_rows = share // 2
    piece = wide_ref.shape[0]

    def across(mask):
        return (flip(me, mask), place)

    anyone, greet = everyone(groups, slices)
    greet()
    sum_start, sum_middle, sum_end = spread_sum(
        values_ref, all_ref, *sum_refs, anyone, groups, slices
    )

    def block_of(other):
        return grad_ref.at[pl.ds(pl.multiple_of(other * share, share), share)]

    def parts(block, side):
        if side is None:
            return near.at[block]
        return near.at[block, pl.ds(side * half_rows, half_rows)]

    start, finish = pair_reduce(
        quads, me, across, block_of, near, far, pair_send, pair_recv, pair_load
    )
    early, middle, end = square_reduce(
        quads, share, across, send, receive, parts, parts, hop_buf, in_buf
    )

    out_cols = outer_sum.shape[1]
    long = outer_near.shape[1]
    half_long = long // 2

    def outer_block(other):
        return outer_ref.at[:, pl.ds(pl.multiple_of(other * out_cols, out_cols), out_cols)]

    def outer_parts(block, side):
        if side is None:
            return outer_near.at[block]
        return outer_near.at[block, pl.ds(side * half_long, half_long)]

    outer_start, outer_finish = pair_reduce(
        quads, me, across, outer_block, outer_near, outer_far,
        outer_pair_send, outer_pair_recv, outer_load,
    )
    outer_early, outer_middle, outer_end = square_reduce(
        quads, long, across, outer_send, outer_recv, outer_parts, outer_parts, outer_hop, outer_in
    )
    line_rows = outer_sum.shape[0]

    def line_block(owner):
        return outer_near.at[0, pl.ds(pl.multiple_of(owner * line_rows, line_rows), line_rows)]

    def line_to(step):
        owner = lax.rem(place + step, slices)
        return remote(
            line_block(owner), line_buf.at[step - 1], line_send.at[step], line_recv.at[step],
            (me, owner),
        )

    def columns_of(other):
        return wide_ref.at[:, pl.ds(pl.multiple_of(other * share, share), share)]

    def rows_of(other):
        return wide_sum.at[pl.ds(pl.multiple_of(other * piece, piece), piece)]

    def wide_to(step):
        other = lax.rem(me + step, groups)
        return remote(
            columns_of(other), rows_of(me), wide_send.at[step], wide_recv.at[step], (other, place)
        )

    def wide_from(step):
        other = lax.rem(me + groups - step, groups)
        return remote(
            columns_of(other), rows_of(other), wide_send.at[step], wide_recv.at[step],
            (other, place),
        )

    order = [quads - 1] + list(range(1, quads - 1))
    outer_start()
    start()
    sum_start()
    for m in order:
        outer_finish(m)
        outer_early(m)
    for m in order:
        finish(m)
        early(m)
    wide_own = pltpu.make_async_copy(columns_of(me), rows_of(me), wide_load)
    wide_own.start()
    outer_finish(0)
    outer_middle()
    for step in range(1, groups):
        wide_to(step).start()
    finish(0)
    sum_middle()
    middle()
    outer_end()
    outer = outer_near[0].astype(jnp.float32)
    for at in range(len(direct_masks(quads))):
        outer = outer + outer_in[at].astype(jnp.float32)
    outer_near[0] = outer.astype(outer_near.dtype)
    for step in range(1, slices):
        line_to(step).start()
    end()
    total = near[0].astype(jnp.float32)
    for at in range(len(direct_masks(quads))):
        total = total + in_buf[at].astype(jnp.float32)
    cols = own_ref.shape[2]
    for part in range(3):
        own_ref[part] = total[:, part * cols : (part + 1) * cols]
    final = line_block(place)[...].astype(jnp.float32)
    for step in range(1, slices):
        line_to(step).wait()
        final = final + line_buf[step - 1].astype(jnp.float32)
    outer_sum[...] = final
    wide_own.wait()
    for step in range(1, groups):
        wide_from(step).wait_recv()
        wide_to(step).wait_send()
    sum_end()


def inward_reduce(grad, outer, wide, values):
    groups = lax.axis_size("dp")
    slices = lax.axis_size("tensor")
    quads = groups // 2
    width = grad.shape[0]
    share = width // groups
    columns = grad.shape[1]
    piece = wide.shape[0]
    out_cols = outer.shape[1] // groups
    out_rows = outer.shape[0] // slices
    packed = sum_room(values)
    dma = pltpu.SemaphoreType.DMA
    vmem = pl.BlockSpec(memory_space=pltpu.VMEM)
    hbm = pl.BlockSpec(memory_space=pltpu.HBM)
    low = jnp.bfloat16

    def pair_scratch(rows, cols):
        return [
            pltpu.VMEM((quads, rows, cols), low),
            pltpu.VMEM((quads, rows, cols), low),
            dma((quads,)),
            dma((quads,)),
            dma((quads,)),
        ] + reduce_scratch(quads, rows, cols)

    return pl.pallas_call(
        functools.partial(inward_kernel, groups=groups, slices=slices),
        in_specs=[hbm, hbm, hbm, vmem],
        out_specs=[vmem, vmem, hbm, vmem],
        out_shape=[
            jax.ShapeDtypeStruct((3, share, columns // 3), jnp.float32),
            jax.ShapeDtypeStruct((out_rows, out_cols), jnp.float32),
            jax.ShapeDtypeStruct((groups * piece, share), low),
            jax.ShapeDtypeStruct(packed.shape, jnp.float32),
        ],
        scratch_shapes=pair_scratch(share, columns)
        + pair_scratch(width, out_cols)
        + [
            pltpu.VMEM((slices - 1, out_rows, out_cols), low),
            dma((slices,)),
            dma((slices,)),
            dma((groups,)),
            dma((groups,)),
            dma,
        ]
        + sum_scratch(groups * slices),
        compiler_params=pltpu.CompilerParams(
            collective_id=6, has_side_effects=True, vmem_limit_bytes=VMEM_BYTES
        ),
        cost_estimate=pl.CostEstimate(
            flops=8 * grad.size, bytes_accessed=250 * 2**20, transcendentals=0
        ),
        name="inward_reduce",
    )(grad, outer, wide, packed)


def swap(values, axis, mask):
    count = lax.axis_size(axis)
    return lax.ppermute(values, axis, [(i, i ^ mask) for i in range(count)])


def sum_room(values):
    count = lax.axis_size("dp") * lax.axis_size("tensor")
    room = count * 8 * 128
    packed = jnp.concatenate([values, jnp.zeros((room - values.shape[0],), jnp.float32)])
    return packed.reshape(count, 8, 128)


def sum_kernel(values_ref, out_ref, *scratch, groups, slices):
    anyone, greet = everyone(groups, slices)
    greet()
    start, middle, end = spread_sum(values_ref, out_ref, *scratch, anyone, groups, slices)
    start()
    middle()
    end()


def sum_everywhere(packed):
    groups = lax.axis_size("dp")
    slices = lax.axis_size("tensor")
    return pl.pallas_call(
        functools.partial(sum_kernel, groups=groups, slices=slices),
        in_specs=[pl.BlockSpec(memory_space=pltpu.VMEM)],
        out_specs=pl.BlockSpec(memory_space=pltpu.VMEM),
        out_shape=jax.ShapeDtypeStruct(packed.shape, jnp.float32),
        scratch_shapes=sum_scratch(groups * slices),
        compiler_params=pltpu.CompilerParams(
            collective_id=0, has_side_effects=True, vmem_limit_bytes=8 * 2**20
        ),
        cost_estimate=pl.CostEstimate(
            flops=packed.size, bytes_accessed=8 * packed.size, transcendentals=0
        ),
        name="sum_everywhere",
    )(packed)


def last_kernel(
    all_ref, factor_ref, late_ref, vectors_ref, first_ref, second_ref, bias_ref, slope_ref, *refs
):
    masters, directions = refs[:4], refs[4:8]
    fresh, halves = refs[8:12], refs[12:16]
    column_out, vectors_out, mean_out, square_out, square_late, norms_out = refs[16:22]
    buffers, load_sem = refs[22:30], refs[30]
    loads = [
        pltpu.make_async_copy(source, target, load_sem.at[at])
        for at, (source, target) in enumerate(zip(masters + directions, buffers))
    ]
    for load in loads:
        load.start()

    cols = bias_ref.shape[1]
    step = cols // 128
    lanes = first_ref.shape[1] // 128
    need = -(-(14 * step + 2 * lanes) // 8)
    rows = all_ref[0:need].reshape(need * 8, 128)

    def total(at):
        return jnp.sqrt(jnp.sum(rows[at * step : (at + 1) * step], keepdims=True))

    weight_norms = [total(at) for at in range(7)]
    update_norms = [total(7 + at) for at in range(7)]

    def rate(weight_norm, update_norm):
        return learn_rate * weight_norm / (update_norm + trust_epsilon)

    for at in range(4):
        loads[at].wait()
        loads[4 + at].wait()
        factor = rate(weight_norms[at], update_norms[at])
        master, direction = buffers[at], buffers[4 + at]
        length = master.shape[0]
        chunk = min(length, 32) if len(master.shape) == 3 and length > 4 else length
        if len(master.shape) == 2:
            chunk = min(length, 128)
        scale = factor.reshape((1,) * len(master.shape))
        for begin in range(0, length, chunk):
            part = slice(begin, begin + chunk)
            updated = master[part] - scale * direction[part]
            fresh[at][part] = updated
            halves[at][part] = updated.astype(jnp.bfloat16)
    for at, (begin, stop) in enumerate(((0, 1), (1, 2), (2, 6))):
        column_out[begin:stop, :] = bias_ref[begin:stop, :] - (
            rate(weight_norms[4 + at], update_norms[4 + at]) * slope_ref[begin:stop, :]
        )
    early = [
        jnp.concatenate(
            [rows[14 * step + row * lanes + at][None, :] for at in range(lanes)], axis=1
        )
        for row in range(2)
    ]
    slopes = jnp.concatenate(early + [late_ref[...]], axis=0) * factor_ref[0:1, 0:1]
    weights = vectors_ref[...]
    mean_new, square_new, direction = adapt_step(
        weights, first_ref[...], second_ref[...], slopes, 0.0
    )
    mean_out[...] = mean_new
    square_out[...] = square_new[0:2]
    square_late[...] = square_new[2:6]
    own = jnp.sqrt(jnp.sum(weights * weights, axis=1, keepdims=True))
    step_norms = jnp.sqrt(jnp.sum(direction * direction, axis=1, keepdims=True))
    vectors_out[...] = weights - rate(own, step_norms) * direction
    for row in range(6):
        weight_norms.append(own[row : row + 1])
        update_norms.append(step_norms[row : row + 1])
    lane = lax.broadcasted_iota(jnp.int32, (8, 128), 1)
    line = lax.broadcasted_iota(jnp.int32, (8, 128), 0)
    norms = jnp.zeros((8, 128), jnp.float32)
    for at in range(13):
        norms = jnp.where((lane == at) & (line == 0), weight_norms[at], norms)
        norms = jnp.where((lane == at) & (line == 1), update_norms[at], norms)
    norms_out[...] = norms[0:2, 0:13]


def last_step(values, factor, late, vectors, first, second, bias, slope, masters, directions):
    packed = sum_room(values)
    width = vectors.shape[1]
    wide = jnp.float32
    vmem = pl.BlockSpec(memory_space=pltpu.VMEM)
    hbm = pl.BlockSpec(memory_space=pltpu.HBM)

    masters = list(masters)
    directions = list(directions)
    masters[0] = masters[0].transpose(1, 0, 2)
    directions[0] = directions[0].transpose(1, 0, 2)
    shapes = [master.shape for master in masters]
    like = jax.ShapeDtypeStruct
    results = pl.pallas_call(
        last_kernel,
        in_specs=[vmem] * 8 + [hbm] * 8,
        out_specs=[vmem] * 14,
        out_shape=[like(shape, wide) for shape in shapes]
        + [like(shape, jnp.bfloat16) for shape in shapes]
        + [like(bias.shape, wide)]
        + [like((rows, width), wide) for rows in (6, 6, 2, 4)]
        + [like((2, 13), wide)],
        scratch_shapes=[pltpu.VMEM(shape, wide) for shape in shapes]
        + [pltpu.VMEM(shape, wide) for shape in shapes]
        + [pltpu.SemaphoreType.DMA((8,))],
        compiler_params=pltpu.CompilerParams(vmem_limit_bytes=VMEM_BYTES),
        cost_estimate=pl.CostEstimate(
            flops=packed.size, bytes_accessed=80 * 2**20, transcendentals=0
        ),
        name="last_step",
    )(
        sum_everywhere(packed),
        jnp.full((8, 128), factor),
        late,
        vectors,
        first,
        second,
        bias,
        slope,
        *masters,
        *directions,
    )
    fresh = list(results[:4])
    halves = list(results[4:8])
    fresh[0] = fresh[0].transpose(1, 0, 2)
    halves[0] = halves[0].transpose(1, 0, 2)
    return (fresh, halves) + tuple(results[8:14])


def after(values, gate):
    return lax.optimization_barrier((values, gate))[0]


def adapt_step(weight, moment_one, moment_two, slope, decay):
    mean_new = beta_one * moment_one + (1.0 - beta_one) * slope
    square_new = beta_two * moment_two + (1.0 - beta_two) * slope * slope
    direction = (
        mean_new
        / (1.0 - beta_one**STEP_COUNT)
        / (jnp.sqrt(square_new / (1.0 - beta_two**STEP_COUNT)) + adam_epsilon)
        + decay * weight
    )
    return (mean_new, square_new, direction)


def on_device(
    tokens,
    cotangent,
    live_mask,
    inward,
    inward_first,
    inward_second,
    outward,
    outward_first,
    outward_second,
    widening,
    widening_first,
    widening_second,
    narrowing,
    narrowing_first,
    narrowing_second,
    column_bias,
    column_first,
    column_second,
    vectors,
    vectors_first,
    vectors_second,
):
    low = jnp.bfloat16
    wide = jnp.float32
    amount, width = tokens.shape
    cols = column_bias.shape[1]
    groups = lax.axis_size("dp")
    slices = lax.axis_size("tensor")
    me = lax.axis_index("dp")
    place = lax.axis_index("tensor")
    share = inward.shape[0]
    piece = 4 * cols // groups

    inputs = tokens.astype(wide)
    living_here = live_mask.astype(wide)
    mixed_bias = jnp.concatenate(
        [column_bias[0], jnp.zeros((cols,), wide), column_bias[1]]
    ).reshape(1, 3 * cols)
    small_length = amount + 4 * cols
    small_rows = -(-small_length // 1024) * 8
    small = jnp.concatenate(
        [
            living_here,
            column_bias[2:].reshape(4 * cols),
            jnp.zeros((small_rows * 128 - small_length,), wide),
        ]
    ).reshape(small_rows, 128)
    (
        normed_full,
        inward_full,
        mixed,
        back_all,
        small_all,
        counts,
        wide_own,
        thin_own,
        outward_full,
    ) = open_step(
        tokens,
        inward,
        cotangent,
        living_here[:, None],
        vectors[0:2],
        mixed_bias,
        small,
        jnp.full((8, 128), jnp.sum(living_here)),
        widening,
        narrowing,
        outward,
    )
    factor = 1.0 / jnp.sum(counts[:, 0, 0])
    small_all = small_all.reshape(slices, small_rows * 128)
    length = normed_full.shape[0]
    bias_keys = jnp.where(small_all[:, :amount].reshape(length) > 0.5, 0.0, MASKED)
    bias_all = small_all[:, amount:small_length]

    if piece % 128:
        wide_own = wide_own.transpose(1, 0, 2).reshape(1, width, slices * piece)

    hidden_bias = jnp.concatenate(
        [
            lax.dynamic_slice_in_dim(bias_all, (me ^ side) * piece, piece, 1).reshape(1, -1)
            for side in range(2)
        ],
        axis=1,
    )

    context_wide, totals, context_own, back_all = attend_forward(
        mixed, bias_keys[None, :], back_all, amount
    )
    thin_own = lax.all_gather(
        after(thin_own, context_own), "tensor", axis=0, tiled=True
    )
    middle = inputs + dot_as(context_own, outward_full, PLAIN) + vectors[2]
    normed_two = layer_norm(middle, vectors[3], vectors[4]).astype(low)

    rows_two_all, active_all, slope, widening_full = hidden_gather(
        normed_two, wide_own, hidden_bias
    )
    half_units = slices * piece

    def pair_sum(left, right, apart):
        other = left(slice(half_units, None), right, low)
        if apart:
            own = left(slice(0, half_units), after(right, other), low)
            own, other = lax.optimization_barrier((own, swap(other, "dp", 1)))
            return (own.astype(wide) + other.astype(wide)).astype(low)
        own = left(slice(0, half_units), after(right, other), wide)
        return (own + swap(other, "dp", 1).astype(wide)).astype(low)

    slope_narrowing = pair_sum(
        lambda part, right, kind: dot_as(active_all[:, part], right, TOKENS, kind),
        after(back_all, thin_own),
        False,
    )
    back_normed_two, back_hidden_all, hidden_sums, widened_all, thin_parts = back_step(
        back_all, slope, thin_own, widening_full, slope_narrowing, active_all
    )
    thin_slope = jnp.sum(thin_parts.astype(wide), axis=0).astype(low)
    slope_widening = pair_sum(
        lambda part, right, kind: dot_as(back_hidden_all[:, part], right, TOKENS, kind),
        rows_two_all,
        True,
    )
    wide_slope = lax.psum_scatter(slope_widening, "tensor", scatter_dimension=0, tiled=True)

    _, norm_two_pull = jax.vjp(layer_norm, middle, vectors[3], vectors[4])
    back_middle_norm, slope_gain_two, slope_shift_two = norm_two_pull(back_normed_two)
    back_out = back_all[:amount]
    back_middle = back_out.astype(wide) + back_middle_norm
    back_low = back_middle.astype(low)

    back_mixed, widened, sum_narrowing = attend_backward(
        after(back_low, slope_widening),
        outward_full,
        mixed,
        context_wide,
        totals,
        bias_keys[:, None],
        widened_all,
        thin_slope,
    )
    layer_output = (middle + widened + vectors[5]).astype(low)

    back_normed_part = dot_as(back_mixed, inward_full, ROWS, low)
    back_normed = lax.psum_scatter(
        after(back_normed_part, wide_slope), "tensor", scatter_dimension=0, tiled=True
    )
    back_mixed = after(back_mixed, back_normed_part)
    slope_inward = dot_as(normed_full, back_mixed, TOKENS, low)
    slope_outward = dot_as(after(context_own, slope_inward), back_low, TOKENS, low)
    hidden_total = hidden_sums.reshape(2, 1, slices, piece)
    hidden_slots = jnp.zeros((groups, slices, piece), wide)
    hidden_slots = lax.dynamic_update_slice(hidden_slots, hidden_total[0], (me, 0, 0))
    hidden_slots = lax.dynamic_update_slice(hidden_slots, hidden_total[1], (me ^ 1, 0, 0))
    mixed_sums = jnp.stack(
        [
            jnp.sum(back_mixed[:, :cols], axis=0, dtype=wide),
            jnp.sum(back_mixed[:, 2 * cols :], axis=0, dtype=wide),
        ]
    )
    mixed_slots = lax.dynamic_update_slice(
        jnp.zeros((slices, 2, cols), wide), mixed_sums[None], (place, 0, 0)
    )
    late_rows = jnp.stack(
        [
            jnp.sum(back_middle, axis=0),
            slope_gain_two,
            slope_shift_two,
            jnp.sum(back_out, axis=0, dtype=wide),
        ]
    )
    packed = jnp.concatenate(
        [hidden_slots.reshape(-1), mixed_slots.reshape(-1), late_rows.reshape(-1)]
    )
    amount_packed = packed.shape[0]
    sum_inward, sum_outward, sum_widening, packed = inward_reduce(
        slope_inward, slope_outward, wide_slope, packed
    )
    packed = packed.reshape(-1)[:amount_packed]
    sum_inward = sum_inward.transpose(1, 0, 2)
    sum_widening = sum_widening.T.reshape(widening.shape)
    sum_narrowing = sum_narrowing.reshape(narrowing.shape)

    first_cut = groups * slices * piece
    second_cut = first_cut + slices * 2 * cols
    hidden_slots = packed[:first_cut].reshape(groups, slices, piece)
    hidden_rows = lax.dynamic_slice_in_dim(hidden_slots, place, 1, 1).reshape(4, cols)
    mixed_rows = lax.dynamic_index_in_dim(
        packed[first_cut:second_cut].reshape(slices, 2, cols), place, 0, keepdims=False
    )
    late_rows = packed[second_cut:].reshape(4, width)
    column_total = jnp.concatenate([mixed_rows, hidden_rows], axis=0)

    column_bias, vectors = after((column_bias, vectors), back_low)
    masters = (inward, outward, widening, narrowing)
    firsts = (inward_first, outward_first, widening_first, narrowing_first)
    seconds = (inward_second, outward_second, widening_second, narrowing_second)
    orders = ((1, 0, 2), (0, 1), (0, 1, 2), (0, 1, 2))
    summed_all = [
        with_layout_constraint(summed.astype(wide), Layout(order))
        for summed, order in zip(
            (sum_inward, sum_outward, sum_widening, sum_narrowing), orders
        )
    ]
    matrix_steps = [
        adapt_step(
            masters[ordinal],
            firsts[ordinal],
            seconds[ordinal],
            summed_all[ordinal] * factor,
            decay_rate,
        )
        for ordinal in range(4)
    ]
    column_mean, column_square, column_direction = adapt_step(
        column_bias, column_first, column_second, column_total * factor, 0.0
    )
    column_groups = ((0, 1), (1, 2), (2, 6))

    def square_sum(array):
        lanes = jnp.sum(array * array, axis=tuple(range(array.ndim - 1)))
        return jnp.concatenate([lanes, jnp.zeros((cols - lanes.shape[0],), wide)])

    squares = [square_sum(master) for master in masters]
    squares += [square_sum(column_bias[start:stop]) / groups for start, stop in column_groups]
    squares += [square_sum(step[2]) for step in matrix_steps]
    squares += [square_sum(column_direction[start:stop]) / groups for start, stop in column_groups]
    squares = jnp.concatenate(squares)

    _, norm_one_pull = jax.vjp(layer_norm, inputs, vectors[0], vectors[1])
    back_inputs_norm, slope_gain_one, slope_shift_one = norm_one_pull(
        after(back_normed, squares).astype(wide)
    )
    back_inputs = back_middle + back_inputs_norm
    (
        fresh,
        halves,
        new_column,
        new_vectors,
        vectors_mean,
        first_square,
        vectors_square,
        trust_norms,
    ) = last_step(
        jnp.concatenate([squares, slope_gain_one, slope_shift_one]),
        factor,
        late_rows,
        vectors,
        vectors_first,
        vectors_second,
        column_bias,
        column_direction,
        masters,
        [step[2] for step in matrix_steps],
    )
    results = []
    for ordinal in range(4):
        results += [
            fresh[ordinal],
            matrix_steps[ordinal][0],
            matrix_steps[ordinal][1],
            halves[ordinal],
        ]
    return (
        layer_output,
        back_inputs * factor,
        *results,
        new_column,
        column_mean,
        column_square[0],
        column_square[1],
        column_square[2:],
        new_vectors,
        vectors_mean,
        first_square,
        vectors_square,
        trust_norms,
    )


def solution(mesh):
    in_specs = (
        P(("dp", "tensor"), None),
        P(("dp", "tensor"), None),
        P(("dp", "tensor")),
        P("dp", None, "tensor"),
        P("dp", None, "tensor"),
        P("dp", None, "tensor"),
        P("tensor", "dp"),
        P("tensor", "dp"),
        P("tensor", "dp"),
        P("dp", None, "tensor"),
        P("dp", None, "tensor"),
        P("dp", None, "tensor"),
        P(None, "tensor", "dp"),
        P(None, "tensor", "dp"),
        P(None, "tensor", "dp"),
        P(None, "tensor"),
        P(None, "tensor"),
        P(None, "tensor"),
        P(),
        P(),
        P(),
    )
    out_specs = (
        P(("dp", "tensor"), None),
        P(("dp", "tensor"), None),
        P("dp", None, "tensor"),
        P("dp", None, "tensor"),
        P("dp", None, "tensor"),
        P("dp", None, "tensor"),
        P("tensor", "dp"),
        P("tensor", "dp"),
        P("tensor", "dp"),
        P("tensor", "dp"),
        P("dp", None, "tensor"),
        P("dp", None, "tensor"),
        P("dp", None, "tensor"),
        P("dp", None, "tensor"),
        P(None, "tensor", "dp"),
        P(None, "tensor", "dp"),
        P(None, "tensor", "dp"),
        P(None, "tensor", "dp"),
        P(None, "tensor"),
        P(None, "tensor"),
        P("tensor"),
        P("tensor"),
        P(None, "tensor"),
        P(),
        P(),
        P(),
        P(),
        P(),
    )
    return jax.shard_map(
        on_device, mesh=mesh, in_specs=in_specs, out_specs=out_specs, check_vma=False
    )
```

```python
import functools

import jax
import jax.numpy as jnp
from jax import lax
from jax.experimental import pallas as pl
from jax.experimental.layout import Layout, with_layout_constraint
from jax.experimental.pallas import tpu as pltpu
from jax.sharding import PartitionSpec as P

HEAD_DIM = 128
QUERY_BLOCK = 512
STEP_COUNT = 10
LOG2E = 1.4426950408889634
MASKED = -1e30
VMEM_BYTES = 56 * 2**20
ROWS = (((1,), (1,)), ((), ()))
TOKENS = (((0,), (0,)), ((), ()))

norm_epsilon = 1e-05
beta_one = 0.9
beta_two = 0.999
adam_epsilon = 1e-06
decay_rate = 0.01
learn_rate = 0.5
trust_epsilon = 1e-06


def layer_norm(values, gain_row, shift_row):
    centre = values - jnp.mean(values, axis=-1, keepdims=True)
    spread = jnp.mean(centre * centre, axis=-1, keepdims=True)
    return centre * lax.rsqrt(spread + norm_epsilon) * gain_row + shift_row


def dot_as(left, right, dims, kind=jnp.float32):
    return lax.dot_general(left, right, dims, preferred_element_type=jnp.float32).astype(kind)


PLAIN = (((1,), (0,)), ((), ()))


def flip(index, mask):
    result = index
    bit = 1
    while bit <= mask:
        if mask & bit:
            result = result + bit - 2 * bit * lax.rem(lax.div(index, bit), 2)
        bit *= 2
    return result


def greet_all(peers):
    barrier = pltpu.get_barrier_semaphore()
    for peer in peers:
        pl.semaphore_signal(barrier, inc=1, device_id=peer, device_id_type=pl.DeviceIdType.MESH)
    pl.semaphore_wait(barrier, len(peers))


def remote(source, target, send, receive, device):
    return pltpu.make_async_remote_copy(
        src_ref=source,
        dst_ref=target,
        send_sem=send,
        recv_sem=receive,
        device_id=device,
        device_id_type=pl.DeviceIdType.MESH,
    )


def everyone(groups, slices):
    count = groups * slices
    me = lax.axis_index("dp") * slices + lax.axis_index("tensor")

    def anyone(step):
        other = lax.rem(me + step, count)
        return (lax.div(other, slices), lax.rem(other, slices))

    def greet():
        barrier = pltpu.get_barrier_semaphore()

        def signal(step, carry):
            pl.semaphore_signal(
                barrier, inc=1, device_id=anyone(step), device_id_type=pl.DeviceIdType.MESH
            )
            return carry

        lax.fori_loop(1, count, signal, 0)
        pl.semaphore_wait(barrier, count - 1)

    return anyone, greet


def spread_sum(
    values_ref, out_ref, held, send_one, recv_one, send_two, recv_two, anyone, groups, slices
):
    count = groups * slices
    me = lax.axis_index("dp") * slices + lax.axis_index("tensor")

    def first(step):
        source = values_ref.at[lax.rem(me + step, count)]
        return remote(
            source, held.at[step], send_one.at[step], recv_one.at[step], anyone(step)
        )

    def second(step):
        return remote(
            held.at[0], out_ref.at[me], send_two.at[step], recv_two.at[step], anyone(step)
        )

    def each(action):
        lax.fori_loop(1, count, lambda step, carry: (action(step), carry)[1], 0)

    def wait_first(step, total):
        first(step).wait()
        return total + held[step]

    def start():
        each(lambda step: first(step).start())

    def middle():
        total = lax.fori_loop(1, count, wait_first, values_ref[me])
        held[0] = total
        out_ref[me] = total
        each(lambda step: second(step).start())

    def end():
        each(lambda step: second(step).wait())

    return start, middle, end


def sum_scratch(count):
    dma = pltpu.SemaphoreType.DMA
    return [pltpu.VMEM((count, 8, 128), jnp.float32)] + [dma((count,))] * 4


def direct_masks(quads):
    return [2, 4] if quads == 4 else [2 * m for m in range(1, quads)]


def two_hops(quads):
    return [(2, 0, 4), (4, 1, 2)] if quads == 4 else []


def square_reduce(quads, rows, across, send, receive, parts, sums, hop_buf, in_buf):
    masks = direct_masks(quads)
    half_rows = rows // 2

    def landing(at, half):
        return in_buf.at[at, pl.ds(half * half_rows, half_rows)]

    def hop(half):
        goal = 4 if half == 0 else 2
        return remote(
            parts(3, half), hop_buf.at[half], send.at[half], receive.at[half], across(goal)
        )

    def plain(at, half, source):
        number = 2 + 2 * at + half
        return remote(
            source, landing(at, half), send.at[number], receive.at[number], across(masks[at])
        )

    def whole(at):
        return remote(
            parts(at + 1, None), in_buf.at[at], send.at[at], receive.at[at], across(masks[at])
        )

    def early(block):
        if quads != 4:
            whole(block - 1).start()
        elif block == 3:
            hop(0).start()
            hop(1).start()
        else:
            half = 1 if block == 1 else 0
            plain(block - 1, half, parts(block, half)).start()

    def middle():
        if quads != 4:
            return
        for block, half in ((1, 0), (2, 1)):
            hop(half).wait_recv()
            target = sums(block, half)
            target[...] = (
                target[...].astype(jnp.float32) + hop_buf[half].astype(jnp.float32)
            ).astype(jnp.bfloat16)
            plain(block - 1, half, target).start()

    def end():
        if quads != 4:
            for at in range(quads - 1):
                whole(at).wait()
            return
        for half in range(2):
            hop(half).wait_send()
            for block in (1, 2):
                plain(block - 1, half, parts(block, half)).wait()

    return early, middle, end


def pair_reduce(quads, me, across, block_of, near, far, send, receive, load_sem):
    copies = []
    for m in range(quads):
        copies.append(
            remote(
                block_of(flip(me, 2 * m + 1)), far.at[m], send.at[m], receive.at[m], across(1)
            )
        )
    loads = [
        pltpu.make_async_copy(block_of(flip(me, 2 * m)), near.at[m], load_sem.at[m])
        for m in range(quads)
    ]

    def start():
        for copy in copies + loads:
            copy.start()

    def finish(m):
        loads[m].wait()
        copies[m].wait()
        near[m] = (near[m].astype(jnp.float32) + far[m].astype(jnp.float32)).astype(near.dtype)

    return start, finish


def reduce_scratch(quads, rows, width):
    dma = pltpu.SemaphoreType.DMA
    return [
        pltpu.VMEM((2, rows // 2, width), jnp.bfloat16),
        pltpu.VMEM((len(direct_masks(quads)), rows, width), jnp.bfloat16),
        dma((max(6, quads - 1),)),
        dma((max(6, quads - 1),)),
    ]


def forward_kernel(
    q_ref, k_ref, v_ref, bias_ref, back_ref, wide_ref, total_ref, own_ref, back_out,
    held, send_sem, recv_sem, keep_sem, e_send, e_recv,
    *, heads, blocks, size, slices, groups
):
    factor = HEAD_DIM**-0.5 * LOG2E
    head = pl.program_id(0)
    which = pl.program_id(1)
    me = lax.axis_index("dp")
    place = lax.axis_index("tensor")
    rows = own_ref.shape[0]
    queries = q_ref[...]
    masks = direct_masks(groups // 2)
    hops = two_hops(groups // 2)

    def across(mask):
        return (flip(me, mask), place)

    def e_hops():
        result = []
        half_rows = rows // 2
        for number, (mask, half, goal) in enumerate(hops):
            start = (masks.index(mask) + 1) * rows + half * half_rows
            source = back_ref.at[pl.ds(start, half_rows)]
            target = back_out.at[pl.ds(3 * rows + half * half_rows, half_rows)]
            result.append(
                remote(source, target, e_send.at[number], e_recv.at[number], across(goal))
            )
        return result

    @pl.when(jnp.logical_and(head == 0, which == 0))
    def _():
        greet_all(
            [(me, lax.rem(place + step, slices)) for step in range(1, slices)]
            + [across(goal) for _, _, goal in hops]
        )
        for copy in e_hops():
            copy.start()

    for last in range(blocks):

        @pl.when(which == last)
        def _():
            parts = []
            peak = None
            for at in range(last + 1):
                keys = slice(at * size, (at + 1) * size)
                scores = dot_as(queries, k_ref[keys, :], ROWS) + bias_ref[0:1, keys]
                if at == last:
                    row = lax.broadcasted_iota(jnp.int32, (size, size), 0)
                    col = lax.broadcasted_iota(jnp.int32, (size, size), 1)
                    scores = jnp.where(col <= row, scores, MASKED)
                top = jnp.max(scores, axis=1, keepdims=True)
                peak = top if peak is None else jnp.maximum(peak, top)
                parts.append(scores)
            low = peak * factor
            total = None
            context = None
            for at in range(last + 1):
                keys = slice(at * size, (at + 1) * size)
                weights = jnp.exp2(parts[at] * factor - low)
                more = jnp.sum(weights, axis=1, keepdims=True)
                total = more if total is None else total + more
                term = dot_as(weights.astype(jnp.bfloat16), v_ref[keys, :], PLAIN)
                context = term if context is None else context + term
            context = context * (1.0 / total)
            held[head, last * size : (last + 1) * size, :] = context.astype(jnp.bfloat16)
            wide_ref[...] = context
            logs = jnp.broadcast_to(low + jnp.log2(total), (size, 128))
            total_ref[...] = jnp.transpose(logs)[0:1, :].reshape(1, 1, size)

    def to_owner(owner, number):
        step = lax.rem(owner - place + slices, slices)
        return remote(
            held.at[number, pl.ds(pl.multiple_of(owner * rows, rows), rows)],
            own_ref.at[:, columns(place, number)],
            send_sem.at[step, number],
            recv_sem.at[step, number],
            (me, owner),
        )

    def columns(other, number):
        start = (other * heads + number) * HEAD_DIM
        return pl.ds(pl.multiple_of(start, HEAD_DIM), HEAD_DIM)

    def stay(number):
        return pltpu.make_async_copy(
            held.at[number, pl.ds(pl.multiple_of(place * rows, rows), rows)],
            own_ref.at[:, columns(place, number)],
            keep_sem.at[number],
        )

    for part in range(size // rows):
        owner = which * (size // rows) + part
        pl.when(owner == place)(lambda: stay(head).start())
        pl.when(owner != place)(lambda: to_owner(owner, head).start())

    @pl.when(jnp.logical_and(head == heads - 1, which == blocks - 1))
    def _():
        for copy in e_hops():
            copy.wait()
        for number in range(heads):
            stay(number).wait()
            for step in range(1, slices):
                to_owner(lax.rem(place + step, slices), number).wait_send()
                source = lax.rem(place + slices - step, slices)
                remote(
                    held.at[number, pl.ds(0, rows)],
                    own_ref.at[:, columns(source, number)],
                    send_sem.at[step, number],
                    recv_sem.at[step, number],
                    (me, source),
                ).wait_recv()


def attend_forward(mixed, bias_row, back, rows):
    slices = lax.axis_size("tensor")
    groups = lax.axis_size("dp")
    hops = max(1, len(two_hops(groups // 2)))
    length = mixed.shape[0]
    cols = mixed.shape[1] // 3
    heads = cols // HEAD_DIM
    size = QUERY_BLOCK
    blocks = length // size
    part = pl.BlockSpec((size, HEAD_DIM), lambda h, i: (i, h))
    keys = pl.BlockSpec((length, HEAD_DIM), lambda h, i: (0, heads + h))
    values = pl.BlockSpec((length, HEAD_DIM), lambda h, i: (0, 2 * heads + h))
    dma = pltpu.SemaphoreType.DMA
    return pl.pallas_call(
        functools.partial(
            forward_kernel, heads=heads, blocks=blocks, size=size, slices=slices, groups=groups
        ),
        grid=(heads, blocks),
        in_specs=[
            part,
            keys,
            values,
            pl.BlockSpec((1, length), lambda h, i: (0, 0)),
            pl.BlockSpec(memory_space=pltpu.HBM),
        ],
        out_specs=[
            part,
            pl.BlockSpec((1, 1, size), lambda h, i: (h, 0, i)),
            pl.BlockSpec(memory_space=pltpu.HBM),
            pl.BlockSpec(memory_space=pltpu.HBM),
        ],
        input_output_aliases={4: 3},
        out_shape=[
            jax.ShapeDtypeStruct((length, cols), jnp.float32),
            jax.ShapeDtypeStruct((heads, 1, length), jnp.float32),
            jax.ShapeDtypeStruct((rows, slices * cols), jnp.bfloat16),
            jax.ShapeDtypeStruct(back.shape, back.dtype),
        ],
        scratch_shapes=[
            pltpu.VMEM((heads, length, HEAD_DIM), jnp.bfloat16),
            dma((slices, heads)),
            dma((slices, heads)),
            dma((heads,)),
            dma((hops,)),
            dma((hops,)),
        ],
        compiler_params=pltpu.CompilerParams(
            collective_id=3, has_side_effects=True, vmem_limit_bytes=VMEM_BYTES
        ),
        cost_estimate=pl.CostEstimate(
            flops=4 * length * length * cols,
            bytes_accessed=100 * 2**20,
            transcendentals=heads * length * length // 2,
        ),
        name="attend_forward",
    )(mixed, mixed, mixed, bias_row, back)


def backward_kernel(
    low_ref, out_ref, mixed_ref, wide_ref, total_ref, bias_ref, part_ref, thin_ref,
    grad_ref, layer_ref, thin_sum,
    sent, back_buf, sum_ref, half_buf, own_buf, hop_buf, in_buf, send, receive,
    send_sem, recv_sem, load_sem, thin_send, thin_recv, thin_load,
    *, blocks, size, slices, groups
):
    scale = HEAD_DIM**-0.5
    factor = scale * LOG2E
    me = lax.axis_index("dp")
    place = lax.axis_index("tensor")
    rows = low_ref.shape[0]
    cols = back_buf.shape[1]
    heads = cols // HEAD_DIM
    quads = groups // 2
    half_rows = rows // 2

    def across(mask):
        return (flip(me, mask), place)

    def parts(block, side):
        if side is None:
            return part_ref.at[pl.ds(block * rows, rows)]
        return part_ref.at[pl.ds(block * rows + side * half_rows, half_rows)]

    def sums(block, side):
        return half_buf.at[side]

    loads = [pltpu.make_async_copy(parts(0, None), own_buf, load_sem.at[0])]
    if quads == 4:
        for block, side in ((1, 0), (2, 1)):
            loads.append(
                pltpu.make_async_copy(parts(block, side), half_buf.at[side], load_sem.at[1 + side])
            )
    for copy in loads:
        copy.start()
    greet_all(
        [(me, lax.rem(place + step, slices)) for step in range(1, slices)]
        + [(lax.rem(me + step, groups), place) for step in range(1, groups)]
    )
    early, middle, end = square_reduce(
        quads, rows, across, send, receive, parts, sums, hop_buf, in_buf
    )

    thin_rows, thin_cols = thin_ref.shape[0], thin_sum.shape[1]

    def thin_columns(other):
        return thin_ref.at[:, pl.ds(pl.multiple_of(other * thin_cols, thin_cols), thin_cols)]

    def thin_place(other):
        return thin_sum.at[pl.ds(pl.multiple_of(other * thin_rows, thin_rows), thin_rows)]

    def thin_to(step):
        other = lax.rem(me + step, groups)
        return remote(
            thin_columns(other), thin_place(me), thin_send.at[step], thin_recv.at[step],
            (other, place),
        )

    def thin_from(step):
        other = lax.rem(me + groups - step, groups)
        return remote(
            thin_columns(other), thin_place(other), thin_send.at[step], thin_recv.at[step],
            (other, place),
        )

    thin_own = pltpu.make_async_copy(thin_columns(me), thin_place(me), thin_load)
    early(quads - 1)

    def span(start, size):
        return pl.ds(pl.multiple_of(start, size), size)

    def product(owner):
        return dot_as(low_ref[...], out_ref[span(owner * cols, cols), :], ROWS, jnp.bfloat16)

    def to_owner(step, head):
        return remote(
            sent.at[step - 1, :, span(head * HEAD_DIM, HEAD_DIM)],
            back_buf.at[span(place * rows, rows), span(head * HEAD_DIM, HEAD_DIM)],
            send_sem.at[step, head],
            recv_sem.at[step, head],
            (me, lax.rem(place + step, slices)),
        )

    for step in range(1, slices):
        sent[step - 1] = product(lax.rem(place + step, slices))
    for head in range(heads):
        for step in range(1, slices):
            to_owner(step, head).start()
    back_buf[span(place * rows, rows), :] = product(place)

    def one_head(head, carry):
        for step in range(1, slices):
            source = lax.rem(place + slices - step, slices)
            remote(
                sent.at[step - 1, :, span(head * HEAD_DIM, HEAD_DIM)],
                back_buf.at[span(source * rows, rows), span(head * HEAD_DIM, HEAD_DIM)],
                send_sem.at[step, head],
                recv_sem.at[step, head],
                (me, source),
            ).wait_recv()
        here = span(head * HEAD_DIM, HEAD_DIM)
        key_here = span(cols + head * HEAD_DIM, HEAD_DIM)
        value_here = span(2 * cols + head * HEAD_DIM, HEAD_DIM)
        inner = []
        for at in range(blocks):
            part = slice(at * size, (at + 1) * size)
            pairs = back_buf[part, here].astype(jnp.float32) * wide_ref[part, here]
            inner.append(jnp.sum(jnp.transpose(pairs), axis=0, keepdims=True))
        for key_at in range(blocks):
            keys = slice(key_at * size, (key_at + 1) * size)
            key_rows = mixed_ref[keys, key_here]
            values = mixed_ref[keys, value_here]
            bias = bias_ref[keys, 0:1]
            back_keys = None
            back_values = None
            for query_at in range(key_at, blocks):
                part = slice(query_at * size, (query_at + 1) * size)
                queries = mixed_ref[part, here]
                back = back_buf[part, here]
                level = dot_as(key_rows, queries, ROWS) * factor - total_ref[head, 0:1, part] + bias
                if query_at == key_at:
                    row = lax.broadcasted_iota(jnp.int32, (size, size), 0)
                    col = lax.broadcasted_iota(jnp.int32, (size, size), 1)
                    level = jnp.where(row <= col, level, MASKED)
                chances = jnp.exp2(level)
                back_chances = dot_as(values, back, ROWS)
                back_scores = (chances * (back_chances - inner[query_at])).astype(jnp.bfloat16)
                more_values = dot_as(chances.astype(jnp.bfloat16), back, PLAIN)
                more_keys = dot_as(back_scores, queries, PLAIN)
                more_queries = dot_as(back_scores, key_rows, TOKENS)
                if key_at == 0:
                    sum_ref[part, :] = more_queries
                else:
                    sum_ref[part, :] += more_queries
                back_keys = more_keys if back_keys is None else back_keys + more_keys
                back_values = more_values if back_values is None else back_values + more_values
            grad_ref[keys, key_here] = (back_keys * scale).astype(jnp.bfloat16)
            grad_ref[keys, value_here] = back_values.astype(jnp.bfloat16)
        grad_ref[:, here] = (sum_ref[...] * scale).astype(jnp.bfloat16)

        @pl.when(head == 0)
        def _():
            for block in range(1, quads - 1):
                early(block)

        @pl.when(head == heads // 2 - 1)
        def _():
            for copy in loads:
                copy.wait()
            middle()

        @pl.when(head == min(2, heads - 1))
        def _():
            thin_own.start()
            for step in range(1, groups):
                thin_to(step).start()

        return carry

    lax.fori_loop(0, heads, one_head, 0)
    end()
    total = own_buf[...].astype(jnp.float32)
    for at in range(len(direct_masks(quads))):
        total = total + in_buf[at].astype(jnp.float32)
    layer_ref[...] = total
    thin_own.wait()
    for step in range(1, groups):
        thin_from(step).wait_recv()
        thin_to(step).wait_send()
    for head in range(heads):
        for step in range(1, slices):
            to_owner(step, head).wait_send()


def attend_backward(back_low, outward, mixed, wide, totals, bias_column, widened, thin):
    slices = lax.axis_size("tensor")
    groups = lax.axis_size("dp")
    quads = groups // 2
    rows, width = back_low.shape
    length, cols = wide.shape
    heads = cols // HEAD_DIM
    size = QUERY_BLOCK
    vmem = pl.BlockSpec(memory_space=pltpu.VMEM)
    hbm = pl.BlockSpec(memory_space=pltpu.HBM)
    dma = pltpu.SemaphoreType.DMA
    low = jnp.bfloat16
    return pl.pallas_call(
        functools.partial(
            backward_kernel, blocks=length // size, size=size, slices=slices, groups=groups
        ),
        in_specs=[vmem] * 6 + [hbm] * 2,
        out_specs=[vmem, vmem, hbm],
        out_shape=[
            jax.ShapeDtypeStruct((length, 3 * cols), low),
            jax.ShapeDtypeStruct((rows, width), jnp.float32),
            jax.ShapeDtypeStruct((groups * thin.shape[0], width // groups), low),
        ],
        scratch_shapes=[
            pltpu.VMEM((slices - 1, rows, cols), low),
            pltpu.VMEM((length, cols), low),
            pltpu.VMEM((length, HEAD_DIM), jnp.float32),
            pltpu.VMEM((2, rows // 2, width), low),
            pltpu.VMEM((rows, width), low),
        ]
        + reduce_scratch(quads, rows, width)
        + [dma((slices, heads)), dma((slices, heads)), dma((3,))]
        + [dma((groups,)), dma((groups,)), dma],
        compiler_params=pltpu.CompilerParams(
            collective_id=4, has_side_effects=True, vmem_limit_bytes=VMEM_BYTES
        ),
        cost_estimate=pl.CostEstimate(
            flops=10 * length * length * cols,
            bytes_accessed=150 * 2**20,
            transcendentals=heads * length * length // 2,
        ),
        name="attend_backward",
    )(back_low, outward, mixed, wide, totals, bias_column, widened, thin)


def back_kernel(
    e_ref, slope_ref, thin_ref, wide_ref, grad_ref, act_ref,
    own_ref, dhid_ref, sum_ref, layer_ref, share_ref,
    thin_buf, wide_buf, e_buf, slope_buf, dhid_buf, part_buf, hop_buf, in_buf, send, receive,
    load_sem, pair_sem, e_sem, slope_sem, dhid_sem, act_sem, layer_sem, grad_send, grad_recv, grad_sem,
    *, groups, slices
):
    quads = groups // 2
    me = lax.axis_index("dp")
    place = lax.axis_index("tensor")
    rows, width = own_ref.shape
    units = wide_buf.shape[1]
    half = units // 2
    tile = min(512, half)
    slab = min(512, width)

    def across(mask):
        return (flip(me, mask), place)

    def load_block(number, at):
        target = pl.ds(at * rows, rows)
        return (
            pltpu.make_async_copy(
                e_ref.at[target], e_buf.at[number % 2, :, pl.ds(0, width)], e_sem.at[number]
            ),
            pltpu.make_async_copy(
                slope_ref.at[target], slope_buf.at[number % 2], slope_sem.at[number]
            ),
        )

    order = [quads - 1] + list(range(1, quads - 1)) + [0]
    thin_load = pltpu.make_async_copy(thin_ref, thin_buf.at[pl.ds(0, half)], load_sem.at[0])
    thin_load.start()
    for copy in load_block(0, order[0]):
        copy.start()
    wide_load = pltpu.make_async_copy(wide_ref, wide_buf, load_sem.at[1])
    wide_load.start()
    greet_all(
        [across(mask) for mask in [1] + direct_masks(quads)]
        + [(me, lax.rem(place + step, slices)) for step in range(1, slices)]
    )
    span = share_ref.shape[1]

    def grad_rows(owner):
        return grad_ref.at[pl.ds(pl.multiple_of(owner * span, span), span)]

    def grad_to(step):
        owner = lax.rem(place + step, slices)
        return remote(
            grad_rows(owner), share_ref.at[step], grad_send.at[step], grad_recv.at[step],
            (me, owner),
        )

    for step in range(1, slices):
        grad_to(step).start()
    grad_own = pltpu.make_async_copy(grad_rows(place), share_ref.at[0], grad_sem)
    grad_own.start()
    pair = remote(
        thin_ref, thin_buf.at[pl.ds(half, half)], pair_sem.at[0], pair_sem.at[1], across(1)
    )
    pair.start()

    half_rows = rows // 2

    def parts(block, side):
        if side is None:
            return part_buf.at[block - 1]
        return part_buf.at[block - 1, pl.ds(side * half_rows, half_rows)]

    early, middle, end = square_reduce(
        quads, rows, across, send, receive, parts, parts, hop_buf, in_buf
    )
    sum_ref[...] = jnp.zeros_like(sum_ref)
    stores = []
    for number, at in enumerate(order):
        slot = number % 2
        if number + 1 < quads:
            for copy in load_block(number + 1, order[number + 1]):
                copy.start()
        if number == 0:
            thin_load.wait()
        for copy in load_block(number, at):
            copy.wait()
        if number >= 2:
            stores[number - 2].wait()

        def back_tile(index, carry):
            columns = pl.ds(pl.multiple_of(index * tile, tile), tile)
            back = dot_as(e_buf[slot, :, :width], thin_buf[columns, :], ROWS)
            back = (back * slope_buf[slot, :, columns]).astype(jnp.bfloat16)
            dhid_buf[slot, :, columns] = back
            sum_ref[:, columns] += jnp.sum(back.astype(jnp.float32), axis=0, keepdims=True)
            return carry

        if number == 0:
            lax.fori_loop(0, half // tile, back_tile, 0)
            pair.wait_recv()
            lax.fori_loop(half // tile, units // tile, back_tile, 0)
            wide_load.wait()
        else:
            lax.fori_loop(0, units // tile, back_tile, 0)
        store = pltpu.make_async_copy(
            dhid_buf.at[slot, :, pl.ds(0, units)],
            dhid_ref.at[pl.ds(at * rows, rows)],
            dhid_sem.at[number],
        )
        store.start()
        stores.append(store)

        def slab_of(index, carry):
            here = pl.ds(pl.multiple_of(index * slab, slab), slab)
            product = dot_as(dhid_buf[slot, :, :units], wide_buf[here, :], ROWS)
            if at:
                part_buf[at - 1, :, here] = product.astype(jnp.bfloat16)
            else:
                own_ref[:, here] = product
            return carry

        lax.fori_loop(0, width // slab, slab_of, 0)
        if at:
            early(at)
        if number == quads - 2:
            middle()
    for store in stores[-2:]:
        store.wait()

    def load_act(number):
        return pltpu.make_async_copy(
            act_ref.at[pl.ds(number * rows, rows)],
            e_buf.at[number % 2, :, pl.ds(0, units)],
            act_sem.at[number],
        )

    outs = []
    load_act(0).start()
    for number in range(quads):
        slot = number % 2
        if number + 1 < quads:
            load_act(number + 1).start()
        load_act(number).wait()
        if number >= 2:
            outs[number - 2].wait()

        def out_of(index, carry):
            here = pl.ds(pl.multiple_of(index * slab, slab), slab)
            dhid_buf[slot, :, here] = dot_as(
                e_buf[slot, :, :units], thin_buf[:, here], PLAIN, jnp.bfloat16
            )
            return carry

        lax.fori_loop(0, width // slab, out_of, 0)
        out = pltpu.make_async_copy(
            dhid_buf.at[slot, :, pl.ds(0, width)],
            layer_ref.at[pl.ds(number * rows, rows)],
            layer_sem.at[number],
        )
        out.start()
        outs.append(out)
    end()
    for at in range(len(direct_masks(quads))):
        own_ref[...] += in_buf[at].astype(jnp.float32)
    pair.wait_send()
    for out in outs[-2:]:
        out.wait()
    for step in range(1, slices):
        grad_to(step).wait()
    grad_own.wait()


def back_step(back, slope, thin, wide, grad, active):
    groups = lax.axis_size("dp")
    slices = lax.axis_size("tensor")
    quads = groups // 2
    length, width = back.shape
    rows = length // quads
    units = slope.shape[1]
    dma = pltpu.SemaphoreType.DMA
    vmem = pl.BlockSpec(memory_space=pltpu.VMEM)
    hbm = pl.BlockSpec(memory_space=pltpu.HBM)
    low = jnp.bfloat16
    return pl.pallas_call(
        functools.partial(back_kernel, groups=groups, slices=slices),
        in_specs=[hbm] * 6,
        out_specs=[vmem, hbm, vmem, hbm, hbm],
        out_shape=[
            jax.ShapeDtypeStruct((rows, width), jnp.float32),
            jax.ShapeDtypeStruct((length, units), low),
            jax.ShapeDtypeStruct((1, units), jnp.float32),
            jax.ShapeDtypeStruct((length, width), low),
            jax.ShapeDtypeStruct((slices, grad.shape[0] // slices, width), low),
        ],
        scratch_shapes=[
            pltpu.VMEM((units, width), low),
            pltpu.VMEM((width, units), low),
            pltpu.VMEM((2, rows, max(units, width)), low),
            pltpu.VMEM((2, rows, units), jnp.float32),
            pltpu.VMEM((2, rows, max(units, width)), low),
            pltpu.VMEM((quads - 1, rows, width), low),
        ]
        + reduce_scratch(quads, rows, width)
        + [dma((2,)), dma((2,))] + [dma((quads,))] * 5
        + [dma((slices,)), dma((slices,)), dma],
        compiler_params=pltpu.CompilerParams(
            collective_id=5, has_side_effects=True, vmem_limit_bytes=60 * 2**20
        ),
        cost_estimate=pl.CostEstimate(
            flops=4 * length * width * units,
            bytes_accessed=150 * 2**20,
            transcendentals=0,
        ),
        name="back_step",
    )(back, slope, thin, wide, grad, active)


def open_kernel(
    x_ref, w_ref, c_ref, live_ref, norm_ref, bias_ref, small_ref, count_ref, wide_ref, thin_ref, out_ref,
    full_ref, weight_ref, mixed_ref, back_ref, all_ref, counts_ref, wide_all, thin_all, out_all,
    a_buf, w_buf, e_ref, wide_buf, thin_buf, out_buf,
    line_send, line_recv, small_send, small_recv, w_send, w_recv, pair_send, pair_recv,
    e_send, e_recv, local_sem, keep_sem, count_send, count_recv,
    wide_send, wide_recv, thin_send, thin_recv, out_send, out_recv, plane_send, plane_recv,
    run_send, run_recv,
    *, groups, slices, piece
):
    quads = groups // 2
    count = groups * slices
    me = lax.axis_index("dp")
    place = lax.axis_index("tensor")
    rows = x_ref.shape[0]
    share = w_buf.shape[0] // groups
    cols = w_buf.shape[1] // 3
    out_cols = out_all.shape[1] // groups
    masks = direct_masks(quads)
    hops = two_hops(quads)
    low = jnp.bfloat16
    raw = piece % 128 == 0

    def across(mask):
        return (flip(me, mask), place)

    def along(other):
        return (me, other)

    def beside(step):
        return (me, lax.rem(place + step, slices))

    def anyone(step):
        other = lax.rem(me * slices + place + step, count)
        return (lax.div(other, slices), lax.rem(other, slices))

    barrier = pltpu.get_barrier_semaphore()

    def greet(step, carry):
        pl.semaphore_signal(
            barrier, inc=1, device_id=anyone(step), device_id_type=pl.DeviceIdType.MESH
        )
        return carry

    lax.fori_loop(1, count, greet, 0)

    def w_rows(mask, half=None):
        start = flip(me, mask) * share
        if half is None:
            return w_buf.at[pl.ds(pl.multiple_of(start, share), share)]
        size = share // 2
        return w_buf.at[pl.ds(pl.multiple_of(start + half * size, size), size)]

    here = pl.ds(pl.multiple_of(me * share, share), share)
    for part in range(3):
        w_buf[here, part * cols : (part + 1) * cols] = w_ref[part].astype(low)
    chunk = 64

    def norm_chunk(at, carry):
        part = pl.ds(pl.multiple_of(at * chunk, chunk), chunk)
        normed = layer_norm(x_ref[part, :].astype(jnp.float32), norm_ref[0:1, :], norm_ref[1:2, :])
        target = pl.ds(pl.multiple_of(place * rows + at * chunk, chunk), chunk)
        a_buf[target, :] = normed.astype(low)
        return carry

    lax.fori_loop(0, rows // chunk, norm_chunk, 0)
    pl.semaphore_wait(barrier, count - 1)

    def a_rows(block):
        return a_buf.at[pl.ds(pl.multiple_of(block * rows, rows), rows)]

    def keep(block):
        return pltpu.make_async_copy(
            a_rows(block),
            full_ref.at[pl.ds(pl.multiple_of(block * rows, rows), rows)],
            keep_sem.at[block],
        )

    def a_half(block, half):
        size = rows // 2
        return a_buf.at[pl.ds(pl.multiple_of(block * rows + half * size, size), size)]

    def a_move(step, side, half, outgoing):
        back = step if outgoing else step + 1
        block = place - back if side == 0 else place + back
        towards = (side == 0) == outgoing
        return remote(
            a_half(block, half), a_half(block, half),
            line_send.at[side, half, step], line_recv.at[side, half, step],
            along(place + 1 if towards else place - 1),
        )

    def sends_right(step):
        return jnp.logical_and(place - step >= 0, place + 1 < slices)

    def sends_left(step):
        return jnp.logical_and(place + step < slices, place >= 1)

    for half in range(2):
        pl.when(sends_right(0))(lambda: a_move(0, 0, half, True).start())
        pl.when(sends_left(0))(lambda: a_move(0, 1, half, True).start())

    w_copies = []
    for at, mask in enumerate(masks):
        copy = remote(w_rows(0), w_rows(0), w_send.at[at], w_recv.at[at], across(mask))
        copy.start()
        w_copies.append(copy)

    e_ref[...] = (c_ref[...].astype(jnp.float32) * live_ref[...]).astype(low)
    keep(place).start()
    all_ref[place] = small_ref[...]
    small_copies = []
    for step in range(1, slices):
        copy = remote(
            small_ref, all_ref.at[place], small_send.at[step], small_recv.at[step], beside(step)
        )
        copy.start()
        small_copies.append(copy)

    def tell(step):
        return remote(
            count_ref, counts_ref.at[step], count_send.at[step], count_recv.at[step], anyone(step)
        )

    counts_ref[0] = count_ref[...]
    lax.fori_loop(1, count, lambda step, carry: (tell(step).start(), carry)[1], 0)

    out_here = pl.ds(pl.multiple_of(place * cols, cols), cols)
    out_buf[out_here, :] = out_ref[...].astype(low)
    out_copies = []
    for step in range(1, slices):
        target = out_buf.at[out_here]
        copy = remote(target, target, out_send.at[step], out_recv.at[step], beside(step))
        copy.start()
        out_copies.append(copy)

    for part in range(groups):
        if raw:
            row = part * piece // cols
            start = part * piece % cols
            wide_buf[part] = wide_ref[:, row, start : start + piece].astype(low)
            thin_buf[part] = thin_ref[row, start : start + piece, :].astype(low)
        else:
            wide_buf[part] = wide_ref[part]
            thin_buf[part] = thin_ref[part]
    thin_cols = thin_buf.shape[2]
    wide_here = wide_all.at[place, here]
    thin_here = thin_all.at[:, pl.ds(pl.multiple_of(me * thin_cols, thin_cols), thin_cols)]

    def wide_to(step):
        other = lax.rem(me + step, groups)
        return remote(
            wide_buf.at[other], wide_here, wide_send.at[step], wide_recv.at[step], (other, place)
        )

    def thin_to(step):
        other = lax.rem(me + step, groups)
        return remote(
            thin_buf.at[other], thin_here, thin_send.at[step], thin_recv.at[step], (other, place)
        )

    own_wide = pltpu.make_async_copy(wide_buf.at[me], wide_here, local_sem.at[2])
    own_wide.start()
    own_thin = pltpu.make_async_copy(thin_buf.at[me], thin_here, local_sem.at[3])
    own_thin.start()
    for step in range(1, groups):
        wide_to(step).start()

    pair_copies = []

    def to_pair(source):
        at = len(pair_copies)
        copy = remote(source, source, pair_send.at[at], pair_recv.at[at], across(1))
        copy.start()
        pair_copies.append(copy)

    to_pair(w_rows(0))
    for at, copy in enumerate(w_copies):
        remote(
            w_rows(masks[at]), w_rows(masks[at]), w_send.at[at], w_recv.at[at], across(masks[at])
        ).wait_recv()
    hop_copies = []
    for number, (mask, half, goal) in enumerate(hops):
        at = len(masks) + number
        source = w_rows(mask, half)
        copy = remote(source, source, w_send.at[at], w_recv.at[at], across(goal))
        copy.start()
        hop_copies.append(copy)
    for mask in masks:
        to_pair(w_rows(mask))

    own = pltpu.make_async_copy(e_ref, back_ref.at[pl.ds(0, rows)], local_sem.at[0])
    own.start()

    def e_moves():
        return [
            remote(
                e_ref, back_ref.at[pl.ds((at + 1) * rows, rows)], e_send.at[at], e_recv.at[at],
                across(mask),
            )
            for at, mask in enumerate(masks)
        ]

    for number, (mask, half, goal) in enumerate(hops):
        at = len(masks) + number
        landed = w_rows(2 + 4, half)
        remote(landed, landed, w_send.at[at], w_recv.at[at], across(goal)).wait_recv()
        to_pair(landed)
    sources = [0] + masks
    for at, mask in enumerate(sources):
        landed = w_rows(mask + 1)
        remote(landed, landed, pair_send.at[at], pair_recv.at[at], across(1)).wait_recv()
    for number, (mask, half, goal) in enumerate(hops):
        at = len(sources) + number
        landed = w_rows(2 + 4 + 1, half)
        remote(landed, landed, pair_send.at[at], pair_recv.at[at], across(1)).wait_recv()
    weights_out = pltpu.make_async_copy(w_buf, weight_ref, local_sem.at[1])
    weights_out.start()

    def multiply(block):
        where = pl.ds(pl.multiple_of(block * rows, rows), rows)
        left = a_buf[where, :]
        for part in range(3):
            columns = slice(part * cols, (part + 1) * cols)
            product = dot_as(left, w_buf[:, columns], PLAIN) + bias_ref[0:1, columns]
            mixed_ref[where, columns] = product.astype(low)

    multiply(place)

    def out_at(mask, half=None):
        start = pl.multiple_of(flip(me, mask) * out_cols, out_cols)
        size = out_all.shape[0] // 2
        if half is None:
            return out_all.at[:, pl.ds(start, out_cols)]
        return out_all.at[half * size : (half + 1) * size, pl.ds(start, out_cols)]

    own_out = pltpu.make_async_copy(out_buf, out_at(0), local_sem.at[4])

    def plane(at, source, target, device):
        return remote(source, target, plane_send.at[at], plane_recv.at[at], device)

    def plane_first():
        return [
            plane(at, out_buf, out_at(0), across(mask)) for at, mask in enumerate([1] + masks)
        ]

    def plane_landed():
        return [
            plane(at, out_buf, out_at(mask), across(mask)) for at, mask in enumerate([1] + masks)
        ]

    def plane_hops():
        return [
            plane(1 + len(masks) + number, out_at(mask, half), out_at(mask, half), across(goal))
            for number, (mask, half, goal) in enumerate(hops)
        ]

    def plane_pairs():
        return [
            plane(1 + len(masks) + len(hops) + at, out_at(mask), out_at(mask), across(1))
            for at, mask in enumerate(masks)
        ]

    def plane_last():
        return [
            plane(
                1 + 2 * len(masks) + len(hops) + number, out_at(6, half), out_at(6, half), across(1)
            )
            for number, (mask, half, goal) in enumerate(hops)
        ]

    def wide_move(step, side, half, outgoing):
        back = step if outgoing else step + 1
        block = place - back if side == 0 else place + back
        towards = (side == 0) == outgoing
        size = wide_all.shape[1] // 2
        part = wide_all.at[block, pl.ds(half * size, size)]
        return remote(
            part, part, run_send.at[side, half, step], run_recv.at[side, half, step],
            along(place + 1 if towards else place - 1),
        )

    def wide_arrived():
        own_wide.wait()
        for step in range(1, groups):
            other = lax.rem(me + groups - step, groups)
            wide_from = wide_all.at[
                place, pl.ds(pl.multiple_of(other * share, share), share)
            ]
            remote(
                wide_buf.at[other], wide_from, wide_send.at[step], wide_recv.at[step],
                (other, place),
            ).wait_recv()
        for half in range(2):
            pl.when(sends_right(0))(lambda: wide_move(0, 0, half, True).start())
            pl.when(sends_left(0))(lambda: wide_move(0, 1, half, True).start())

    def pass_on(step, carry):
        got_left = place - 1 - step >= 0
        got_right = place + 1 + step < slices

        for half in range(2):
            for side, got, sends in ((0, got_left, sends_right), (1, got_right, sends_left)):

                @pl.when(got)
                def _():
                    a_move(step, side, half, False).wait_recv()

                    @pl.when(jnp.logical_and(step + 1 < slices - 1, sends(step + 1)))
                    def _():
                        a_move(step + 1, side, half, True).start()

        pl.when(got_left)(lambda: keep(place - 1 - step).start())
        pl.when(got_right)(lambda: keep(place + 1 + step).start())

        @pl.when(step == 0)
        def _():
            for copy in out_copies:
                copy.wait_recv()
            own_out.start()
            for copy in plane_first():
                copy.start()
            for step_to in range(1, groups):
                thin_to(step_to).start()
            for copy in e_moves():
                copy.start()

        @pl.when(got_left)
        def _():
            multiply(place - 1 - step)

        @pl.when(got_right)
        def _():
            multiply(place + 1 + step)

        @pl.when(step == 1)
        def _():
            wide_arrived()
            for copy in plane_landed():
                copy.wait_recv()
            for copy in plane_hops() + plane_pairs():
                copy.start()

        return carry

    lax.fori_loop(0, slices - 1, pass_on, 0)

    def wide_on(step, carry):
        gots = (place - 1 - step >= 0, place + 1 + step < slices)
        for half in range(2):
            for side, sends in ((0, sends_right), (1, sends_left)):

                @pl.when(gots[side])
                def _():
                    wide_move(step, side, half, False).wait_recv()

                    @pl.when(jnp.logical_and(step + 1 < slices - 1, sends(step + 1)))
                    def _():
                        wide_move(step + 1, side, half, True).start()

        return carry

    lax.fori_loop(0, slices - 1, wide_on, 0)

    for number, (mask, half, goal) in enumerate(hops):
        at = 1 + len(masks) + number
        plane(at, out_at(6, half), out_at(6, half), across(goal)).wait_recv()
    for copy in plane_last():
        copy.start()
    for at, mask in enumerate(masks):
        landed = out_at(mask + 1)
        plane(1 + len(masks) + len(hops) + at, landed, landed, across(1)).wait_recv()
    for number, (mask, half, goal) in enumerate(hops):
        landed = out_at(7, half)
        plane(1 + 2 * len(masks) + len(hops) + number, landed, landed, across(1)).wait_recv()
    for copy in plane_first() + plane_hops() + plane_pairs() + plane_last():
        copy.wait_send()
    for at, mask in enumerate(masks):
        landed = back_ref.at[pl.ds((at + 1) * rows, rows)]
        remote(e_ref, landed, e_send.at[at], e_recv.at[at], across(mask)).wait_recv()
    for copy in e_moves() + w_copies + hop_copies + pair_copies + out_copies:
        copy.wait_send()
    for copy in small_copies:
        copy.wait()
    for step in range(1, groups):
        other = lax.rem(me + groups - step, groups)
        thin_from = thin_all.at[
            :, pl.ds(pl.multiple_of(other * thin_cols, thin_cols), thin_cols)
        ]
        device = (other, place)
        remote(
            thin_buf.at[other], thin_from, thin_send.at[step], thin_recv.at[step], device
        ).wait_recv()
        wide_to(step).wait_send()
        thin_to(step).wait_send()
    lax.fori_loop(1, count, lambda step, carry: (tell(step).wait(), carry)[1], 0)
    for copy in (own, weights_out, own_thin, own_out):
        copy.wait()

    def finish(step, carry):
        for half in range(2):
            pl.when(sends_right(step))(lambda: a_move(step, 0, half, True).wait_send())
            pl.when(sends_left(step))(lambda: a_move(step, 1, half, True).wait_send())
            pl.when(sends_right(step))(lambda: wide_move(step, 0, half, True).wait_send())
            pl.when(sends_left(step))(lambda: wide_move(step, 1, half, True).wait_send())
        return carry

    lax.fori_loop(0, slices - 1, finish, 0)
    for block in range(slices):
        keep(block).wait()


def open_step(
    tokens, inward, cotangent, live, norms, bias, small, living, widening, narrowing, outward
):
    groups = lax.axis_size("dp")
    slices = lax.axis_size("tensor")
    count = groups * slices
    quads = groups // 2
    rows, width = tokens.shape
    share, _, cols = inward.shape
    piece = 4 * cols // groups
    out_cols = outward.shape[1]
    hops = len(two_hops(quads))
    direct = len(direct_masks(quads))
    dma = pltpu.SemaphoreType.DMA
    vmem = pl.BlockSpec(memory_space=pltpu.VMEM)
    hbm = pl.BlockSpec(memory_space=pltpu.HBM)
    low = jnp.bfloat16
    wide = jnp.float32
    if piece % 128:
        widening = widening.astype(low).reshape(share, groups, piece).transpose(1, 0, 2)
        narrowing = narrowing.astype(low).reshape(groups, piece, out_cols)
    shape = jax.ShapeDtypeStruct
    planes = 1 + 2 * direct + 2 * hops
    return pl.pallas_call(
        functools.partial(open_kernel, groups=groups, slices=slices, piece=piece),
        in_specs=[vmem] * 11,
        out_specs=[hbm, hbm, vmem, hbm, vmem, vmem, hbm, hbm, hbm],
        out_shape=[
            shape((slices * rows, width), low),
            shape((width, 3 * cols), low),
            shape((slices * rows, 3 * cols), low),
            shape((quads * rows, width), low),
            shape((slices,) + small.shape, wide),
            shape((count, 8, 128), wide),
            shape((slices, width, piece), low),
            shape((piece, width), low),
            shape((width, width), low),
        ],
        scratch_shapes=[
            pltpu.VMEM((slices * rows, width), low),
            pltpu.VMEM((width, 3 * cols), low),
            pltpu.VMEM((rows, width), low),
            pltpu.VMEM((groups, share, piece), low),
            pltpu.VMEM((groups, piece, out_cols), low),
            pltpu.VMEM((slices * cols, out_cols), low),
            dma((2, 2, slices)),
            dma((2, 2, slices)),
            dma((slices,)),
            dma((slices,)),
            dma((direct + hops,)),
            dma((direct + hops,)),
            dma((1 + direct + hops,)),
            dma((1 + direct + hops,)),
            dma((direct,)),
            dma((direct,)),
            dma((5,)),
            dma((slices,)),
            dma((count,)),
            dma((count,)),
            dma((groups,)),
            dma((groups,)),
            dma((groups,)),
            dma((groups,)),
            dma((slices,)),
            dma((slices,)),
            dma((planes,)),
            dma((planes,)),
            dma((2, 2, slices)),
            dma((2, 2, slices)),
        ],
        compiler_params=pltpu.CompilerParams(
            collective_id=1, has_side_effects=True, vmem_limit_bytes=VMEM_BYTES
        ),
        cost_estimate=pl.CostEstimate(
            flops=2 * slices * rows * width * 3 * cols,
            bytes_accessed=400 * 2**20,
            transcendentals=0,
        ),
        name="open_step",
    )(
        tokens,
        inward.transpose(1, 0, 2),
        cotangent,
        live,
        norms,
        bias,
        small,
        living,
        widening,
        narrowing,
        outward,
    )


def hidden_gather_kernel(
    b_ref, weight_ref, bias_ref, all_ref, act_ref, slope_ref, full_ref,
    b_buf, w_buf, act_buf, slope_buf,
    b_send, b_recv, keep_sem, act_sem, slope_sem, w_sem, pair_sem, out_sem,
    *, groups
):
    quads = groups // 2
    me = lax.axis_index("dp")
    place = lax.axis_index("tensor")
    rows = b_ref.shape[0]
    tiles, _, tile = weight_ref.shape
    masks = direct_masks(quads)
    hops = two_hops(quads)
    half_rows = rows // 2

    def across(mask):
        return (flip(me, mask), place)

    load = pltpu.make_async_copy(weight_ref, w_buf.at[pl.ds(0, tiles)], w_sem)
    load.start()
    greet_all([across(mask) for mask in [1] + masks])

    def block(at):
        return b_buf.at[pl.ds(at * rows, rows)]

    def piece(at, half):
        return b_buf.at[pl.ds(at * rows + half * half_rows, half_rows)]

    copies = []
    for at, mask in enumerate(masks):
        copy = remote(b_ref, block(at + 1), b_send.at[at], b_recv.at[at], across(mask))
        copy.start()
        copies.append(copy)
    pair = remote(
        weight_ref, w_buf.at[pl.ds(tiles, tiles)], pair_sem.at[0], pair_sem.at[1], across(1)
    )
    pair.start()
    b_buf[0:rows, :] = b_ref[...]
    keeps = []
    stores = []

    def keep(at):
        copy = pltpu.make_async_copy(
            block(at), all_ref.at[pl.ds(at * rows, rows)], keep_sem.at[at]
        )
        copy.start()
        keeps.append(copy)

    def multiply(at, first, amount):
        def part(number, carry):
            columns = pl.ds(pl.multiple_of(number * tile, tile), tile)
            hidden = (
                dot_as(b_buf[at * rows : (at + 1) * rows, :], w_buf[number], PLAIN)
                + bias_ref[0:1, columns]
            )
            root = 0.7978845608028654
            square = hidden * hidden
            bent = jnp.tanh(root * hidden * (1.0 + 0.044715 * square))
            half = 0.5 * (1.0 + bent)
            act_buf[at % 2, :, columns] = (hidden * half).astype(jnp.bfloat16)
            slope_buf[at % 2, :, columns] = half + 0.5 * hidden * (1.0 - bent * bent) * (
                root * (1.0 + 3.0 * 0.044715 * square)
            )
            return carry

        lax.fori_loop(first, first + amount, part, 0)

    def store(at):
        target = pl.ds(at * rows, rows)
        pair_of = [
            pltpu.make_async_copy(act_buf.at[at % 2], act_ref.at[target], act_sem.at[at]),
            pltpu.make_async_copy(slope_buf.at[at % 2], slope_ref.at[target], slope_sem.at[at]),
        ]
        for copy in pair_of:
            copy.start()
        stores.append(pair_of)

    keep(0)
    load.wait()
    multiply(0, 0, tiles)
    pair.wait_recv()
    multiply(0, tiles, tiles)
    store(0)
    outs = []
    for number in range(2 * tiles):
        copy = pltpu.make_async_copy(
            w_buf.at[number],
            full_ref.at[:, pl.ds(number * tile, tile)],
            out_sem.at[number],
        )
        copy.start()
        outs.append(copy)
    for at in range(len(masks)):
        copies[at].wait_recv()
    for number, (mask, half, goal) in enumerate(hops):
        at = len(masks) + number
        copy = remote(
            piece(masks.index(mask) + 1, half), piece(3, half), b_send.at[at], b_recv.at[at],
            across(goal),
        )
        copy.start()
        copies.append(copy)
    for at in range(1, quads):
        if at == 1 + len(masks):
            for copy in copies[len(masks) :]:
                copy.wait_recv()
        keep(at)
        if at >= 2:
            for copy in stores[at - 2]:
                copy.wait()
        multiply(at, 0, 2 * tiles)
        store(at)
    for copy in copies + [pair]:
        copy.wait_send()
    for copy in keeps + outs + sum(stores[-2:], []):
        copy.wait()


def hidden_gather(rows_own, weight, bias):
    groups = lax.axis_size("dp")
    quads = groups // 2
    rows, width = rows_own.shape
    tiles, _, tile = weight.shape
    units = 2 * tiles * tile
    pieces = len(two_hops(quads)) + len(direct_masks(quads))
    dma = pltpu.SemaphoreType.DMA
    vmem = pl.BlockSpec(memory_space=pltpu.VMEM)
    hbm = pl.BlockSpec(memory_space=pltpu.HBM)
    return pl.pallas_call(
        functools.partial(hidden_gather_kernel, groups=groups),
        in_specs=[vmem, hbm, vmem],
        out_specs=[hbm, hbm, hbm, hbm],
        out_shape=[
            jax.ShapeDtypeStruct((quads * rows, width), jnp.bfloat16),
            jax.ShapeDtypeStruct((quads * rows, units), jnp.bfloat16),
            jax.ShapeDtypeStruct((quads * rows, units), jnp.float32),
            jax.ShapeDtypeStruct((width, units), jnp.bfloat16),
        ],
        scratch_shapes=[
            pltpu.VMEM((quads * rows, width), jnp.bfloat16),
            pltpu.VMEM((2 * tiles, width, tile), jnp.bfloat16),
            pltpu.VMEM((2, rows, units), jnp.bfloat16),
            pltpu.VMEM((2, rows, units), jnp.float32),
            dma((pieces,)),
            dma((pieces,)),
            dma((quads,)),
            dma((quads,)),
            dma((quads,)),
            dma,
            dma((2,)),
            dma((2 * tiles,)),
        ],
        compiler_params=pltpu.CompilerParams(
            collective_id=2, has_side_effects=True, vmem_limit_bytes=VMEM_BYTES
        ),
        cost_estimate=pl.CostEstimate(
            flops=2 * quads * rows * width * units,
            bytes_accessed=200 * 2**20,
            transcendentals=0,
        ),
        name="hidden_gather",
    )(rows_own, weight, bias)


def inward_kernel(
    grad_ref, outer_ref, wide_ref, values_ref, own_ref, outer_sum, wide_sum, all_ref,
    near, far, pair_send, pair_recv, pair_load, hop_buf, in_buf, send, receive,
    outer_near, outer_far, outer_pair_send, outer_pair_recv, outer_load,
    outer_hop, outer_in, outer_send, outer_recv,
    wide_send, wide_recv, wide_load, *sum_refs,
    groups, slices
):
    quads = groups // 2
    me = lax.axis_index("dp")
    place = lax.axis_index("tensor")
    share = near.shape[1]
    half_rows = share // 2
    piece = wide_ref.shape[0]

    def across(mask):
        return (flip(me, mask), place)

    anyone, greet = everyone(groups, slices)
    greet()
    sum_start, sum_middle, sum_end = spread_sum(
        values_ref, all_ref, *sum_refs, anyone, groups, slices
    )

    def block_of(other):
        return grad_ref.at[pl.ds(pl.multiple_of(other * share, share), share)]

    def parts(block, side):
        if side is None:
            return near.at[block]
        return near.at[block, pl.ds(side * half_rows, half_rows)]

    start, finish = pair_reduce(
        quads, me, across, block_of, near, far, pair_send, pair_recv, pair_load
    )
    early, middle, end = square_reduce(
        quads, share, across, send, receive, parts, parts, hop_buf, in_buf
    )

    out_cols = outer_sum.shape[1]
    long = outer_near.shape[1]
    half_long = long // 2

    def outer_block(other):
        return outer_ref.at[:, pl.ds(pl.multiple_of(other * out_cols, out_cols), out_cols)]

    def outer_parts(block, side):
        if side is None:
            return outer_near.at[block]
        return outer_near.at[block, pl.ds(side * half_long, half_long)]

    outer_start, outer_finish = pair_reduce(
        quads, me, across, outer_block, outer_near, outer_far,
        outer_pair_send, outer_pair_recv, outer_load,
    )
    outer_early, outer_middle, outer_end = square_reduce(
        quads, long, across, outer_send, outer_recv, outer_parts, outer_parts, outer_hop, outer_in
    )
    def columns_of(other):
        return wide_ref.at[:, pl.ds(pl.multiple_of(other * share, share), share)]

    def rows_of(other):
        return wide_sum.at[pl.ds(pl.multiple_of(other * piece, piece), piece)]

    def wide_to(step):
        other = lax.rem(me + step, groups)
        return remote(
            columns_of(other), rows_of(me), wide_send.at[step], wide_recv.at[step], (other, place)
        )

    def wide_from(step):
        other = lax.rem(me + groups - step, groups)
        return remote(
            columns_of(other), rows_of(other), wide_send.at[step], wide_recv.at[step],
            (other, place),
        )

    order = [quads - 1] + list(range(1, quads - 1))
    outer_start()
    start()
    sum_start()
    for m in order:
        outer_finish(m)
        outer_early(m)
    for m in order:
        finish(m)
        early(m)
    wide_own = pltpu.make_async_copy(columns_of(me), rows_of(me), wide_load)
    wide_own.start()
    outer_finish(0)
    outer_middle()
    for step in range(1, groups):
        wide_to(step).start()
    finish(0)
    sum_middle()
    middle()
    outer_end()
    outer = outer_near[0].astype(jnp.float32)
    for at in range(len(direct_masks(quads))):
        outer = outer + outer_in[at].astype(jnp.float32)
    outer_sum[...] = outer.astype(outer_near.dtype)
    end()
    total = near[0].astype(jnp.float32)
    for at in range(len(direct_masks(quads))):
        total = total + in_buf[at].astype(jnp.float32)
    cols = own_ref.shape[2]
    for part in range(3):
        own_ref[part] = total[:, part * cols : (part + 1) * cols]
    wide_own.wait()
    for step in range(1, groups):
        wide_from(step).wait_recv()
        wide_to(step).wait_send()
    sum_end()


def inward_reduce(grad, outer, wide, values):
    groups = lax.axis_size("dp")
    slices = lax.axis_size("tensor")
    quads = groups // 2
    width = grad.shape[0]
    share = width // groups
    columns = grad.shape[1]
    piece = wide.shape[0]
    out_cols = outer.shape[1] // groups
    packed = sum_room(values)
    dma = pltpu.SemaphoreType.DMA
    vmem = pl.BlockSpec(memory_space=pltpu.VMEM)
    hbm = pl.BlockSpec(memory_space=pltpu.HBM)
    low = jnp.bfloat16

    def pair_scratch(rows, cols):
        return [
            pltpu.VMEM((quads, rows, cols), low),
            pltpu.VMEM((quads, rows, cols), low),
            dma((quads,)),
            dma((quads,)),
            dma((quads,)),
        ] + reduce_scratch(quads, rows, cols)

    return pl.pallas_call(
        functools.partial(inward_kernel, groups=groups, slices=slices),
        in_specs=[hbm, hbm, hbm, vmem],
        out_specs=[vmem, vmem, hbm, vmem],
        out_shape=[
            jax.ShapeDtypeStruct((3, share, columns // 3), jnp.float32),
            jax.ShapeDtypeStruct((width, out_cols), low),
            jax.ShapeDtypeStruct((groups * piece, share), low),
            jax.ShapeDtypeStruct(packed.shape, jnp.float32),
        ],
        scratch_shapes=pair_scratch(share, columns)
        + pair_scratch(width, out_cols)
        + [
            dma((groups,)),
            dma((groups,)),
            dma,
        ]
        + sum_scratch(groups * slices),
        compiler_params=pltpu.CompilerParams(
            collective_id=6, has_side_effects=True, vmem_limit_bytes=VMEM_BYTES
        ),
        cost_estimate=pl.CostEstimate(
            flops=8 * grad.size, bytes_accessed=250 * 2**20, transcendentals=0
        ),
        name="inward_reduce",
    )(grad, outer, wide, packed)


def swap(values, axis, mask):
    count = lax.axis_size(axis)
    return lax.ppermute(values, axis, [(i, i ^ mask) for i in range(count)])


def sum_room(values):
    count = lax.axis_size("dp") * lax.axis_size("tensor")
    room = count * 8 * 128
    packed = jnp.concatenate([values, jnp.zeros((room - values.shape[0],), jnp.float32)])
    return packed.reshape(count, 8, 128)


def sum_kernel(values_ref, out_ref, *scratch, groups, slices):
    anyone, greet = everyone(groups, slices)
    greet()
    start, middle, end = spread_sum(values_ref, out_ref, *scratch, anyone, groups, slices)
    start()
    middle()
    end()


def sum_everywhere(packed):
    groups = lax.axis_size("dp")
    slices = lax.axis_size("tensor")
    return pl.pallas_call(
        functools.partial(sum_kernel, groups=groups, slices=slices),
        in_specs=[pl.BlockSpec(memory_space=pltpu.VMEM)],
        out_specs=pl.BlockSpec(memory_space=pltpu.VMEM),
        out_shape=jax.ShapeDtypeStruct(packed.shape, jnp.float32),
        scratch_shapes=sum_scratch(groups * slices),
        compiler_params=pltpu.CompilerParams(
            collective_id=0, has_side_effects=True, vmem_limit_bytes=8 * 2**20
        ),
        cost_estimate=pl.CostEstimate(
            flops=packed.size, bytes_accessed=8 * packed.size, transcendentals=0
        ),
        name="sum_everywhere",
    )(packed)


def last_kernel(
    all_ref, factor_ref, late_ref, vectors_ref, first_ref, second_ref, bias_ref, slope_ref, *refs
):
    masters, directions = refs[:4], refs[4:8]
    fresh, halves = refs[8:12], refs[12:16]
    column_out, vectors_out, mean_out, square_out, square_late, norms_out = refs[16:22]
    buffers, load_sem = refs[22:30], refs[30]
    loads = [
        pltpu.make_async_copy(source, target, load_sem.at[at])
        for at, (source, target) in enumerate(zip(masters + directions, buffers))
    ]
    for load in loads:
        load.start()

    cols = bias_ref.shape[1]
    step = cols // 128
    lanes = first_ref.shape[1] // 128
    need = -(-(14 * step + 2 * lanes) // 8)
    rows = all_ref[0:need].reshape(need * 8, 128)

    def total(at):
        return jnp.sqrt(jnp.sum(rows[at * step : (at + 1) * step], keepdims=True))

    weight_norms = [total(at) for at in range(7)]
    update_norms = [total(7 + at) for at in range(7)]

    def rate(weight_norm, update_norm):
        return learn_rate * weight_norm / (update_norm + trust_epsilon)

    for at in range(4):
        loads[at].wait()
        loads[4 + at].wait()
        factor = rate(weight_norms[at], update_norms[at])
        master, direction = buffers[at], buffers[4 + at]
        length = master.shape[0]
        chunk = min(length, 32) if len(master.shape) == 3 and length > 4 else length
        if len(master.shape) == 2:
            chunk = min(length, 128)
        scale = factor.reshape((1,) * len(master.shape))
        for begin in range(0, length, chunk):
            part = slice(begin, begin + chunk)
            updated = master[part] - scale * direction[part]
            fresh[at][part] = updated
            halves[at][part] = updated.astype(jnp.bfloat16)
    for at, (begin, stop) in enumerate(((0, 1), (1, 2), (2, 6))):
        column_out[begin:stop, :] = bias_ref[begin:stop, :] - (
            rate(weight_norms[4 + at], update_norms[4 + at]) * slope_ref[begin:stop, :]
        )
    early = [
        jnp.concatenate(
            [rows[14 * step + row * lanes + at][None, :] for at in range(lanes)], axis=1
        )
        for row in range(2)
    ]
    slopes = jnp.concatenate(early + [late_ref[...]], axis=0) * factor_ref[0:1, 0:1]
    weights = vectors_ref[...]
    mean_new, square_new, direction = adapt_step(
        weights, first_ref[...], second_ref[...], slopes, 0.0
    )
    mean_out[...] = mean_new
    square_out[...] = square_new[0:2]
    square_late[...] = square_new[2:6]
    own = jnp.sqrt(jnp.sum(weights * weights, axis=1, keepdims=True))
    step_norms = jnp.sqrt(jnp.sum(direction * direction, axis=1, keepdims=True))
    vectors_out[...] = weights - rate(own, step_norms) * direction
    for row in range(6):
        weight_norms.append(own[row : row + 1])
        update_norms.append(step_norms[row : row + 1])
    lane = lax.broadcasted_iota(jnp.int32, (8, 128), 1)
    line = lax.broadcasted_iota(jnp.int32, (8, 128), 0)
    norms = jnp.zeros((8, 128), jnp.float32)
    for at in range(13):
        norms = jnp.where((lane == at) & (line == 0), weight_norms[at], norms)
        norms = jnp.where((lane == at) & (line == 1), update_norms[at], norms)
    norms_out[...] = norms[0:2, 0:13]


def last_step(values, factor, late, vectors, first, second, bias, slope, masters, directions):
    packed = sum_room(values)
    width = vectors.shape[1]
    wide = jnp.float32
    vmem = pl.BlockSpec(memory_space=pltpu.VMEM)
    hbm = pl.BlockSpec(memory_space=pltpu.HBM)

    masters = list(masters)
    directions = list(directions)
    masters[0] = masters[0].transpose(1, 0, 2)
    directions[0] = directions[0].transpose(1, 0, 2)
    shapes = [master.shape for master in masters]
    like = jax.ShapeDtypeStruct
    results = pl.pallas_call(
        last_kernel,
        in_specs=[vmem] * 8 + [hbm] * 8,
        out_specs=[vmem] * 14,
        out_shape=[like(shape, wide) for shape in shapes]
        + [like(shape, jnp.bfloat16) for shape in shapes]
        + [like(bias.shape, wide)]
        + [like((rows, width), wide) for rows in (6, 6, 2, 4)]
        + [like((2, 13), wide)],
        scratch_shapes=[pltpu.VMEM(shape, wide) for shape in shapes]
        + [pltpu.VMEM(shape, wide) for shape in shapes]
        + [pltpu.SemaphoreType.DMA((8,))],
        compiler_params=pltpu.CompilerParams(vmem_limit_bytes=VMEM_BYTES),
        cost_estimate=pl.CostEstimate(
            flops=packed.size, bytes_accessed=80 * 2**20, transcendentals=0
        ),
        name="last_step",
    )(
        sum_everywhere(packed),
        jnp.full((8, 128), factor),
        late,
        vectors,
        first,
        second,
        bias,
        slope,
        *masters,
        *directions,
    )
    fresh = list(results[:4])
    halves = list(results[4:8])
    fresh[0] = fresh[0].transpose(1, 0, 2)
    halves[0] = halves[0].transpose(1, 0, 2)
    return (fresh, halves) + tuple(results[8:14])


def after(values, gate):
    return lax.optimization_barrier((values, gate))[0]


def adapt_step(weight, moment_one, moment_two, slope, decay):
    mean_new = beta_one * moment_one + (1.0 - beta_one) * slope
    square_new = beta_two * moment_two + (1.0 - beta_two) * slope * slope
    direction = (
        mean_new
        / (1.0 - beta_one**STEP_COUNT)
        / (jnp.sqrt(square_new / (1.0 - beta_two**STEP_COUNT)) + adam_epsilon)
        + decay * weight
    )
    return (mean_new, square_new, direction)


def on_device(
    tokens,
    cotangent,
    live_mask,
    inward,
    inward_first,
    inward_second,
    outward,
    outward_first,
    outward_second,
    widening,
    widening_first,
    widening_second,
    narrowing,
    narrowing_first,
    narrowing_second,
    column_bias,
    column_first,
    column_second,
    vectors,
    vectors_first,
    vectors_second,
):
    low = jnp.bfloat16
    wide = jnp.float32
    amount, width = tokens.shape
    cols = column_bias.shape[1]
    groups = lax.axis_size("dp")
    slices = lax.axis_size("tensor")
    me = lax.axis_index("dp")
    place = lax.axis_index("tensor")
    share = inward.shape[0]
    piece = 4 * cols // groups

    inputs = tokens.astype(wide)
    living_here = live_mask.astype(wide)
    mixed_bias = jnp.concatenate(
        [column_bias[0], jnp.zeros((cols,), wide), column_bias[1]]
    ).reshape(1, 3 * cols)
    small_length = amount + 4 * cols
    small_rows = -(-small_length // 1024) * 8
    small = jnp.concatenate(
        [
            living_here,
            column_bias[2:].reshape(4 * cols),
            jnp.zeros((small_rows * 128 - small_length,), wide),
        ]
    ).reshape(small_rows, 128)
    (
        normed_full,
        inward_full,
        mixed,
        back_all,
        small_all,
        counts,
        wide_own,
        thin_own,
        outward_full,
    ) = open_step(
        tokens,
        inward,
        cotangent,
        living_here[:, None],
        vectors[0:2],
        mixed_bias,
        small,
        jnp.full((8, 128), jnp.sum(living_here)),
        widening,
        narrowing,
        outward,
    )
    factor = 1.0 / jnp.sum(counts[:, 0, 0])
    small_all = small_all.reshape(slices, small_rows * 128)
    length = normed_full.shape[0]
    bias_keys = jnp.where(small_all[:, :amount].reshape(length) > 0.5, 0.0, MASKED)
    bias_all = small_all[:, amount:small_length]

    if piece % 128:
        wide_own = wide_own.transpose(1, 0, 2).reshape(1, width, slices * piece)

    hidden_bias = jnp.concatenate(
        [
            lax.dynamic_slice_in_dim(bias_all, (me ^ side) * piece, piece, 1).reshape(1, -1)
            for side in range(2)
        ],
        axis=1,
    )

    context_wide, totals, context_own, back_all = attend_forward(
        mixed, bias_keys[None, :], back_all, amount
    )
    thin_own = lax.all_gather(
        after(thin_own, context_own), "tensor", axis=0, tiled=True
    )
    middle = inputs + dot_as(context_own, outward_full, PLAIN) + vectors[2]
    normed_two = layer_norm(middle, vectors[3], vectors[4]).astype(low)

    rows_two_all, active_all, slope, widening_full = hidden_gather(
        normed_two, wide_own, hidden_bias
    )
    half_units = slices * piece

    def pair_sum(left, right, apart):
        other = left(slice(half_units, None), right, low)
        if apart:
            own = left(slice(0, half_units), after(right, other), low)
            own, other = lax.optimization_barrier((own, swap(other, "dp", 1)))
            return (own.astype(wide) + other.astype(wide)).astype(low)
        own = left(slice(0, half_units), after(right, other), wide)
        return (own + swap(other, "dp", 1).astype(wide)).astype(low)

    slope_narrowing = pair_sum(
        lambda part, right, kind: dot_as(active_all[:, part], right, TOKENS, kind),
        after(back_all, thin_own),
        False,
    )
    back_normed_two, back_hidden_all, hidden_sums, widened_all, thin_parts = back_step(
        back_all, slope, thin_own, widening_full, slope_narrowing, active_all
    )
    thin_slope = jnp.sum(thin_parts.astype(wide), axis=0).astype(low)
    slope_widening = pair_sum(
        lambda part, right, kind: dot_as(back_hidden_all[:, part], right, TOKENS, kind),
        rows_two_all,
        True,
    )
    wide_slope = lax.psum_scatter(slope_widening, "tensor", scatter_dimension=0, tiled=True)

    _, norm_two_pull = jax.vjp(layer_norm, middle, vectors[3], vectors[4])
    back_middle_norm, slope_gain_two, slope_shift_two = norm_two_pull(back_normed_two)
    back_out = back_all[:amount]
    back_middle = back_out.astype(wide) + back_middle_norm
    back_low = back_middle.astype(low)

    back_mixed, widened, sum_narrowing = attend_backward(
        after(back_low, slope_widening),
        outward_full,
        mixed,
        context_wide,
        totals,
        bias_keys[:, None],
        widened_all,
        thin_slope,
    )
    layer_output = (middle + widened + vectors[5]).astype(low)

    back_normed_part = dot_as(back_mixed, inward_full, ROWS, low)
    back_normed = lax.psum_scatter(
        after(back_normed_part, wide_slope), "tensor", scatter_dimension=0, tiled=True
    )
    back_mixed = after(back_mixed, back_normed_part)
    slope_inward = dot_as(normed_full, back_mixed, TOKENS, low)
    slope_outward = dot_as(after(context_own, slope_inward), back_low, TOKENS, low)
    hidden_total = hidden_sums.reshape(2, 1, slices, piece)
    hidden_slots = jnp.zeros((groups, slices, piece), wide)
    hidden_slots = lax.dynamic_update_slice(hidden_slots, hidden_total[0], (me, 0, 0))
    hidden_slots = lax.dynamic_update_slice(hidden_slots, hidden_total[1], (me ^ 1, 0, 0))
    mixed_sums = jnp.stack(
        [
            jnp.sum(back_mixed[:, :cols], axis=0, dtype=wide),
            jnp.sum(back_mixed[:, 2 * cols :], axis=0, dtype=wide),
        ]
    )
    mixed_slots = lax.dynamic_update_slice(
        jnp.zeros((slices, 2, cols), wide), mixed_sums[None], (place, 0, 0)
    )
    late_rows = jnp.stack(
        [
            jnp.sum(back_middle, axis=0),
            slope_gain_two,
            slope_shift_two,
            jnp.sum(back_out, axis=0, dtype=wide),
        ]
    )
    packed = jnp.concatenate(
        [hidden_slots.reshape(-1), mixed_slots.reshape(-1), late_rows.reshape(-1)]
    )
    amount_packed = packed.shape[0]
    sum_inward, sum_outward, sum_widening, packed = inward_reduce(
        slope_inward, slope_outward, wide_slope, packed
    )
    packed = packed.reshape(-1)[:amount_packed]
    out_rows = outward.shape[0]

    def outer_rows(other):
        return lax.dynamic_slice_in_dim(sum_outward, other * out_rows, out_rows, 0)

    moved = [swap(outer_rows(place ^ m), "tensor", m) for m in range(1, slices)]
    moved = [outer_rows(place)] + moved
    sum_outward = functools.reduce(jnp.add, [part.astype(wide) for part in moved])
    sum_inward = sum_inward.transpose(1, 0, 2)
    sum_widening = sum_widening.T.reshape(widening.shape)
    sum_narrowing = sum_narrowing.reshape(narrowing.shape)

    first_cut = groups * slices * piece
    second_cut = first_cut + slices * 2 * cols
    hidden_slots = packed[:first_cut].reshape(groups, slices, piece)
    hidden_rows = lax.dynamic_slice_in_dim(hidden_slots, place, 1, 1).reshape(4, cols)
    mixed_rows = lax.dynamic_index_in_dim(
        packed[first_cut:second_cut].reshape(slices, 2, cols), place, 0, keepdims=False
    )
    late_rows = packed[second_cut:].reshape(4, width)
    column_total = jnp.concatenate([mixed_rows, hidden_rows], axis=0)

    column_bias, vectors = after((column_bias, vectors), back_low)
    masters = (inward, outward, widening, narrowing)
    firsts = (inward_first, outward_first, widening_first, narrowing_first)
    seconds = (inward_second, outward_second, widening_second, narrowing_second)
    orders = ((1, 0, 2), (0, 1), (0, 1, 2), (0, 1, 2))
    summed_all = [
        with_layout_constraint(summed, Layout(order)).astype(wide)
        for summed, order in zip(
            (sum_inward, sum_outward, sum_widening, sum_narrowing), orders
        )
    ]
    matrix_steps = [
        adapt_step(
            masters[ordinal],
            firsts[ordinal],
            seconds[ordinal],
            summed_all[ordinal] * factor,
            decay_rate,
        )
        for ordinal in range(4)
    ]
    column_mean, column_square, column_direction = adapt_step(
        column_bias, column_first, column_second, column_total * factor, 0.0
    )
    column_groups = ((0, 1), (1, 2), (2, 6))

    def square_sum(array):
        lanes = jnp.sum(array * array, axis=tuple(range(array.ndim - 1)))
        return jnp.concatenate([lanes, jnp.zeros((cols - lanes.shape[0],), wide)])

    squares = [square_sum(master) for master in masters]
    squares += [square_sum(column_bias[start:stop]) / groups for start, stop in column_groups]
    squares += [square_sum(step[2]) for step in matrix_steps]
    squares += [square_sum(column_direction[start:stop]) / groups for start, stop in column_groups]
    squares = jnp.concatenate(squares)

    _, norm_one_pull = jax.vjp(layer_norm, inputs, vectors[0], vectors[1])
    back_inputs_norm, slope_gain_one, slope_shift_one = norm_one_pull(
        after(back_normed, squares).astype(wide)
    )
    back_inputs = back_middle + back_inputs_norm
    (
        fresh,
        halves,
        new_column,
        new_vectors,
        vectors_mean,
        first_square,
        vectors_square,
        trust_norms,
    ) = last_step(
        jnp.concatenate([squares, slope_gain_one, slope_shift_one]),
        factor,
        late_rows,
        vectors,
        vectors_first,
        vectors_second,
        column_bias,
        column_direction,
        masters,
        [step[2] for step in matrix_steps],
    )
    results = []
    for ordinal in range(4):
        results += [
            fresh[ordinal],
            matrix_steps[ordinal][0],
            matrix_steps[ordinal][1],
            halves[ordinal],
        ]
    return (
        layer_output,
        back_inputs * factor,
        *results,
        new_column,
        column_mean,
        column_square[0],
        column_square[1],
        column_square[2:],
        new_vectors,
        vectors_mean,
        first_square,
        vectors_square,
        trust_norms,
    )


def solution(mesh):
    in_specs = (
        P(("dp", "tensor"), None),
        P(("dp", "tensor"), None),
        P(("dp", "tensor")),
        P("dp", None, "tensor"),
        P("dp", None, "tensor"),
        P("dp", None, "tensor"),
        P("tensor", "dp"),
        P("tensor", "dp"),
        P("tensor", "dp"),
        P("dp", None, "tensor"),
        P("dp", None, "tensor"),
        P("dp", None, "tensor"),
        P(None, "tensor", "dp"),
        P(None, "tensor", "dp"),
        P(None, "tensor", "dp"),
        P(None, "tensor"),
        P(None, "tensor"),
        P(None, "tensor"),
        P(),
        P(),
        P(),
    )
    out_specs = (
        P(("dp", "tensor"), None),
        P(("dp", "tensor"), None),
        P("dp", None, "tensor"),
        P("dp", None, "tensor"),
        P("dp", None, "tensor"),
        P("dp", None, "tensor"),
        P("tensor", "dp"),
        P("tensor", "dp"),
        P("tensor", "dp"),
        P("tensor", "dp"),
        P("dp", None, "tensor"),
        P("dp", None, "tensor"),
        P("dp", None, "tensor"),
        P("dp", None, "tensor"),
        P(None, "tensor", "dp"),
        P(None, "tensor", "dp"),
        P(None, "tensor", "dp"),
        P(None, "tensor", "dp"),
        P(None, "tensor"),
        P(None, "tensor"),
        P("tensor"),
        P("tensor"),
        P(None, "tensor"),
        P(),
        P(),
        P(),
        P(),
        P(),
    )
    return jax.shard_map(
        on_device, mesh=mesh, in_specs=in_specs, out_specs=out_specs, check_vma=False
    )
```
